32 devices in a mesh: rep: 2 (over x), pool: 2 (over core), tp: 8 (over z, y).
Axes of the slice: x: 2, y: 2, z: 4, core: 2. Of those that a mesh axis runs over, the one named last changes fastest.
Arguments:
- prompt_x: bfloat16 [8192, 5120], P(('rep', 'pool')), parts along dimension 0, may hold values from -40 to 40
- q_weight: bfloat16 [5120, 4096], P(None, 'tp'), may hold values from -0.078125 to 0.078125
- kv_weight: bfloat16 [5120, 2048], P(None, 'tp'), may hold values from -0.078125 to 0.078125
- prompt_blocks: int32 [4, 3], P('rep'), parts along dimension 0, may hold values from 1 to 8, as said below
- finished: int32 [4, 3], P('rep'), parts along dimension 0, may hold values from 0 to 1, as said below
- placement: int32 [4, 16, 2], P('rep'), parts along dimension 0, may hold values from 0 to 7, as said below
- page_table: int32 [96, 2], P(('rep', 'pool', 'tp')), parts along dimension 0, may hold values from 0 to 5, as said below
- row_lens: int32 [96], P(('rep', 'pool', 'tp')), parts along dimension 0, may hold values from 128 to 256, as said below
- kv_cache: bfloat16 [192, 128, 2048], P(('rep', 'pool', 'tp')), parts along dimension 0, may hold values from -40 to 40
- decode_x: bfloat16 [2, 96, 5120], P(None, ('rep', 'pool')), parts along dimension 1, may hold values from -40 to 40
Outputs:
- prompt_attn: bfloat16 [8192, 4096], P(('rep', 'pool'), 'tp'), parts along dimension 0
- decode_attn: bfloat16 [2, 96, 4096], P(None, ('rep', 'pool', 'tp')), parts along dimension 1
The draws below stay inside these ranges and needn't reach their ends.
There are 2 independent parts, one for each index of `rep`. The reference program is written for one: setup_inputs(seed, part) draws one part's arguments, and reference() takes and returns one part's arrays. A program takes and returns all parts, laid end to end along the dimension named above; an argument that names none is the same for every part. Nothing has to cross between parts.
Inputs may be any that keep to these rules, and one draw needn't show every extreme that they name: `prompt_blocks`: the counts of each group sum to 16; in each group one prompt holds exactly 8 blocks. Every group has at least one finished prompt. placement[g, b, 0] is a device index on tp of group 1 - g and placement[g, b, 1] a slot there; no two blocks of a group share a device and slot; a device receives at most 3 blocks of a group, and one device receives exactly 3; each named slot is a page of some row owned by that device. `page_table`: the rows of one device name each of its 6 slots exactly once. `row_lens`: both bounds are reached in every draw.
All inputs are finite; a program needn't handle non-finite values.
Results may differ from the reference program's by a relative error of at most 0.006.
The reference program's roundings to bfloat16 on the way count: a program that leaves them out, or rounds other values in their place, can miss the bound.
Values may be sent and summed in bfloat16 or wider, within the bound.
No kernel may reach another device: no remote copies, remote signals or barrier semaphores. Data moves between devices by JAX's collectives and lax.ppermute only.
A program may use at most 256 MiB of HBM per device.

```python
import math
import jax
import jax.numpy as jnp
from jax import lax

D = 5120
QH = 32
KVH = 8
HD = 128
BLOCK_TOKENS = 128
PTOK = 2048
NPROMPT = 3
ROWS_DEV = 3
PAGES = 2
STEPS = 2
NBLK = 16
DEVICE_SLOTS = 6
KEY_VALUE_COLUMNS = 2048
ALL_ROWS = 48
ALL_SLOTS = 96
N_TP = 8


def rough(key, extent, lowest, highest):
    first_key, second_key = jax.random.split(key)
    values = jax.random.truncated_normal(first_key, -4.0, 4.0, extent, jnp.float32)
    scales = jnp.exp(jax.random.uniform(second_key, extent[:-1] + (1,), jnp.float32, math.log(lowest), math.log(highest)))
    return values * scales


def page_layout(key):
    devices = 2 * N_TP
    slot_random_keys = jax.random.split(jax.random.fold_in(key, 11), devices)
    slot_ranking = jax.vmap(lambda single_random_key: jax.random.permutation(single_random_key, DEVICE_SLOTS))(slot_random_keys)
    page_ids = slot_ranking.reshape(devices, ROWS_DEV, PAGES).astype(jnp.int32)
    placed = []
    for sender_rows in range(2):
        group_key = jax.random.fold_in(key, 20 + sender_rows)
        order_key, device_key, row_key = jax.random.split(group_key, 3)
        order = jax.random.permutation(order_key, NBLK)
        chosen = jax.random.permutation(device_key, N_TP)
        receiver_rows = chosen[jnp.maximum(order - 1, 0) % N_TP].astype(jnp.int32)
        blocks_idx = jnp.arange(NBLK)
        earlier = (receiver_rows[None, :] == receiver_rows[:, None]) & (blocks_idx[None, :] < blocks_idx[:, None])
        arrival = jnp.sum(earlier.astype(jnp.int32), axis=1)
        row_keys = jax.random.split(row_key, N_TP)
        row_order = jax.vmap(lambda single_random_key: jax.random.permutation(single_random_key, ROWS_DEV))(row_keys)
        row_pick = row_order[receiver_rows, arrival % ROWS_DEV]
        page_pick = arrival // ROWS_DEV
        slot_numbers = page_ids[(1 - sender_rows) * N_TP + receiver_rows, row_pick, page_pick]
        placed.append(jnp.stack([receiver_rows, slot_numbers.astype(jnp.int32)], axis=1))
    return (page_ids.reshape(devices * ROWS_DEV, PAGES), jnp.stack(placed, axis=0).astype(jnp.int32))


def draw_page_table(key, part):
    shared = page_layout(key)
    return shared[0]


def draw_placement(key, part):
    shared = page_layout(key)
    return shared[1]


def draw_prompt_blocks(key, part):
    key = jax.random.fold_in(key, 8)
    first_key, second_key = jax.random.split(key)
    big_at = jax.random.randint(first_key, (2,), 0, NPROMPT)
    remaining = NBLK - NBLK // 2
    cut = jax.random.randint(second_key, (2,), 1, remaining)
    after = (jnp.arange(NPROMPT)[None, :] - big_at[:, None]) % NPROMPT
    blocks = jnp.where(after == 0, NBLK // 2, jnp.where(after == 1, cut[:, None], remaining - cut[:, None]))
    return blocks.astype(jnp.int32)


def draw_row_lens(key, part):
    key = jax.random.fold_in(key, 3)
    first_key, second_key = jax.random.split(key)
    lengths = jax.random.randint(first_key, (ALL_ROWS,), BLOCK_TOKENS, PAGES * BLOCK_TOKENS + 1)
    picks = jax.random.permutation(second_key, ALL_ROWS)
    lengths = lengths.at[picks[0]].set(PAGES * BLOCK_TOKENS).at[picks[1]].set(BLOCK_TOKENS)
    return lengths.astype(jnp.int32)


def draw_finished(key, part):
    key = jax.random.fold_in(key, 4)
    first_key, second_key = jax.random.split(key)
    bits = jax.random.randint(first_key, (2, NPROMPT), 0, 2)
    which = jax.random.randint(second_key, (2,), 0, NPROMPT)
    forced = (jnp.arange(NPROMPT)[None, :] == which[:, None]).astype(jnp.int32)
    return jnp.maximum(bits, forced).astype(jnp.int32)


def draw_prompt_x(key, part):
    key = jax.random.fold_in(key, 5)
    return rough(key, (2 * PTOK, D), 0.5, 2.0).astype(jnp.bfloat16)


def draw_decode_x(key, part):
    key = jax.random.fold_in(key, 6)
    return rough(key, (STEPS, ALL_ROWS, D), 0.5, 2.0).astype(jnp.bfloat16)


def draw_kv_cache(key, part):
    key = jax.random.fold_in(key, 7)
    return rough(key, (ALL_SLOTS, BLOCK_TOKENS, KEY_VALUE_COLUMNS), 0.5, 2.0).astype(jnp.bfloat16)


def shard_levels(rng, shape, cuts, least, high):
    factor_of, own = 1.0, jax.random.fold_in(rng, 6)
    for axis_at, shards_of in cuts:
        steps = jnp.exp(jax.random.uniform(jax.random.fold_in(own, axis_at), (shards_of,), jnp.float32, least / len(cuts), high / len(cuts)))
        factor_of = factor_of * jnp.repeat(steps, shape[axis_at] // shards_of).reshape([-1 if axis == axis_at else 1 for axis in range(len(shape))])
    return factor_of


def noise(stream_key, shape, scale, most, cuts=(), dtype=jnp.bfloat16):
    drawn = scale * jax.random.normal(stream_key, shape, jnp.float32)
    if cuts:
        drawn = drawn * shard_levels(stream_key, shape, cuts, -0.22, 0.18)
    return jnp.clip(drawn, -most, most).astype(dtype)


def setup_inputs(seed: int = 0, part: int = 0) -> dict:
    key_of = jax.random.split(jax.random.key(seed), 11)
    own_keys = jax.random.split(jax.random.fold_in(key_of[10], part), 11)
    prompt_x = draw_prompt_x(jax.random.fold_in(jax.random.fold_in(key_of[10], part), 71), part)
    q_weight = noise(key_of[1], (D, QH * HD), D ** -0.5, 0.078125, ((1, 8),))
    kv_weight = noise(key_of[2], (D, KEY_VALUE_COLUMNS), D ** -0.5, 0.078125, ((1, 8),))
    prompt_blocks = draw_prompt_blocks(jax.random.fold_in(jax.random.fold_in(key_of[10], part), 71), part)
    finished = draw_finished(jax.random.fold_in(jax.random.fold_in(key_of[10], part), 71), part)
    placement = draw_placement(jax.random.fold_in(jax.random.fold_in(key_of[10], part), 71), part)
    page_table = draw_page_table(jax.random.fold_in(jax.random.fold_in(key_of[10], part), 71), part)
    row_lens = draw_row_lens(jax.random.fold_in(jax.random.fold_in(key_of[10], part), 71), part)
    kv_cache = draw_kv_cache(jax.random.fold_in(jax.random.fold_in(key_of[10], part), 71), part)
    decode_x = draw_decode_x(jax.random.fold_in(jax.random.fold_in(key_of[10], part), 71), part)
    return {"prompt_x": prompt_x, "q_weight": q_weight, "kv_weight": kv_weight, "prompt_blocks": prompt_blocks, "finished": finished, "placement": placement, "page_table": page_table, "row_lens": row_lens, "kv_cache": kv_cache, "decode_x": decode_x}


def block_table(prompt_blocks, finished, placement, sender_rows):
    prompt_end = jnp.cumsum(prompt_blocks[sender_rows])
    blocks_idx = jnp.arange(NBLK)
    owner_of = jnp.sum((blocks_idx[:, None] >= prompt_end[None, :]).astype(jnp.int32), axis=1)
    is_live = jnp.take(finished[sender_rows], owner_of)
    return placement[sender_rows, :, 0], placement[sender_rows, :, 1], is_live


def decode_rows(queries, fresh, slots_of, table, length):
    rows_dev = table.shape[0]
    context_len = PAGES * BLOCK_TOKENS
    score_scale = HD ** -0.5
    context = slots_of[table.reshape(-1)].reshape(rows_dev, context_len, KVH, 2, HD).astype(jnp.float32)
    q_full = queries.astype(jnp.float32)
    new_full = fresh.astype(jnp.float32)
    old_scores = jnp.einsum("srhgd,rthd->srhgt", q_full, context[:, :, :, 0]) * score_scale
    usable = jnp.arange(context_len)[None, :] < length[:, None]
    old_scores = jnp.where(usable[None, :, None, None, :], old_scores, -jnp.inf)
    new_scores = jnp.einsum("srhgd,urhd->srhgu", q_full, new_full[:, :, :, 0]) * score_scale
    visible = jnp.arange(STEPS)[None, :] <= jnp.arange(STEPS)[:, None]
    new_scores = jnp.where(visible[:, None, None, None, :], new_scores, -jnp.inf)
    row_peak = jnp.maximum(jnp.max(old_scores, axis=-1), jnp.max(new_scores, axis=-1))[..., None]
    old_raised = jnp.exp(old_scores - row_peak)
    new_raised = jnp.exp(new_scores - row_peak)
    totals = jnp.sum(old_raised, axis=-1, keepdims=True) + jnp.sum(new_raised, axis=-1, keepdims=True)
    old_weights = lax.optimization_barrier((old_raised / totals).astype(jnp.bfloat16)).astype(jnp.float32)
    new_weights = lax.optimization_barrier((new_raised / totals).astype(jnp.bfloat16)).astype(jnp.float32)
    blended = jnp.einsum("srhgt,rthd->srhgd", old_weights, context[:, :, :, 1])
    blended = blended + jnp.einsum("srhgu,urhd->srhgd", new_weights, new_full[:, :, :, 1])
    return blended.astype(jnp.bfloat16).reshape(STEPS, rows_dev, QH * HD)


def reference(prompt_x, q_weight, kv_weight, prompt_blocks, finished, placement, page_table, row_lens, kv_cache, decode_x):
    score_scale = HD ** -0.5
    q_per_kv = QH // KVH
    position = jnp.arange(PTOK)
    outputs = []
    refreshed_cache = kv_cache
    for sender_rows in range(2):
        inputs = prompt_x[sender_rows * PTOK:(sender_rows + 1) * PTOK]
        queries = jnp.dot(inputs, q_weight, preferred_element_type=jnp.float32).astype(jnp.bfloat16)
        keys_vals = jnp.dot(inputs, kv_weight, preferred_element_type=jnp.float32).astype(jnp.bfloat16)
        prompt_end = jnp.cumsum(prompt_blocks[sender_rows]) * BLOCK_TOKENS
        segment = jnp.sum((position[:, None] >= prompt_end[None, :]).astype(jnp.int32), axis=1)
        allowed = (segment[:, None] == segment[None, :]) & (position[:, None] >= position[None, :])
        head_q = queries.reshape(PTOK, KVH, q_per_kv, HD).astype(jnp.float32)
        kv_split = keys_vals.reshape(PTOK, KVH, 2, HD).astype(jnp.float32)
        scores = jnp.einsum("ihgd,jhd->hgij", head_q, kv_split[:, :, 0]) * score_scale
        scores = jnp.where(allowed[None, None], scores, -jnp.inf)
        row_peak = jnp.max(scores, axis=-1, keepdims=True)
        raised = jnp.exp(scores - row_peak)
        weights = lax.optimization_barrier((raised / jnp.sum(raised, axis=-1, keepdims=True)).astype(jnp.bfloat16))
        blended = jnp.einsum("hgij,jhd->ihgd", weights.astype(jnp.float32), kv_split[:, :, 1])
        outputs.append(blended.astype(jnp.bfloat16).reshape(PTOK, QH * HD))
        receiver_rows, slot_numbers, is_live = block_table(prompt_blocks, finished, placement, sender_rows)
        flattened_index = (((1 - sender_rows) * N_TP + receiver_rows) * DEVICE_SLOTS + slot_numbers).astype(jnp.int32)
        blocks = keys_vals.reshape(NBLK, BLOCK_TOKENS, KEY_VALUE_COLUMNS)
        kept = refreshed_cache[flattened_index]
        refreshed_cache = refreshed_cache.at[flattened_index].set(jnp.where(is_live[:, None, None] > 0, blocks, kept))
    prompt_attn = jnp.concatenate(outputs, axis=0)
    rows_in = decode_x.reshape(STEPS * ALL_ROWS, D)
    decode_q = jnp.dot(rows_in, q_weight, preferred_element_type=jnp.float32).astype(jnp.bfloat16)
    decode_kv = jnp.dot(rows_in, kv_weight, preferred_element_type=jnp.float32).astype(jnp.bfloat16)
    decode_q = jnp.moveaxis(decode_q.reshape(STEPS, 2 * N_TP, ROWS_DEV, KVH, q_per_kv, HD), 1, 0)
    decode_kv = jnp.moveaxis(decode_kv.reshape(STEPS, 2 * N_TP, ROWS_DEV, KVH, 2, HD), 1, 0)
    device_share = refreshed_cache.reshape(2 * N_TP, DEVICE_SLOTS, BLOCK_TOKENS, KEY_VALUE_COLUMNS)
    tables = page_table.reshape(2 * N_TP, ROWS_DEV, PAGES)
    lengths = row_lens.reshape(2 * N_TP, ROWS_DEV)

    def one_device(operands):
        return decode_rows(*operands)

    result = lax.map(one_device, (decode_q, decode_kv, device_share, tables, lengths))
    decode_attn = jnp.moveaxis(result, 0, 1).reshape(STEPS, ALL_ROWS, QH * HD)
    return prompt_attn, decode_attn
```

```python
import functools

import jax
import jax.numpy as jnp
from jax import lax
from jax.experimental import pallas as pl
from jax.experimental.pallas import tpu as pltpu
from jax.sharding import PartitionSpec as P

QH = 32
KVH = 8
GQ = QH // KVH
HD = 128
BLOCK_TOKENS = 128
PTOK = 2048
NPROMPT = 3
MOST_BLOCKS = 8
PAGES = 2
STEPS = 2
NBLK = 16
DEVICE_SLOTS = 6
ROWS_DEV = 3
GROUP_ROWS = 8
KEY_VALUE_COLUMNS = 2048
SCALE = HD ** (-0.5)
MASKED = -1e30
PIECES = 5
MIB = 1 << 20
VMEM = pltpu.VMEM
SMEM = pltpu.SMEM


def dot(a, b):
    return jnp.dot(a, b, preferred_element_type=jnp.float32)


def dot_t(a, b):
    return lax.dot_general(a, b, (((1,), (1,)), ((), ())), preferred_element_type=jnp.float32)


def iota(shape, axis):
    return lax.broadcasted_iota(jnp.int32, shape, axis)


def row_of(rs):
    return jnp.where(rs >= 2 * ROWS_DEV, ROWS_DEV, jnp.where(rs >= ROWS_DEV, rs - ROWS_DEV, rs))


def project(first, n, lq, *refs):
    if first:
        dx_ref, x_ref, wq_hbm, wkv_hbm, q_ref, kv_ref, qh_ref = refs[:7]
        out_msgs = refs[7 : 7 + n]
        wq, wkv, sems, held = refs[7 + n :]
    else:
        x_ref, wq_hbm, wkv_hbm, _, _, q_ref, kv_ref, wq, wkv, sems = refs
    piece = wq.shape[0] // PIECES

    def copies(c):
        part = pl.ds(c * piece, piece)
        return (
            pltpu.make_async_copy(wq_hbm.at[part], wq.at[part], sems.at[0, c]),
            pltpu.make_async_copy(wkv_hbm.at[part], wkv.at[part], sems.at[1, c]),
        )

    @pl.when(pl.program_id(0) == 0)
    def _():
        for c in range(PIECES):
            for copy in copies(c):
                copy.start()
        totals = [0.0] * 4
        for c in range(PIECES):
            for copy in copies(c):
                copy.wait()
            part = slice(c * piece, (c + 1) * piece)
            x = x_ref[:, part]
            totals[0] += dot(x, wq[part, :])
            totals[1] += dot(x, wkv[part, :])
            if first:
                dx = dx_ref[:, part]
                totals[2] += dot(dx, wq[part, :])
                totals[3] += dot(dx, wkv[part, :])
        q_ref[...] = totals[0].astype(jnp.bfloat16)
        kv_ref[...] = totals[1].astype(jnp.bfloat16)
        if first:
            me = lax.axis_index("tp")
            rows = STEPS * ROWS_DEV * n
            shape = (n * GROUP_ROWS, rows)
            to, fro = iota(shape, 0), iota(shape, 1)
            owner, rs = to // GROUP_ROWS, to % GROUP_ROWS
            late = rs >= ROWS_DEV
            wanted = owner * ROWS_DEV + row_of(rs) + jnp.where(late, ROWS_DEV * n, 0)
            pick = ((fro == wanted) & (rs < STEPS * ROWS_DEV)).astype(jnp.float32).astype(jnp.bfloat16)
            dq = dot(pick, totals[2].astype(jnp.bfloat16))
            dkv = dot(pick, totals[3].astype(jnp.bfloat16))
            cq = lq * HD
            held[:, :cq] = dq
            held[:, cq:] = dkv
            for h in range(lq):
                part = slice(h * n * GROUP_ROWS, (h + 1) * n * GROUP_ROWS)
                qh_ref[part, :] = dq[:, h * HD : (h + 1) * HD].astype(jnp.bfloat16)
            for d in range(n):
                to = lax.rem(me + d, n)
                out_msgs[d][...] = held[pl.ds(pl.multiple_of(to * GROUP_ROWS, GROUP_ROWS), GROUP_ROWS), :]

    @pl.when(pl.program_id(0) > 0)
    def _():
        x = x_ref[...]
        q_ref[...] = dot(x, wq[...]).astype(jnp.bfloat16)
        kv_ref[...] = dot(x, wkv[...]).astype(jnp.bfloat16)


def project_rows(x, wq, wkv, start, count, block, held=None, dx=None, n=None):
    rows, depth = x.shape
    cq, ckv = wq.shape[1], wkv.shape[1]
    lq = cq // HD
    first = held is None
    offset = start // block
    out_shape = [
        jax.ShapeDtypeStruct((rows, cq), jnp.bfloat16),
        jax.ShapeDtypeStruct((rows, ckv), jnp.bfloat16),
    ]
    out_specs = [
        pl.BlockSpec((block, cq), lambda i: (i + offset, 0)),
        pl.BlockSpec((block, ckv), lambda i: (i + offset, 0)),
    ]
    any_spec = pl.BlockSpec(memory_space=pl.ANY)
    x_spec = pl.BlockSpec((block, depth), lambda i: (i + offset, 0))
    scratch = [
        VMEM((depth, cq), jnp.bfloat16),
        VMEM((depth, ckv), jnp.bfloat16),
        pltpu.SemaphoreType.DMA((2, PIECES)),
    ]
    if first:
        whole = pl.BlockSpec(dx.shape, lambda i: (0, 0))
        args = (dx, x, wq, wkv)
        in_specs = [whole, x_spec, any_spec, any_spec]
        out_shape.append(jax.ShapeDtypeStruct((lq * n * GROUP_ROWS, HD), jnp.bfloat16))
        out_specs.append(pl.BlockSpec((lq * n * GROUP_ROWS, HD), lambda i: (0, 0)))
        for _ in range(n):
            out_shape.append(jax.ShapeDtypeStruct((GROUP_ROWS, cq + ckv), jnp.float32))
            out_specs.append(pl.BlockSpec((GROUP_ROWS, cq + ckv), lambda i: (0, 0)))
        scratch.append(VMEM((n * GROUP_ROWS, cq + ckv), jnp.float32))
        aliases = {}
    else:
        args = (x, wq, wkv) + held
        in_specs = [x_spec] + [any_spec] * 4
        aliases = {3: 0, 4: 1}
    return pl.pallas_call(
        functools.partial(project, first, n, lq),
        grid=(count // block,),
        in_specs=in_specs,
        out_specs=out_specs,
        out_shape=out_shape,
        scratch_shapes=scratch,
        input_output_aliases=aliases,
        compiler_params=pltpu.CompilerParams(vmem_limit_bytes=40 * MIB),
        cost_estimate=pl.CostEstimate(
            flops=2 * count * depth * (cq + ckv),
            bytes_accessed=2 * (count + cq + ckv) * depth + 2 * count * (cq + ckv),
            transcendentals=0,
        ),
        name="project_first" if first else "project",
    )(*args)


def attend_prompt(lq, counts, q_ref, kv_ref, o_ref):
    group = lax.axis_index("pool")
    i = pl.program_id(0)
    first_end = counts[group, 0]
    second_end = first_end + counts[group, 1]
    start = jnp.where(i < first_end, 0, jnp.where(i < second_end, first_end, second_end))
    blocks = i - start + 1
    for k in range(1, MOST_BLOCKS + 1):

        @pl.when(blocks == k)
        def _(k=k):
            rows = pl.ds(pl.multiple_of(start * BLOCK_TOKENS, BLOCK_TOKENS), k * BLOCK_TOKENS)
            keys = kv_ref[rows, :HD]
            values = kv_ref[rows, HD:]
            shape = (BLOCK_TOKENS, BLOCK_TOKENS)
            causal = iota(shape, 0) >= iota(shape, 1)
            for h in range(lq):
                cols = slice(h * HD, (h + 1) * HD)
                scores = dot_t(q_ref[:, cols], keys) * SCALE
                last = jnp.where(causal, scores[:, (k - 1) * BLOCK_TOKENS :], MASKED)
                if k > 1:
                    scores = jnp.concatenate([scores[:, : (k - 1) * BLOCK_TOKENS], last], axis=1)
                else:
                    scores = last
                raised = jnp.exp(scores - jnp.max(scores, axis=1, keepdims=True))
                inverse = 1.0 / jnp.sum(raised, axis=1, keepdims=True)
                weights = (raised * inverse).astype(jnp.bfloat16)
                o_ref[:, cols] = dot(weights, values).astype(jnp.bfloat16)


def prompt_attention(counts, q, kv):
    rows, cq = q.shape
    return pl.pallas_call(
        functools.partial(attend_prompt, cq // HD),
        grid=(rows // BLOCK_TOKENS,),
        in_specs=[
            pl.BlockSpec(memory_space=SMEM),
            pl.BlockSpec((BLOCK_TOKENS, cq), lambda i: (i, 0)),
            pl.BlockSpec(kv.shape, lambda i: (0, 0)),
        ],
        out_specs=pl.BlockSpec((BLOCK_TOKENS, cq), lambda i: (i, 0)),
        out_shape=jax.ShapeDtypeStruct((rows, cq), jnp.bfloat16),
        compiler_params=pltpu.CompilerParams(vmem_limit_bytes=32 * MIB),
        cost_estimate=pl.CostEstimate(
            flops=8 * rows * rows // 2 * cq, bytes_accessed=8 * rows * cq, transcendentals=rows * rows
        ),
        name="prompt_attention",
    )(counts, q, kv)


def row_head(n, lq, h, hh):
    at = h * GQ + hh
    return at // lq, at % lq


def owner_scores(n, lq, counts, done, placed, table, lens, cache, *refs):
    msgs = refs[:n]
    scores_ref, fresh_ref = refs[n : n + 2]
    outs = refs[n + 2 : 2 * n + 2]
    slot_row, slot_limit, held, stats = refs[2 * n + 2 :]
    me = lax.axis_index("tp")
    other = 1 - lax.axis_index("pool")
    first_end = counts[other, 0]
    second_end = first_end + counts[other, 1]
    block_of = [[jnp.int32(-1)] * PAGES for _ in range(ROWS_DEV)]
    for b in range(NBLK):
        live = jnp.where(
            b < first_end, done[other, 0], jnp.where(b < second_end, done[other, 1], done[other, 2])
        )
        slot = jnp.where((live > 0) & (placed[other, b, 0] == me), placed[other, b, 1], -1)
        for r in range(ROWS_DEV):
            for p in range(PAGES):
                block_of[r][p] = jnp.where(slot == table[r, p], b, block_of[r][p])
    for r in range(ROWS_DEV):
        for p in range(PAGES):
            slot_row[table[r, p]] = jnp.int32(r)
            slot_limit[table[r, p]] = jnp.where(block_of[r][p] < 0, lens[r] - p * BLOCK_TOKENS, 0)
    for d in range(n):
        source = lax.rem(me + n - d, n)
        held[pl.ds(pl.multiple_of(source * GROUP_ROWS, GROUP_ROWS), GROUP_ROWS), :] = msgs[d][...]

    cq = lq * HD
    queries, keys, scores = [], [], []
    for h in range(KVH):
        own = []
        for hh in range(GQ):
            t, at = row_head(n, lq, h, hh)
            own.append(held[t * GROUP_ROWS : (t + 1) * GROUP_ROWS, at * HD : (at + 1) * HD])
        own = jnp.concatenate(own, axis=0)
        t, _ = row_head(n, lq, h, 0)
        new_key = held[t * GROUP_ROWS : (t + 1) * GROUP_ROWS, cq : cq + HD]
        queries.append(own)
        keys += [new_key] * GQ
        scores.append(dot_t(own.astype(jnp.bfloat16), cache[:, h * 2 * HD : h * 2 * HD + HD]) * SCALE)
    queries = jnp.concatenate(queries, axis=0)
    earlier = jnp.concatenate([pltpu.roll(key, ROWS_DEV, 0) for key in keys], axis=0)
    keys = jnp.concatenate(keys, axis=0)
    scores = jnp.concatenate(scores, axis=0)
    rows = queries.shape[0]
    shape = (rows, HD)
    at_row, lane = iota(shape, 0), iota(shape, 1)
    rs = at_row % GROUP_ROWS
    r = row_of(rs)
    parts = []
    for slot in range(DEVICE_SLOTS):
        usable = (r == slot_row[slot]) & (lane < slot_limit[slot])
        parts.append(jnp.where(usable, scores[:, slot * BLOCK_TOKENS : (slot + 1) * BLOCK_TOKENS], MASKED))
    scores = jnp.concatenate(parts, axis=1)
    now = jnp.sum(queries * keys, axis=1, keepdims=True) * SCALE
    before = jnp.sum(queries * earlier, axis=1, keepdims=True) * SCALE
    rs1 = iota((rows, 1), 0) % GROUP_ROWS
    r1 = row_of(rs1)
    before = jnp.where((rs1 >= ROWS_DEV) & (rs1 < STEPS * ROWS_DEV), before, MASKED)
    peak = jnp.maximum(jnp.max(scores, axis=1, keepdims=True), jnp.maximum(now, before))
    total = jnp.sum(jnp.exp(scores - peak), axis=1, keepdims=True) + jnp.exp(now - peak) + jnp.exp(before - peak)
    scores_ref[...] = scores
    fresh_ref[...] = jnp.where(lane == 0, now, jnp.where(lane == 1, before, 0.0))

    def by_row(values, rest):
        out = jnp.full((rows, 1), rest, jnp.int32)
        for k in range(ROWS_DEV):
            out = jnp.where(r1 == k, values[k], out)
        return out.astype(jnp.float32)

    kinds = [
        peak,
        total,
        by_row([block_of[k][0] for k in range(ROWS_DEV)], -1),
        by_row([block_of[k][1] for k in range(ROWS_DEV)], -1),
        by_row([lens[k] for k in range(ROWS_DEV)], 0),
    ]
    span = lq * GROUP_ROWS
    spread = [jnp.where(lane == at_row % span, kind, 0.0) for kind in kinds]
    for t in range(n):
        lines = [jnp.sum(kind[t * span : (t + 1) * span], axis=0, keepdims=True) for kind in spread]
        lines.append(jnp.zeros((8 - len(lines), HD), jnp.float32))
        stats[t] = jnp.concatenate(lines, axis=0)
    for d in range(n):
        outs[d][...] = stats[lax.rem(me + d, n)]


def decode_scores(counts, done, placed, table, lens, cache, msgs, lq):
    n = len(msgs)
    rows = QH * GROUP_ROWS
    smem, vmem = pl.BlockSpec(memory_space=SMEM), pl.BlockSpec(memory_space=VMEM)
    out = pl.pallas_call(
        functools.partial(owner_scores, n, lq),
        in_specs=[smem] * 5 + [vmem] * (n + 1),
        out_specs=[vmem] * (n + 2),
        out_shape=[
            jax.ShapeDtypeStruct((rows, DEVICE_SLOTS * BLOCK_TOKENS), jnp.float32),
            jax.ShapeDtypeStruct((rows, HD), jnp.float32),
        ]
        + [jax.ShapeDtypeStruct((8, HD), jnp.float32)] * n,
        scratch_shapes=[
            SMEM((DEVICE_SLOTS,), jnp.int32),
            SMEM((DEVICE_SLOTS,), jnp.int32),
            VMEM((n * GROUP_ROWS, msgs[0].shape[1]), jnp.float32),
            VMEM((n, 8, HD), jnp.float32),
        ],
        compiler_params=pltpu.CompilerParams(vmem_limit_bytes=32 * MIB),
        cost_estimate=pl.CostEstimate(flops=2 * rows * HD * 768, bytes_accessed=4 * MIB, transcendentals=rows * 768),
        name="decode_scores",
    )(counts, done, placed, table, lens, cache, *msgs)
    return out[0], out[1], out[2:]


def handed_part(n, lq, kv_ref, q_ref, *refs):
    msgs = refs[:n]
    outs = refs[n : 2 * n]
    stats, held = refs[2 * n :]
    me = lax.axis_index("tp")
    for d in range(n):
        stats[lax.rem(me + n - d, n)] = msgs[d][...]
    rows = lq * n * GROUP_ROWS
    shape = (rows, HD)
    at_row, lane = iota(shape, 0), iota(shape, 1)
    head, rs = at_row // (n * GROUP_ROWS), at_row % GROUP_ROWS
    mine = lane == head * GROUP_ROWS + rs

    def column(kind):
        lines = [jnp.broadcast_to(stats[u, kind : kind + 1, :], (GROUP_ROWS, HD)) for u in range(n)] * lq
        return jnp.sum(jnp.where(mine, jnp.concatenate(lines, axis=0), 0.0), axis=1, keepdims=True)

    peak, total, first_block, second_block, length = [column(kind) for kind in range(5)]
    scores = dot_t(q_ref[...], kv_ref[:, :HD]) * SCALE
    lane_f = lane.astype(jnp.float32)
    parts = []
    for b in range(NBLK):
        limit = jnp.where(
            first_block == b, length, jnp.where(second_block == b, length - BLOCK_TOKENS, 0.0)
        )
        part = scores[:, b * BLOCK_TOKENS : (b + 1) * BLOCK_TOKENS]
        parts.append(jnp.where(lane_f < limit, part, MASKED))
    scores = jnp.concatenate(parts, axis=1)
    top = jnp.maximum(peak, jnp.max(scores, axis=1, keepdims=True))
    raised = jnp.exp(scores - top)
    total = total * jnp.exp(peak - top) + jnp.sum(raised, axis=1, keepdims=True)
    weights = (raised * (1.0 / total)).astype(jnp.bfloat16)
    mixed = dot(weights, kv_ref[:, HD:]).reshape(lq * n, GROUP_ROWS, HD)

    def line(col):
        spread = jnp.where(lane == rs, col, 0.0).reshape(lq * n, GROUP_ROWS, HD)
        return jnp.sum(spread, axis=1, keepdims=True)

    rs3 = rs.reshape(lq * n, GROUP_ROWS, HD)
    mixed = jnp.where(rs3 == 6, line(top), jnp.where(rs3 == 7, line(total), mixed))
    held[...] = mixed.reshape(lq, n, GROUP_ROWS, HD)
    for d in range(n):
        to = lax.rem(me + d, n)
        for h in range(lq):
            outs[d][h * GROUP_ROWS : (h + 1) * GROUP_ROWS, :] = held[h, to]


def handed_attention(kv, q_other, msgs, lq):
    n = len(msgs)
    rows = lq * n * GROUP_ROWS
    vmem = pl.BlockSpec(memory_space=VMEM)
    return pl.pallas_call(
        functools.partial(handed_part, n, lq),
        in_specs=[vmem] * (n + 2),
        out_specs=[vmem] * n,
        out_shape=[jax.ShapeDtypeStruct((lq * GROUP_ROWS, HD), jnp.float32)] * n,
        scratch_shapes=[VMEM((n, 8, HD), jnp.float32), VMEM((lq, n, GROUP_ROWS, HD), jnp.float32)],
        compiler_params=pltpu.CompilerParams(vmem_limit_bytes=32 * MIB),
        cost_estimate=pl.CostEstimate(flops=4 * rows * HD * PTOK, bytes_accessed=2 * MIB, transcendentals=rows * PTOK),
        name="handed_attention",
    )(kv, q_other, *msgs)


def owner_mix(n, lq, scores_ref, fresh_ref, cache, *refs):
    msgs, parts = refs[:n], refs[n : 2 * n]
    o_ref, held, handed = refs[2 * n :]
    me = lax.axis_index("tp")
    for d in range(n):
        source = lax.rem(me + n - d, n)
        held[pl.ds(pl.multiple_of(source * GROUP_ROWS, GROUP_ROWS), GROUP_ROWS), :] = msgs[d][...]
        handed[source] = parts[d][...]
    groups = QH
    rows = groups * GROUP_ROWS
    mixed = handed[...].reshape(groups, GROUP_ROWS, HD)
    shape = (groups, GROUP_ROWS, HD)
    mine = iota(shape, 1) == iota(shape, 2)

    def column(at):
        line = jnp.broadcast_to(mixed[:, at : at + 1, :], shape)
        return jnp.sum(jnp.where(mine, line, 0.0), axis=2, keepdims=True).reshape(rows, 1)

    peak, inverse = column(6), 1.0 / column(7)
    weights = (jnp.exp(scores_ref[...] - peak) * inverse).astype(jnp.bfloat16)
    fresh = (jnp.exp(fresh_ref[...] - peak) * inverse).astype(jnp.bfloat16).astype(jnp.float32)
    mixed = mixed.reshape(rows, HD)
    span = GQ * GROUP_ROWS
    out = []
    for h in range(KVH):
        part = slice(h * span, (h + 1) * span)
        own = mixed[part] + dot(weights[part], cache[:, (2 * h + 1) * HD : (2 * h + 2) * HD])
        t, _ = row_head(n, lq, h, 0)
        value = held[t * GROUP_ROWS : (t + 1) * GROUP_ROWS, lq * HD + HD : lq * HD + 2 * HD]
        earlier = pltpu.roll(value, ROWS_DEV, 0)
        for hh in range(GQ):
            at = h * span + hh * GROUP_ROWS
            some = slice(at, at + GROUP_ROWS)
            line = own[hh * GROUP_ROWS : (hh + 1) * GROUP_ROWS]
            out.append(line + fresh[some, 0:1] * value + fresh[some, 1:2] * earlier)
    out = jnp.concatenate(out, axis=1)
    for s in range(STEPS):
        o_ref[s] = out[s * ROWS_DEV : (s + 1) * ROWS_DEV].astype(jnp.bfloat16)


def decode_mix(scores, fresh, cache, msgs, parts, lq):
    n = len(msgs)
    vmem = pl.BlockSpec(memory_space=VMEM)
    return pl.pallas_call(
        functools.partial(owner_mix, n, lq),
        in_specs=[vmem] * (2 * n + 3),
        out_specs=vmem,
        out_shape=jax.ShapeDtypeStruct((STEPS, ROWS_DEV, QH * HD), jnp.bfloat16),
        scratch_shapes=[
            VMEM((n * GROUP_ROWS, msgs[0].shape[1]), jnp.float32),
            VMEM((n, lq * GROUP_ROWS, HD), jnp.float32),
        ],
        compiler_params=pltpu.CompilerParams(vmem_limit_bytes=32 * MIB),
        cost_estimate=pl.CostEstimate(flops=2 * 256 * HD * 768, bytes_accessed=4 * MIB, transcendentals=256 * 768),
        name="decode_mix",
    )(scores, fresh, cache, *msgs, *parts)


def along_tp(msgs):
    n = len(msgs)
    return [msgs[0]] + [
        lax.ppermute(msgs[d], "tp", [(i, (i + d) % n) for i in range(n)]) for d in range(1, n)
    ]


def to_other_group(msgs):
    n = len(msgs)
    return [
        lax.ppermute(
            msgs[d],
            ("pool", "tp"),
            [(g * n + i, (1 - g) * n + (i + d) % n) for g in range(2) for i in range(n)],
        )
        for d in range(n)
    ]


def local(
    prompt_x,
    q_weight,
    kv_weight,
    prompt_blocks,
    finished,
    placement,
    page_table,
    row_lens,
    kv_cache,
    decode_x,
):
    n = lax.axis_size("tp")
    lq = q_weight.shape[1] // HD
    share = GQ // lq
    if share > 1:
        sets = [[k * share + i for i in range(share)] for k in range(n // share)]
        kv_weight = lax.all_gather(kv_weight, "tp", axis=1, tiled=True, axis_index_groups=sets)
    cache = kv_cache.reshape(-1, kv_cache.shape[2])
    dx = decode_x.reshape(-1, decode_x.shape[2])
    block = 256
    q, kv, q_own, *msgs = project_rows(prompt_x, q_weight, kv_weight, 0, 2 * block, block, dx=dx, n=n)
    q_other = lax.ppermute(q_own, "pool", [(0, 1), (1, 0)])
    msgs = along_tp(msgs)
    q, kv = project_rows(prompt_x, q_weight, kv_weight, 2 * block, 3 * block, block, held=(q, kv))
    scores, fresh, stats = decode_scores(
        prompt_blocks, finished, placement, page_table, row_lens, cache, msgs, lq
    )
    stats = to_other_group(stats)
    q, kv = project_rows(prompt_x, q_weight, kv_weight, 5 * block, 3 * block, block, held=(q, kv))
    parts = to_other_group(handed_attention(kv, q_other, stats, lq))
    prompt_attn = prompt_attention(prompt_blocks, q, kv)
    decode_attn = decode_mix(scores, fresh, cache, msgs, parts, lq)
    return prompt_attn, decode_attn


def solution(mesh):
    return jax.shard_map(
        local,
        mesh=mesh,
        in_specs=(
            P(("rep", "pool"), None),
            P(None, "tp"),
            P(None, "tp"),
            P("rep", None),
            P("rep", None),
            P("rep", None, None),
            P(("rep", "pool", "tp"), None),
            P(("rep", "pool", "tp")),
            P(("rep", "pool", "tp"), None, None),
            P(None, ("rep", "pool"), None),
        ),
        out_specs=(P(("rep", "pool"), "tp"), P(None, ("rep", "pool", "tp"), None)),
        check_vma=False,
    )
```

```python
import functools

import jax
import jax.numpy as jnp
from jax import lax
from jax.experimental import pallas as pl
from jax.experimental.pallas import tpu as pltpu
from jax.sharding import PartitionSpec as P

QH = 32
KVH = 8
GQ = QH // KVH
HD = 128
BLOCK_TOKENS = 128
PTOK = 2048
NPROMPT = 3
MOST_BLOCKS = 8
PAGES = 2
STEPS = 2
NBLK = 16
DEVICE_SLOTS = 6
ROWS_DEV = 3
GROUP_ROWS = 8
KEY_VALUE_COLUMNS = 2048
SCALE = HD ** (-0.5)
MASKED = -1e30
PIECES = 5
MIB = 1 << 20
VMEM = pltpu.VMEM
SMEM = pltpu.SMEM


def dot(a, b):
    return jnp.dot(a, b, preferred_element_type=jnp.float32)


def dot_t(a, b):
    return lax.dot_general(a, b, (((1,), (1,)), ((), ())), preferred_element_type=jnp.float32)


def iota(shape, axis):
    return lax.broadcasted_iota(jnp.int32, shape, axis)


def row_of(rs):
    return jnp.where(rs >= 2 * ROWS_DEV, ROWS_DEV, jnp.where(rs >= ROWS_DEV, rs - ROWS_DEV, rs))


def block_of_pages(counts, done, placed, table):
    me = lax.axis_index("tp")
    other = 1 - lax.axis_index("pool")
    first_end = counts[other, 0]
    second_end = first_end + counts[other, 1]
    found = [[jnp.int32(-1)] * PAGES for _ in range(ROWS_DEV)]
    for b in range(NBLK):
        live = jnp.where(
            b < first_end, done[other, 0], jnp.where(b < second_end, done[other, 1], done[other, 2])
        )
        slot = jnp.where((live > 0) & (placed[other, b, 0] == me), placed[other, b, 1], -1)
        for r in range(ROWS_DEV):
            for p in range(PAGES):
                found[r][p] = jnp.where(slot == table[r, p], b, found[r][p])
    return found


def by_row(r, values, rest):
    out = jnp.full(r.shape, rest, jnp.int32)
    for k in range(ROWS_DEV):
        out = jnp.where(r == k, values[k], out)
    return out


def project(n, lq, blocks, with_q, with_kv, with_decode, *refs):
    refs = list(refs)
    if with_decode:
        counts, done, placed, table, lens, dx_ref = refs[:6]
        del refs[:6]
    x_hbm, wq_hbm = refs[:2]
    del refs[:2]
    wkv_hbm = refs.pop(0) if with_kv else None
    if not with_decode:
        refs.pop(0)
    q_hbm = refs.pop(0)
    kv_hbm = refs.pop(0) if with_kv else None
    if with_decode:
        qh_ref, msg_ref = refs[:2]
        del refs[:2]
    xs, w, q_out, kv_out, x_sems, w_sems, out_sems = refs
    size, depth = xs.shape[1:]
    cq = lq * HD
    piece = depth // PIECES

    def w_copies(c):
        part = pl.ds(c * piece, piece)
        copies = [pltpu.make_async_copy(wq_hbm.at[part], w.at[part, pl.ds(0, cq)], w_sems.at[0, c])]
        if with_kv:
            cols = pl.ds(cq, 2 * HD)
            copies.append(pltpu.make_async_copy(wkv_hbm.at[part], w.at[part, cols], w_sems.at[1, c]))
        return copies

    def x_piece(c):
        rows, cols = pl.ds(blocks[0] * size, size), pl.ds(c * piece, piece)
        return pltpu.make_async_copy(x_hbm.at[rows, cols], xs.at[0, :, cols], x_sems.at[c])

    def x_copy(k):
        rows = pl.ds(blocks[k] * size, size)
        return pltpu.make_async_copy(x_hbm.at[rows], xs.at[k % 2], x_sems.at[PIECES + k % 2])

    for c in range(PIECES):
        x_piece(c).start()
        for copy in w_copies(c):
            copy.start()
    pending = {}
    for k, block in enumerate(blocks):
        if k + 1 < len(blocks):
            x_copy(k + 1).start()
        low = 0 if block in with_q else cq
        high = cq + 2 * HD if with_kv else cq
        if k == 0:
            total, own = 0.0, 0.0
            for c in range(PIECES):
                x_piece(c).wait()
                for copy in w_copies(c):
                    copy.wait()
                part = slice(c * piece, (c + 1) * piece)
                total += dot(xs[0, :, part], w[part, low:high])
                if with_decode:
                    own += dot(dx_ref[:, part], w[part, :])
        else:
            x_copy(k).wait()
            total = dot(xs[k % 2], w[:, low:high])
        slot = k % 2
        for copy in pending.pop(slot, []):
            copy.wait()
        rows = pl.ds(block * size, size)
        copies = []
        if low == 0:
            q_out[slot] = total[:, :cq].astype(jnp.bfloat16)
            copies.append(pltpu.make_async_copy(q_out.at[slot], q_hbm.at[rows], out_sems.at[0, slot]))
        if with_kv:
            kv_out[slot] = total[:, cq - low :].astype(jnp.bfloat16)
            copies.append(pltpu.make_async_copy(kv_out.at[slot], kv_hbm.at[rows], out_sems.at[1, slot]))
        for copy in copies:
            copy.start()
        pending[slot] = copies
        if with_decode and k == 0:
            rows = STEPS * ROWS_DEV * n
            shape = (n * GROUP_ROWS, rows)
            to, fro = iota(shape, 0), iota(shape, 1)
            owner, rs = to // GROUP_ROWS, to % GROUP_ROWS
            wanted = owner * ROWS_DEV + row_of(rs) + jnp.where(rs >= ROWS_DEV, ROWS_DEV * n, 0)
            pick = ((fro == wanted) & (rs < STEPS * ROWS_DEV)).astype(jnp.float32).astype(jnp.bfloat16)
            own = dot(pick, own.astype(jnp.bfloat16))
            for h in range(lq):
                part = slice(h * n * GROUP_ROWS, (h + 1) * n * GROUP_ROWS)
                qh_ref[part, :] = own[:, h * HD : (h + 1) * HD].astype(jnp.bfloat16)
            found = block_of_pages(counts, done, placed, table)
            lane = iota((n * GROUP_ROWS, HD), 1)
            r = row_of(lane % GROUP_ROWS)
            kind = lane // GROUP_ROWS
            facts = jnp.where(
                kind == 0,
                by_row(r, [found[i][0] for i in range(ROWS_DEV)], -1),
                jnp.where(
                    kind == 1,
                    by_row(r, [found[i][1] for i in range(ROWS_DEV)], -1),
                    by_row(r, [lens[i] for i in range(ROWS_DEV)], 0),
                ),
            ).astype(jnp.float32)
            sixth = iota((n * GROUP_ROWS, HD), 0) % GROUP_ROWS == 6
            msg_ref[:, :HD] = jnp.where(sixth, facts, own[:, :HD])
            msg_ref[:, HD:] = own[:, HD:]
    for copies in pending.values():
        for copy in copies:
            copy.wait()


def project_first(ints, dx, x, wq, wkv, n, size, q_blocks):
    rows, depth = x.shape
    cq = wq.shape[1]
    lq = cq // HD
    blocks = list(range(rows // size))
    smem, vmem = pl.BlockSpec(memory_space=SMEM), pl.BlockSpec(memory_space=VMEM)
    hbm = pl.BlockSpec(memory_space=pl.ANY)
    return pl.pallas_call(
        functools.partial(project, n, lq, blocks, blocks[:q_blocks], True, True),
        in_specs=[smem] * 5 + [vmem] + [hbm] * 3,
        out_specs=[hbm, hbm, vmem, vmem],
        out_shape=[
            jax.ShapeDtypeStruct((rows, cq), jnp.bfloat16),
            jax.ShapeDtypeStruct((rows, 2 * HD), jnp.bfloat16),
            jax.ShapeDtypeStruct((lq * n * GROUP_ROWS, HD), jnp.bfloat16),
            jax.ShapeDtypeStruct((n * GROUP_ROWS, cq + 2 * HD), jnp.float32),
        ],
        scratch_shapes=projection_scratch(size, depth, cq, 2 * HD),
        compiler_params=pltpu.CompilerParams(vmem_limit_bytes=62 * MIB),
        cost_estimate=pl.CostEstimate(
            flops=2 * rows * depth * (2 * HD + cq * q_blocks * size // rows),
            bytes_accessed=2 * rows * depth + 2 * depth * (cq + 2 * HD),
            transcendentals=0,
        ),
        name="project_first",
    )(*ints, dx, x, wq, wkv)


def projection_scratch(size, depth, cq, ckv):
    return [
        VMEM((2, size, depth), jnp.bfloat16),
        VMEM((depth, cq + ckv), jnp.bfloat16),
        VMEM((2, size, cq), jnp.bfloat16),
        VMEM((2, size, 2 * HD), jnp.bfloat16),
        pltpu.SemaphoreType.DMA((PIECES + 2,)),
        pltpu.SemaphoreType.DMA((2, PIECES)),
        pltpu.SemaphoreType.DMA((2, 2)),
    ]


def project_rest(x, wq, q, size, q_blocks):
    rows, depth = x.shape
    cq = wq.shape[1]
    blocks = list(range(q_blocks, rows // size))
    hbm = pl.BlockSpec(memory_space=pl.ANY)
    return pl.pallas_call(
        functools.partial(project, 0, cq // HD, blocks, blocks, False, False),
        in_specs=[hbm] * 3,
        out_specs=hbm,
        out_shape=jax.ShapeDtypeStruct((rows, cq), jnp.bfloat16),
        scratch_shapes=projection_scratch(size, depth, cq, 0),
        input_output_aliases={2: 0},
        compiler_params=pltpu.CompilerParams(vmem_limit_bytes=62 * MIB),
        cost_estimate=pl.CostEstimate(
            flops=2 * len(blocks) * size * depth * cq,
            bytes_accessed=2 * len(blocks) * size * depth + 2 * depth * cq,
            transcendentals=0,
        ),
        name="project_rest",
    )(x, wq, q)


LOG2E = 1.4426950408889634
SLAB = 32


def attend_prompt(lq, counts, q_ref, kv_ref, o_ref, held):
    group = lax.axis_index("pool")
    c0, c1 = counts[group, 0], counts[group, 1]
    big = jnp.where(c0 == MOST_BLOCKS, 0, jnp.where(c1 == MOST_BLOCKS, c0, c0 + c1))
    cut = jnp.where(c0 == MOST_BLOCKS, c1, c0)
    causal = iota((SLAB, BLOCK_TOKENS), 1) - iota((SLAB, BLOCK_TOKENS), 0)
    for half in range(2):

        def rows_at(j, half=half):
            block = big + j if half == 0 else j + jnp.where(j >= big, MOST_BLOCKS, 0)
            return pl.ds(pl.multiple_of(block * BLOCK_TOKENS, BLOCK_TOKENS), BLOCK_TOKENS)

        for j in range(MOST_BLOCKS):
            held[half, j * BLOCK_TOKENS : (j + 1) * BLOCK_TOKENS, :] = kv_ref[rows_at(j), :]

        def scores_of(j, half=half):
            q = q_ref[rows_at(j), :]
            q = jnp.concatenate([q[:, h * HD : (h + 1) * HD] for h in range(lq)], axis=0)
            return dot_t(q, held[half, : (j + 1) * BLOCK_TOKENS, :HD])

        scores = scores_of(0)
        for j in range(MOST_BLOCKS):
            later = scores_of(j + 1) if j + 1 < MOST_BLOCKS else None
            weights = []
            for at in range(0, lq * BLOCK_TOKENS, SLAB):
                tiles = []
                for i in range(j + 1):
                    tile = scores[at : at + SLAB, i * BLOCK_TOKENS : (i + 1) * BLOCK_TOKENS]
                    if i == j:
                        tile = jnp.where(causal <= at % BLOCK_TOKENS, tile, MASKED)
                    elif half == 1:
                        tile = tile + jnp.where((i < cut) & (cut <= j), MASKED, 0.0)
                    tiles.append(tile)
                peak = jnp.max(functools.reduce(jnp.maximum, tiles), axis=1, keepdims=True)
                raised = [jnp.exp2((tile - peak) * (SCALE * LOG2E)) for tile in tiles]
                inverse = 1.0 / jnp.sum(functools.reduce(jnp.add, raised), axis=1, keepdims=True)
                weights.append(jnp.concatenate([(t * inverse).astype(jnp.bfloat16) for t in raised], axis=1))
            mixed = dot(jnp.concatenate(weights, axis=0), held[half, : (j + 1) * BLOCK_TOKENS, HD:])
            for h in range(lq):
                part = mixed[h * BLOCK_TOKENS : (h + 1) * BLOCK_TOKENS]
                o_ref[rows_at(j), h * HD : (h + 1) * HD] = part.astype(jnp.bfloat16)
            scores = later


def prompt_attention(counts, q, kv):
    rows, cq = q.shape
    vmem = pl.BlockSpec(memory_space=VMEM)
    return pl.pallas_call(
        functools.partial(attend_prompt, cq // HD),
        in_specs=[pl.BlockSpec(memory_space=SMEM), vmem, vmem],
        out_specs=vmem,
        out_shape=jax.ShapeDtypeStruct((rows, cq), jnp.bfloat16),
        scratch_shapes=[VMEM((2, MOST_BLOCKS * BLOCK_TOKENS, 2 * HD), jnp.bfloat16)],
        compiler_params=pltpu.CompilerParams(vmem_limit_bytes=48 * MIB),
        cost_estimate=pl.CostEstimate(flops=2 * rows * rows * cq, bytes_accessed=8 * rows * cq, transcendentals=rows * rows),
        name="prompt_attention",
    )(counts, q, kv)


def row_head(n, lq, h, hh):
    at = h * GQ + hh
    return at // lq, at % lq


def handed_part(n, lq, kv_ref, q_ref, msg_ref, o_ref):
    rows = lq * n * GROUP_ROWS
    shape = (rows, HD)
    at_row, lane = iota(shape, 0), iota(shape, 1)
    rs = at_row % GROUP_ROWS
    facts = msg_ref[:, :HD].reshape(n, GROUP_ROWS, HD)[:, 6:7, :]
    facts = jnp.broadcast_to(facts, (n, GROUP_ROWS, HD)).reshape(n * GROUP_ROWS, HD)
    facts = jnp.concatenate([facts] * lq, axis=0)

    def column(kind):
        return jnp.sum(jnp.where(lane == kind * GROUP_ROWS + rs, facts, 0.0), axis=1, keepdims=True)

    first_block, second_block, length = [column(kind) for kind in range(3)]
    scores = dot_t(q_ref[...], kv_ref[:, :HD]) * SCALE
    lane_f = lane.astype(jnp.float32)
    parts = []
    for b in range(NBLK):
        limit = jnp.where(
            first_block == b, length, jnp.where(second_block == b, length - BLOCK_TOKENS, 0.0)
        )
        part = scores[:, b * BLOCK_TOKENS : (b + 1) * BLOCK_TOKENS]
        parts.append(jnp.where(lane_f < limit, part, MASKED))
    scores = jnp.concatenate(parts, axis=1)
    top = jnp.max(scores, axis=1, keepdims=True)
    raised = jnp.exp(scores - top)
    total = jnp.sum(raised, axis=1, keepdims=True)
    near = raised.astype(jnp.bfloat16)
    rest = (raised - near.astype(jnp.float32)).astype(jnp.bfloat16)
    values = kv_ref[:, HD:]
    mixed = (dot(near, values) + dot(rest, values)).reshape(lq * n, GROUP_ROWS, HD)

    def line(col):
        spread = jnp.where(lane == rs, col, 0.0).reshape(lq * n, GROUP_ROWS, HD)
        return jnp.sum(spread, axis=1, keepdims=True)

    rs3 = rs.reshape(lq * n, GROUP_ROWS, HD)
    mixed = jnp.where(rs3 == 6, line(top), jnp.where(rs3 == 7, line(total), mixed))
    for h in range(lq):
        o_ref[:, h * GROUP_ROWS : (h + 1) * GROUP_ROWS, :] = mixed[h * n : (h + 1) * n]


def handed_attention(kv, q_own, msgs, n, lq):
    rows = lq * n * GROUP_ROWS
    vmem = pl.BlockSpec(memory_space=VMEM)
    return pl.pallas_call(
        functools.partial(handed_part, n, lq),
        in_specs=[vmem] * 3,
        out_specs=vmem,
        out_shape=jax.ShapeDtypeStruct((n, lq * GROUP_ROWS, HD), jnp.float32),
        compiler_params=pltpu.CompilerParams(vmem_limit_bytes=32 * MIB),
        cost_estimate=pl.CostEstimate(flops=6 * rows * HD * PTOK, bytes_accessed=2 * MIB, transcendentals=rows * PTOK),
        name="handed_attention",
    )(kv, q_own, msgs)


def owner_part(n, lq, counts, done, placed, table, lens, cache_hbm, held, handed, o_ref, cache, sems, slot_row, slot_limit):
    def slot_copy(slot):
        rows = pl.ds(slot * BLOCK_TOKENS, BLOCK_TOKENS)
        return pltpu.make_async_copy(cache_hbm.at[rows], cache.at[rows], sems.at[slot])

    for slot in range(DEVICE_SLOTS):
        slot_copy(slot).start()
    found = block_of_pages(counts, done, placed, table)
    for r in range(ROWS_DEV):
        for p in range(PAGES):
            slot_row[table[r, p]] = jnp.int32(r)
            slot_limit[table[r, p]] = jnp.where(found[r][p] < 0, lens[r] - p * BLOCK_TOKENS, 0)

    cq = lq * HD
    groups = QH
    rows = groups * GROUP_ROWS
    span = GQ * GROUP_ROWS
    queries, keys = [], []
    for h in range(KVH):
        for hh in range(GQ):
            t, at = row_head(n, lq, h, hh)
            queries.append(held[t * GROUP_ROWS : (t + 1) * GROUP_ROWS, at * HD : (at + 1) * HD])
        t, _ = row_head(n, lq, h, 0)
        keys += [held[t * GROUP_ROWS : (t + 1) * GROUP_ROWS, cq : cq + HD]] * GQ
    queries = jnp.concatenate(queries, axis=0)
    earlier = jnp.concatenate([pltpu.roll(key, ROWS_DEV, 0) for key in keys], axis=0)
    keys = jnp.concatenate(keys, axis=0)
    at_row, lane = iota((rows, HD), 0), iota((rows, HD), 1)
    r = row_of(at_row % GROUP_ROWS)
    rounded = queries.astype(jnp.bfloat16)
    scores = []
    for slot in range(DEVICE_SLOTS):
        slot_copy(slot).wait()
        part = slice(slot * BLOCK_TOKENS, (slot + 1) * BLOCK_TOKENS)
        some = [
            dot_t(rounded[h * span : (h + 1) * span], cache[part, 2 * h * HD : (2 * h + 1) * HD])
            for h in range(KVH)
        ]
        usable = (r == slot_row[slot]) & (lane < slot_limit[slot])
        scores.append(jnp.where(usable, jnp.concatenate(some, axis=0) * SCALE, MASKED))
    scores = jnp.concatenate(scores, axis=1)
    now = jnp.sum(queries * keys, axis=1, keepdims=True) * SCALE
    before = jnp.sum(queries * earlier, axis=1, keepdims=True) * SCALE
    rs1 = iota((rows, 1), 0) % GROUP_ROWS
    before = jnp.where((rs1 >= ROWS_DEV) & (rs1 < STEPS * ROWS_DEV), before, MASKED)

    mixed = handed[...].reshape(groups, GROUP_ROWS, HD)
    shape = (groups, GROUP_ROWS, HD)
    mine = iota(shape, 1) == iota(shape, 2)

    def column(at):
        line = jnp.broadcast_to(mixed[:, at : at + 1, :], shape)
        return jnp.sum(jnp.where(mine, line, 0.0), axis=2, keepdims=True).reshape(rows, 1)

    other_peak, other_total = column(6), column(7)
    peak = jnp.maximum(jnp.max(scores, axis=1, keepdims=True), jnp.maximum(now, before))
    peak = jnp.maximum(peak, other_peak)
    raised, now, before = jnp.exp(scores - peak), jnp.exp(now - peak), jnp.exp(before - peak)
    other = jnp.exp(other_peak - peak)
    inverse = 1.0 / (jnp.sum(raised, axis=1, keepdims=True) + now + before + other * other_total)
    weights = (raised * inverse).astype(jnp.bfloat16)
    now = (now * inverse).astype(jnp.bfloat16).astype(jnp.float32)
    before = (before * inverse).astype(jnp.bfloat16).astype(jnp.float32)
    mixed = mixed.reshape(rows, HD) * (other * inverse)
    out = []
    for h in range(KVH):
        part = slice(h * span, (h + 1) * span)
        own = mixed[part] + dot(weights[part], cache[:, (2 * h + 1) * HD : (2 * h + 2) * HD])
        t, _ = row_head(n, lq, h, 0)
        value = held[t * GROUP_ROWS : (t + 1) * GROUP_ROWS, cq + HD : cq + 2 * HD]
        last = pltpu.roll(value, ROWS_DEV, 0)
        for hh in range(GQ):
            some = slice(h * span + hh * GROUP_ROWS, h * span + (hh + 1) * GROUP_ROWS)
            line = own[hh * GROUP_ROWS : (hh + 1) * GROUP_ROWS]
            out.append(line + now[some] * value + before[some] * last)
    out = jnp.concatenate(out, axis=1)
    for s in range(STEPS):
        o_ref[s] = out[s * ROWS_DEV : (s + 1) * ROWS_DEV].astype(jnp.bfloat16)


def decode_attention(ints, cache, msgs, parts, n, lq):
    smem, vmem = pl.BlockSpec(memory_space=SMEM), pl.BlockSpec(memory_space=VMEM)
    return pl.pallas_call(
        functools.partial(owner_part, n, lq),
        in_specs=[smem] * 5 + [pl.BlockSpec(memory_space=pl.ANY), vmem, vmem],
        out_specs=vmem,
        out_shape=jax.ShapeDtypeStruct((STEPS, ROWS_DEV, QH * HD), jnp.bfloat16),
        scratch_shapes=[
            VMEM(cache.shape, jnp.bfloat16),
            pltpu.SemaphoreType.DMA((DEVICE_SLOTS,)),
            SMEM((DEVICE_SLOTS,), jnp.int32),
            SMEM((DEVICE_SLOTS,), jnp.int32),
        ],
        compiler_params=pltpu.CompilerParams(vmem_limit_bytes=48 * MIB),
        cost_estimate=pl.CostEstimate(flops=4 * 256 * HD * 768, bytes_accessed=4 * MIB, transcendentals=256 * 768),
        name="decode_attention",
    )(*ints, cache, msgs, parts)


def local(
    prompt_x,
    q_weight,
    kv_weight,
    prompt_blocks,
    finished,
    placement,
    page_table,
    row_lens,
    kv_cache,
    decode_x,
):
    n = lax.axis_size("tp")
    lq = q_weight.shape[1] // HD
    share = GQ // lq
    if share > 1:
        sets = [[k * share + i for i in range(share)] for k in range(n // share)]
        kv_weight = lax.all_gather(kv_weight, "tp", axis=1, tiled=True, axis_index_groups=sets)
    cache = kv_cache.reshape(-1, kv_cache.shape[2])
    dx = decode_x.reshape(-1, decode_x.shape[2])
    ints = (prompt_blocks, finished, placement, page_table, row_lens)
    size, q_blocks = 512, 1
    q, kv, q_own, msgs = project_first(ints, dx, prompt_x, q_weight, kv_weight, n, size, q_blocks)
    kv_other = lax.ppermute(kv, "pool", [(0, 1), (1, 0)])
    msgs = lax.all_to_all(msgs, "tp", split_axis=0, concat_axis=0, tiled=True)
    q = project_rest(prompt_x, q_weight, q, size, q_blocks)
    parts = handed_attention(kv_other, q_own, msgs, n, lq)
    parts = lax.all_to_all(parts, "tp", split_axis=0, concat_axis=0, tiled=True)
    prompt_attn = prompt_attention(prompt_blocks, q, kv)
    decode_attn = decode_attention(ints, cache, msgs, parts, n, lq)
    return prompt_attn, decode_attn


def solution(mesh):
    return jax.shard_map(
        local,
        mesh=mesh,
        in_specs=(
            P(("rep", "pool"), None),
            P(None, "tp"),
            P(None, "tp"),
            P("rep", None),
            P("rep", None),
            P("rep", None, None),
            P(("rep", "pool", "tp"), None),
            P(("rep", "pool", "tp")),
            P(("rep", "pool", "tp"), None, None),
            P(None, ("rep", "pool"), None),
        ),
        out_specs=(P(("rep", "pool"), "tp"), P(None, ("rep", "pool", "tp"), None)),
        check_vma=False,
    )
```

```python
import functools

import jax
import jax.numpy as jnp
from jax import lax
from jax.experimental import pallas as pl
from jax.experimental.pallas import tpu as pltpu
from jax.sharding import PartitionSpec as P

QH = 32
KVH = 8
GQ = QH // KVH
HD = 128
BLOCK_TOKENS = 128
PTOK = 2048
NPROMPT = 3
MOST_BLOCKS = 8
PAGES = 2
STEPS = 2
NBLK = 16
DEVICE_SLOTS = 6
ROWS_DEV = 3
GROUP_ROWS = 8
KEY_VALUE_COLUMNS = 2048
SCALE = HD ** (-0.5)
MASKED = -1e30
PIECES = 5
MIB = 1 << 20
VMEM = pltpu.VMEM
SMEM = pltpu.SMEM


def dot(a, b):
    return jnp.dot(a, b, preferred_element_type=jnp.float32)


def dot_t(a, b):
    return lax.dot_general(a, b, (((1,), (1,)), ((), ())), preferred_element_type=jnp.float32)


def iota(shape, axis):
    return lax.broadcasted_iota(jnp.int32, shape, axis)


def row_of(rs):
    return jnp.where(rs >= 2 * ROWS_DEV, ROWS_DEV, jnp.where(rs >= ROWS_DEV, rs - ROWS_DEV, rs))


def block_of_pages(counts, done, placed, table):
    me = lax.axis_index("tp")
    other = 1 - lax.axis_index("pool")
    first_end = counts[other, 0]
    second_end = first_end + counts[other, 1]
    found = [[jnp.int32(-1)] * PAGES for _ in range(ROWS_DEV)]
    for b in range(NBLK):
        live = jnp.where(
            b < first_end, done[other, 0], jnp.where(b < second_end, done[other, 1], done[other, 2])
        )
        slot = jnp.where((live > 0) & (placed[other, 0, b] == me), placed[other, 1, b], -1)
        for r in range(ROWS_DEV):
            for p in range(PAGES):
                found[r][p] = jnp.where(slot == table[p, r], b, found[r][p])
    return found


def by_row(r, values, rest):
    out = jnp.full(r.shape, rest, jnp.int32)
    for k in range(ROWS_DEV):
        out = jnp.where(r == k, values[k], out)
    return out


def project(n, lq, start, with_decode, *refs):
    refs = list(refs)
    if with_decode:
        counts, done, placed, table, lens, dx_ref = refs[:6]
        x_hbm, wq_hbm, wkv_hbm, q_ref, kv_ref, qh_ref, msg_ref = refs[6:13]
        del refs[:13]
    else:
        x_hbm, wq_hbm, wkv_hbm, _, _, q_ref, kv_ref = refs[:7]
        del refs[:7]
    xs, w, x_sems, w_sems = refs
    size, depth = xs.shape[1:]
    cq = lq * HD
    piece = depth // PIECES
    step, steps = pl.program_id(0), pl.num_programs(0)
    slot = lax.rem(step, 2)

    def w_copies(c):
        part = pl.ds(c * piece, piece)
        return [
            pltpu.make_async_copy(wq_hbm.at[part], w.at[part, pl.ds(0, cq)], w_sems.at[0, c]),
            pltpu.make_async_copy(wkv_hbm.at[part], w.at[part, pl.ds(cq, 2 * HD)], w_sems.at[1, c]),
        ]

    def x_copy(at, c):
        rows = pl.ds(pl.multiple_of((start + at) * size, size), size)
        cols = pl.ds(c * piece, piece)
        to = lax.rem(at, 2)
        return pltpu.make_async_copy(x_hbm.at[rows, cols], xs.at[to, :, cols], x_sems.at[to, c])

    @pl.when(step == 0)
    def _():
        for c in range(PIECES):
            x_copy(step, c).start()
            for copy in w_copies(c):
                copy.start()

    @pl.when(step + 1 < steps)
    def _():
        for c in range(PIECES):
            x_copy(step + 1, c).start()

    total = 0.0
    for c in range(PIECES):
        x_copy(step, c).wait()

        @pl.when(step == 0)
        def _(c=c):
            for copy in w_copies(c):
                copy.wait()

        part = slice(c * piece, (c + 1) * piece)
        total += dot(xs[slot, :, part], w[part, :])
    q_ref[...] = total[:, :cq].astype(jnp.bfloat16)
    kv_ref[...] = total[:, cq:].astype(jnp.bfloat16)
    if with_decode:

        @pl.when(step == 0)
        def _():
            rows = STEPS * ROWS_DEV * n
            shape = (n * GROUP_ROWS, rows)
            to, fro = iota(shape, 0), iota(shape, 1)
            owner, rs = to // GROUP_ROWS, to % GROUP_ROWS
            wanted = owner * ROWS_DEV + row_of(rs) + jnp.where(rs >= ROWS_DEV, ROWS_DEV * n, 0)
            pick = ((fro == wanted) & (rs < STEPS * ROWS_DEV)).astype(jnp.float32).astype(jnp.bfloat16)
            own = dot(pick, dot(dx_ref[...], w[...]).astype(jnp.bfloat16))
            for h in range(lq):
                part = slice(h * n * GROUP_ROWS, (h + 1) * n * GROUP_ROWS)
                qh_ref[part, :] = own[:, h * HD : (h + 1) * HD].astype(jnp.bfloat16)
            found = block_of_pages(counts, done, placed, table)
            lane = iota((n * GROUP_ROWS, HD), 1)
            r = row_of(lane % GROUP_ROWS)
            kind = lane // GROUP_ROWS
            facts = jnp.where(
                kind == 0,
                by_row(r, [found[i][0] for i in range(ROWS_DEV)], -1),
                jnp.where(
                    kind == 1,
                    by_row(r, [found[i][1] for i in range(ROWS_DEV)], -1),
                    by_row(r, [lens[i] for i in range(ROWS_DEV)], 0),
                ),
            ).astype(jnp.float32)
            sixth = iota((n * GROUP_ROWS, HD), 0) % GROUP_ROWS == 6
            msg_ref[:, :HD] = jnp.where(sixth, facts, own[:, :HD])
            msg_ref[:, HD:] = own[:, HD:]


def project_rows(x, wq, wkv, start, count, size, held=None, ints=None, dx=None, n=None):
    rows, depth = x.shape
    cq, ckv = wq.shape[1], wkv.shape[1]
    lq = cq // HD
    first = held is None
    offset = start // size
    smem, vmem = pl.BlockSpec(memory_space=SMEM), pl.BlockSpec(memory_space=VMEM)
    hbm = pl.BlockSpec(memory_space=pl.ANY)
    out_shape = [
        jax.ShapeDtypeStruct((rows, cq), jnp.bfloat16),
        jax.ShapeDtypeStruct((rows, ckv), jnp.bfloat16),
    ]
    out_specs = [
        pl.BlockSpec((size, cq), lambda i: (i + offset, 0)),
        pl.BlockSpec((size, ckv), lambda i: (i + offset, 0)),
    ]
    if first:
        args = tuple(ints) + (dx, x, wq, wkv)
        in_specs = [smem] * 5 + [vmem] + [hbm] * 3
        out_shape += [
            jax.ShapeDtypeStruct((lq * n * GROUP_ROWS, HD), jnp.bfloat16),
            jax.ShapeDtypeStruct((n * GROUP_ROWS, cq + ckv), jnp.float32),
        ]
        out_specs += [vmem, vmem]
        aliases = {}
    else:
        args = (x, wq, wkv) + held
        in_specs = [hbm] * 5
        aliases = {3: 0, 4: 1}
    return pl.pallas_call(
        functools.partial(project, n, lq, offset, first),
        grid=(count // size,),
        in_specs=in_specs,
        out_specs=out_specs,
        out_shape=out_shape,
        scratch_shapes=[
            VMEM((2, size, depth), jnp.bfloat16),
            VMEM((depth, cq + ckv), jnp.bfloat16),
            pltpu.SemaphoreType.DMA((2, PIECES)),
            pltpu.SemaphoreType.DMA((2, PIECES)),
        ],
        input_output_aliases=aliases,
        compiler_params=pltpu.CompilerParams(vmem_limit_bytes=62 * MIB),
        cost_estimate=pl.CostEstimate(
            flops=2 * count * depth * (cq + ckv),
            bytes_accessed=2 * (count + cq + ckv) * depth + 2 * count * (cq + ckv),
            transcendentals=0,
        ),
        name="project_first" if first else "project_rest",
    )(*args)


LOG2E = 1.4426950408889634
SLAB = 32


def attend_prompt(lq, half, counts, q_hbm, kv_hbm, *refs):
    o_hbm, qs, kvs, outs, sems = refs[-5:]
    group = lax.axis_index("pool")
    c0, c1 = counts[group, 0], counts[group, 1]
    big = jnp.where(c0 == MOST_BLOCKS, 0, jnp.where(c1 == MOST_BLOCKS, c0, c0 + c1))
    cut = jnp.where(c0 == MOST_BLOCKS, c1, c0)

    loads, stores = [], []
    for j in range(MOST_BLOCKS):
        block = big + j if half == 0 else j + jnp.where(j >= big, MOST_BLOCKS, 0)
        rows = pl.ds(pl.multiple_of(block * BLOCK_TOKENS, BLOCK_TOKENS), BLOCK_TOKENS)
        here = pl.ds(j * BLOCK_TOKENS, BLOCK_TOKENS)
        loads.append(
            (
                pltpu.make_async_copy(kv_hbm.at[rows], kvs.at[here], sems.at[0, j]),
                pltpu.make_async_copy(q_hbm.at[rows], qs.at[here], sems.at[1, j]),
            )
        )
        stores.append(pltpu.make_async_copy(outs.at[here], o_hbm.at[rows], sems.at[2, j]))
        for copy in loads[j]:
            copy.start()

    def scores_of(j):
        for copy in loads[j]:
            copy.wait()
        q = qs[j * BLOCK_TOKENS : (j + 1) * BLOCK_TOKENS, :]
        q = jnp.concatenate([q[:, h * HD : (h + 1) * HD] for h in range(lq)], axis=0)
        return dot_t(q, kvs[: (j + 1) * BLOCK_TOKENS, :HD])

    causal = iota((SLAB, BLOCK_TOKENS), 1) - iota((SLAB, BLOCK_TOKENS), 0)
    scores = scores_of(0)
    for j in range(MOST_BLOCKS):
        later = scores_of(j + 1) if j + 1 < MOST_BLOCKS else None
        weights = []
        for at in range(0, lq * BLOCK_TOKENS, SLAB):
            tiles = []
            for i in range(j + 1):
                tile = scores[at : at + SLAB, i * BLOCK_TOKENS : (i + 1) * BLOCK_TOKENS]
                if i == j:
                    tile = jnp.where(causal <= at % BLOCK_TOKENS, tile, MASKED)
                elif half == 1:
                    tile = tile + jnp.where((i < cut) & (cut <= j), MASKED, 0.0)
                tiles.append(tile)
            peak = jnp.max(functools.reduce(jnp.maximum, tiles), axis=1, keepdims=True)
            raised = [jnp.exp2((tile - peak) * (SCALE * LOG2E)) for tile in tiles]
            inverse = 1.0 / jnp.sum(functools.reduce(jnp.add, raised), axis=1, keepdims=True)
            weights.append(jnp.concatenate([(t * inverse).astype(jnp.bfloat16) for t in raised], axis=1))
        mixed = dot(jnp.concatenate(weights, axis=0), kvs[: (j + 1) * BLOCK_TOKENS, HD:])
        for h in range(lq):
            part = mixed[h * BLOCK_TOKENS : (h + 1) * BLOCK_TOKENS]
            outs[j * BLOCK_TOKENS : (j + 1) * BLOCK_TOKENS, h * HD : (h + 1) * HD] = part.astype(jnp.bfloat16)
        stores[j].start()
        scores = later
    for copy in stores:
        copy.wait()


def prompt_attention(counts, q, kv, half, so_far=None, after=None):
    rows, cq = q.shape
    hbm = pl.BlockSpec(memory_space=pl.ANY)
    more = () if so_far is None else (so_far, after)
    tokens = MOST_BLOCKS * BLOCK_TOKENS
    return pl.pallas_call(
        functools.partial(attend_prompt, cq // HD, half),
        in_specs=[pl.BlockSpec(memory_space=SMEM), hbm, hbm] + [hbm] * len(more),
        out_specs=hbm,
        out_shape=jax.ShapeDtypeStruct((rows, cq), jnp.bfloat16),
        scratch_shapes=[
            VMEM((tokens, cq), jnp.bfloat16),
            VMEM((tokens, 2 * HD), jnp.bfloat16),
            VMEM((tokens, cq), jnp.bfloat16),
            pltpu.SemaphoreType.DMA((3, MOST_BLOCKS)),
        ],
        input_output_aliases={3: 0} if more else {},
        compiler_params=pltpu.CompilerParams(vmem_limit_bytes=62 * MIB),
        cost_estimate=pl.CostEstimate(flops=rows * rows * cq, bytes_accessed=4 * rows * cq, transcendentals=rows * rows // 2),
        name="long_prompt" if half == 0 else "short_prompts",
    )(counts, q, kv, *more)


def row_head(n, lq, h, hh):
    at = h * GQ + hh
    return at // lq, at % lq


def handed_part(n, lq, kv_ref, q_ref, msg_ref, o_ref):
    rows = lq * n * GROUP_ROWS
    shape = (rows, HD)
    at_row, lane = iota(shape, 0), iota(shape, 1)
    rs = at_row % GROUP_ROWS
    facts = msg_ref[:, :HD].reshape(n, GROUP_ROWS, HD)[:, 6:7, :]
    facts = jnp.broadcast_to(facts, (n, GROUP_ROWS, HD)).reshape(n * GROUP_ROWS, HD)
    facts = jnp.concatenate([facts] * lq, axis=0)

    def column(kind):
        return jnp.sum(jnp.where(lane == kind * GROUP_ROWS + rs, facts, 0.0), axis=1, keepdims=True)

    first_block, second_block, length = [column(kind) for kind in range(3)]
    scores = dot_t(q_ref[...], kv_ref[:, :HD]) * SCALE
    lane_f = lane.astype(jnp.float32)
    parts = []
    for b in range(NBLK):
        limit = jnp.where(
            first_block == b, length, jnp.where(second_block == b, length - BLOCK_TOKENS, 0.0)
        )
        part = scores[:, b * BLOCK_TOKENS : (b + 1) * BLOCK_TOKENS]
        parts.append(jnp.where(lane_f < limit, part, MASKED))
    scores = jnp.concatenate(parts, axis=1)
    top = jnp.max(scores, axis=1, keepdims=True)
    raised = jnp.exp(scores - top)
    total = jnp.sum(raised, axis=1, keepdims=True)
    near = raised.astype(jnp.bfloat16)
    rest = (raised - near.astype(jnp.float32)).astype(jnp.bfloat16)
    values = kv_ref[:, HD:]
    mixed = (dot(near, values) + dot(rest, values)).reshape(lq * n, GROUP_ROWS, HD)

    def line(col):
        spread = jnp.where(lane == rs, col, 0.0).reshape(lq * n, GROUP_ROWS, HD)
        return jnp.sum(spread, axis=1, keepdims=True)

    rs3 = rs.reshape(lq * n, GROUP_ROWS, HD)
    mixed = jnp.where(rs3 == 6, line(top), jnp.where(rs3 == 7, line(total), mixed))
    for h in range(lq):
        o_ref[:, h * GROUP_ROWS : (h + 1) * GROUP_ROWS, :] = mixed[h * n : (h + 1) * n]


def handed_attention(kv, q_own, msgs, n, lq):
    rows = lq * n * GROUP_ROWS
    vmem = pl.BlockSpec(memory_space=VMEM)
    return pl.pallas_call(
        functools.partial(handed_part, n, lq),
        in_specs=[vmem] * 3,
        out_specs=vmem,
        out_shape=jax.ShapeDtypeStruct((n, lq * GROUP_ROWS, HD), jnp.float32),
        compiler_params=pltpu.CompilerParams(vmem_limit_bytes=32 * MIB),
        cost_estimate=pl.CostEstimate(flops=6 * rows * HD * PTOK, bytes_accessed=2 * MIB, transcendentals=rows * PTOK),
        name="handed_attention",
    )(kv, q_own, msgs)


def owner_part(n, lq, counts, done, placed, table, lens, cache_hbm, held, handed, o_ref, cache, sems, slot_row, slot_limit):
    def slot_copy(slot):
        rows = pl.ds(slot * BLOCK_TOKENS, BLOCK_TOKENS)
        return pltpu.make_async_copy(cache_hbm.at[rows], cache.at[rows], sems.at[slot])

    for slot in range(DEVICE_SLOTS):
        slot_copy(slot).start()
    found = block_of_pages(counts, done, placed, table)
    for r in range(ROWS_DEV):
        for p in range(PAGES):
            slot_row[table[p, r]] = jnp.int32(r)
            slot_limit[table[p, r]] = jnp.where(found[r][p] < 0, lens[r] - p * BLOCK_TOKENS, 0)

    cq = lq * HD
    groups = QH
    rows = groups * GROUP_ROWS
    span = GQ * GROUP_ROWS
    queries, keys = [], []
    for h in range(KVH):
        for hh in range(GQ):
            t, at = row_head(n, lq, h, hh)
            queries.append(held[t * GROUP_ROWS : (t + 1) * GROUP_ROWS, at * HD : (at + 1) * HD])
        t, _ = row_head(n, lq, h, 0)
        keys += [held[t * GROUP_ROWS : (t + 1) * GROUP_ROWS, cq : cq + HD]] * GQ
    queries = jnp.concatenate(queries, axis=0)
    earlier = jnp.concatenate([pltpu.roll(key, ROWS_DEV, 0) for key in keys], axis=0)
    keys = jnp.concatenate(keys, axis=0)
    at_row, lane = iota((rows, HD), 0), iota((rows, HD), 1)
    r = row_of(at_row % GROUP_ROWS)
    rounded = queries.astype(jnp.bfloat16)
    scores = []
    for slot in range(DEVICE_SLOTS):
        slot_copy(slot).wait()
        part = slice(slot * BLOCK_TOKENS, (slot + 1) * BLOCK_TOKENS)
        some = [
            dot_t(rounded[h * span : (h + 1) * span], cache[part, 2 * h * HD : (2 * h + 1) * HD])
            for h in range(KVH)
        ]
        usable = (r == slot_row[slot]) & (lane < slot_limit[slot])
        scores.append(jnp.where(usable, jnp.concatenate(some, axis=0) * SCALE, MASKED))
    scores = jnp.concatenate(scores, axis=1)
    now = jnp.sum(queries * keys, axis=1, keepdims=True) * SCALE
    before = jnp.sum(queries * earlier, axis=1, keepdims=True) * SCALE
    rs1 = iota((rows, 1), 0) % GROUP_ROWS
    before = jnp.where((rs1 >= ROWS_DEV) & (rs1 < STEPS * ROWS_DEV), before, MASKED)

    mixed = handed[...].reshape(groups, GROUP_ROWS, HD)
    shape = (groups, GROUP_ROWS, HD)
    mine = iota(shape, 1) == iota(shape, 2)

    def column(at):
        line = jnp.broadcast_to(mixed[:, at : at + 1, :], shape)
        return jnp.sum(jnp.where(mine, line, 0.0), axis=2, keepdims=True).reshape(rows, 1)

    other_peak, other_total = column(6), column(7)
    peak = jnp.maximum(jnp.max(scores, axis=1, keepdims=True), jnp.maximum(now, before))
    peak = jnp.maximum(peak, other_peak)
    raised, now, before = jnp.exp(scores - peak), jnp.exp(now - peak), jnp.exp(before - peak)
    other = jnp.exp(other_peak - peak)
    inverse = 1.0 / (jnp.sum(raised, axis=1, keepdims=True) + now + before + other * other_total)
    weights = (raised * inverse).astype(jnp.bfloat16)
    now = (now * inverse).astype(jnp.bfloat16).astype(jnp.float32)
    before = (before * inverse).astype(jnp.bfloat16).astype(jnp.float32)
    mixed = mixed.reshape(rows, HD) * (other * inverse)
    out = []
    for h in range(KVH):
        part = slice(h * span, (h + 1) * span)
        own = mixed[part] + dot(weights[part], cache[:, (2 * h + 1) * HD : (2 * h + 2) * HD])
        t, _ = row_head(n, lq, h, 0)
        value = held[t * GROUP_ROWS : (t + 1) * GROUP_ROWS, cq + HD : cq + 2 * HD]
        last = pltpu.roll(value, ROWS_DEV, 0)
        for hh in range(GQ):
            some = slice(h * span + hh * GROUP_ROWS, h * span + (hh + 1) * GROUP_ROWS)
            line = own[hh * GROUP_ROWS : (hh + 1) * GROUP_ROWS]
            out.append(line + now[some] * value + before[some] * last)
    out = jnp.concatenate(out, axis=1)
    for k in range(ROWS_DEV):
        steps = [out[s * ROWS_DEV + k : s * ROWS_DEV + k + 1] for s in range(STEPS)]
        o_ref[k] = jnp.concatenate(steps, axis=0).astype(jnp.bfloat16)


def decode_attention(ints, cache, msgs, parts, n, lq):
    smem, vmem = pl.BlockSpec(memory_space=SMEM), pl.BlockSpec(memory_space=VMEM)
    return pl.pallas_call(
        functools.partial(owner_part, n, lq),
        in_specs=[smem] * 5 + [pl.BlockSpec(memory_space=pl.ANY), vmem, vmem],
        out_specs=vmem,
        out_shape=jax.ShapeDtypeStruct((ROWS_DEV, STEPS, QH * HD), jnp.bfloat16),
        scratch_shapes=[
            VMEM(cache.shape, jnp.bfloat16),
            pltpu.SemaphoreType.DMA((DEVICE_SLOTS,)),
            SMEM((DEVICE_SLOTS,), jnp.int32),
            SMEM((DEVICE_SLOTS,), jnp.int32),
        ],
        compiler_params=pltpu.CompilerParams(vmem_limit_bytes=62 * MIB),
        cost_estimate=pl.CostEstimate(flops=4 * 256 * HD * 768, bytes_accessed=4 * MIB, transcendentals=256 * 768),
        name="decode_attention",
    )(*ints, cache, msgs, parts)


def local(
    prompt_x,
    q_weight,
    kv_weight,
    prompt_blocks,
    finished,
    placement,
    page_table,
    row_lens,
    kv_cache,
    decode_x,
):
    n = lax.axis_size("tp")
    lq = q_weight.shape[1] // HD
    share = GQ // lq
    if share > 1:
        sets = [[k * share + i for i in range(share)] for k in range(n // share)]
        kv_weight = lax.all_gather(kv_weight, "tp", axis=1, tiled=True, axis_index_groups=sets)
    cache = kv_cache.reshape(-1, kv_cache.shape[2])
    dx = decode_x.reshape(-1, decode_x.shape[2])
    placement = placement.transpose(0, 2, 1)
    page_table = page_table.transpose(1, 0)
    ints = (prompt_blocks, finished, placement, page_table, row_lens)
    size = 256
    first = 2 * size
    q, kv, q_own, msgs = project_rows(
        prompt_x, q_weight, kv_weight, 0, first, size, ints=ints, dx=dx, n=n
    )
    msgs = lax.all_to_all(msgs, "tp", split_axis=0, concat_axis=0, tiled=True)
    rest = prompt_x.shape[0] - first
    q, kv = project_rows(prompt_x, q_weight, kv_weight, first, rest, size, held=(q, kv))
    kv_other = lax.ppermute(kv, "pool", [(0, 1), (1, 0)])
    prompt_attn = prompt_attention(prompt_blocks, q, kv, 0)
    handed = handed_attention(kv_other, q_own, msgs, n, lq)
    parts = lax.all_to_all(handed, "tp", split_axis=0, concat_axis=0, tiled=True)
    prompt_attn = prompt_attention(prompt_blocks, q, kv, 1, prompt_attn, handed)
    decode_attn = decode_attention(ints, cache, msgs, parts, n, lq)
    return prompt_attn, decode_attn.transpose(1, 0, 2)


def solution(mesh):
    return jax.shard_map(
        local,
        mesh=mesh,
        in_specs=(
            P(("rep", "pool"), None),
            P(None, "tp"),
            P(None, "tp"),
            P("rep", None),
            P("rep", None),
            P("rep", None, None),
            P(("rep", "pool", "tp"), None),
            P(("rep", "pool", "tp")),
            P(("rep", "pool", "tp"), None, None),
            P(None, ("rep", "pool"), None),
        ),
        out_specs=(P(("rep", "pool"), "tp"), P(None, ("rep", "pool", "tp"), None)),
        check_vma=False,
    )
```

```python
import functools

import jax
import jax.numpy as jnp
from jax import lax
from jax.experimental import pallas as pl
from jax.experimental.pallas import tpu as pltpu
from jax.sharding import PartitionSpec as P

QH = 32
KVH = 8
GQ = QH // KVH
HD = 128
BLOCK_TOKENS = 128
PTOK = 2048
NPROMPT = 3
MOST_BLOCKS = 8
PAGES = 2
STEPS = 2
NBLK = 16
DEVICE_SLOTS = 6
ROWS_DEV = 3
GROUP_ROWS = 8
KEY_VALUE_COLUMNS = 2048
SCALE = HD ** (-0.5)
MASKED = -1e30
PIECES = 5
STRIPS = 4
MIB = 1 << 20
VMEM = pltpu.VMEM
SMEM = pltpu.SMEM


def dot(a, b):
    return jnp.dot(a, b, preferred_element_type=jnp.float32)


def dot_t(a, b):
    return lax.dot_general(a, b, (((1,), (1,)), ((), ())), preferred_element_type=jnp.float32)


def iota(shape, axis):
    return lax.broadcasted_iota(jnp.int32, shape, axis)


def row_of(rs):
    return jnp.where(rs >= 2 * ROWS_DEV, ROWS_DEV, jnp.where(rs >= ROWS_DEV, rs - ROWS_DEV, rs))


def block_of_pages(counts, done, placed, table):
    me = lax.axis_index("tp")
    other = 1 - lax.axis_index("pool")
    first_end = counts[other, 0]
    second_end = first_end + counts[other, 1]
    found = [[jnp.int32(-1)] * PAGES for _ in range(ROWS_DEV)]
    for b in range(NBLK):
        live = jnp.where(
            b < first_end, done[other, 0], jnp.where(b < second_end, done[other, 1], done[other, 2])
        )
        slot = jnp.where((live > 0) & (placed[other, 0, b] == me), placed[other, 1, b], -1)
        for r in range(ROWS_DEV):
            for p in range(PAGES):
                found[r][p] = jnp.where(slot == table[p, r], b, found[r][p])
    return found


def by_row(r, values, rest):
    out = jnp.full(r.shape, rest, jnp.int32)
    for k in range(ROWS_DEV):
        out = jnp.where(r == k, values[k], out)
    return out


def project(n, lq, first, size, *refs):
    counts, done, placed, table, lens, dx_hbm, x_hbm, wq_hbm, wkv_hbm = refs[:9]
    q_hbm, kv_hbm, qh_ref, msg_ref = refs[9:13]
    x0, xs, w, q_out, kv_out, x_sems, w_sems, out_sems = refs[13:]
    depth = w.shape[0]
    count = xs.shape[0]
    cq = lq * HD
    piece = depth // PIECES
    own_rows = dx_hbm.shape[0]
    step = pl.program_id(0)

    def piece_copies(c):
        part = pl.ds(c * piece, piece)
        return [
            pltpu.make_async_copy(x_hbm.at[pl.ds(0, first), part], x0.at[pl.ds(0, first), part], w_sems.at[0, c]),
            pltpu.make_async_copy(dx_hbm.at[:, part], x0.at[pl.ds(first, own_rows), part], w_sems.at[1, c]),
            pltpu.make_async_copy(wq_hbm.at[part], w.at[part, pl.ds(0, cq)], w_sems.at[2, c]),
            pltpu.make_async_copy(wkv_hbm.at[part], w.at[part, pl.ds(cq, 2 * HD)], w_sems.at[3, c]),
        ]

    def x_copies(k):
        strip = size // STRIPS
        copies = []
        for i in range(STRIPS):
            rows = pl.ds(pl.multiple_of(first + k * size + i * strip, 16), strip)
            copies.append(
                pltpu.make_async_copy(x_hbm.at[rows], xs.at[k, pl.ds(i * strip, strip)], x_sems.at[k, i])
            )
        return copies

    def out_copies(k):
        if isinstance(k, int):
            rows = pl.ds(0, first)
        else:
            rows = pl.ds(pl.multiple_of(first + (k - 1) * size, BLOCK_TOKENS), size)
        return [
            pltpu.make_async_copy(q_out.at[rows], q_hbm.at[rows], out_sems.at[0, k]),
            pltpu.make_async_copy(kv_out.at[rows], kv_hbm.at[rows], out_sems.at[1, k]),
        ]

    def keep(total, rows):
        q_out[rows, :] = total[:, :cq].astype(jnp.bfloat16)
        kv_out[rows, :] = total[:, cq:].astype(jnp.bfloat16)

    @pl.when(step == 0)
    def _():
        for c in range(PIECES):
            for copy in piece_copies(c):
                copy.start()
        for k in range(count):
            for copy in x_copies(k):
                copy.start()
        total = 0.0
        for c in range(PIECES):
            for copy in piece_copies(c):
                copy.wait()
            part = slice(c * piece, (c + 1) * piece)
            total += dot(x0[:, part], w[part, :])
        keep(total[:first], pl.ds(0, first))
        for copy in out_copies(0):
            copy.start()
        shape = (n * GROUP_ROWS, own_rows)
        to, fro = iota(shape, 0), iota(shape, 1)
        owner, rs = to // GROUP_ROWS, to % GROUP_ROWS
        wanted = owner * ROWS_DEV + row_of(rs) + jnp.where(rs >= ROWS_DEV, ROWS_DEV * n, 0)
        pick = ((fro == wanted) & (rs < STEPS * ROWS_DEV)).astype(jnp.float32).astype(jnp.bfloat16)
        own = dot(pick, total[first:].astype(jnp.bfloat16))
        for h in range(lq):
            part = slice(h * n * GROUP_ROWS, (h + 1) * n * GROUP_ROWS)
            qh_ref[part, :] = own[:, h * HD : (h + 1) * HD].astype(jnp.bfloat16)
        found = block_of_pages(counts, done, placed, table)
        lane = iota((n * GROUP_ROWS, HD), 1)
        r = row_of(lane % GROUP_ROWS)
        kind = lane // GROUP_ROWS
        facts = jnp.where(
            kind == 0,
            by_row(r, [found[i][0] for i in range(ROWS_DEV)], -1),
            jnp.where(
                kind == 1,
                by_row(r, [found[i][1] for i in range(ROWS_DEV)], -1),
                by_row(r, [lens[i] for i in range(ROWS_DEV)], 0),
            ),
        ).astype(jnp.float32)
        sixth = iota((n * GROUP_ROWS, HD), 0) % GROUP_ROWS == 6
        msg_ref[:, :HD] = jnp.where(sixth, facts, own[:, :HD])
        msg_ref[:, HD:] = own[:, HD:]

    @pl.when(step > 0)
    def _():
        for copy in x_copies(step - 1):
            copy.wait()
        keep(dot(xs[step - 1], w[...]), pl.ds(pl.multiple_of(first + (step - 1) * size, BLOCK_TOKENS), size))
        for copy in out_copies(step):
            copy.start()

    @pl.when(step == count)
    def _():
        for copy in out_copies(0):
            copy.wait()
        for k in range(1, count + 1):
            for copy in out_copies(jnp.int32(k)):
                copy.wait()


def project_all(ints, dx, x, wq, wkv, n, first, size):
    rows, depth = x.shape
    cq, ckv = wq.shape[1], wkv.shape[1]
    lq = cq // HD
    count = (rows - first) // size
    smem, vmem = pl.BlockSpec(memory_space=SMEM), pl.BlockSpec(memory_space=VMEM)
    hbm = pl.BlockSpec(memory_space=pl.ANY)
    return pl.pallas_call(
        functools.partial(project, n, lq, first, size),
        grid=(1 + count,),
        in_specs=[smem] * 5 + [hbm] * 4,
        out_specs=[hbm, hbm, vmem, vmem],
        out_shape=[
            jax.ShapeDtypeStruct((rows, cq), jnp.bfloat16),
            jax.ShapeDtypeStruct((rows, ckv), jnp.bfloat16),
            jax.ShapeDtypeStruct((lq * n * GROUP_ROWS, HD), jnp.bfloat16),
            jax.ShapeDtypeStruct((n * GROUP_ROWS, cq + ckv), jnp.float32),
        ],
        scratch_shapes=[
            VMEM((first + dx.shape[0], depth), jnp.bfloat16),
            VMEM((count, size, depth), jnp.bfloat16),
            VMEM((depth, cq + ckv), jnp.bfloat16),
            VMEM((rows, cq), jnp.bfloat16),
            VMEM((rows, ckv), jnp.bfloat16),
            pltpu.SemaphoreType.DMA((count, STRIPS)),
            pltpu.SemaphoreType.DMA((4, PIECES)),
            pltpu.SemaphoreType.DMA((2, count + 1)),
        ],
        compiler_params=pltpu.CompilerParams(vmem_limit_bytes=62 * MIB),
        cost_estimate=pl.CostEstimate(
            flops=2 * rows * depth * (cq + ckv),
            bytes_accessed=2 * (rows + cq + ckv) * depth + 2 * rows * (cq + ckv),
            transcendentals=0,
        ),
        name="project",
    )(*ints, dx, x, wq, wkv)


LOG2E = 1.4426950408889634
SLAB = 32


def attend_prompt(lq, half, counts, q_hbm, kv_hbm, *refs):
    o_hbm, done_ref, qs, kvs, outs, sems = refs[-6:]
    done_ref[...] = jnp.zeros_like(done_ref)
    group = lax.axis_index("pool")
    c0, c1 = counts[group, 0], counts[group, 1]
    big = jnp.where(c0 == MOST_BLOCKS, 0, jnp.where(c1 == MOST_BLOCKS, c0, c0 + c1))
    cut = jnp.where(c0 == MOST_BLOCKS, c1, c0)

    loads, stores = [], []
    for j in range(MOST_BLOCKS):
        block = big + j if half == 0 else j + jnp.where(j >= big, MOST_BLOCKS, 0)
        rows = pl.ds(pl.multiple_of(block * BLOCK_TOKENS, BLOCK_TOKENS), BLOCK_TOKENS)
        here = pl.ds(j * BLOCK_TOKENS, BLOCK_TOKENS)
        loads.append(pltpu.make_async_copy(kv_hbm.at[rows], kvs.at[here], sems.at[0, j]))
        loads.append(pltpu.make_async_copy(q_hbm.at[rows], qs.at[here], sems.at[1, j]))
        stores.append(pltpu.make_async_copy(outs.at[here], o_hbm.at[rows], sems.at[2, j]))
    for copy in loads:
        copy.start()
    for copy in loads:
        copy.wait()

    def scores_of(j):
        q = qs[j * BLOCK_TOKENS : (j + 1) * BLOCK_TOKENS, :]
        q = jnp.concatenate([q[:, h * HD : (h + 1) * HD] for h in range(lq)], axis=0)
        return dot_t(q, kvs[: (j + 1) * BLOCK_TOKENS, :HD])

    causal = iota((SLAB, BLOCK_TOKENS), 1) - iota((SLAB, BLOCK_TOKENS), 0)
    scores = scores_of(0)
    for j in range(MOST_BLOCKS):
        later = scores_of(j + 1) if j + 1 < MOST_BLOCKS else None
        weights = []
        for at in range(0, lq * BLOCK_TOKENS, SLAB):
            tiles = []
            for i in range(j + 1):
                tile = scores[at : at + SLAB, i * BLOCK_TOKENS : (i + 1) * BLOCK_TOKENS]
                if i == j:
                    tile = jnp.where(causal <= at % BLOCK_TOKENS, tile, MASKED)
                elif half == 1:
                    tile = tile + jnp.where((i < cut) & (cut <= j), MASKED, 0.0)
                tiles.append(tile)
            peak = jnp.max(functools.reduce(jnp.maximum, tiles), axis=1, keepdims=True)
            raised = [jnp.exp2((tile - peak) * (SCALE * LOG2E)) for tile in tiles]
            inverse = 1.0 / jnp.sum(functools.reduce(jnp.add, raised), axis=1, keepdims=True)
            weights.append(jnp.concatenate([(t * inverse).astype(jnp.bfloat16) for t in raised], axis=1))
        mixed = dot(jnp.concatenate(weights, axis=0), kvs[: (j + 1) * BLOCK_TOKENS, HD:])
        for h in range(lq):
            part = mixed[h * BLOCK_TOKENS : (h + 1) * BLOCK_TOKENS]
            outs[j * BLOCK_TOKENS : (j + 1) * BLOCK_TOKENS, h * HD : (h + 1) * HD] = part.astype(jnp.bfloat16)
        scores = later
    for copy in stores:
        copy.start()
    for copy in stores:
        copy.wait()


def prompt_attention(counts, q, kv, half, so_far=None, after=None):
    rows, cq = q.shape
    hbm = pl.BlockSpec(memory_space=pl.ANY)
    more = () if so_far is None else (so_far, after)
    tokens = MOST_BLOCKS * BLOCK_TOKENS
    return pl.pallas_call(
        functools.partial(attend_prompt, cq // HD, half),
        in_specs=[pl.BlockSpec(memory_space=SMEM), hbm, hbm] + [hbm] * len(more),
        out_specs=[hbm, pl.BlockSpec(memory_space=VMEM)],
        out_shape=[
            jax.ShapeDtypeStruct((rows, cq), jnp.bfloat16),
            jax.ShapeDtypeStruct((8, HD), jnp.float32),
        ],
        scratch_shapes=[
            VMEM((tokens, cq), jnp.bfloat16),
            VMEM((tokens, 2 * HD), jnp.bfloat16),
            VMEM((tokens, cq), jnp.bfloat16),
            pltpu.SemaphoreType.DMA((3, MOST_BLOCKS)),
        ],
        input_output_aliases={3: 0} if more else {},
        compiler_params=pltpu.CompilerParams(vmem_limit_bytes=62 * MIB),
        cost_estimate=pl.CostEstimate(flops=rows * rows * cq, bytes_accessed=4 * rows * cq, transcendentals=rows * rows // 2),
        name="long_prompt" if half == 0 else "short_prompts",
    )(counts, q, kv, *more)


def row_head(n, lq, h, hh):
    at = h * GQ + hh
    return at // lq, at % lq


def handed_part(n, lq, kv_ref, q_ref, msg_ref, _, o_ref):
    rows = lq * n * GROUP_ROWS
    shape = (rows, HD)
    at_row, lane = iota(shape, 0), iota(shape, 1)
    rs = at_row % GROUP_ROWS
    facts = msg_ref[:, :HD].reshape(n, GROUP_ROWS, HD)[:, 6:7, :]
    facts = jnp.broadcast_to(facts, (n, GROUP_ROWS, HD)).reshape(n * GROUP_ROWS, HD)
    facts = jnp.concatenate([facts] * lq, axis=0)

    def column(kind):
        return jnp.sum(jnp.where(lane == kind * GROUP_ROWS + rs, facts, 0.0), axis=1, keepdims=True)

    first_block, second_block, length = [column(kind) for kind in range(3)]
    scores = dot_t(q_ref[...], kv_ref[:, :HD]) * SCALE
    lane_f = lane.astype(jnp.float32)
    parts = []
    for b in range(NBLK):
        limit = jnp.where(
            first_block == b, length, jnp.where(second_block == b, length - BLOCK_TOKENS, 0.0)
        )
        part = scores[:, b * BLOCK_TOKENS : (b + 1) * BLOCK_TOKENS]
        parts.append(jnp.where(lane_f < limit, part, MASKED))
    scores = jnp.concatenate(parts, axis=1)
    top = jnp.max(scores, axis=1, keepdims=True)
    raised = jnp.exp(scores - top)
    total = jnp.sum(raised, axis=1, keepdims=True)
    near = raised.astype(jnp.bfloat16)
    rest = (raised - near.astype(jnp.float32)).astype(jnp.bfloat16)
    values = kv_ref[:, HD:]
    mixed = (dot(near, values) + dot(rest, values)).reshape(lq * n, GROUP_ROWS, HD)

    def line(col):
        spread = jnp.where(lane == rs, col, 0.0).reshape(lq * n, GROUP_ROWS, HD)
        return jnp.sum(spread, axis=1, keepdims=True)

    rs3 = rs.reshape(lq * n, GROUP_ROWS, HD)
    mixed = jnp.where(rs3 == 6, line(top), jnp.where(rs3 == 7, line(total), mixed))
    for h in range(lq):
        o_ref[:, h * GROUP_ROWS : (h + 1) * GROUP_ROWS, :] = mixed[h * n : (h + 1) * n]


def handed_attention(kv, q_own, msgs, after, n, lq):
    rows = lq * n * GROUP_ROWS
    vmem = pl.BlockSpec(memory_space=VMEM)
    return pl.pallas_call(
        functools.partial(handed_part, n, lq),
        in_specs=[vmem] * 3 + [pl.BlockSpec(memory_space=pl.ANY)],
        out_specs=vmem,
        out_shape=jax.ShapeDtypeStruct((n, lq * GROUP_ROWS, HD), jnp.float32),
        compiler_params=pltpu.CompilerParams(vmem_limit_bytes=24 * MIB),
        cost_estimate=pl.CostEstimate(flops=6 * rows * HD * PTOK, bytes_accessed=2 * MIB, transcendentals=rows * PTOK),
        name="handed_attention",
    )(kv, q_own, msgs, after)


def owner_part(n, lq, counts, done, placed, table, lens, cache_hbm, held, handed, o_ref, cache, sem, slot_row, slot_limit):
    load = pltpu.make_async_copy(cache_hbm, cache, sem)
    load.start()
    found = block_of_pages(counts, done, placed, table)
    for r in range(ROWS_DEV):
        for p in range(PAGES):
            slot_row[table[p, r]] = jnp.int32(r)
            slot_limit[table[p, r]] = jnp.where(found[r][p] < 0, lens[r] - p * BLOCK_TOKENS, 0)

    cq = lq * HD
    groups = QH
    rows = groups * GROUP_ROWS
    span = GQ * GROUP_ROWS
    queries, keys = [], []
    for h in range(KVH):
        for hh in range(GQ):
            t, at = row_head(n, lq, h, hh)
            queries.append(held[t * GROUP_ROWS : (t + 1) * GROUP_ROWS, at * HD : (at + 1) * HD])
        t, _ = row_head(n, lq, h, 0)
        keys += [held[t * GROUP_ROWS : (t + 1) * GROUP_ROWS, cq : cq + HD]] * GQ
    queries = jnp.concatenate(queries, axis=0)
    earlier = jnp.concatenate([pltpu.roll(key, ROWS_DEV, 0) for key in keys], axis=0)
    keys = jnp.concatenate(keys, axis=0)
    at_row, lane = iota((rows, HD), 0), iota((rows, HD), 1)
    r = row_of(at_row % GROUP_ROWS)
    rounded = queries.astype(jnp.bfloat16)
    now = jnp.sum(queries * keys, axis=1, keepdims=True) * SCALE
    before = jnp.sum(queries * earlier, axis=1, keepdims=True) * SCALE
    load.wait()
    scores = jnp.concatenate(
        [dot_t(rounded[h * span : (h + 1) * span], cache[:, 2 * h * HD : (2 * h + 1) * HD]) for h in range(KVH)],
        axis=0,
    )
    parts = []
    for slot in range(DEVICE_SLOTS):
        part = scores[:, slot * BLOCK_TOKENS : (slot + 1) * BLOCK_TOKENS]
        usable = (r == slot_row[slot]) & (lane < slot_limit[slot])
        parts.append(jnp.where(usable, part * SCALE, MASKED))
    scores = jnp.concatenate(parts, axis=1)
    rs1 = iota((rows, 1), 0) % GROUP_ROWS
    before = jnp.where((rs1 >= ROWS_DEV) & (rs1 < STEPS * ROWS_DEV), before, MASKED)

    mixed = handed[...].reshape(groups, GROUP_ROWS, HD)
    shape = (groups, GROUP_ROWS, HD)
    mine = iota(shape, 1) == iota(shape, 2)

    def column(at):
        line = jnp.broadcast_to(mixed[:, at : at + 1, :], shape)
        return jnp.sum(jnp.where(mine, line, 0.0), axis=2, keepdims=True).reshape(rows, 1)

    other_peak, other_total = column(6), column(7)
    peak = jnp.maximum(jnp.max(scores, axis=1, keepdims=True), jnp.maximum(now, before))
    peak = jnp.maximum(peak, other_peak)
    raised, now, before = jnp.exp(scores - peak), jnp.exp(now - peak), jnp.exp(before - peak)
    other = jnp.exp(other_peak - peak)
    inverse = 1.0 / (jnp.sum(raised, axis=1, keepdims=True) + now + before + other * other_total)
    weights = (raised * inverse).astype(jnp.bfloat16)
    now = (now * inverse).astype(jnp.bfloat16).astype(jnp.float32)
    before = (before * inverse).astype(jnp.bfloat16).astype(jnp.float32)
    mixed = mixed.reshape(rows, HD) * (other * inverse)
    out = []
    for h in range(KVH):
        part = slice(h * span, (h + 1) * span)
        own = mixed[part] + dot(weights[part], cache[:, (2 * h + 1) * HD : (2 * h + 2) * HD])
        t, _ = row_head(n, lq, h, 0)
        value = held[t * GROUP_ROWS : (t + 1) * GROUP_ROWS, cq + HD : cq + 2 * HD]
        last = pltpu.roll(value, ROWS_DEV, 0)
        for hh in range(GQ):
            some = slice(h * span + hh * GROUP_ROWS, h * span + (hh + 1) * GROUP_ROWS)
            line = own[hh * GROUP_ROWS : (hh + 1) * GROUP_ROWS]
            out.append(line + now[some] * value + before[some] * last)
    out = jnp.concatenate(out, axis=1)
    for k in range(ROWS_DEV):
        steps = [out[s * ROWS_DEV + k : s * ROWS_DEV + k + 1] for s in range(STEPS)]
        o_ref[k] = jnp.concatenate(steps, axis=0).astype(jnp.bfloat16)


def decode_attention(ints, cache, msgs, parts, n, lq):
    smem, vmem = pl.BlockSpec(memory_space=SMEM), pl.BlockSpec(memory_space=VMEM)
    return pl.pallas_call(
        functools.partial(owner_part, n, lq),
        in_specs=[smem] * 5 + [pl.BlockSpec(memory_space=pl.ANY), vmem, vmem],
        out_specs=vmem,
        out_shape=jax.ShapeDtypeStruct((ROWS_DEV, STEPS, QH * HD), jnp.bfloat16),
        scratch_shapes=[
            VMEM(cache.shape, jnp.bfloat16),
            pltpu.SemaphoreType.DMA,
            SMEM((DEVICE_SLOTS,), jnp.int32),
            SMEM((DEVICE_SLOTS,), jnp.int32),
        ],
        compiler_params=pltpu.CompilerParams(vmem_limit_bytes=62 * MIB),
        cost_estimate=pl.CostEstimate(flops=4 * 256 * HD * 768, bytes_accessed=4 * MIB, transcendentals=256 * 768),
        name="decode_attention",
    )(*ints, cache, msgs, parts)


def local(
    prompt_x,
    q_weight,
    kv_weight,
    prompt_blocks,
    finished,
    placement,
    page_table,
    row_lens,
    kv_cache,
    decode_x,
):
    n = lax.axis_size("tp")
    lq = q_weight.shape[1] // HD
    share = GQ // lq
    if share > 1:
        sets = [[k * share + i for i in range(share)] for k in range(n // share)]
        kv_weight = lax.all_gather(kv_weight, "tp", axis=1, tiled=True, axis_index_groups=sets)
    cache = kv_cache.reshape(-1, kv_cache.shape[2])
    dx = decode_x.reshape(-1, decode_x.shape[2])
    placement = placement.transpose(0, 2, 1)
    page_table = page_table.transpose(1, 0)
    ints = (prompt_blocks, finished, placement, page_table, row_lens)
    first, size = 256, 896
    q, kv, q_own, msgs = project_all(ints, dx, prompt_x, q_weight, kv_weight, n, first, size)
    msgs = lax.all_to_all(msgs, "tp", split_axis=0, concat_axis=0, tiled=True)
    kv_other = lax.ppermute(kv, "pool", [(0, 1), (1, 0)])
    prompt_attn, made = prompt_attention(prompt_blocks, q, kv, 0)
    handed = handed_attention(kv_other, q_own, msgs, made, n, lq)
    parts = lax.all_to_all(handed, "tp", split_axis=0, concat_axis=0, tiled=True)
    prompt_attn, _ = prompt_attention(prompt_blocks, q, kv, 1, prompt_attn, handed)
    decode_attn = decode_attention(ints, cache, msgs, parts, n, lq)
    return prompt_attn, decode_attn.transpose(1, 0, 2)


def solution(mesh):
    return jax.shard_map(
        local,
        mesh=mesh,
        in_specs=(
            P(("rep", "pool"), None),
            P(None, "tp"),
            P(None, "tp"),
            P("rep", None),
            P("rep", None),
            P("rep", None, None),
            P(("rep", "pool", "tp"), None),
            P(("rep", "pool", "tp")),
            P(("rep", "pool", "tp"), None, None),
            P(None, ("rep", "pool"), None),
        ),
        out_specs=(P(("rep", "pool"), "tp"), P(None, ("rep", "pool", "tp"), None)),
        check_vma=False,
    )
```

```python
import functools

import jax
import jax.numpy as jnp
from jax import lax
from jax.experimental import pallas as pl
from jax.experimental.pallas import tpu as pltpu
from jax.sharding import PartitionSpec as P

QH = 32
KVH = 8
GQ = QH // KVH
HD = 128
BLOCK_TOKENS = 128
PTOK = 2048
NPROMPT = 3
MOST_BLOCKS = 8
PAGES = 2
STEPS = 2
NBLK = 16
DEVICE_SLOTS = 6
ROWS_DEV = 3
GROUP_ROWS = 8
KEY_VALUE_COLUMNS = 2048
SCALE = HD ** (-0.5)
MASKED = -1e30
PIECES = 5
STRIPS = 4
MIB = 1 << 20
VMEM = pltpu.VMEM
SMEM = pltpu.SMEM


def dot(a, b):
    return jnp.dot(a, b, preferred_element_type=jnp.float32)


def dot_t(a, b):
    return lax.dot_general(a, b, (((1,), (1,)), ((), ())), preferred_element_type=jnp.float32)


def iota(shape, axis):
    return lax.broadcasted_iota(jnp.int32, shape, axis)


def row_of(rs):
    return jnp.where(rs >= 2 * ROWS_DEV, ROWS_DEV, jnp.where(rs >= ROWS_DEV, rs - ROWS_DEV, rs))


def block_of_pages(counts, done, placed, table):
    me = lax.axis_index("tp")
    other = 1 - lax.axis_index("pool")
    first_end = counts[other, 0]
    second_end = first_end + counts[other, 1]
    found = [[jnp.int32(-1)] * PAGES for _ in range(ROWS_DEV)]
    for b in range(NBLK):
        live = jnp.where(
            b < first_end, done[other, 0], jnp.where(b < second_end, done[other, 1], done[other, 2])
        )
        slot = jnp.where((live > 0) & (placed[other, 0, b] == me), placed[other, 1, b], -1)
        for r in range(ROWS_DEV):
            for p in range(PAGES):
                found[r][p] = jnp.where(slot == table[p, r], b, found[r][p])
    return found


def by_row(r, values, rest):
    out = jnp.full(r.shape, rest, jnp.int32)
    for k in range(ROWS_DEV):
        out = jnp.where(r == k, values[k], out)
    return out


def project(n, lq, first, size, *refs):
    counts, done, placed, table, lens, dx_hbm, x_hbm, wq_hbm, wkv_hbm = refs[:9]
    q_hbm, kv_hbm, qh_ref, msg_ref = refs[9:13]
    x0, xs, w, q_out, kv_out, x_sems, w_sems, out_sems = refs[13:]
    depth = w.shape[0]
    count = xs.shape[0]
    cq = lq * HD
    piece = depth // PIECES
    own_rows = dx_hbm.shape[0]
    step = pl.program_id(0)

    def piece_copies(c):
        part = pl.ds(c * piece, piece)
        return [
            pltpu.make_async_copy(x_hbm.at[pl.ds(0, first), part], x0.at[pl.ds(0, first), part], w_sems.at[0, c]),
            pltpu.make_async_copy(dx_hbm.at[:, part], x0.at[pl.ds(first, own_rows), part], w_sems.at[1, c]),
            pltpu.make_async_copy(wq_hbm.at[part], w.at[part, pl.ds(0, cq)], w_sems.at[2, c]),
            pltpu.make_async_copy(wkv_hbm.at[part], w.at[part, pl.ds(cq, 2 * HD)], w_sems.at[3, c]),
        ]

    def x_copies(k):
        strip = size // STRIPS
        copies = []
        for i in range(STRIPS):
            rows = pl.ds(pl.multiple_of(first + k * size + i * strip, 16), strip)
            copies.append(
                pltpu.make_async_copy(x_hbm.at[rows], xs.at[k, pl.ds(i * strip, strip)], x_sems.at[k, i])
            )
        return copies

    def out_copies(k):
        if isinstance(k, int):
            rows = pl.ds(0, first)
        else:
            rows = pl.ds(pl.multiple_of(first + (k - 1) * size, BLOCK_TOKENS), size)
        return [
            pltpu.make_async_copy(q_out.at[rows], q_hbm.at[rows], out_sems.at[0, k]),
            pltpu.make_async_copy(kv_out.at[rows], kv_hbm.at[rows], out_sems.at[1, k]),
        ]

    def keep(total, rows):
        q_out[rows, :] = total[:, :cq].astype(jnp.bfloat16)
        kv_out[rows, :] = total[:, cq:].astype(jnp.bfloat16)

    @pl.when(step == 0)
    def _():
        for c in range(PIECES):
            for copy in piece_copies(c):
                copy.start()
        for k in range(count):
            for copy in x_copies(k):
                copy.start()
        total = 0.0
        for c in range(PIECES):
            for copy in piece_copies(c):
                copy.wait()
            part = slice(c * piece, (c + 1) * piece)
            total += dot(x0[:, part], w[part, :])
        keep(total[:first], pl.ds(0, first))
        for copy in out_copies(0):
            copy.start()
        shape = (n * GROUP_ROWS, own_rows)
        to, fro = iota(shape, 0), iota(shape, 1)
        owner, rs = to // GROUP_ROWS, to % GROUP_ROWS
        wanted = owner * ROWS_DEV + row_of(rs) + jnp.where(rs >= ROWS_DEV, ROWS_DEV * n, 0)
        pick = ((fro == wanted) & (rs < STEPS * ROWS_DEV)).astype(jnp.float32).astype(jnp.bfloat16)
        own = dot(pick, total[first:].astype(jnp.bfloat16))
        for h in range(lq):
            part = slice(h * n * GROUP_ROWS, (h + 1) * n * GROUP_ROWS)
            qh_ref[part, :] = own[:, h * HD : (h + 1) * HD].astype(jnp.bfloat16)
        found = block_of_pages(counts, done, placed, table)
        lane = iota((n * GROUP_ROWS, HD), 1)
        r = row_of(lane % GROUP_ROWS)
        kind = lane // GROUP_ROWS
        facts = jnp.where(
            kind == 0,
            by_row(r, [found[i][0] for i in range(ROWS_DEV)], -1),
            jnp.where(
                kind == 1,
                by_row(r, [found[i][1] for i in range(ROWS_DEV)], -1),
                by_row(r, [lens[i] for i in range(ROWS_DEV)], 0),
            ),
        ).astype(jnp.float32)
        sixth = iota((n * GROUP_ROWS, HD), 0) % GROUP_ROWS == 6
        msg_ref[:, :HD] = jnp.where(sixth, facts, own[:, :HD]).astype(jnp.bfloat16)
        msg_ref[:, HD:] = own[:, HD:].astype(jnp.bfloat16)

    @pl.when(step > 0)
    def _():
        for copy in x_copies(step - 1):
            copy.wait()
        rows = pl.ds(pl.multiple_of(first + (step - 1) * size, BLOCK_TOKENS), size)
        half = depth // 2
        x = xs.at[step - 1]
        q_out[rows, :] = dot(x[...], w[:, :cq]).astype(jnp.bfloat16)
        low, high = dot(x[:, :half], w[:half, cq:]), dot(x[:, half:], w[half:, cq:])
        kv_out[rows, :] = (low + high).astype(jnp.bfloat16)
        for copy in out_copies(step):
            copy.start()

    @pl.when(step == count)
    def _():
        for copy in out_copies(0):
            copy.wait()
        for k in range(1, count + 1):
            for copy in out_copies(jnp.int32(k)):
                copy.wait()


def project_all(ints, dx, x, wq, wkv, n, first, size):
    rows, depth = x.shape
    cq, ckv = wq.shape[1], wkv.shape[1]
    lq = cq // HD
    count = (rows - first) // size
    smem, vmem = pl.BlockSpec(memory_space=SMEM), pl.BlockSpec(memory_space=VMEM)
    hbm = pl.BlockSpec(memory_space=pl.ANY)
    return pl.pallas_call(
        functools.partial(project, n, lq, first, size),
        grid=(1 + count,),
        in_specs=[smem] * 5 + [hbm] * 4,
        out_specs=[hbm, hbm, vmem, vmem],
        out_shape=[
            jax.ShapeDtypeStruct((rows, cq), jnp.bfloat16),
            jax.ShapeDtypeStruct((rows, ckv), jnp.bfloat16),
            jax.ShapeDtypeStruct((lq * n * GROUP_ROWS, HD), jnp.bfloat16),
            jax.ShapeDtypeStruct((n * GROUP_ROWS, cq + ckv), jnp.bfloat16),
        ],
        scratch_shapes=[
            VMEM((first + dx.shape[0], depth), jnp.bfloat16),
            VMEM((count, size, depth), jnp.bfloat16),
            VMEM((depth, cq + ckv), jnp.bfloat16),
            VMEM((rows, cq), jnp.bfloat16),
            VMEM((rows, ckv), jnp.bfloat16),
            pltpu.SemaphoreType.DMA((count, STRIPS)),
            pltpu.SemaphoreType.DMA((4, PIECES)),
            pltpu.SemaphoreType.DMA((2, count + 1)),
        ],
        compiler_params=pltpu.CompilerParams(vmem_limit_bytes=62 * MIB),
        cost_estimate=pl.CostEstimate(
            flops=2 * rows * depth * (cq + ckv),
            bytes_accessed=2 * (rows + cq + ckv) * depth + 2 * rows * (cq + ckv),
            transcendentals=0,
        ),
        name="project",
    )(*ints, dx, x, wq, wkv)


LOG2E = 1.4426950408889634


def attend_prompt(lq, counts, q_hbm, kv_hbm, o_hbm, made_ref, qs, kvs, outs, sems):
    made_ref[...] = jnp.zeros_like(made_ref)
    group = lax.axis_index("pool")
    c0, c1 = counts[group, 0], counts[group, 1]
    big = jnp.where(c0 == MOST_BLOCKS, 0, jnp.where(c1 == MOST_BLOCKS, c0, c0 + c1))
    cut = jnp.where(c0 == MOST_BLOCKS, c1, c0)
    loads, stores = [], []
    for half in range(2):
        for j in range(MOST_BLOCKS):
            block = big + j if half == 0 else j + jnp.where(j >= big, MOST_BLOCKS, 0)
            rows = pl.ds(pl.multiple_of(block * BLOCK_TOKENS, BLOCK_TOKENS), BLOCK_TOKENS)
            here = pl.ds(j * BLOCK_TOKENS, BLOCK_TOKENS)
            loads.append(pltpu.make_async_copy(kv_hbm.at[rows], kvs.at[half, here], sems.at[0, half, j]))
            loads.append(pltpu.make_async_copy(q_hbm.at[rows], qs.at[half, here], sems.at[1, half, j]))
            stores.append(pltpu.make_async_copy(outs.at[half, here], o_hbm.at[rows], sems.at[2, half, j]))
    for copy in loads:
        copy.start()
    for copy in loads:
        copy.wait()
    tokens = MOST_BLOCKS * BLOCK_TOKENS
    shape = (BLOCK_TOKENS, lq * BLOCK_TOKENS)
    causal = iota(shape, 0) <= iota(shape, 1) % BLOCK_TOKENS
    flipped = [kvs[half, :, HD:].T for half in range(2)]

    def scores_of(half, j):
        q = qs[half, j * BLOCK_TOKENS : (j + 1) * BLOCK_TOKENS, :]
        q = jnp.concatenate([q[:, h * HD : (h + 1) * HD] for h in range(lq)], axis=0)
        return dot_t(kvs[half, : (j + 1) * BLOCK_TOKENS, :HD], q)

    order = [(half, j) for half in range(2) for j in range(MOST_BLOCKS)]
    scores = scores_of(*order[0])
    for k, (half, j) in enumerate(order):
        later = scores_of(*order[k + 1]) if k + 1 < len(order) else None
        weights = []
        for h in range(lq):
            cols = slice(h * BLOCK_TOKENS, (h + 1) * BLOCK_TOKENS)
            tiles = []
            for i in range(j + 1):
                tile = scores[i * BLOCK_TOKENS : (i + 1) * BLOCK_TOKENS, cols]
                if i == j:
                    tile = jnp.where(causal[:, cols], tile, MASKED)
                elif half == 1:
                    tile = tile + jnp.where((i < cut) & (cut <= j), MASKED, 0.0)
                tiles.append(tile)
            peak = jnp.max(functools.reduce(jnp.maximum, tiles), axis=0, keepdims=True)
            raised = [jnp.exp2((tile - peak) * (SCALE * LOG2E)) for tile in tiles]
            inverse = 1.0 / jnp.sum(functools.reduce(jnp.add, raised), axis=0, keepdims=True)
            weights.append(jnp.concatenate([(t * inverse).astype(jnp.bfloat16) for t in raised], axis=0))
        mixed = dot(flipped[half][:, : (j + 1) * BLOCK_TOKENS], jnp.concatenate(weights, axis=1))
        mixed = mixed.astype(jnp.bfloat16)
        for h in range(lq):
            part = mixed[:, h * BLOCK_TOKENS : (h + 1) * BLOCK_TOKENS].T
            outs[half, j * BLOCK_TOKENS : (j + 1) * BLOCK_TOKENS, h * HD : (h + 1) * HD] = part
        scores = later
    for copy in stores:
        copy.start()
    for copy in stores:
        copy.wait()


def prompt_attention(counts, q, kv):
    rows, cq = q.shape
    hbm = pl.BlockSpec(memory_space=pl.ANY)
    tokens = MOST_BLOCKS * BLOCK_TOKENS
    return pl.pallas_call(
        functools.partial(attend_prompt, cq // HD),
        in_specs=[pl.BlockSpec(memory_space=SMEM), hbm, hbm],
        out_specs=[hbm, pl.BlockSpec(memory_space=VMEM)],
        out_shape=[
            jax.ShapeDtypeStruct((rows, cq), jnp.bfloat16),
            jax.ShapeDtypeStruct((8, HD), jnp.float32),
        ],
        scratch_shapes=[
            VMEM((2, tokens, cq), jnp.bfloat16),
            VMEM((2, tokens, 2 * HD), jnp.bfloat16),
            VMEM((2, tokens, cq), jnp.bfloat16),
            pltpu.SemaphoreType.DMA((3, 2, MOST_BLOCKS)),
        ],
        compiler_params=pltpu.CompilerParams(vmem_limit_bytes=62 * MIB),
        cost_estimate=pl.CostEstimate(flops=2 * rows * rows * cq, bytes_accessed=8 * rows * cq, transcendentals=rows * rows),
        name="prompt_attention",
    )(counts, q, kv)


def row_head(n, lq, h, hh):
    at = h * GQ + hh
    return at // lq, at % lq


def handed_part(n, lq, kv_ref, q_ref, msg_ref, _, o_ref):
    rows = lq * n * GROUP_ROWS
    shape = (rows, HD)
    at_row, lane = iota(shape, 0), iota(shape, 1)
    rs = at_row % GROUP_ROWS
    facts = msg_ref[:, :HD].astype(jnp.float32).reshape(n, GROUP_ROWS, HD)[:, 6:7, :]
    facts = jnp.broadcast_to(facts, (n, GROUP_ROWS, HD)).reshape(n * GROUP_ROWS, HD)
    facts = jnp.concatenate([facts] * lq, axis=0)

    def column(kind):
        return jnp.sum(jnp.where(lane == kind * GROUP_ROWS + rs, facts, 0.0), axis=1, keepdims=True)

    first_block, second_block, length = [column(kind) for kind in range(3)]
    scores = dot_t(q_ref[...], kv_ref[:, :HD]) * SCALE
    lane_f = lane.astype(jnp.float32)
    parts = []
    for b in range(NBLK):
        limit = jnp.where(
            first_block == b, length, jnp.where(second_block == b, length - BLOCK_TOKENS, 0.0)
        )
        part = scores[:, b * BLOCK_TOKENS : (b + 1) * BLOCK_TOKENS]
        parts.append(jnp.where(lane_f < limit, part, MASKED))
    scores = jnp.concatenate(parts, axis=1)
    top = jnp.max(scores, axis=1, keepdims=True)
    raised = jnp.exp(scores - top)
    total = jnp.sum(raised, axis=1, keepdims=True)
    near = raised.astype(jnp.bfloat16)
    rest = (raised - near.astype(jnp.float32)).astype(jnp.bfloat16)
    values = kv_ref[:, HD:]
    mixed = (dot(near, values) + dot(rest, values)).reshape(lq * n, GROUP_ROWS, HD)

    def line(col):
        spread = jnp.where(lane == rs, col, 0.0).reshape(lq * n, GROUP_ROWS, HD)
        return jnp.sum(spread, axis=1, keepdims=True)

    rs3 = rs.reshape(lq * n, GROUP_ROWS, HD)
    mixed = jnp.where(rs3 == 6, line(top), jnp.where(rs3 == 7, line(total), mixed))
    for h in range(lq):
        o_ref[:, h * GROUP_ROWS : (h + 1) * GROUP_ROWS, :] = mixed[h * n : (h + 1) * n]


def handed_attention(kv, q_own, msgs, after, n, lq):
    rows = lq * n * GROUP_ROWS
    vmem = pl.BlockSpec(memory_space=VMEM)
    return pl.pallas_call(
        functools.partial(handed_part, n, lq),
        in_specs=[vmem] * 3 + [pl.BlockSpec(memory_space=pl.ANY)],
        out_specs=vmem,
        out_shape=jax.ShapeDtypeStruct((n, lq * GROUP_ROWS, HD), jnp.float32),
        compiler_params=pltpu.CompilerParams(vmem_limit_bytes=24 * MIB),
        cost_estimate=pl.CostEstimate(flops=6 * rows * HD * PTOK, bytes_accessed=2 * MIB, transcendentals=rows * PTOK),
        name="handed_attention",
    )(kv, q_own, msgs, after)


def owner_scores(n, lq, counts, done, placed, table, lens, cache_hbm, msgs, _, s_ref, v_ref, new_ref, cache, sem, slot_row, slot_limit):
    load = pltpu.make_async_copy(cache_hbm, cache, sem)
    load.start()
    held = msgs[...].astype(jnp.float32)
    found = block_of_pages(counts, done, placed, table)
    for r in range(ROWS_DEV):
        for p in range(PAGES):
            slot_row[table[p, r]] = jnp.int32(r)
            slot_limit[table[p, r]] = jnp.where(found[r][p] < 0, lens[r] - p * BLOCK_TOKENS, 0)
    cq = lq * HD
    rows = QH * GROUP_ROWS
    span = GQ * GROUP_ROWS
    queries, keys = [], []
    for h in range(KVH):
        for hh in range(GQ):
            t, at = row_head(n, lq, h, hh)
            queries.append(held[t * GROUP_ROWS : (t + 1) * GROUP_ROWS, at * HD : (at + 1) * HD])
        t, _ = row_head(n, lq, h, 0)
        keys += [held[t * GROUP_ROWS : (t + 1) * GROUP_ROWS, cq : cq + HD]] * GQ
        new_ref[h * GROUP_ROWS : (h + 1) * GROUP_ROWS, :] = held[
            t * GROUP_ROWS : (t + 1) * GROUP_ROWS, cq + HD : cq + 2 * HD
        ]
    queries = jnp.concatenate(queries, axis=0)
    earlier = jnp.concatenate([pltpu.roll(key, ROWS_DEV, 0) for key in keys], axis=0)
    keys = jnp.concatenate(keys, axis=0)
    at_row, lane = iota((rows, HD), 0), iota((rows, HD), 1)
    rs = at_row % GROUP_ROWS
    r = row_of(rs)
    rounded = queries.astype(jnp.bfloat16)
    now = jnp.sum(queries * keys, axis=1, keepdims=True) * SCALE
    before = jnp.sum(queries * earlier, axis=1, keepdims=True) * SCALE
    second = (rs >= ROWS_DEV) & (rs < STEPS * ROWS_DEV)
    before = jnp.where(second, before, MASKED)
    load.wait()
    scores = jnp.concatenate(
        [dot_t(rounded[h * span : (h + 1) * span], cache[:, 2 * h * HD : (2 * h + 1) * HD]) for h in range(KVH)],
        axis=0,
    )
    for slot in range(DEVICE_SLOTS):
        part = slice(slot * BLOCK_TOKENS, (slot + 1) * BLOCK_TOKENS)
        usable = (r == slot_row[slot]) & (lane < slot_limit[slot])
        s_ref[:, part] = jnp.where(usable, scores[:, part] * SCALE, MASKED)
    last = jnp.where(lane == 0, now, jnp.where(lane == 1, before, MASKED))
    s_ref[:, DEVICE_SLOTS * BLOCK_TOKENS :] = last
    for h in range(KVH):
        v_ref[:, h * HD : (h + 1) * HD] = cache[:, (2 * h + 1) * HD : (2 * h + 2) * HD]


def decode_scores(ints, cache, msgs, after, n, lq):
    smem, vmem, hbm = [pl.BlockSpec(memory_space=space) for space in (SMEM, VMEM, pl.ANY)]
    rows = QH * GROUP_ROWS
    return pl.pallas_call(
        functools.partial(owner_scores, n, lq),
        in_specs=[smem] * 5 + [hbm, vmem, hbm],
        out_specs=[vmem] * 3,
        out_shape=[
            jax.ShapeDtypeStruct((rows, (DEVICE_SLOTS + 1) * BLOCK_TOKENS), jnp.float32),
            jax.ShapeDtypeStruct((cache.shape[0], KVH * HD), jnp.bfloat16),
            jax.ShapeDtypeStruct((KVH * GROUP_ROWS, HD), jnp.float32),
        ],
        scratch_shapes=[
            VMEM(cache.shape, jnp.bfloat16),
            pltpu.SemaphoreType.DMA,
            SMEM((DEVICE_SLOTS,), jnp.int32),
            SMEM((DEVICE_SLOTS,), jnp.int32),
        ],
        compiler_params=pltpu.CompilerParams(vmem_limit_bytes=24 * MIB),
        cost_estimate=pl.CostEstimate(flops=2 * rows * HD * 768, bytes_accessed=4 * MIB, transcendentals=0),
        name="decode_scores",
    )(*ints, cache, msgs, after)


def owner_mix(s_ref, v_ref, new_ref, handed, o_ref):
    groups = QH
    rows = groups * GROUP_ROWS
    span = GQ * GROUP_ROWS
    mixed = handed[...].reshape(groups, GROUP_ROWS, HD)
    shape = (groups, GROUP_ROWS, HD)
    mine = iota(shape, 1) == iota(shape, 2)

    def column(at):
        line = jnp.broadcast_to(mixed[:, at : at + 1, :], shape)
        return jnp.sum(jnp.where(mine, line, 0.0), axis=2, keepdims=True).reshape(rows, 1)

    other_peak, other_total = column(6), column(7)
    scores = s_ref[...]
    peak = jnp.maximum(jnp.max(scores, axis=1, keepdims=True), other_peak)
    raised = jnp.exp(scores - peak)
    other = jnp.exp(other_peak - peak)
    inverse = 1.0 / (jnp.sum(raised, axis=1, keepdims=True) + other * other_total)
    weights = (raised * inverse).astype(jnp.bfloat16)
    old = DEVICE_SLOTS * BLOCK_TOKENS
    fresh = weights[:, old:].astype(jnp.float32)
    now, before = fresh[:, 0:1], fresh[:, 1:2]
    mixed = mixed.reshape(rows, HD) * (other * inverse)
    out = []
    for h in range(KVH):
        part = slice(h * span, (h + 1) * span)
        own = mixed[part] + dot(weights[part, :old], v_ref[:, h * HD : (h + 1) * HD])
        value = new_ref[h * GROUP_ROWS : (h + 1) * GROUP_ROWS, :]
        last = pltpu.roll(value, ROWS_DEV, 0)
        for hh in range(GQ):
            some = slice(h * span + hh * GROUP_ROWS, h * span + (hh + 1) * GROUP_ROWS)
            line = own[hh * GROUP_ROWS : (hh + 1) * GROUP_ROWS]
            out.append(line + now[some] * value + before[some] * last)
    out = jnp.concatenate(out, axis=1)
    for k in range(ROWS_DEV):
        steps = [out[s * ROWS_DEV + k : s * ROWS_DEV + k + 1] for s in range(STEPS)]
        o_ref[k] = jnp.concatenate(steps, axis=0).astype(jnp.bfloat16)


def decode_mix(scores, values, new, parts):
    vmem = pl.BlockSpec(memory_space=VMEM)
    rows = QH * GROUP_ROWS
    return pl.pallas_call(
        owner_mix,
        in_specs=[vmem] * 4,
        out_specs=vmem,
        out_shape=jax.ShapeDtypeStruct((ROWS_DEV, STEPS, QH * HD), jnp.bfloat16),
        compiler_params=pltpu.CompilerParams(vmem_limit_bytes=24 * MIB),
        cost_estimate=pl.CostEstimate(flops=2 * rows * HD * 768, bytes_accessed=4 * MIB, transcendentals=rows * 768),
        name="decode_mix",
    )(scores, values, new, parts)


def local(
    prompt_x,
    q_weight,
    kv_weight,
    prompt_blocks,
    finished,
    placement,
    page_table,
    row_lens,
    kv_cache,
    decode_x,
):
    n = lax.axis_size("tp")
    lq = q_weight.shape[1] // HD
    share = GQ // lq
    if share > 1:
        sets = [[k * share + i for i in range(share)] for k in range(n // share)]
        kv_weight = lax.all_gather(kv_weight, "tp", axis=1, tiled=True, axis_index_groups=sets)
    cache = kv_cache.reshape(-1, kv_cache.shape[2])
    dx = decode_x.reshape(-1, decode_x.shape[2])
    placement = placement.transpose(0, 2, 1)
    page_table = page_table.transpose(1, 0)
    ints = (prompt_blocks, finished, placement, page_table, row_lens)
    first, size = 256, 896
    q, kv, q_own, msgs = project_all(ints, dx, prompt_x, q_weight, kv_weight, n, first, size)
    msgs = lax.all_to_all(msgs, "tp", split_axis=0, concat_axis=0, tiled=True)
    kv_other = lax.ppermute(kv, "pool", [(0, 1), (1, 0)])
    prompt_attn, made = prompt_attention(prompt_blocks, q, kv)
    handed = handed_attention(kv_other, q_own, msgs, made, n, lq)
    parts = lax.all_to_all(handed, "tp", split_axis=0, concat_axis=0, tiled=True)
    scores, values, new = decode_scores(ints, cache, msgs, handed, n, lq)
    decode_attn = decode_mix(scores, values, new, parts)
    return prompt_attn, decode_attn.transpose(1, 0, 2)


def solution(mesh):
    return jax.shard_map(
        local,
        mesh=mesh,
        in_specs=(
            P(("rep", "pool"), None),
            P(None, "tp"),
            P(None, "tp"),
            P("rep", None),
            P("rep", None),
            P("rep", None, None),
            P(("rep", "pool", "tp"), None),
            P(("rep", "pool", "tp")),
            P(("rep", "pool", "tp"), None, None),
            P(None, ("rep", "pool"), None),
        ),
        out_specs=(P(("rep", "pool"), "tp"), P(None, ("rep", "pool", "tp"), None)),
        check_vma=False,
    )
```

```python
import functools

import jax
import jax.numpy as jnp
from jax import lax
from jax.experimental import pallas as pl
from jax.experimental.pallas import tpu as pltpu
from jax.sharding import PartitionSpec as P

QH = 32
KVH = 8
GQ = QH // KVH
HD = 128
BLOCK_TOKENS = 128
PTOK = 2048
NPROMPT = 3
MOST_BLOCKS = 8
PAGES = 2
STEPS = 2
NBLK = 16
DEVICE_SLOTS = 6
ROWS_DEV = 3
GROUP_ROWS = 8
KEY_VALUE_COLUMNS = 2048
SCALE = HD ** (-0.5)
MASKED = -1e30
PIECES = 5
STRIPS = 4
AHEAD = 2
MIB = 1 << 20
VMEM = pltpu.VMEM
SMEM = pltpu.SMEM


def dot(a, b):
    return jnp.dot(a, b, preferred_element_type=jnp.float32)


def dot_t(a, b):
    return lax.dot_general(a, b, (((1,), (1,)), ((), ())), preferred_element_type=jnp.float32)


def iota(shape, axis):
    return lax.broadcasted_iota(jnp.int32, shape, axis)


def row_of(rs):
    return jnp.where(rs >= 2 * ROWS_DEV, ROWS_DEV, jnp.where(rs >= ROWS_DEV, rs - ROWS_DEV, rs))


def block_of_pages(counts, done, placed, table):
    me = lax.axis_index("tp")
    other = 1 - lax.axis_index("pool")
    first_end = counts[other, 0]
    second_end = first_end + counts[other, 1]
    found = [[jnp.int32(-1)] * PAGES for _ in range(ROWS_DEV)]
    for b in range(NBLK):
        live = jnp.where(
            b < first_end, done[other, 0], jnp.where(b < second_end, done[other, 1], done[other, 2])
        )
        slot = jnp.where((live > 0) & (placed[other, 0, b] == me), placed[other, 1, b], -1)
        for r in range(ROWS_DEV):
            for p in range(PAGES):
                found[r][p] = jnp.where(slot == table[p, r], b, found[r][p])
    return found


def by_row(r, values, rest):
    out = jnp.full(r.shape, rest, jnp.int32)
    for k in range(ROWS_DEV):
        out = jnp.where(r == k, values[k], out)
    return out


def project(n, lq, first, size, *refs):
    counts, done, placed, table, lens, dx_hbm, x_hbm, wq_hbm, wkv_hbm = refs[:9]
    q_hbm, kv_hbm, qh_ref, msg_ref = refs[9:13]
    x0, xs, w, q_out, kv_out, x_sems, w_sems, out_sems = refs[13:]
    depth = w.shape[0]
    count = xs.shape[0]
    cq = lq * HD
    piece = depth // PIECES
    own_rows = dx_hbm.shape[0]
    step = pl.program_id(0)

    def piece_copies(c):
        part = pl.ds(c * piece, piece)
        return [
            pltpu.make_async_copy(x_hbm.at[pl.ds(0, first), part], x0.at[pl.ds(0, first), part], w_sems.at[0, c]),
            pltpu.make_async_copy(dx_hbm.at[:, part], x0.at[pl.ds(first, own_rows), part], w_sems.at[1, c]),
            pltpu.make_async_copy(wq_hbm.at[part], w.at[part, pl.ds(0, cq)], w_sems.at[2, c]),
            pltpu.make_async_copy(wkv_hbm.at[part], w.at[part, pl.ds(cq, 2 * HD)], w_sems.at[3, c]),
        ]

    def x_copies(k):
        strip = size // STRIPS
        copies = []
        for i in range(STRIPS):
            rows = pl.ds(pl.multiple_of(first + k * size + i * strip, 16), strip)
            copies.append(
                pltpu.make_async_copy(x_hbm.at[rows], xs.at[k, pl.ds(i * strip, strip)], x_sems.at[k, i])
            )
        return copies

    def out_copies(k):
        if isinstance(k, int):
            rows = pl.ds(0, first)
        else:
            rows = pl.ds(pl.multiple_of(first + (k - 1) * size, BLOCK_TOKENS), size)
        return [
            pltpu.make_async_copy(q_out.at[rows], q_hbm.at[rows], out_sems.at[0, k]),
            pltpu.make_async_copy(kv_out.at[rows], kv_hbm.at[rows], out_sems.at[1, k]),
        ]

    def keep(total, rows):
        q_out[rows, :] = total[:, :cq].astype(jnp.bfloat16)
        kv_out[rows, :] = total[:, cq:].astype(jnp.bfloat16)

    @pl.when(step == 0)
    def _():
        for c in range(AHEAD):
            for copy in piece_copies(c):
                copy.start()
        total = 0.0
        for c in range(PIECES):
            for copy in piece_copies(c):
                copy.wait()
            if c + AHEAD < PIECES:
                for copy in piece_copies(c + AHEAD):
                    copy.start()
            if c + AHEAD == PIECES:
                for copy in x_copies(0):
                    copy.start()
            part = slice(c * piece, (c + 1) * piece)
            total += dot(x0[:, part], w[part, :])
        keep(total[:first], pl.ds(0, first))
        for copy in out_copies(0):
            copy.start()
        shape = (n * GROUP_ROWS, own_rows)
        to, fro = iota(shape, 0), iota(shape, 1)
        owner, rs = to // GROUP_ROWS, to % GROUP_ROWS
        wanted = owner * ROWS_DEV + row_of(rs) + jnp.where(rs >= ROWS_DEV, ROWS_DEV * n, 0)
        pick = ((fro == wanted) & (rs < STEPS * ROWS_DEV)).astype(jnp.float32).astype(jnp.bfloat16)
        own = dot(pick, total[first:].astype(jnp.bfloat16))
        for h in range(lq):
            part = slice(h * n * GROUP_ROWS, (h + 1) * n * GROUP_ROWS)
            qh_ref[part, :] = own[:, h * HD : (h + 1) * HD].astype(jnp.bfloat16)
        found = block_of_pages(counts, done, placed, table)
        lane = iota((n * GROUP_ROWS, HD), 1)
        r = row_of(lane % GROUP_ROWS)
        kind = lane // GROUP_ROWS
        facts = jnp.where(
            kind == 0,
            by_row(r, [found[i][0] for i in range(ROWS_DEV)], -1),
            jnp.where(
                kind == 1,
                by_row(r, [found[i][1] for i in range(ROWS_DEV)], -1),
                by_row(r, [lens[i] for i in range(ROWS_DEV)], 0),
            ),
        ).astype(jnp.float32)
        sixth = iota((n * GROUP_ROWS, HD), 0) % GROUP_ROWS == 6
        msg_ref[:, :HD] = jnp.where(sixth, facts, own[:, :HD]).astype(jnp.bfloat16)
        msg_ref[:, HD:] = own[:, HD:].astype(jnp.bfloat16)

    @pl.when((step > 0) & (step < count))
    def _():
        for copy in x_copies(step):
            copy.start()

    @pl.when(step > 0)
    def _():
        for copy in x_copies(step - 1):
            copy.wait()
        keep(dot(xs[step - 1], w[...]), pl.ds(pl.multiple_of(first + (step - 1) * size, BLOCK_TOKENS), size))
        for copy in out_copies(step):
            copy.start()

    @pl.when(step == count)
    def _():
        for copy in out_copies(0):
            copy.wait()
        for k in range(1, count + 1):
            for copy in out_copies(jnp.int32(k)):
                copy.wait()


def project_all(ints, dx, x, wq, wkv, n, first, size):
    rows, depth = x.shape
    cq, ckv = wq.shape[1], wkv.shape[1]
    lq = cq // HD
    count = (rows - first) // size
    smem, vmem = pl.BlockSpec(memory_space=SMEM), pl.BlockSpec(memory_space=VMEM)
    hbm = pl.BlockSpec(memory_space=pl.ANY)
    return pl.pallas_call(
        functools.partial(project, n, lq, first, size),
        grid=(1 + count,),
        in_specs=[smem] * 5 + [hbm] * 4,
        out_specs=[hbm, hbm, vmem, vmem],
        out_shape=[
            jax.ShapeDtypeStruct((rows, cq), jnp.bfloat16),
            jax.ShapeDtypeStruct((rows, ckv), jnp.bfloat16),
            jax.ShapeDtypeStruct((lq * n * GROUP_ROWS, HD), jnp.bfloat16),
            jax.ShapeDtypeStruct((n * GROUP_ROWS, cq + ckv), jnp.bfloat16),
        ],
        scratch_shapes=[
            VMEM((first + dx.shape[0], depth), jnp.bfloat16),
            VMEM((count, size, depth), jnp.bfloat16),
            VMEM((depth, cq + ckv), jnp.bfloat16),
            VMEM((rows, cq), jnp.bfloat16),
            VMEM((rows, ckv), jnp.bfloat16),
            pltpu.SemaphoreType.DMA((count, STRIPS)),
            pltpu.SemaphoreType.DMA((4, PIECES)),
            pltpu.SemaphoreType.DMA((2, count + 1)),
        ],
        compiler_params=pltpu.CompilerParams(vmem_limit_bytes=62 * MIB),
        cost_estimate=pl.CostEstimate(
            flops=2 * rows * depth * (cq + ckv),
            bytes_accessed=2 * (rows + cq + ckv) * depth + 2 * rows * (cq + ckv),
            transcendentals=0,
        ),
        name="project",
    )(*ints, dx, x, wq, wkv)


def attend_prompt(lq, counts, q_hbm, kv_hbm, o_hbm, made_ref, qs, kvs, outs, sems):
    made_ref[...] = jnp.zeros_like(made_ref)
    group = lax.axis_index("pool")
    c0, c1 = counts[group, 0], counts[group, 1]
    big = jnp.where(c0 == MOST_BLOCKS, 0, jnp.where(c1 == MOST_BLOCKS, c0, c0 + c1))
    cut = jnp.where(c0 == MOST_BLOCKS, c1, c0)
    loads, stores = [], []
    for half in range(2):
        for j in range(MOST_BLOCKS):
            block = big + j if half == 0 else j + jnp.where(j >= big, MOST_BLOCKS, 0)
            rows = pl.ds(pl.multiple_of(block * BLOCK_TOKENS, BLOCK_TOKENS), BLOCK_TOKENS)
            here = pl.ds(j * BLOCK_TOKENS, BLOCK_TOKENS)
            loads.append(pltpu.make_async_copy(kv_hbm.at[rows], kvs.at[half, here], sems.at[0, half, j]))
            loads.append(pltpu.make_async_copy(q_hbm.at[rows], qs.at[half, here], sems.at[1, half, j]))
            stores.append(pltpu.make_async_copy(outs.at[half, here], o_hbm.at[rows], sems.at[2, half, j]))
    for copy in loads:
        copy.start()
    for copy in loads:
        copy.wait()
    tokens = MOST_BLOCKS * BLOCK_TOKENS
    shape = (BLOCK_TOKENS, lq * BLOCK_TOKENS)
    causal = iota(shape, 0) <= iota(shape, 1) % BLOCK_TOKENS
    flipped = [kvs[half, :, HD:].T for half in range(2)]

    def scores_of(half, j):
        q = qs[half, j * BLOCK_TOKENS : (j + 1) * BLOCK_TOKENS, :]
        q = jnp.concatenate([q[:, h * HD : (h + 1) * HD] for h in range(lq)], axis=0)
        return dot_t(kvs[half, : (j + 1) * BLOCK_TOKENS, :HD], q)

    order = [(half, j) for half in range(2) for j in range(MOST_BLOCKS)]
    scores = scores_of(*order[0])
    for k, (half, j) in enumerate(order):
        later = scores_of(*order[k + 1]) if k + 1 < len(order) else None
        weights = []
        for h in range(lq):
            cols = slice(h * BLOCK_TOKENS, (h + 1) * BLOCK_TOKENS)
            tiles = []
            for i in range(j + 1):
                tile = scores[i * BLOCK_TOKENS : (i + 1) * BLOCK_TOKENS, cols]
                if i == j:
                    tile = jnp.where(causal[:, cols], tile, MASKED)
                elif half == 1:
                    tile = tile + jnp.where((i < cut) & (cut <= j), MASKED, 0.0)
                tiles.append(tile)
            peak = jnp.max(functools.reduce(jnp.maximum, tiles), axis=0, keepdims=True)
            raised = [jnp.exp((tile - peak) * SCALE) for tile in tiles]
            inverse = 1.0 / jnp.sum(functools.reduce(jnp.add, raised), axis=0, keepdims=True)
            weights.append(jnp.concatenate([(t * inverse).astype(jnp.bfloat16) for t in raised], axis=0))
        mixed = dot(flipped[half][:, : (j + 1) * BLOCK_TOKENS], jnp.concatenate(weights, axis=1))
        mixed = mixed.astype(jnp.bfloat16)
        for h in range(lq):
            part = mixed[:, h * BLOCK_TOKENS : (h + 1) * BLOCK_TOKENS].T
            outs[half, j * BLOCK_TOKENS : (j + 1) * BLOCK_TOKENS, h * HD : (h + 1) * HD] = part
        scores = later
    for copy in stores:
        copy.start()
    for copy in stores:
        copy.wait()


def prompt_attention(counts, q, kv):
    rows, cq = q.shape
    hbm = pl.BlockSpec(memory_space=pl.ANY)
    tokens = MOST_BLOCKS * BLOCK_TOKENS
    return pl.pallas_call(
        functools.partial(attend_prompt, cq // HD),
        in_specs=[pl.BlockSpec(memory_space=SMEM), hbm, hbm],
        out_specs=[hbm, pl.BlockSpec(memory_space=VMEM)],
        out_shape=[
            jax.ShapeDtypeStruct((rows, cq), jnp.bfloat16),
            jax.ShapeDtypeStruct((8, HD), jnp.float32),
        ],
        scratch_shapes=[
            VMEM((2, tokens, cq), jnp.bfloat16),
            VMEM((2, tokens, 2 * HD), jnp.bfloat16),
            VMEM((2, tokens, cq), jnp.bfloat16),
            pltpu.SemaphoreType.DMA((3, 2, MOST_BLOCKS)),
        ],
        compiler_params=pltpu.CompilerParams(vmem_limit_bytes=62 * MIB),
        cost_estimate=pl.CostEstimate(flops=2 * rows * rows * cq, bytes_accessed=8 * rows * cq, transcendentals=rows * rows),
        name="prompt_attention",
    )(counts, q, kv)


def row_head(n, lq, h, hh):
    at = h * GQ + hh
    return at // lq, at % lq


def handed_part(n, lq, kv_ref, q_ref, msg_ref, _, o_ref):
    rows = lq * n * GROUP_ROWS
    shape = (rows, HD)
    at_row, lane = iota(shape, 0), iota(shape, 1)
    rs = at_row % GROUP_ROWS
    facts = msg_ref[:, :HD].astype(jnp.float32).reshape(n, GROUP_ROWS, HD)[:, 6:7, :]
    facts = jnp.broadcast_to(facts, (n, GROUP_ROWS, HD)).reshape(n * GROUP_ROWS, HD)
    facts = jnp.concatenate([facts] * lq, axis=0)

    def column(kind):
        return jnp.sum(jnp.where(lane == kind * GROUP_ROWS + rs, facts, 0.0), axis=1, keepdims=True)

    first_block, second_block, length = [column(kind) for kind in range(3)]
    scores = dot_t(q_ref[...], kv_ref[:, :HD]) * SCALE
    lane_f = lane.astype(jnp.float32)
    parts = []
    for b in range(NBLK):
        limit = jnp.where(
            first_block == b, length, jnp.where(second_block == b, length - BLOCK_TOKENS, 0.0)
        )
        part = scores[:, b * BLOCK_TOKENS : (b + 1) * BLOCK_TOKENS]
        parts.append(jnp.where(lane_f < limit, part, MASKED))
    scores = jnp.concatenate(parts, axis=1)
    top = jnp.max(scores, axis=1, keepdims=True)
    raised = jnp.exp(scores - top)
    total = jnp.sum(raised, axis=1, keepdims=True)
    near = raised.astype(jnp.bfloat16)
    rest = (raised - near.astype(jnp.float32)).astype(jnp.bfloat16)
    values = kv_ref[:, HD:]
    mixed = (dot(near, values) + dot(rest, values)).reshape(lq * n, GROUP_ROWS, HD)

    def line(col):
        spread = jnp.where(lane == rs, col, 0.0).reshape(lq * n, GROUP_ROWS, HD)
        return jnp.sum(spread, axis=1, keepdims=True)

    rs3 = rs.reshape(lq * n, GROUP_ROWS, HD)
    mixed = jnp.where(rs3 == 6, line(top), jnp.where(rs3 == 7, line(total), mixed))
    for h in range(lq):
        o_ref[:, h * GROUP_ROWS : (h + 1) * GROUP_ROWS, :] = mixed[h * n : (h + 1) * n]


def handed_attention(kv, q_own, msgs, after, n, lq):
    rows = lq * n * GROUP_ROWS
    vmem = pl.BlockSpec(memory_space=VMEM)
    return pl.pallas_call(
        functools.partial(handed_part, n, lq),
        in_specs=[vmem] * 3 + [pl.BlockSpec(memory_space=pl.ANY)],
        out_specs=vmem,
        out_shape=jax.ShapeDtypeStruct((n, lq * GROUP_ROWS, HD), jnp.float32),
        compiler_params=pltpu.CompilerParams(vmem_limit_bytes=24 * MIB),
        cost_estimate=pl.CostEstimate(flops=6 * rows * HD * PTOK, bytes_accessed=2 * MIB, transcendentals=rows * PTOK),
        name="handed_attention",
    )(kv, q_own, msgs, after)


def owner_scores(n, lq, counts, done, placed, table, lens, cache_hbm, msgs, _, s_ref, v_ref, new_ref, cache, sem, slot_row, slot_limit):
    load = pltpu.make_async_copy(cache_hbm, cache, sem)
    load.start()
    held = msgs[...].astype(jnp.float32)
    found = block_of_pages(counts, done, placed, table)
    for r in range(ROWS_DEV):
        for p in range(PAGES):
            slot_row[table[p, r]] = jnp.int32(r)
            slot_limit[table[p, r]] = jnp.where(found[r][p] < 0, lens[r] - p * BLOCK_TOKENS, 0)
    cq = lq * HD
    rows = QH * GROUP_ROWS
    span = GQ * GROUP_ROWS
    queries, keys = [], []
    for h in range(KVH):
        for hh in range(GQ):
            t, at = row_head(n, lq, h, hh)
            queries.append(held[t * GROUP_ROWS : (t + 1) * GROUP_ROWS, at * HD : (at + 1) * HD])
        t, _ = row_head(n, lq, h, 0)
        keys += [held[t * GROUP_ROWS : (t + 1) * GROUP_ROWS, cq : cq + HD]] * GQ
        new_ref[h * GROUP_ROWS : (h + 1) * GROUP_ROWS, :] = held[
            t * GROUP_ROWS : (t + 1) * GROUP_ROWS, cq + HD : cq + 2 * HD
        ]
    queries = jnp.concatenate(queries, axis=0)
    earlier = jnp.concatenate([pltpu.roll(key, ROWS_DEV, 0) for key in keys], axis=0)
    keys = jnp.concatenate(keys, axis=0)
    at_row, lane = iota((rows, HD), 0), iota((rows, HD), 1)
    rs = at_row % GROUP_ROWS
    r = row_of(rs)
    rounded = queries.astype(jnp.bfloat16)
    now = jnp.sum(queries * keys, axis=1, keepdims=True) * SCALE
    before = jnp.sum(queries * earlier, axis=1, keepdims=True) * SCALE
    second = (rs >= ROWS_DEV) & (rs < STEPS * ROWS_DEV)
    before = jnp.where(second, before, MASKED)
    load.wait()
    scores = jnp.concatenate(
        [dot_t(rounded[h * span : (h + 1) * span], cache[:, 2 * h * HD : (2 * h + 1) * HD]) for h in range(KVH)],
        axis=0,
    )
    for slot in range(DEVICE_SLOTS):
        part = slice(slot * BLOCK_TOKENS, (slot + 1) * BLOCK_TOKENS)
        usable = (r == slot_row[slot]) & (lane < slot_limit[slot])
        s_ref[:, part] = jnp.where(usable, scores[:, part] * SCALE, MASKED)
    last = jnp.where(lane == 0, now, jnp.where(lane == 1, before, MASKED))
    s_ref[:, DEVICE_SLOTS * BLOCK_TOKENS :] = last
    for h in range(KVH):
        v_ref[:, h * HD : (h + 1) * HD] = cache[:, (2 * h + 1) * HD : (2 * h + 2) * HD]


def decode_scores(ints, cache, msgs, after, n, lq):
    smem, vmem, hbm = [pl.BlockSpec(memory_space=space) for space in (SMEM, VMEM, pl.ANY)]
    rows = QH * GROUP_ROWS
    return pl.pallas_call(
        functools.partial(owner_scores, n, lq),
        in_specs=[smem] * 5 + [hbm, vmem, hbm],
        out_specs=[vmem] * 3,
        out_shape=[
            jax.ShapeDtypeStruct((rows, (DEVICE_SLOTS + 1) * BLOCK_TOKENS), jnp.float32),
            jax.ShapeDtypeStruct((cache.shape[0], KVH * HD), jnp.bfloat16),
            jax.ShapeDtypeStruct((KVH * GROUP_ROWS, HD), jnp.float32),
        ],
        scratch_shapes=[
            VMEM(cache.shape, jnp.bfloat16),
            pltpu.SemaphoreType.DMA,
            SMEM((DEVICE_SLOTS,), jnp.int32),
            SMEM((DEVICE_SLOTS,), jnp.int32),
        ],
        compiler_params=pltpu.CompilerParams(vmem_limit_bytes=24 * MIB),
        cost_estimate=pl.CostEstimate(flops=2 * rows * HD * 768, bytes_accessed=4 * MIB, transcendentals=0),
        name="decode_scores",
    )(*ints, cache, msgs, after)


def owner_mix(s_ref, v_ref, new_ref, handed, o_ref):
    groups = QH
    rows = groups * GROUP_ROWS
    span = GQ * GROUP_ROWS
    mixed = handed[...].reshape(groups, GROUP_ROWS, HD)
    shape = (groups, GROUP_ROWS, HD)
    mine = iota(shape, 1) == iota(shape, 2)

    def column(at):
        line = jnp.broadcast_to(mixed[:, at : at + 1, :], shape)
        return jnp.sum(jnp.where(mine, line, 0.0), axis=2, keepdims=True).reshape(rows, 1)

    other_peak, other_total = column(6), column(7)
    scores = s_ref[...]
    peak = jnp.maximum(jnp.max(scores, axis=1, keepdims=True), other_peak)
    raised = jnp.exp(scores - peak)
    other = jnp.exp(other_peak - peak)
    inverse = 1.0 / (jnp.sum(raised, axis=1, keepdims=True) + other * other_total)
    weights = (raised * inverse).astype(jnp.bfloat16)
    old = DEVICE_SLOTS * BLOCK_TOKENS
    fresh = weights[:, old:].astype(jnp.float32)
    now, before = fresh[:, 0:1], fresh[:, 1:2]
    mixed = mixed.reshape(rows, HD) * (other * inverse)
    out = []
    for h in range(KVH):
        part = slice(h * span, (h + 1) * span)
        own = mixed[part] + dot(weights[part, :old], v_ref[:, h * HD : (h + 1) * HD])
        value = new_ref[h * GROUP_ROWS : (h + 1) * GROUP_ROWS, :]
        last = pltpu.roll(value, ROWS_DEV, 0)
        for hh in range(GQ):
            some = slice(h * span + hh * GROUP_ROWS, h * span + (hh + 1) * GROUP_ROWS)
            line = own[hh * GROUP_ROWS : (hh + 1) * GROUP_ROWS]
            out.append(line + now[some] * value + before[some] * last)
    out = jnp.concatenate(out, axis=1)
    for k in range(ROWS_DEV):
        steps = [out[s * ROWS_DEV + k : s * ROWS_DEV + k + 1] for s in range(STEPS)]
        o_ref[k] = jnp.concatenate(steps, axis=0).astype(jnp.bfloat16)


def decode_mix(scores, values, new, parts):
    vmem = pl.BlockSpec(memory_space=VMEM)
    rows = QH * GROUP_ROWS
    return pl.pallas_call(
        owner_mix,
        in_specs=[vmem] * 4,
        out_specs=vmem,
        out_shape=jax.ShapeDtypeStruct((ROWS_DEV, STEPS, QH * HD), jnp.bfloat16),
        compiler_params=pltpu.CompilerParams(vmem_limit_bytes=24 * MIB),
        cost_estimate=pl.CostEstimate(flops=2 * rows * HD * 768, bytes_accessed=4 * MIB, transcendentals=rows * 768),
        name="decode_mix",
    )(scores, values, new, parts)


def local(
    prompt_x,
    q_weight,
    kv_weight,
    prompt_blocks,
    finished,
    placement,
    page_table,
    row_lens,
    kv_cache,
    decode_x,
):
    n = lax.axis_size("tp")
    lq = q_weight.shape[1] // HD
    share = GQ // lq
    if share > 1:
        sets = [[k * share + i for i in range(share)] for k in range(n // share)]
        kv_weight = lax.all_gather(kv_weight, "tp", axis=1, tiled=True, axis_index_groups=sets)
    cache = kv_cache.reshape(-1, kv_cache.shape[2])
    dx = decode_x.reshape(-1, decode_x.shape[2])
    placement = placement.transpose(0, 2, 1)
    page_table = page_table.transpose(1, 0)
    ints = (prompt_blocks, finished, placement, page_table, row_lens)
    first, size = 256, 896
    q, kv, q_own, msgs = project_all(ints, dx, prompt_x, q_weight, kv_weight, n, first, size)
    msgs = lax.all_to_all(msgs, "tp", split_axis=0, concat_axis=0, tiled=True)
    kv_other = lax.ppermute(kv, "pool", [(0, 1), (1, 0)])
    prompt_attn, made = prompt_attention(prompt_blocks, q, kv)
    handed = handed_attention(kv_other, q_own, msgs, made, n, lq)
    parts = lax.all_to_all(handed, "tp", split_axis=0, concat_axis=0, tiled=True)
    scores, values, new = decode_scores(ints, cache, msgs, handed, n, lq)
    decode_attn = decode_mix(scores, values, new, parts)
    return prompt_attn, decode_attn.transpose(1, 0, 2)


def solution(mesh):
    return jax.shard_map(
        local,
        mesh=mesh,
        in_specs=(
            P(("rep", "pool"), None),
            P(None, "tp"),
            P(None, "tp"),
            P("rep", None),
            P("rep", None),
            P("rep", None, None),
            P(("rep", "pool", "tp"), None),
            P(("rep", "pool", "tp")),
            P(("rep", "pool", "tp"), None, None),
            P(None, ("rep", "pool"), None),
        ),
        out_specs=(P(("rep", "pool"), "tp"), P(None, ("rep", "pool", "tp"), None)),
        check_vma=False,
    )
```

```python
import functools

import jax
import jax.numpy as jnp
from jax import lax
from jax.experimental import pallas as pl
from jax.experimental.pallas import tpu as pltpu
from jax.sharding import PartitionSpec as P

QH = 32
KVH = 8
GQ = QH // KVH
HD = 128
BLOCK_TOKENS = 128
PTOK = 2048
NPROMPT = 3
MOST_BLOCKS = 8
PAGES = 2
STEPS = 2
NBLK = 16
DEVICE_SLOTS = 6
ROWS_DEV = 3
GROUP_ROWS = 8
KEY_VALUE_COLUMNS = 2048
SCALE = HD ** (-0.5)
MASKED = -1e30
PIECES = 5
STRIPS = 2
LOG2E = 1.4426950408889634
AHEAD = 2
MIB = 1 << 20
VMEM = pltpu.VMEM
SMEM = pltpu.SMEM


def dot(a, b):
    return jnp.dot(a, b, preferred_element_type=jnp.float32)


def dot_t(a, b):
    return lax.dot_general(a, b, (((1,), (1,)), ((), ())), preferred_element_type=jnp.float32)


def iota(shape, axis):
    return lax.broadcasted_iota(jnp.int32, shape, axis)


def row_of(rs):
    return jnp.where(rs >= 2 * ROWS_DEV, ROWS_DEV, jnp.where(rs >= ROWS_DEV, rs - ROWS_DEV, rs))


def block_of_pages(counts, done, placed, table):
    me = lax.axis_index("tp")
    other = 1 - lax.axis_index("pool")
    first_end = counts[other, 0]
    second_end = first_end + counts[other, 1]
    found = [[jnp.int32(-1)] * PAGES for _ in range(ROWS_DEV)]
    for b in range(NBLK):
        live = jnp.where(
            b < first_end, done[other, 0], jnp.where(b < second_end, done[other, 1], done[other, 2])
        )
        slot = jnp.where((live > 0) & (placed[other, 0, b] == me), placed[other, 1, b], -1)
        for r in range(ROWS_DEV):
            for p in range(PAGES):
                found[r][p] = jnp.where(slot == table[p, r], b, found[r][p])
    return found


def by_row(r, values, rest):
    out = jnp.full(r.shape, rest, jnp.int32)
    for k in range(ROWS_DEV):
        out = jnp.where(r == k, values[k], out)
    return out


def project(n, lq, first, size, *refs):
    counts, done, placed, table, lens, dx_hbm, x_hbm, wq_hbm, wkv_hbm = refs[:9]
    q_hbm, kv_hbm, qh_ref, msg_ref = refs[9:13]
    x0, xs, w, q_out, kv_out, x_sems, w_sems, out_sems = refs[13:]
    depth = w.shape[0]
    count = xs.shape[0]
    cq = lq * HD
    piece = depth // PIECES
    own_rows = dx_hbm.shape[0]
    step = pl.program_id(0)

    def piece_copies(c):
        part = pl.ds(c * piece, piece)
        return [
            pltpu.make_async_copy(x_hbm.at[pl.ds(0, first), part], x0.at[pl.ds(0, first), part], w_sems.at[0, c]),
            pltpu.make_async_copy(dx_hbm.at[:, part], x0.at[pl.ds(first, own_rows), part], w_sems.at[1, c]),
            pltpu.make_async_copy(wq_hbm.at[part], w.at[part, pl.ds(0, cq)], w_sems.at[2, c]),
            pltpu.make_async_copy(wkv_hbm.at[part], w.at[part, pl.ds(cq, 2 * HD)], w_sems.at[3, c]),
        ]

    def x_copies(k):
        strip = size // STRIPS
        copies = []
        for i in range(STRIPS):
            rows = pl.ds(pl.multiple_of(first + k * size + i * strip, 16), strip)
            copies.append(
                pltpu.make_async_copy(x_hbm.at[rows], xs.at[k, pl.ds(i * strip, strip)], x_sems.at[k, i])
            )
        return copies

    def out_copies(k):
        if isinstance(k, int):
            rows = pl.ds(0, first)
        else:
            rows = pl.ds(pl.multiple_of(first + (k - 1) * size, BLOCK_TOKENS), size)
        return [
            pltpu.make_async_copy(q_out.at[rows], q_hbm.at[rows], out_sems.at[0, k]),
            pltpu.make_async_copy(kv_out.at[rows], kv_hbm.at[rows], out_sems.at[1, k]),
        ]

    def keep(total, rows):
        q_out[rows, :] = total[:, :cq].astype(jnp.bfloat16)
        kv_out[rows, :] = total[:, cq:].astype(jnp.bfloat16)

    @pl.when(step == 0)
    def _():
        for c in range(AHEAD):
            for copy in piece_copies(c):
                copy.start()
        total = 0.0
        for c in range(PIECES):
            for copy in piece_copies(c):
                copy.wait()
            if c + AHEAD < PIECES:
                for copy in piece_copies(c + AHEAD):
                    copy.start()
            if c + AHEAD >= PIECES:
                for copy in x_copies(c + AHEAD - PIECES):
                    copy.start()
            part = slice(c * piece, (c + 1) * piece)
            total += dot(x0[:, part], w[part, :])
        keep(total[:first], pl.ds(0, first))
        for copy in out_copies(0):
            copy.start()
        shape = (n * GROUP_ROWS, own_rows)
        to, fro = iota(shape, 0), iota(shape, 1)
        owner, rs = to // GROUP_ROWS, to % GROUP_ROWS
        wanted = owner * ROWS_DEV + row_of(rs) + jnp.where(rs >= ROWS_DEV, ROWS_DEV * n, 0)
        pick = ((fro == wanted) & (rs < STEPS * ROWS_DEV)).astype(jnp.float32).astype(jnp.bfloat16)
        own = dot(pick, total[first:].astype(jnp.bfloat16))
        for h in range(lq):
            part = slice(h * n * GROUP_ROWS, (h + 1) * n * GROUP_ROWS)
            qh_ref[part, :] = own[:, h * HD : (h + 1) * HD].astype(jnp.bfloat16)
        found = block_of_pages(counts, done, placed, table)
        lane = iota((n * GROUP_ROWS, HD), 1)
        r = row_of(lane % GROUP_ROWS)
        kind = lane // GROUP_ROWS
        facts = jnp.where(
            kind == 0,
            by_row(r, [found[i][0] for i in range(ROWS_DEV)], -1),
            jnp.where(
                kind == 1,
                by_row(r, [found[i][1] for i in range(ROWS_DEV)], -1),
                by_row(r, [lens[i] for i in range(ROWS_DEV)], 0),
            ),
        ).astype(jnp.float32)
        sixth = iota((n * GROUP_ROWS, HD), 0) % GROUP_ROWS == 6
        msg_ref[:, :HD] = jnp.where(sixth, facts, own[:, :HD]).astype(jnp.bfloat16)
        msg_ref[:, HD:] = own[:, HD:].astype(jnp.bfloat16)

    @pl.when((step > 0) & (step + AHEAD <= count))
    def _():
        for copy in x_copies(step + AHEAD - 1):
            copy.start()

    @pl.when(step > 0)
    def _():
        for copy in x_copies(step - 1):
            copy.wait()
        keep(dot(xs[step - 1], w[...]), pl.ds(pl.multiple_of(first + (step - 1) * size, BLOCK_TOKENS), size))
        for copy in out_copies(step):
            copy.start()

    @pl.when(step == count)
    def _():
        for copy in out_copies(0):
            copy.wait()
        for k in range(1, count + 1):
            for copy in out_copies(jnp.int32(k)):
                copy.wait()


def project_all(ints, dx, x, wq, wkv, n, first, size):
    rows, depth = x.shape
    cq, ckv = wq.shape[1], wkv.shape[1]
    lq = cq // HD
    count = (rows - first) // size
    smem, vmem = pl.BlockSpec(memory_space=SMEM), pl.BlockSpec(memory_space=VMEM)
    hbm = pl.BlockSpec(memory_space=pl.ANY)
    return pl.pallas_call(
        functools.partial(project, n, lq, first, size),
        grid=(1 + count,),
        in_specs=[smem] * 5 + [hbm] * 4,
        out_specs=[hbm, hbm, vmem, vmem],
        out_shape=[
            jax.ShapeDtypeStruct((rows, cq), jnp.bfloat16),
            jax.ShapeDtypeStruct((rows, ckv), jnp.bfloat16),
            jax.ShapeDtypeStruct((lq * n * GROUP_ROWS, HD), jnp.bfloat16),
            jax.ShapeDtypeStruct((n * GROUP_ROWS, cq + ckv), jnp.bfloat16),
        ],
        scratch_shapes=[
            VMEM((first + dx.shape[0], depth), jnp.bfloat16),
            VMEM((count, size, depth), jnp.bfloat16),
            VMEM((depth, cq + ckv), jnp.bfloat16),
            VMEM((rows, cq), jnp.bfloat16),
            VMEM((rows, ckv), jnp.bfloat16),
            pltpu.SemaphoreType.DMA((count, STRIPS)),
            pltpu.SemaphoreType.DMA((4, PIECES)),
            pltpu.SemaphoreType.DMA((2, count + 1)),
        ],
        compiler_params=pltpu.CompilerParams(vmem_limit_bytes=62 * MIB),
        cost_estimate=pl.CostEstimate(
            flops=2 * rows * depth * (cq + ckv),
            bytes_accessed=2 * (rows + cq + ckv) * depth + 2 * rows * (cq + ckv),
            transcendentals=0,
        ),
        name="project",
    )(*ints, dx, x, wq, wkv)


def attend_prompt(lq, half, counts, q_hbm, kv_hbm, *refs):
    o_hbm, made_ref, qs, kvs, outs, sems = refs[-6:]
    made_ref[...] = jnp.zeros_like(made_ref)
    group = lax.axis_index("pool")
    c0, c1 = counts[group, 0], counts[group, 1]
    big = jnp.where(c0 == MOST_BLOCKS, 0, jnp.where(c1 == MOST_BLOCKS, c0, c0 + c1))
    cut = jnp.where(c0 == MOST_BLOCKS, c1, c0)
    loads, stores = [], []
    for j in range(MOST_BLOCKS):
        block = big + j if half == 0 else j + jnp.where(j >= big, MOST_BLOCKS, 0)
        rows = pl.ds(pl.multiple_of(block * BLOCK_TOKENS, BLOCK_TOKENS), BLOCK_TOKENS)
        here = pl.ds(j * BLOCK_TOKENS, BLOCK_TOKENS)
        loads.append(pltpu.make_async_copy(kv_hbm.at[rows], kvs.at[here], sems.at[0, j]))
        loads.append(pltpu.make_async_copy(q_hbm.at[rows], qs.at[here], sems.at[1, j]))
        stores.append(pltpu.make_async_copy(outs.at[here], o_hbm.at[rows], sems.at[2, j]))
    for copy in loads:
        copy.start()
    for copy in loads:
        copy.wait()
    shape = (BLOCK_TOKENS, lq * BLOCK_TOKENS)
    causal = iota(shape, 0) <= iota(shape, 1) % BLOCK_TOKENS
    flipped = kvs[:, HD:].T

    def scores_of(j):
        q = qs[j * BLOCK_TOKENS : (j + 1) * BLOCK_TOKENS, :]
        q = jnp.concatenate([q[:, h * HD : (h + 1) * HD] for h in range(lq)], axis=0)
        return dot_t(kvs[: (j + 1) * BLOCK_TOKENS, :HD], q)

    scores = scores_of(0)
    for j in range(MOST_BLOCKS):
        later = scores_of(j + 1) if j + 1 < MOST_BLOCKS else None
        weights = []
        for h in range(lq):
            cols = slice(h * BLOCK_TOKENS, (h + 1) * BLOCK_TOKENS)
            tiles = []
            for i in range(j + 1):
                tile = scores[i * BLOCK_TOKENS : (i + 1) * BLOCK_TOKENS, cols]
                if i == j:
                    tile = jnp.where(causal[:, cols], tile, MASKED)
                elif half == 1:
                    tile = tile + jnp.where((i < cut) & (cut <= j), MASKED, 0.0)
                tiles.append(tile)
            peak = jnp.max(functools.reduce(jnp.maximum, tiles), axis=0, keepdims=True)
            raised = [jnp.exp2((tile - peak) * (SCALE * LOG2E)) for tile in tiles]
            inverse = 1.0 / jnp.sum(functools.reduce(jnp.add, raised), axis=0, keepdims=True)
            weights.append(jnp.concatenate([(t * inverse).astype(jnp.bfloat16) for t in raised], axis=0))
        mixed = dot(flipped[:, : (j + 1) * BLOCK_TOKENS], jnp.concatenate(weights, axis=1))
        mixed = mixed.astype(jnp.bfloat16)
        for h in range(lq):
            part = mixed[:, h * BLOCK_TOKENS : (h + 1) * BLOCK_TOKENS].T
            outs[j * BLOCK_TOKENS : (j + 1) * BLOCK_TOKENS, h * HD : (h + 1) * HD] = part
        scores = later
        if j == MOST_BLOCKS - 3:
            for copy in stores[: j + 1]:
                copy.start()
    for copy in stores[MOST_BLOCKS - 2 :]:
        copy.start()
    for copy in stores:
        copy.wait()


def prompt_attention(counts, q, kv, half, so_far=None, after=None):
    rows, cq = q.shape
    hbm = pl.BlockSpec(memory_space=pl.ANY)
    more = () if so_far is None else (so_far, after)
    tokens = MOST_BLOCKS * BLOCK_TOKENS
    return pl.pallas_call(
        functools.partial(attend_prompt, cq // HD, half),
        in_specs=[pl.BlockSpec(memory_space=SMEM), hbm, hbm] + [hbm] * len(more),
        out_specs=[hbm, pl.BlockSpec(memory_space=VMEM)],
        out_shape=[
            jax.ShapeDtypeStruct((rows, cq), jnp.bfloat16),
            jax.ShapeDtypeStruct((8, HD), jnp.float32),
        ],
        scratch_shapes=[
            VMEM((tokens, cq), jnp.bfloat16),
            VMEM((tokens, 2 * HD), jnp.bfloat16),
            VMEM((tokens, cq), jnp.bfloat16),
            pltpu.SemaphoreType.DMA((3, MOST_BLOCKS)),
        ],
        input_output_aliases={3: 0} if more else {},
        compiler_params=pltpu.CompilerParams(vmem_limit_bytes=62 * MIB),
        cost_estimate=pl.CostEstimate(flops=2 * rows * rows * cq, bytes_accessed=4 * rows * cq, transcendentals=rows * rows // 2),
        name="long_prompt" if half == 0 else "short_prompts",
    )(counts, q, kv, *more)


def row_head(n, lq, h, hh):
    at = h * GQ + hh
    return at // lq, at % lq


def handed_part(n, lq, kv_ref, q_ref, msg_ref, o_ref):
    rows = lq * n * GROUP_ROWS
    shape = (rows, HD)
    at_row, lane = iota(shape, 0), iota(shape, 1)
    rs = at_row % GROUP_ROWS
    facts = msg_ref[:, :HD].astype(jnp.float32).reshape(n, GROUP_ROWS, HD)[:, 6:7, :]
    facts = jnp.broadcast_to(facts, (n, GROUP_ROWS, HD)).reshape(n * GROUP_ROWS, HD)
    facts = jnp.concatenate([facts] * lq, axis=0)

    def column(kind):
        return jnp.sum(jnp.where(lane == kind * GROUP_ROWS + rs, facts, 0.0), axis=1, keepdims=True)

    first_block, second_block, length = [column(kind) for kind in range(3)]
    scores = dot_t(q_ref[...], kv_ref[:, :HD]) * SCALE
    lane_f = lane.astype(jnp.float32)
    parts = []
    for b in range(NBLK):
        limit = jnp.where(
            first_block == b, length, jnp.where(second_block == b, length - BLOCK_TOKENS, 0.0)
        )
        part = scores[:, b * BLOCK_TOKENS : (b + 1) * BLOCK_TOKENS]
        parts.append(jnp.where(lane_f < limit, part, MASKED))
    scores = jnp.concatenate(parts, axis=1)
    top = jnp.max(scores, axis=1, keepdims=True)
    raised = jnp.exp(scores - top)
    total = jnp.sum(raised, axis=1, keepdims=True)
    near = raised.astype(jnp.bfloat16)
    rest = (raised - near.astype(jnp.float32)).astype(jnp.bfloat16)
    values = kv_ref[:, HD:]
    mixed = (dot(near, values) + dot(rest, values)).reshape(lq * n, GROUP_ROWS, HD)

    def line(col):
        spread = jnp.where(lane == rs, col, 0.0).reshape(lq * n, GROUP_ROWS, HD)
        return jnp.sum(spread, axis=1, keepdims=True)

    rs3 = rs.reshape(lq * n, GROUP_ROWS, HD)
    mixed = jnp.where(rs3 == 6, line(top), jnp.where(rs3 == 7, line(total), mixed))
    for h in range(lq):
        o_ref[:, h * GROUP_ROWS : (h + 1) * GROUP_ROWS, :] = mixed[h * n : (h + 1) * n]


def exchange_part(n, lq, *refs):
    counts, done, placed, table, lens, cache_hbm, msgs, kv_ref, q_ref, _ = refs[:10]
    handed_ref, s_ref, v_ref, new_ref, cache, sem, slot_row, slot_limit = refs[10:]
    load = pltpu.make_async_copy(cache_hbm, cache, sem)
    load.start()
    handed_part(n, lq, kv_ref, q_ref, msgs, handed_ref)
    held = msgs[...].astype(jnp.float32)
    found = block_of_pages(counts, done, placed, table)
    for r in range(ROWS_DEV):
        for p in range(PAGES):
            slot_row[table[p, r]] = jnp.int32(r)
            slot_limit[table[p, r]] = jnp.where(found[r][p] < 0, lens[r] - p * BLOCK_TOKENS, 0)
    cq = lq * HD
    rows = QH * GROUP_ROWS
    span = GQ * GROUP_ROWS
    queries, keys = [], []
    for h in range(KVH):
        for hh in range(GQ):
            t, at = row_head(n, lq, h, hh)
            queries.append(held[t * GROUP_ROWS : (t + 1) * GROUP_ROWS, at * HD : (at + 1) * HD])
        t, _ = row_head(n, lq, h, 0)
        keys += [held[t * GROUP_ROWS : (t + 1) * GROUP_ROWS, cq : cq + HD]] * GQ
        new_ref[h * GROUP_ROWS : (h + 1) * GROUP_ROWS, :] = held[
            t * GROUP_ROWS : (t + 1) * GROUP_ROWS, cq + HD : cq + 2 * HD
        ]
    queries = jnp.concatenate(queries, axis=0)
    earlier = jnp.concatenate([pltpu.roll(key, ROWS_DEV, 0) for key in keys], axis=0)
    keys = jnp.concatenate(keys, axis=0)
    at_row, lane = iota((rows, HD), 0), iota((rows, HD), 1)
    rs = at_row % GROUP_ROWS
    r = row_of(rs)
    rounded = queries.astype(jnp.bfloat16)
    now = jnp.sum(queries * keys, axis=1, keepdims=True) * SCALE
    before = jnp.sum(queries * earlier, axis=1, keepdims=True) * SCALE
    second = (rs >= ROWS_DEV) & (rs < STEPS * ROWS_DEV)
    before = jnp.where(second, before, MASKED)
    load.wait()
    scores = jnp.concatenate(
        [dot_t(rounded[h * span : (h + 1) * span], cache[:, 2 * h * HD : (2 * h + 1) * HD]) for h in range(KVH)],
        axis=0,
    )
    for slot in range(DEVICE_SLOTS):
        part = slice(slot * BLOCK_TOKENS, (slot + 1) * BLOCK_TOKENS)
        usable = (r == slot_row[slot]) & (lane < slot_limit[slot])
        s_ref[:, part] = jnp.where(usable, scores[:, part] * SCALE, MASKED)
    last = jnp.where(lane == 0, now, jnp.where(lane == 1, before, MASKED))
    s_ref[:, DEVICE_SLOTS * BLOCK_TOKENS :] = last
    for h in range(KVH):
        v_ref[:, h * HD : (h + 1) * HD] = cache[:, (2 * h + 1) * HD : (2 * h + 2) * HD]


def decode_scores(ints, cache, msgs, kv, q_own, after, n, lq):
    smem, vmem, hbm = [pl.BlockSpec(memory_space=space) for space in (SMEM, VMEM, pl.ANY)]
    rows = QH * GROUP_ROWS
    return pl.pallas_call(
        functools.partial(exchange_part, n, lq),
        in_specs=[smem] * 5 + [hbm, vmem, vmem, vmem, hbm],
        out_specs=[vmem] * 4,
        out_shape=[
            jax.ShapeDtypeStruct((n, lq * GROUP_ROWS, HD), jnp.float32),
            jax.ShapeDtypeStruct((rows, (DEVICE_SLOTS + 1) * BLOCK_TOKENS), jnp.float32),
            jax.ShapeDtypeStruct((cache.shape[0], KVH * HD), jnp.bfloat16),
            jax.ShapeDtypeStruct((KVH * GROUP_ROWS, HD), jnp.float32),
        ],
        scratch_shapes=[
            VMEM(cache.shape, jnp.bfloat16),
            pltpu.SemaphoreType.DMA,
            SMEM((DEVICE_SLOTS,), jnp.int32),
            SMEM((DEVICE_SLOTS,), jnp.int32),
        ],
        compiler_params=pltpu.CompilerParams(vmem_limit_bytes=61 * MIB),
        cost_estimate=pl.CostEstimate(flops=2 * rows * HD * 768, bytes_accessed=4 * MIB, transcendentals=0),
        name="decode_scores",
    )(*ints, cache, msgs, kv, q_own, after)


def owner_mix(s_ref, v_ref, new_ref, handed, o_ref):
    groups = QH
    rows = groups * GROUP_ROWS
    span = GQ * GROUP_ROWS
    mixed = handed[...].reshape(groups, GROUP_ROWS, HD)
    shape = (groups, GROUP_ROWS, HD)
    mine = iota(shape, 1) == iota(shape, 2)

    def column(at):
        line = jnp.broadcast_to(mixed[:, at : at + 1, :], shape)
        return jnp.sum(jnp.where(mine, line, 0.0), axis=2, keepdims=True).reshape(rows, 1)

    other_peak, other_total = column(6), column(7)
    scores = s_ref[...]
    peak = jnp.maximum(jnp.max(scores, axis=1, keepdims=True), other_peak)
    raised = jnp.exp(scores - peak)
    other = jnp.exp(other_peak - peak)
    inverse = 1.0 / (jnp.sum(raised, axis=1, keepdims=True) + other * other_total)
    weights = (raised * inverse).astype(jnp.bfloat16)
    old = DEVICE_SLOTS * BLOCK_TOKENS
    fresh = weights[:, old:].astype(jnp.float32)
    now, before = fresh[:, 0:1], fresh[:, 1:2]
    mixed = mixed.reshape(rows, HD) * (other * inverse)
    out = []
    for h in range(KVH):
        part = slice(h * span, (h + 1) * span)
        own = mixed[part] + dot(weights[part, :old], v_ref[:, h * HD : (h + 1) * HD])
        value = new_ref[h * GROUP_ROWS : (h + 1) * GROUP_ROWS, :]
        last = pltpu.roll(value, ROWS_DEV, 0)
        for hh in range(GQ):
            some = slice(h * span + hh * GROUP_ROWS, h * span + (hh + 1) * GROUP_ROWS)
            line = own[hh * GROUP_ROWS : (hh + 1) * GROUP_ROWS]
            out.append(line + now[some] * value + before[some] * last)
    out = jnp.concatenate(out, axis=1)
    for k in range(ROWS_DEV):
        steps = [out[s * ROWS_DEV + k : s * ROWS_DEV + k + 1] for s in range(STEPS)]
        o_ref[k] = jnp.concatenate(steps, axis=0).astype(jnp.bfloat16)


def decode_mix(scores, values, new, parts):
    vmem = pl.BlockSpec(memory_space=VMEM)
    rows = QH * GROUP_ROWS
    return pl.pallas_call(
        owner_mix,
        in_specs=[vmem] * 4,
        out_specs=vmem,
        out_shape=jax.ShapeDtypeStruct((ROWS_DEV, STEPS, QH * HD), jnp.bfloat16),
        compiler_params=pltpu.CompilerParams(vmem_limit_bytes=62 * MIB),
        cost_estimate=pl.CostEstimate(flops=2 * rows * HD * 768, bytes_accessed=4 * MIB, transcendentals=rows * 768),
        name="decode_mix",
    )(scores, values, new, parts)


def local(
    prompt_x,
    q_weight,
    kv_weight,
    prompt_blocks,
    finished,
    placement,
    page_table,
    row_lens,
    kv_cache,
    decode_x,
):
    n = lax.axis_size("tp")
    lq = q_weight.shape[1] // HD
    share = GQ // lq
    if share > 1:
        sets = [[k * share + i for i in range(share)] for k in range(n // share)]
        kv_weight = lax.all_gather(kv_weight, "tp", axis=1, tiled=True, axis_index_groups=sets)
    cache = kv_cache.reshape(-1, kv_cache.shape[2])
    dx = decode_x.reshape(-1, decode_x.shape[2])
    placement = placement.transpose(0, 2, 1)
    page_table = page_table.transpose(1, 0)
    ints = (prompt_blocks, finished, placement, page_table, row_lens)
    first, size = 256, 256
    q, kv, q_own, msgs = project_all(ints, dx, prompt_x, q_weight, kv_weight, n, first, size)
    msgs = lax.all_to_all(msgs, "tp", split_axis=0, concat_axis=0, tiled=True)
    kv_other = lax.ppermute(kv, "pool", [(0, 1), (1, 0)])
    prompt_attn, made = prompt_attention(prompt_blocks, q, kv, 0)
    handed, scores, values, new = decode_scores(ints, cache, msgs, kv_other, q_own, made, n, lq)
    parts = lax.all_to_all(handed, "tp", split_axis=0, concat_axis=0, tiled=True)
    prompt_attn, _ = prompt_attention(prompt_blocks, q, kv, 1, prompt_attn, handed)
    decode_attn = decode_mix(scores, values, new, parts)
    return prompt_attn, decode_attn.transpose(1, 0, 2)


def solution(mesh):
    return jax.shard_map(
        local,
        mesh=mesh,
        in_specs=(
            P(("rep", "pool"), None),
            P(None, "tp"),
            P(None, "tp"),
            P("rep", None),
            P("rep", None),
            P("rep", None, None),
            P(("rep", "pool", "tp"), None),
            P(("rep", "pool", "tp")),
            P(("rep", "pool", "tp"), None, None),
            P(None, ("rep", "pool"), None),
        ),
        out_specs=(P(("rep", "pool"), "tp"), P(None, ("rep", "pool", "tp"), None)),
        check_vma=False,
    )
```

```python
import functools

import jax
import jax.numpy as jnp
from jax import lax
from jax.experimental import pallas as pl
from jax.experimental.pallas import tpu as pltpu
from jax.sharding import PartitionSpec as P

QH = 32
KVH = 8
GQ = QH // KVH
HD = 128
BLOCK_TOKENS = 128
PTOK = 2048
NPROMPT = 3
MOST_BLOCKS = 8
PAGES = 2
STEPS = 2
NBLK = 16
DEVICE_SLOTS = 6
ROWS_DEV = 3
GROUP_ROWS = 8
KEY_VALUE_COLUMNS = 2048
SCALE = HD ** (-0.5)
MASKED = -1e30
PIECES = 5
STRIPS = 4
LOG2E = 1.4426950408889634
AHEAD = 2
MIB = 1 << 20
VMEM = pltpu.VMEM
SMEM = pltpu.SMEM


def dot(a, b):
    return jnp.dot(a, b, preferred_element_type=jnp.float32)


def dot_t(a, b):
    return lax.dot_general(a, b, (((1,), (1,)), ((), ())), preferred_element_type=jnp.float32)


def iota(shape, axis):
    return lax.broadcasted_iota(jnp.int32, shape, axis)


def row_of(rs):
    return jnp.where(rs >= 2 * ROWS_DEV, ROWS_DEV, jnp.where(rs >= ROWS_DEV, rs - ROWS_DEV, rs))


def block_of_pages(counts, done, placed, table):
    me = lax.axis_index("tp")
    other = 1 - lax.axis_index("pool")
    first_end = counts[other, 0]
    second_end = first_end + counts[other, 1]
    found = [[jnp.int32(-1)] * PAGES for _ in range(ROWS_DEV)]
    for b in range(NBLK):
        live = jnp.where(
            b < first_end, done[other, 0], jnp.where(b < second_end, done[other, 1], done[other, 2])
        )
        slot = jnp.where((live > 0) & (placed[other, 0, b] == me), placed[other, 1, b], -1)
        for r in range(ROWS_DEV):
            for p in range(PAGES):
                found[r][p] = jnp.where(slot == table[p, r], b, found[r][p])
    return found


def project(n, lq, first, size, *refs):
    dx_hbm, x_hbm, wq_hbm, wkv_hbm, q_hbm, kv_hbm, own_ref = refs[:7]
    x0, xs, w, q_out, kv_out, x_sems, w_sems, out_sems = refs[7:]
    depth = w.shape[0]
    count = xs.shape[0]
    cq = lq * HD
    piece = depth // PIECES
    own_rows = dx_hbm.shape[0]
    step = pl.program_id(0)

    def piece_copies(c):
        part = pl.ds(c * piece, piece)
        return [
            pltpu.make_async_copy(x_hbm.at[pl.ds(0, first), part], x0.at[pl.ds(0, first), part], w_sems.at[0, c]),
            pltpu.make_async_copy(dx_hbm.at[:, part], x0.at[pl.ds(first, own_rows), part], w_sems.at[1, c]),
            pltpu.make_async_copy(wq_hbm.at[part], w.at[part, pl.ds(0, cq)], w_sems.at[2, c]),
            pltpu.make_async_copy(wkv_hbm.at[part], w.at[part, pl.ds(cq, 2 * HD)], w_sems.at[3, c]),
        ]

    def x_copies(k):
        strip = size // STRIPS
        copies = []
        for i in range(STRIPS):
            rows = pl.ds(pl.multiple_of(first + k * size + i * strip, 16), strip)
            copies.append(
                pltpu.make_async_copy(x_hbm.at[rows], xs.at[k, pl.ds(i * strip, strip)], x_sems.at[k, i])
            )
        return copies

    def out_copies(k):
        if isinstance(k, int):
            rows = pl.ds(0, first)
        else:
            rows = pl.ds(pl.multiple_of(first + (k - 1) * size, 64), size)
        return [
            pltpu.make_async_copy(q_out.at[rows], q_hbm.at[rows], out_sems.at[0, k]),
            pltpu.make_async_copy(kv_out.at[rows], kv_hbm.at[rows], out_sems.at[1, k]),
        ]

    def keep(total, rows):
        q_out[rows, :] = total[:, :cq].astype(jnp.bfloat16)
        kv_out[rows, :] = total[:, cq:].astype(jnp.bfloat16)

    @pl.when(step == 0)
    def _():
        for c in range(AHEAD):
            for copy in piece_copies(c):
                copy.start()
        total = 0.0
        for c in range(PIECES):
            for copy in piece_copies(c):
                copy.wait()
            if c + AHEAD < PIECES:
                for copy in piece_copies(c + AHEAD):
                    copy.start()
            if c + AHEAD >= PIECES:
                for copy in x_copies(c + AHEAD - PIECES):
                    copy.start()
            part = slice(c * piece, (c + 1) * piece)
            total += dot(x0[:, part], w[part, :])
        keep(total[:first], pl.ds(0, first))
        for copy in out_copies(0):
            copy.start()
        shape = (n * GROUP_ROWS, own_rows)
        to, fro = iota(shape, 0), iota(shape, 1)
        owner, rs = to // GROUP_ROWS, to % GROUP_ROWS
        wanted = owner * ROWS_DEV + row_of(rs) + jnp.where(rs >= ROWS_DEV, ROWS_DEV * n, 0)
        pick = ((fro == wanted) & (rs < STEPS * ROWS_DEV)).astype(jnp.float32).astype(jnp.bfloat16)
        own_ref[...] = dot(pick, total[first:].astype(jnp.bfloat16)).astype(jnp.bfloat16)

    @pl.when((step > 0) & (step + AHEAD <= count))
    def _():
        for copy in x_copies(step + AHEAD - 1):
            copy.start()

    @pl.when(step > 0)
    def _():
        for copy in x_copies(step - 1):
            copy.wait()
        keep(dot(xs[step - 1], w[...]), pl.ds(pl.multiple_of(first + (step - 1) * size, 64), size))
        for copy in out_copies(step):
            copy.start()

    @pl.when(step == count)
    def _():
        for copy in out_copies(0):
            copy.wait()
        for k in range(1, count + 1):
            for copy in out_copies(jnp.int32(k)):
                copy.wait()


def project_all(dx, x, wq, wkv, n, first, size):
    rows, depth = x.shape
    cq, ckv = wq.shape[1], wkv.shape[1]
    lq = cq // HD
    count = (rows - first) // size
    vmem, hbm = pl.BlockSpec(memory_space=VMEM), pl.BlockSpec(memory_space=pl.ANY)
    return pl.pallas_call(
        functools.partial(project, n, lq, first, size),
        grid=(1 + count,),
        in_specs=[hbm] * 4,
        out_specs=[hbm, hbm, vmem],
        out_shape=[
            jax.ShapeDtypeStruct((rows, cq), jnp.bfloat16),
            jax.ShapeDtypeStruct((rows, ckv), jnp.bfloat16),
            jax.ShapeDtypeStruct((n * GROUP_ROWS, cq + ckv), jnp.bfloat16),
        ],
        scratch_shapes=[
            VMEM((first + dx.shape[0], depth), jnp.bfloat16),
            VMEM((count, size, depth), jnp.bfloat16),
            VMEM((depth, cq + ckv), jnp.bfloat16),
            VMEM((rows, cq), jnp.bfloat16),
            VMEM((rows, ckv), jnp.bfloat16),
            pltpu.SemaphoreType.DMA((count, STRIPS)),
            pltpu.SemaphoreType.DMA((4, PIECES)),
            pltpu.SemaphoreType.DMA((2, count + 1)),
        ],
        compiler_params=pltpu.CompilerParams(vmem_limit_bytes=62 * MIB),
        cost_estimate=pl.CostEstimate(
            flops=2 * rows * depth * (cq + ckv),
            bytes_accessed=2 * (rows + cq + ckv) * depth + 2 * rows * (cq + ckv),
            transcendentals=0,
        ),
        name="project",
    )(dx, x, wq, wkv)


def attend_prompt(lq, counts, q_hbm, kv_hbm, _, o_hbm, qs, kvs, outs, sems):
    group = lax.axis_index("pool")
    c0, c1 = counts[group, 0], counts[group, 1]
    big = jnp.where(c0 == MOST_BLOCKS, 0, jnp.where(c1 == MOST_BLOCKS, c0, c0 + c1))
    cut = jnp.where(c0 == MOST_BLOCKS, c1, c0)
    loads, stores = [], []
    for half in range(2):
        for j in range(MOST_BLOCKS):
            block = big + j if half == 0 else j + jnp.where(j >= big, MOST_BLOCKS, 0)
            rows = pl.ds(pl.multiple_of(block * BLOCK_TOKENS, BLOCK_TOKENS), BLOCK_TOKENS)
            here = pl.ds(j * BLOCK_TOKENS, BLOCK_TOKENS)
            loads.append(pltpu.make_async_copy(kv_hbm.at[rows], kvs.at[half, here], sems.at[0, half, j]))
            loads.append(pltpu.make_async_copy(q_hbm.at[rows], qs.at[half, here], sems.at[1, half, j]))
            stores.append(pltpu.make_async_copy(outs.at[half, here], o_hbm.at[rows], sems.at[2, half, j]))
    for copy in loads:
        copy.start()
    for copy in loads[: len(loads) // 2]:
        copy.wait()
    shape = (BLOCK_TOKENS, lq * BLOCK_TOKENS)
    causal = iota(shape, 0) <= iota(shape, 1) % BLOCK_TOKENS

    def scores_of(half, j):
        q = qs[half, j * BLOCK_TOKENS : (j + 1) * BLOCK_TOKENS, :]
        q = jnp.concatenate([q[:, h * HD : (h + 1) * HD] for h in range(lq)], axis=0)
        return dot_t(kvs[half, : (j + 1) * BLOCK_TOKENS, :HD], q)

    flipped = [kvs[0, :, HD:].T, None]
    order = [(half, j) for half in range(2) for j in range(MOST_BLOCKS)]
    scores = scores_of(*order[0])
    for k, (half, j) in enumerate(order):
        if k + 1 == MOST_BLOCKS:
            for copy in loads[len(loads) // 2 :]:
                copy.wait()
            flipped[1] = kvs[1, :, HD:].T
        later = scores_of(*order[k + 1]) if k + 1 < len(order) else None
        weights = []
        for h in range(lq):
            cols = slice(h * BLOCK_TOKENS, (h + 1) * BLOCK_TOKENS)
            tiles = []
            for i in range(j + 1):
                tile = scores[i * BLOCK_TOKENS : (i + 1) * BLOCK_TOKENS, cols]
                if i == j:
                    tile = jnp.where(causal[:, cols], tile, MASKED)
                elif half == 1:
                    tile = tile + jnp.where((i < cut) & (cut <= j), MASKED, 0.0)
                tiles.append(tile)
            peak = jnp.max(functools.reduce(jnp.maximum, tiles), axis=0, keepdims=True) * (SCALE * LOG2E)
            raised = [jnp.exp2(tile * (SCALE * LOG2E) - peak) for tile in tiles]
            total = jnp.sum(functools.reduce(jnp.add, raised), axis=0, keepdims=True)
            peak = peak + jnp.log2(total)
            raised = [jnp.exp2(tile * (SCALE * LOG2E) - peak).astype(jnp.bfloat16) for tile in tiles]
            weights.append(jnp.concatenate(raised, axis=0))
        mixed = dot(flipped[half][:, : (j + 1) * BLOCK_TOKENS], jnp.concatenate(weights, axis=1))
        mixed = mixed.astype(jnp.bfloat16)
        for h in range(lq):
            part = mixed[:, h * BLOCK_TOKENS : (h + 1) * BLOCK_TOKENS].T
            outs[half, j * BLOCK_TOKENS : (j + 1) * BLOCK_TOKENS, h * HD : (h + 1) * HD] = part
        scores = later
        if k + 1 == MOST_BLOCKS:
            for copy in stores[:MOST_BLOCKS]:
                copy.start()
    for copy in stores[MOST_BLOCKS:]:
        copy.start()
    for copy in stores:
        copy.wait()


def prompt_attention(counts, q, kv, after):
    rows, cq = q.shape
    hbm = pl.BlockSpec(memory_space=pl.ANY)
    tokens = MOST_BLOCKS * BLOCK_TOKENS
    return pl.pallas_call(
        functools.partial(attend_prompt, cq // HD),
        in_specs=[pl.BlockSpec(memory_space=SMEM)] + [hbm] * 3,
        out_specs=hbm,
        out_shape=jax.ShapeDtypeStruct((rows, cq), jnp.bfloat16),
        scratch_shapes=[
            VMEM((2, tokens, cq), jnp.bfloat16),
            VMEM((2, tokens, 2 * HD), jnp.bfloat16),
            VMEM((2, tokens, cq), jnp.bfloat16),
            pltpu.SemaphoreType.DMA((3, 2, MOST_BLOCKS)),
        ],
        compiler_params=pltpu.CompilerParams(vmem_limit_bytes=62 * MIB),
        cost_estimate=pl.CostEstimate(flops=4 * rows * rows * cq, bytes_accessed=8 * rows * cq, transcendentals=rows * rows),
        name="prompt_attention",
    )(counts, q, kv, after)


def row_head(n, lq, h, hh):
    at = h * GQ + hh
    return at // lq, at % lq


def pass_on(*refs):
    pass


def wait_for(kv, facts):
    hbm = pl.BlockSpec(memory_space=pl.ANY)
    return pl.pallas_call(
        pass_on,
        in_specs=[hbm, hbm],
        out_specs=hbm,
        out_shape=jax.ShapeDtypeStruct(kv.shape, kv.dtype),
        input_output_aliases={0: 0},
        compiler_params=pltpu.CompilerParams(vmem_limit_bytes=62 * MIB),
        name="wait_for",
    )(kv, facts)


def handed_part(n, lq, counts, done, placed, facts_ref, kv_ref, own_ref, o_ref):
    rows = lq * n * GROUP_ROWS
    shape = (rows, HD)
    at_row, lane = iota(shape, 0), iota(shape, 1)
    rs = at_row % GROUP_ROWS
    owner = (iota((rows, 1), 0) // GROUP_ROWS) % n
    own = own_ref[...]
    queries = jnp.concatenate([own[:, h * HD : (h + 1) * HD] for h in range(lq)], axis=0)
    scores = dot_t(queries, kv_ref[:, :HD]) * SCALE
    facts = jnp.broadcast_to(facts_ref[...], (n, GROUP_ROWS, HD)).reshape(n * GROUP_ROWS, HD)
    facts = jnp.concatenate([facts] * lq, axis=0)

    def column(kind):
        return jnp.sum(jnp.where(lane == kind * GROUP_ROWS + rs, facts, 0.0), axis=1, keepdims=True)

    slots = [column(page) for page in range(PAGES)]
    length = column(PAGES)
    other = 1 - lax.axis_index("pool")
    first_end = counts[other, 0]
    second_end = first_end + counts[other, 1]
    lane_f = lane.astype(jnp.float32)
    parts = []
    for b in range(NBLK):
        live = jnp.where(
            b < first_end, done[other, 0], jnp.where(b < second_end, done[other, 1], done[other, 2])
        )
        to = jnp.where(live > 0, placed[other, 0, b], -1)
        slot = placed[other, 1, b].astype(jnp.float32)
        limit = jnp.where(slots[0] == slot, length, jnp.where(slots[1] == slot, length - BLOCK_TOKENS, 0.0))
        limit = jnp.where(owner == to, limit, 0.0)
        part = scores[:, b * BLOCK_TOKENS : (b + 1) * BLOCK_TOKENS]
        parts.append(jnp.where(lane_f < limit, part, MASKED))
    scores = jnp.concatenate(parts, axis=1)
    top = jnp.max(scores, axis=1, keepdims=True)
    raised = jnp.exp(scores - top)
    total = jnp.sum(raised, axis=1, keepdims=True)
    near = raised.astype(jnp.bfloat16)
    rest = (raised - near.astype(jnp.float32)).astype(jnp.bfloat16)
    values = kv_ref[:, HD:]
    mixed = (dot(near, values) + dot(rest, values)).reshape(lq * n, GROUP_ROWS, HD)

    def line(col):
        spread = jnp.where(lane == rs, col, 0.0).reshape(lq * n, GROUP_ROWS, HD)
        return jnp.sum(spread, axis=1, keepdims=True)

    rs3 = rs.reshape(lq * n, GROUP_ROWS, HD)
    mixed = jnp.where(rs3 == 6, line(top), jnp.where(rs3 == 7, line(total), mixed))
    for h in range(lq):
        o_ref[:, h * GROUP_ROWS : (h + 1) * GROUP_ROWS, :] = mixed[h * n : (h + 1) * n]
    for k in range(lq + 2):
        tile = own[:, k * HD : (k + 1) * HD].astype(jnp.float32).reshape(n, GROUP_ROWS, HD)
        o_ref[:, (lq + k) * GROUP_ROWS : (lq + k + 1) * GROUP_ROWS, :] = tile


def handed_attention(ints, facts, kv, own, n, lq):
    rows = lq * n * GROUP_ROWS
    smem, vmem = pl.BlockSpec(memory_space=SMEM), pl.BlockSpec(memory_space=VMEM)
    return pl.pallas_call(
        functools.partial(handed_part, n, lq),
        in_specs=[smem] * 3 + [vmem] * 3,
        out_specs=vmem,
        out_shape=jax.ShapeDtypeStruct((n, 2 * (lq + 1) * GROUP_ROWS, HD), jnp.float32),
        compiler_params=pltpu.CompilerParams(vmem_limit_bytes=24 * MIB),
        cost_estimate=pl.CostEstimate(flops=6 * rows * HD * PTOK, bytes_accessed=2 * MIB, transcendentals=rows * PTOK),
        name="handed_attention",
    )(*ints[:3], facts, kv, own)


def owner_part(n, lq, counts, done, placed, table, lens, cache_hbm, msgs, o_ref, cache, sems, slot_row, slot_limit):
    loads = []
    for slot in range(DEVICE_SLOTS):
        part = pl.ds(slot * BLOCK_TOKENS, BLOCK_TOKENS)
        loads.append(pltpu.make_async_copy(cache_hbm.at[part], cache.at[part], sems.at[slot]))
    for load in loads:
        load.start()
    found = block_of_pages(counts, done, placed, table)
    for r in range(ROWS_DEV):
        for p in range(PAGES):
            slot_row[table[p, r]] = jnp.int32(r)
            slot_limit[table[p, r]] = jnp.where(found[r][p] < 0, lens[r] - p * BLOCK_TOKENS, 0)

    def tile(t, k):
        return msgs[t, k * GROUP_ROWS : (k + 1) * GROUP_ROWS, :]

    groups = QH
    rows = groups * GROUP_ROWS
    span = GQ * GROUP_ROWS
    queries, keys, values, mixed = [], [], [], []
    for h in range(KVH):
        for hh in range(GQ):
            t, at = row_head(n, lq, h, hh)
            queries.append(tile(t, lq + at))
            mixed.append(tile(t, at))
        t, _ = row_head(n, lq, h, 0)
        keys += [tile(t, 2 * lq)] * GQ
        values.append(tile(t, 2 * lq + 1))
    queries = jnp.concatenate(queries, axis=0)
    earlier = jnp.concatenate([pltpu.roll(key, ROWS_DEV, 0) for key in keys], axis=0)
    keys = jnp.concatenate(keys, axis=0)
    at_row, lane = iota((rows, HD), 0), iota((rows, HD), 1)
    r = row_of(at_row % GROUP_ROWS)
    rounded = queries.astype(jnp.bfloat16)
    now = jnp.sum(queries * keys, axis=1, keepdims=True) * SCALE
    before = jnp.sum(queries * earlier, axis=1, keepdims=True) * SCALE
    rs1 = iota((rows, 1), 0) % GROUP_ROWS
    before = jnp.where((rs1 >= ROWS_DEV) & (rs1 < STEPS * ROWS_DEV), before, MASKED)
    mixed = jnp.concatenate(mixed, axis=0).reshape(groups, GROUP_ROWS, HD)
    shape = (groups, GROUP_ROWS, HD)
    mine = iota(shape, 1) == iota(shape, 2)

    def column(at):
        line = jnp.broadcast_to(mixed[:, at : at + 1, :], shape)
        return jnp.sum(jnp.where(mine, line, 0.0), axis=2, keepdims=True).reshape(rows, 1)

    other_peak, other_total = column(6), column(7)
    for load in loads:
        load.wait()
    scores = jnp.concatenate(
        [dot_t(rounded[h * span : (h + 1) * span], cache[:, 2 * h * HD : (2 * h + 1) * HD]) for h in range(KVH)],
        axis=0,
    )
    parts = []
    for slot in range(DEVICE_SLOTS):
        part = scores[:, slot * BLOCK_TOKENS : (slot + 1) * BLOCK_TOKENS]
        usable = (r == slot_row[slot]) & (lane < slot_limit[slot])
        parts.append(jnp.where(usable, part * SCALE, MASKED))
    scores = jnp.concatenate(parts, axis=1)
    peak = jnp.maximum(jnp.max(scores, axis=1, keepdims=True), jnp.maximum(now, before))
    peak = jnp.maximum(peak, other_peak)
    raised, now, before = jnp.exp(scores - peak), jnp.exp(now - peak), jnp.exp(before - peak)
    other = jnp.exp(other_peak - peak)
    inverse = 1.0 / (jnp.sum(raised, axis=1, keepdims=True) + now + before + other * other_total)
    weights = (raised * inverse).astype(jnp.bfloat16)
    now = (now * inverse).astype(jnp.bfloat16).astype(jnp.float32)
    before = (before * inverse).astype(jnp.bfloat16).astype(jnp.float32)
    mixed = mixed.reshape(rows, HD) * (other * inverse)
    out = []
    for h in range(KVH):
        part = slice(h * span, (h + 1) * span)
        own = mixed[part] + dot(weights[part], cache[:, (2 * h + 1) * HD : (2 * h + 2) * HD])
        last = pltpu.roll(values[h], ROWS_DEV, 0)
        for hh in range(GQ):
            some = slice(h * span + hh * GROUP_ROWS, h * span + (hh + 1) * GROUP_ROWS)
            line = own[hh * GROUP_ROWS : (hh + 1) * GROUP_ROWS]
            out.append(line + now[some] * values[h] + before[some] * last)
    out = jnp.concatenate(out, axis=1)
    for k in range(ROWS_DEV):
        steps = [out[s * ROWS_DEV + k : s * ROWS_DEV + k + 1] for s in range(STEPS)]
        o_ref[k] = jnp.concatenate(steps, axis=0).astype(jnp.bfloat16)


def decode_attention(ints, cache, msgs, n, lq):
    smem, vmem, hbm = [pl.BlockSpec(memory_space=space) for space in (SMEM, VMEM, pl.ANY)]
    rows = QH * GROUP_ROWS
    return pl.pallas_call(
        functools.partial(owner_part, n, lq),
        in_specs=[smem] * 5 + [hbm, vmem],
        out_specs=vmem,
        out_shape=jax.ShapeDtypeStruct((ROWS_DEV, STEPS, QH * HD), jnp.bfloat16),
        scratch_shapes=[
            VMEM(cache.shape, jnp.bfloat16),
            pltpu.SemaphoreType.DMA((DEVICE_SLOTS,)),
            SMEM((DEVICE_SLOTS,), jnp.int32),
            SMEM((DEVICE_SLOTS,), jnp.int32),
        ],
        compiler_params=pltpu.CompilerParams(vmem_limit_bytes=62 * MIB),
        cost_estimate=pl.CostEstimate(flops=4 * rows * HD * 768, bytes_accessed=4 * MIB, transcendentals=rows * 768),
        name="decode_attention",
    )(*ints, cache, msgs)


def local(
    prompt_x,
    q_weight,
    kv_weight,
    prompt_blocks,
    finished,
    placement,
    page_table,
    row_lens,
    kv_cache,
    decode_x,
):
    n = lax.axis_size("tp")
    lq = q_weight.shape[1] // HD
    share = GQ // lq
    if share > 1:
        sets = [[k * share + i for i in range(share)] for k in range(n // share)]
        kv_weight = lax.all_gather(kv_weight, "tp", axis=1, tiled=True, axis_index_groups=sets)
    cache = kv_cache.reshape(-1, kv_cache.shape[2])
    dx = decode_x.reshape(-1, decode_x.shape[2])
    placement = placement.transpose(0, 2, 1)
    page_table = page_table.transpose(1, 0)
    ints = (prompt_blocks, finished, placement, page_table, row_lens)
    spare = jnp.zeros((GROUP_ROWS - STEPS * ROWS_DEV,), jnp.int32)
    facts = []
    for fact in (page_table[0], page_table[1], row_lens):
        facts += [fact] * STEPS + [spare]
    facts.append(jnp.zeros((HD - 3 * GROUP_ROWS,), jnp.int32))
    facts = jnp.broadcast_to(jnp.concatenate(facts).astype(jnp.float32), (n, 1, HD))
    facts = lax.all_to_all(facts, "tp", split_axis=0, concat_axis=0, tiled=True)
    first, size = 256, 448
    q, kv, own = project_all(dx, prompt_x, q_weight, kv_weight, n, first, size)
    kv = wait_for(kv, facts)
    kv_other = lax.ppermute(kv, "pool", [(0, 1), (1, 0)])
    msgs = handed_attention(ints, facts, kv_other, own, n, lq)
    prompt_attn = prompt_attention(prompt_blocks, q, kv, msgs)
    msgs = lax.all_to_all(msgs, "tp", split_axis=0, concat_axis=0, tiled=True)
    decode_attn = decode_attention(ints, cache, msgs, n, lq)
    return prompt_attn, decode_attn.transpose(1, 0, 2)


def solution(mesh):
    return jax.shard_map(
        local,
        mesh=mesh,
        in_specs=(
            P(("rep", "pool"), None),
            P(None, "tp"),
            P(None, "tp"),
            P("rep", None),
            P("rep", None),
            P("rep", None, None),
            P(("rep", "pool", "tp"), None),
            P(("rep", "pool", "tp")),
            P(("rep", "pool", "tp"), None, None),
            P(None, ("rep", "pool"), None),
        ),
        out_specs=(P(("rep", "pool"), "tp"), P(None, ("rep", "pool", "tp"), None)),
        check_vma=False,
    )
```

```python
import functools

import jax
import jax.numpy as jnp
from jax import lax
from jax.experimental import pallas as pl
from jax.experimental.pallas import tpu as pltpu
from jax.sharding import PartitionSpec as P

QH = 32
KVH = 8
GQ = QH // KVH
HD = 128
BLOCK_TOKENS = 128
PTOK = 2048
NPROMPT = 3
MOST_BLOCKS = 8
PAGES = 2
STEPS = 2
NBLK = 16
DEVICE_SLOTS = 6
ROWS_DEV = 3
GROUP_ROWS = 8
KEY_VALUE_COLUMNS = 2048
SCALE = HD ** (-0.5)
MASKED = -1e30
PIECES = 5
STRIPS = 4
LOG2E = 1.4426950408889634
AHEAD = 2
MIB = 1 << 20
VMEM = pltpu.VMEM
SMEM = pltpu.SMEM


def dot(a, b):
    return jnp.dot(a, b, preferred_element_type=jnp.float32)


def dot_t(a, b):
    return lax.dot_general(a, b, (((1,), (1,)), ((), ())), preferred_element_type=jnp.float32)


def iota(shape, axis):
    return lax.broadcasted_iota(jnp.int32, shape, axis)


def row_of(rs):
    return jnp.where(rs >= 2 * ROWS_DEV, ROWS_DEV, jnp.where(rs >= ROWS_DEV, rs - ROWS_DEV, rs))


def block_of_pages(counts, done, placed, table):
    me = lax.axis_index("tp")
    other = 1 - lax.axis_index("pool")
    first_end = counts[other, 0]
    second_end = first_end + counts[other, 1]
    found = [[jnp.int32(-1)] * PAGES for _ in range(ROWS_DEV)]
    for b in range(NBLK):
        live = jnp.where(
            b < first_end, done[other, 0], jnp.where(b < second_end, done[other, 1], done[other, 2])
        )
        slot = jnp.where((live > 0) & (placed[other, 0, b] == me), placed[other, 1, b], -1)
        for r in range(ROWS_DEV):
            for p in range(PAGES):
                found[r][p] = jnp.where(slot == table[p, r], b, found[r][p])
    return found


def by_row(r, values, rest):
    out = jnp.full(r.shape, rest, jnp.int32)
    for k in range(ROWS_DEV):
        out = jnp.where(r == k, values[k], out)
    return out


def project(n, lq, first, size, *refs):
    dx_hbm, x_hbm, wq_hbm, wkv_hbm, q_hbm, kv_hbm, own_ref = refs[:7]
    x0, xs, w, q_out, kv_out, x_sems, w_sems, out_sems = refs[7:]
    depth = w.shape[0]
    count = xs.shape[0]
    cq = lq * HD
    piece = depth // PIECES
    own_rows = dx_hbm.shape[0]
    step = pl.program_id(0)

    def piece_copies(c):
        part = pl.ds(c * piece, piece)
        return [
            pltpu.make_async_copy(x_hbm.at[pl.ds(0, first), part], x0.at[pl.ds(0, first), part], w_sems.at[0, c]),
            pltpu.make_async_copy(dx_hbm.at[:, part], x0.at[pl.ds(first, own_rows), part], w_sems.at[1, c]),
            pltpu.make_async_copy(wq_hbm.at[part], w.at[part, pl.ds(0, cq)], w_sems.at[2, c]),
            pltpu.make_async_copy(wkv_hbm.at[part], w.at[part, pl.ds(cq, 2 * HD)], w_sems.at[3, c]),
        ]

    def x_copies(k):
        strip = size // STRIPS
        copies = []
        for i in range(STRIPS):
            rows = pl.ds(pl.multiple_of(first + k * size + i * strip, 16), strip)
            copies.append(
                pltpu.make_async_copy(x_hbm.at[rows], xs.at[k, pl.ds(i * strip, strip)], x_sems.at[k, i])
            )
        return copies

    def out_copies(k):
        if isinstance(k, int):
            rows = pl.ds(0, first)
        else:
            rows = pl.ds(pl.multiple_of(first + (k - 1) * size, 64), size)
        return [
            pltpu.make_async_copy(q_out.at[rows], q_hbm.at[rows], out_sems.at[0, k]),
            pltpu.make_async_copy(kv_out.at[rows], kv_hbm.at[rows], out_sems.at[1, k]),
        ]

    def keep(total, rows):
        q_out[rows, :] = total[:, :cq].astype(jnp.bfloat16)
        kv_out[rows, :] = total[:, cq:].astype(jnp.bfloat16)

    @pl.when(step == 0)
    def _():
        for c in range(AHEAD):
            for copy in piece_copies(c):
                copy.start()
        total = 0.0
        for c in range(PIECES):
            for copy in piece_copies(c):
                copy.wait()
            if c + AHEAD < PIECES:
                for copy in piece_copies(c + AHEAD):
                    copy.start()
            if c + AHEAD >= PIECES:
                for copy in x_copies(c + AHEAD - PIECES):
                    copy.start()
            part = slice(c * piece, (c + 1) * piece)
            total += dot(x0[:, part], w[part, :])
        keep(total[:first], pl.ds(0, first))
        for copy in out_copies(0):
            copy.start()
        shape = (n * GROUP_ROWS, own_rows)
        to, fro = iota(shape, 0), iota(shape, 1)
        owner, rs = to // GROUP_ROWS, to % GROUP_ROWS
        wanted = owner * ROWS_DEV + row_of(rs) + jnp.where(rs >= ROWS_DEV, ROWS_DEV * n, 0)
        pick = ((fro == wanted) & (rs < STEPS * ROWS_DEV)).astype(jnp.float32).astype(jnp.bfloat16)
        own_ref[...] = dot(pick, total[first:].astype(jnp.bfloat16)).astype(jnp.bfloat16)

    @pl.when((step > 0) & (step + AHEAD <= count))
    def _():
        for copy in x_copies(step + AHEAD - 1):
            copy.start()

    @pl.when(step > 0)
    def _():
        for copy in x_copies(step - 1):
            copy.wait()
        keep(dot(xs[step - 1], w[...]), pl.ds(pl.multiple_of(first + (step - 1) * size, 64), size))
        for copy in out_copies(step):
            copy.start()

    @pl.when(step == count)
    def _():
        for copy in out_copies(0):
            copy.wait()
        for k in range(1, count + 1):
            for copy in out_copies(jnp.int32(k)):
                copy.wait()


def project_all(dx, x, wq, wkv, n, first, size):
    rows, depth = x.shape
    cq, ckv = wq.shape[1], wkv.shape[1]
    lq = cq // HD
    count = (rows - first) // size
    vmem, hbm = pl.BlockSpec(memory_space=VMEM), pl.BlockSpec(memory_space=pl.ANY)
    return pl.pallas_call(
        functools.partial(project, n, lq, first, size),
        grid=(1 + count,),
        in_specs=[hbm] * 4,
        out_specs=[hbm, hbm, vmem],
        out_shape=[
            jax.ShapeDtypeStruct((rows, cq), jnp.bfloat16),
            jax.ShapeDtypeStruct((rows, ckv), jnp.bfloat16),
            jax.ShapeDtypeStruct((n * GROUP_ROWS, cq + ckv), jnp.bfloat16),
        ],
        scratch_shapes=[
            VMEM((first + dx.shape[0], depth), jnp.bfloat16),
            VMEM((count, size, depth), jnp.bfloat16),
            VMEM((depth, cq + ckv), jnp.bfloat16),
            VMEM((rows, cq), jnp.bfloat16),
            VMEM((rows, ckv), jnp.bfloat16),
            pltpu.SemaphoreType.DMA((count, STRIPS)),
            pltpu.SemaphoreType.DMA((4, PIECES)),
            pltpu.SemaphoreType.DMA((2, count + 1)),
        ],
        compiler_params=pltpu.CompilerParams(vmem_limit_bytes=50 * MIB),
        cost_estimate=pl.CostEstimate(
            flops=2 * rows * depth * (cq + ckv),
            bytes_accessed=2 * (rows + cq + ckv) * depth + 2 * rows * (cq + ckv),
            transcendentals=0,
        ),
        name="project",
    )(dx, x, wq, wkv)


def add_facts(n, counts, done, placed, table, lens, own_ref, msg_ref):
    found = block_of_pages(counts, done, placed, table)
    shape = (n * GROUP_ROWS, HD)
    lane = iota(shape, 1)
    r = row_of(lane % GROUP_ROWS)
    kind = lane // GROUP_ROWS
    facts = jnp.where(
        kind == 0,
        by_row(r, [found[i][0] for i in range(ROWS_DEV)], -1),
        jnp.where(
            kind == 1,
            by_row(r, [found[i][1] for i in range(ROWS_DEV)], -1),
            by_row(r, [lens[i] for i in range(ROWS_DEV)], 0),
        ),
    ).astype(jnp.float32)
    sixth = iota(shape, 0) % GROUP_ROWS == 6
    head = jnp.where(sixth, facts, own_ref[:, :HD].astype(jnp.float32))
    msg_ref[:, :HD] = head.astype(jnp.bfloat16)
    msg_ref[:, HD:] = own_ref[:, HD:]


def make_messages(ints, own, n):
    smem, vmem = pl.BlockSpec(memory_space=SMEM), pl.BlockSpec(memory_space=VMEM)
    return pl.pallas_call(
        functools.partial(add_facts, n),
        in_specs=[smem] * 5 + [vmem],
        out_specs=vmem,
        out_shape=jax.ShapeDtypeStruct(own.shape, own.dtype),
        compiler_params=pltpu.CompilerParams(vmem_limit_bytes=24 * MIB),
        cost_estimate=pl.CostEstimate(flops=0, bytes_accessed=4 * own.size, transcendentals=0),
        name="make_messages",
    )(*ints, own)


def attend_prompt(lq, half, counts, q_ref, kv_ref, *refs):
    o_hbm, made_ref, kvs, outs, sems = refs[-5:]
    made_ref[...] = jnp.zeros_like(made_ref)
    group = lax.axis_index("pool")
    c0, c1 = counts[group, 0], counts[group, 1]
    big = jnp.where(c0 == MOST_BLOCKS, 0, jnp.where(c1 == MOST_BLOCKS, c0, c0 + c1))
    cut = jnp.where(c0 == MOST_BLOCKS, c1, c0)
    places, stores = [], []
    strip, early = (4, 3) if half == 0 else (1, 5)
    for j in range(MOST_BLOCKS):
        block = big + j if half == 0 else j + jnp.where(j >= big, MOST_BLOCKS, 0)
        at = pl.multiple_of(block * BLOCK_TOKENS, BLOCK_TOKENS)
        places.append(pl.ds(at, BLOCK_TOKENS))
        kvs[j * BLOCK_TOKENS : (j + 1) * BLOCK_TOKENS, :] = kv_ref[places[j], :]
        if j % strip == 0:
            rows, here = pl.ds(at, strip * BLOCK_TOKENS), pl.ds(j * BLOCK_TOKENS, strip * BLOCK_TOKENS)
            stores.append(pltpu.make_async_copy(outs.at[here], o_hbm.at[rows], sems.at[j]))
    shape = (BLOCK_TOKENS, lq * BLOCK_TOKENS)
    causal = iota(shape, 0) <= iota(shape, 1) % BLOCK_TOKENS
    flipped = kvs[:, HD:].T

    def scores_of(j):
        q = q_ref[places[j], :]
        q = jnp.concatenate([q[:, h * HD : (h + 1) * HD] for h in range(lq)], axis=0)
        return dot_t(kvs[: (j + 1) * BLOCK_TOKENS, :HD], q)

    scores = scores_of(0)
    for j in range(MOST_BLOCKS):
        later = scores_of(j + 1) if j + 1 < MOST_BLOCKS else None
        weights = []
        for h in range(lq):
            cols = slice(h * BLOCK_TOKENS, (h + 1) * BLOCK_TOKENS)
            tiles = []
            for i in range(j + 1):
                tile = scores[i * BLOCK_TOKENS : (i + 1) * BLOCK_TOKENS, cols]
                if i == j:
                    tile = jnp.where(causal[:, cols], tile, MASKED)
                elif half == 1:
                    tile = tile + jnp.where((i < cut) & (cut <= j), MASKED, 0.0)
                tiles.append(tile)
            peak = jnp.max(functools.reduce(jnp.maximum, tiles), axis=0, keepdims=True)
            raised = [jnp.exp2((tile - peak) * (SCALE * LOG2E)) for tile in tiles]
            inverse = 1.0 / jnp.sum(functools.reduce(jnp.add, raised), axis=0, keepdims=True)
            weights.append(jnp.concatenate([(t * inverse).astype(jnp.bfloat16) for t in raised], axis=0))
        mixed = dot(flipped[:, : (j + 1) * BLOCK_TOKENS], jnp.concatenate(weights, axis=1))
        mixed = mixed.astype(jnp.bfloat16)
        for h in range(lq):
            part = mixed[:, h * BLOCK_TOKENS : (h + 1) * BLOCK_TOKENS].T
            outs[j * BLOCK_TOKENS : (j + 1) * BLOCK_TOKENS, h * HD : (h + 1) * HD] = part
        scores = later
        if j == early:
            for copy in stores[: (j + 1) // strip]:
                copy.start()
    for copy in stores[(early + 1) // strip :]:
        copy.start()
    for copy in stores:
        copy.wait()


def prompt_attention(counts, q, kv, half, so_far=None, after=None):
    rows, cq = q.shape
    hbm, vmem = pl.BlockSpec(memory_space=pl.ANY), pl.BlockSpec(memory_space=VMEM)
    more = () if so_far is None else (so_far, after)
    tokens = MOST_BLOCKS * BLOCK_TOKENS
    return pl.pallas_call(
        functools.partial(attend_prompt, cq // HD, half),
        in_specs=[pl.BlockSpec(memory_space=SMEM), vmem, vmem] + [hbm] * len(more),
        out_specs=[hbm, pl.BlockSpec(memory_space=VMEM)],
        out_shape=[
            jax.ShapeDtypeStruct((rows, cq), jnp.bfloat16),
            jax.ShapeDtypeStruct((8, HD), jnp.float32),
        ],
        scratch_shapes=[
            VMEM((tokens, 2 * HD), jnp.bfloat16),
            VMEM((tokens, cq), jnp.bfloat16),
            pltpu.SemaphoreType.DMA((MOST_BLOCKS,)),
        ],
        input_output_aliases={3: 0} if more else {},
        compiler_params=pltpu.CompilerParams(vmem_limit_bytes=24 * MIB),
        cost_estimate=pl.CostEstimate(flops=2 * rows * rows * cq, bytes_accessed=4 * rows * cq, transcendentals=rows * rows // 2),
        name="long_prompt" if half == 0 else "short_prompts",
    )(counts, q, kv, *more)


def row_head(n, lq, h, hh):
    at = h * GQ + hh
    return at // lq, at % lq


def handed_part(n, lq, kv_ref, own_ref, msg_ref, o_ref):
    rows = lq * n * GROUP_ROWS
    shape = (rows, HD)
    at_row, lane = iota(shape, 0), iota(shape, 1)
    rs = at_row % GROUP_ROWS
    facts = msg_ref[:, :HD].astype(jnp.float32).reshape(n, GROUP_ROWS, HD)[:, 6:7, :]
    facts = jnp.broadcast_to(facts, (n, GROUP_ROWS, HD)).reshape(n * GROUP_ROWS, HD)
    facts = jnp.concatenate([facts] * lq, axis=0)

    def column(kind):
        return jnp.sum(jnp.where(lane == kind * GROUP_ROWS + rs, facts, 0.0), axis=1, keepdims=True)

    first_block, second_block, length = [column(kind) for kind in range(3)]
    own = own_ref[...]
    queries = jnp.concatenate([own[:, h * HD : (h + 1) * HD] for h in range(lq)], axis=0)
    scores = dot_t(queries, kv_ref[:, :HD]) * SCALE
    lane_f = lane.astype(jnp.float32)
    parts = []
    for b in range(NBLK):
        limit = jnp.where(
            first_block == b, length, jnp.where(second_block == b, length - BLOCK_TOKENS, 0.0)
        )
        part = scores[:, b * BLOCK_TOKENS : (b + 1) * BLOCK_TOKENS]
        parts.append(jnp.where(lane_f < limit, part, MASKED))
    scores = jnp.concatenate(parts, axis=1)
    top = jnp.max(scores, axis=1, keepdims=True)
    raised = jnp.exp(scores - top)
    total = jnp.sum(raised, axis=1, keepdims=True)
    near = raised.astype(jnp.bfloat16)
    rest = (raised - near.astype(jnp.float32)).astype(jnp.bfloat16)
    values = kv_ref[:, HD:]
    mixed = (dot(near, values) + dot(rest, values)).reshape(lq * n, GROUP_ROWS, HD)

    def line(col):
        spread = jnp.where(lane == rs, col, 0.0).reshape(lq * n, GROUP_ROWS, HD)
        return jnp.sum(spread, axis=1, keepdims=True)

    rs3 = rs.reshape(lq * n, GROUP_ROWS, HD)
    mixed = jnp.where(rs3 == 6, line(top), jnp.where(rs3 == 7, line(total), mixed))
    for h in range(lq):
        o_ref[:, h * GROUP_ROWS : (h + 1) * GROUP_ROWS, :] = mixed[h * n : (h + 1) * n]


def exchange_part(n, lq, *refs):
    counts, done, placed, table, lens, cache, msgs, kv_ref, own_ref, _ = refs[:10]
    handed_ref, s_ref, v_ref, new_ref, slot_row, slot_limit = refs[10:]
    handed_part(n, lq, kv_ref, own_ref, msgs, handed_ref)
    held = msgs[...].astype(jnp.float32)
    found = block_of_pages(counts, done, placed, table)
    for r in range(ROWS_DEV):
        for p in range(PAGES):
            slot_row[table[p, r]] = jnp.int32(r)
            slot_limit[table[p, r]] = jnp.where(found[r][p] < 0, lens[r] - p * BLOCK_TOKENS, 0)
    cq = lq * HD
    rows = QH * GROUP_ROWS
    span = GQ * GROUP_ROWS
    queries, keys = [], []
    for h in range(KVH):
        for hh in range(GQ):
            t, at = row_head(n, lq, h, hh)
            queries.append(held[t * GROUP_ROWS : (t + 1) * GROUP_ROWS, at * HD : (at + 1) * HD])
        t, _ = row_head(n, lq, h, 0)
        keys += [held[t * GROUP_ROWS : (t + 1) * GROUP_ROWS, cq : cq + HD]] * GQ
        new_ref[h * GROUP_ROWS : (h + 1) * GROUP_ROWS, :] = held[
            t * GROUP_ROWS : (t + 1) * GROUP_ROWS, cq + HD : cq + 2 * HD
        ]
    queries = jnp.concatenate(queries, axis=0)
    earlier = jnp.concatenate([pltpu.roll(key, ROWS_DEV, 0) for key in keys], axis=0)
    keys = jnp.concatenate(keys, axis=0)
    at_row, lane = iota((rows, HD), 0), iota((rows, HD), 1)
    rs = at_row % GROUP_ROWS
    r = row_of(rs)
    rounded = queries.astype(jnp.bfloat16)
    now = jnp.sum(queries * keys, axis=1, keepdims=True) * SCALE
    before = jnp.sum(queries * earlier, axis=1, keepdims=True) * SCALE
    second = (rs >= ROWS_DEV) & (rs < STEPS * ROWS_DEV)
    before = jnp.where(second, before, MASKED)
    scores = jnp.concatenate(
        [dot_t(rounded[h * span : (h + 1) * span], cache[:, 2 * h * HD : (2 * h + 1) * HD]) for h in range(KVH)],
        axis=0,
    )
    for slot in range(DEVICE_SLOTS):
        part = slice(slot * BLOCK_TOKENS, (slot + 1) * BLOCK_TOKENS)
        usable = (r == slot_row[slot]) & (lane < slot_limit[slot])
        s_ref[:, part] = jnp.where(usable, scores[:, part] * SCALE, MASKED)
    last = jnp.where(lane == 0, now, jnp.where(lane == 1, before, MASKED))
    s_ref[:, DEVICE_SLOTS * BLOCK_TOKENS :] = last
    for h in range(KVH):
        v_ref[:, h * HD : (h + 1) * HD] = cache[:, (2 * h + 1) * HD : (2 * h + 2) * HD]


def decode_scores(ints, cache, msgs, kv, own, after, n, lq):
    smem, vmem, hbm = [pl.BlockSpec(memory_space=space) for space in (SMEM, VMEM, pl.ANY)]
    rows = QH * GROUP_ROWS
    return pl.pallas_call(
        functools.partial(exchange_part, n, lq),
        in_specs=[smem] * 5 + [vmem] * 4 + [hbm],
        out_specs=[vmem] * 4,
        out_shape=[
            jax.ShapeDtypeStruct((n, lq * GROUP_ROWS, HD), jnp.float32),
            jax.ShapeDtypeStruct((rows, (DEVICE_SLOTS + 1) * BLOCK_TOKENS), jnp.float32),
            jax.ShapeDtypeStruct((cache.shape[0], KVH * HD), jnp.bfloat16),
            jax.ShapeDtypeStruct((KVH * GROUP_ROWS, HD), jnp.float32),
        ],
        scratch_shapes=[
            SMEM((DEVICE_SLOTS,), jnp.int32),
            SMEM((DEVICE_SLOTS,), jnp.int32),
        ],
        compiler_params=pltpu.CompilerParams(vmem_limit_bytes=24 * MIB),
        cost_estimate=pl.CostEstimate(flops=2 * rows * HD * 768, bytes_accessed=4 * MIB, transcendentals=0),
        name="decode_scores",
    )(*ints, cache, msgs, kv, own, after)


def owner_mix(s_ref, v_ref, new_ref, handed, o_ref):
    groups = QH
    rows = groups * GROUP_ROWS
    span = GQ * GROUP_ROWS
    mixed = handed[...].reshape(groups, GROUP_ROWS, HD)
    shape = (groups, GROUP_ROWS, HD)
    mine = iota(shape, 1) == iota(shape, 2)

    def column(at):
        line = jnp.broadcast_to(mixed[:, at : at + 1, :], shape)
        return jnp.sum(jnp.where(mine, line, 0.0), axis=2, keepdims=True).reshape(rows, 1)

    other_peak, other_total = column(6), column(7)
    scores = s_ref[...]
    peak = jnp.maximum(jnp.max(scores, axis=1, keepdims=True), other_peak)
    raised = jnp.exp(scores - peak)
    other = jnp.exp(other_peak - peak)
    inverse = 1.0 / (jnp.sum(raised, axis=1, keepdims=True) + other * other_total)
    weights = (raised * inverse).astype(jnp.bfloat16)
    old = DEVICE_SLOTS * BLOCK_TOKENS
    fresh = weights[:, old:].astype(jnp.float32)
    now, before = fresh[:, 0:1], fresh[:, 1:2]
    mixed = mixed.reshape(rows, HD) * (other * inverse)
    out = []
    for h in range(KVH):
        part = slice(h * span, (h + 1) * span)
        own = mixed[part] + dot(weights[part, :old], v_ref[:, h * HD : (h + 1) * HD])
        value = new_ref[h * GROUP_ROWS : (h + 1) * GROUP_ROWS, :]
        last = pltpu.roll(value, ROWS_DEV, 0)
        for hh in range(GQ):
            some = slice(h * span + hh * GROUP_ROWS, h * span + (hh + 1) * GROUP_ROWS)
            line = own[hh * GROUP_ROWS : (hh + 1) * GROUP_ROWS]
            out.append(line + now[some] * value + before[some] * last)
    out = jnp.concatenate(out, axis=1)
    for k in range(ROWS_DEV):
        steps = [out[s * ROWS_DEV + k : s * ROWS_DEV + k + 1] for s in range(STEPS)]
        o_ref[k] = jnp.concatenate(steps, axis=0).astype(jnp.bfloat16)


def decode_mix(scores, values, new, parts):
    vmem = pl.BlockSpec(memory_space=VMEM)
    rows = QH * GROUP_ROWS
    return pl.pallas_call(
        owner_mix,
        in_specs=[vmem] * 4,
        out_specs=vmem,
        out_shape=jax.ShapeDtypeStruct((ROWS_DEV, STEPS, QH * HD), jnp.bfloat16),
        compiler_params=pltpu.CompilerParams(vmem_limit_bytes=24 * MIB),
        cost_estimate=pl.CostEstimate(flops=2 * rows * HD * 768, bytes_accessed=4 * MIB, transcendentals=rows * 768),
        name="decode_mix",
    )(scores, values, new, parts)


def local(
    prompt_x,
    q_weight,
    kv_weight,
    prompt_blocks,
    finished,
    placement,
    page_table,
    row_lens,
    kv_cache,
    decode_x,
):
    n = lax.axis_size("tp")
    lq = q_weight.shape[1] // HD
    share = GQ // lq
    if share > 1:
        sets = [[k * share + i for i in range(share)] for k in range(n // share)]
        kv_weight = lax.all_gather(kv_weight, "tp", axis=1, tiled=True, axis_index_groups=sets)
    cache = kv_cache.reshape(-1, kv_cache.shape[2])
    dx = decode_x.reshape(-1, decode_x.shape[2])
    placement = placement.transpose(0, 2, 1)
    page_table = page_table.transpose(1, 0)
    ints = (prompt_blocks, finished, placement, page_table, row_lens)
    first, size = 512, 512
    q, kv, own = project_all(dx, prompt_x, q_weight, kv_weight, n, first, size)
    msgs = make_messages(ints, own, n)
    msgs = lax.all_to_all(msgs, "tp", split_axis=0, concat_axis=0, tiled=True)
    kv_other = lax.ppermute(kv, "pool", [(0, 1), (1, 0)])
    prompt_attn, made = prompt_attention(prompt_blocks, q, kv, 0)
    handed, scores, values, new = decode_scores(ints, cache, msgs, kv_other, own, made, n, lq)
    parts = lax.all_to_all(handed, "tp", split_axis=0, concat_axis=0, tiled=True)
    prompt_attn, _ = prompt_attention(prompt_blocks, q, kv, 1, prompt_attn, handed)
    decode_attn = decode_mix(scores, values, new, parts)
    return prompt_attn, decode_attn.transpose(1, 0, 2)


def solution(mesh):
    return jax.shard_map(
        local,
        mesh=mesh,
        in_specs=(
            P(("rep", "pool"), None),
            P(None, "tp"),
            P(None, "tp"),
            P("rep", None),
            P("rep", None),
            P("rep", None, None),
            P(("rep", "pool", "tp"), None),
            P(("rep", "pool", "tp")),
            P(("rep", "pool", "tp"), None, None),
            P(None, ("rep", "pool"), None),
        ),
        out_specs=(P(("rep", "pool"), "tp"), P(None, ("rep", "pool", "tp"), None)),
        check_vma=False,
    )
```

```python
import functools

import jax
import jax.numpy as jnp
from jax import lax
from jax.experimental import pallas as pl
from jax.experimental.pallas import tpu as pltpu
from jax.sharding import PartitionSpec as P

QH = 32
KVH = 8
GQ = QH // KVH
HD = 128
BLOCK_TOKENS = 128
PTOK = 2048
NPROMPT = 3
MOST_BLOCKS = 8
PAGES = 2
STEPS = 2
NBLK = 16
DEVICE_SLOTS = 6
ROWS_DEV = 3
GROUP_ROWS = 8
KEY_VALUE_COLUMNS = 2048
SCALE = HD ** (-0.5)
MASKED = -1e30
PIECES = 5
STRIPS = 4
MIX_STRIPS = 4
WIDE = 4096
LOG2E = 1.4426950408889634
AHEAD = 2
MIB = 1 << 20
VMEM = pltpu.VMEM
SMEM = pltpu.SMEM


def dot(a, b):
    return jnp.dot(a, b, preferred_element_type=jnp.float32)


def dot_t(a, b):
    return lax.dot_general(a, b, (((1,), (1,)), ((), ())), preferred_element_type=jnp.float32)


def iota(shape, axis):
    return lax.broadcasted_iota(jnp.int32, shape, axis)


def row_of(rs):
    return jnp.where(rs >= 2 * ROWS_DEV, ROWS_DEV, jnp.where(rs >= ROWS_DEV, rs - ROWS_DEV, rs))


def block_of_pages(counts, done, placed, table):
    me = lax.axis_index("tp")
    other = 1 - lax.axis_index("pool")
    first_end = counts[other, 0]
    second_end = first_end + counts[other, 1]
    found = [[jnp.int32(-1)] * PAGES for _ in range(ROWS_DEV)]
    for b in range(NBLK):
        live = jnp.where(
            b < first_end, done[other, 0], jnp.where(b < second_end, done[other, 1], done[other, 2])
        )
        slot = jnp.where((live > 0) & (placed[other, 0, b] == me), placed[other, 1, b], -1)
        for r in range(ROWS_DEV):
            for p in range(PAGES):
                found[r][p] = jnp.where(slot == table[p, r], b, found[r][p])
    return found


def by_row(r, values, rest):
    out = jnp.full(r.shape, rest, jnp.int32)
    for k in range(ROWS_DEV):
        out = jnp.where(r == k, values[k], out)
    return out


def project(n, lq, first, size, *refs):
    counts, done, placed, table, lens, dx_hbm, x_hbm, wq_hbm, wkv_hbm = refs[:9]
    q_hbm, kv_hbm, qh_ref, msg_ref = refs[9:13]
    x0, xs, w, q_out, kv_out, x_sems, w_sems, out_sems = refs[13:]
    depth = w.shape[0]
    count = xs.shape[0]
    cq = lq * HD
    piece = depth // PIECES
    own_rows = dx_hbm.shape[0]
    step = pl.program_id(0)

    def piece_copies(c):
        part = pl.ds(c * piece, piece)
        return [
            pltpu.make_async_copy(x_hbm.at[pl.ds(0, first), part], x0.at[pl.ds(0, first), part], w_sems.at[0, c]),
            pltpu.make_async_copy(dx_hbm.at[:, part], x0.at[pl.ds(first, own_rows), part], w_sems.at[1, c]),
            pltpu.make_async_copy(wq_hbm.at[part], w.at[part, pl.ds(0, cq)], w_sems.at[2, c]),
            pltpu.make_async_copy(wkv_hbm.at[part], w.at[part, pl.ds(cq, 2 * HD)], w_sems.at[3, c]),
        ]

    def x_copies(k):
        strip = size // STRIPS
        copies = []
        for i in range(STRIPS):
            rows = pl.ds(pl.multiple_of(first + k * size + i * strip, 16), strip)
            copies.append(
                pltpu.make_async_copy(x_hbm.at[rows], xs.at[k, pl.ds(i * strip, strip)], x_sems.at[k, i])
            )
        return copies

    def out_copies(k):
        if isinstance(k, int):
            rows = pl.ds(0, first)
        else:
            rows = pl.ds(pl.multiple_of(first + (k - 1) * size, 64), size)
        return [
            pltpu.make_async_copy(q_out.at[rows], q_hbm.at[rows], out_sems.at[0, k]),
            pltpu.make_async_copy(kv_out.at[rows], kv_hbm.at[rows], out_sems.at[1, k]),
        ]

    def keep(total, rows):
        q_out[rows, :] = total[:, :cq].astype(jnp.bfloat16)
        kv_out[rows, :] = total[:, cq:].astype(jnp.bfloat16)

    @pl.when(step == 0)
    def _():
        for c in range(AHEAD):
            for copy in piece_copies(c):
                copy.start()
        total = 0.0
        for c in range(PIECES):
            for copy in piece_copies(c):
                copy.wait()
            if c + AHEAD < PIECES:
                for copy in piece_copies(c + AHEAD):
                    copy.start()
            if c + AHEAD >= PIECES:
                for copy in x_copies(c + AHEAD - PIECES):
                    copy.start()
            part = slice(c * piece, (c + 1) * piece)
            total += dot(x0[:, part], w[part, :])
        keep(total[:first], pl.ds(0, first))
        for copy in out_copies(0):
            copy.start()
        shape = (n * GROUP_ROWS, own_rows)
        to, fro = iota(shape, 0), iota(shape, 1)
        owner, rs = to // GROUP_ROWS, to % GROUP_ROWS
        wanted = owner * ROWS_DEV + row_of(rs) + jnp.where(rs >= ROWS_DEV, ROWS_DEV * n, 0)
        pick = ((fro == wanted) & (rs < STEPS * ROWS_DEV)).astype(jnp.float32).astype(jnp.bfloat16)
        own = dot(pick, total[first:].astype(jnp.bfloat16))
        for h in range(lq):
            part = slice(h * n * GROUP_ROWS, (h + 1) * n * GROUP_ROWS)
            qh_ref[part, :] = own[:, h * HD : (h + 1) * HD].astype(jnp.bfloat16)
        found = block_of_pages(counts, done, placed, table)
        lane = iota((n * GROUP_ROWS, HD), 1)
        r = row_of(lane % GROUP_ROWS)
        kind = lane // GROUP_ROWS
        facts = jnp.where(
            kind == 0,
            by_row(r, [found[i][0] for i in range(ROWS_DEV)], -1),
            jnp.where(
                kind == 1,
                by_row(r, [found[i][1] for i in range(ROWS_DEV)], -1),
                by_row(r, [lens[i] for i in range(ROWS_DEV)], 0),
            ),
        ).astype(jnp.float32)
        sixth = iota((n * GROUP_ROWS, HD), 0) % GROUP_ROWS == 6
        msg_ref[:, :HD] = jnp.where(sixth, facts, own[:, :HD]).astype(jnp.bfloat16)
        msg_ref[:, HD:] = own[:, HD:].astype(jnp.bfloat16)

    @pl.when((step > 0) & (step + AHEAD <= count))
    def _():
        for copy in x_copies(step + AHEAD - 1):
            copy.start()

    @pl.when(step > 0)
    def _():
        for copy in x_copies(step - 1):
            copy.wait()
        keep(dot(xs[step - 1], w[...]), pl.ds(pl.multiple_of(first + (step - 1) * size, 64), size))
        for copy in out_copies(step):
            copy.start()

    @pl.when(step == count)
    def _():
        for copy in out_copies(0):
            copy.wait()
        for k in range(1, count + 1):
            for copy in out_copies(jnp.int32(k)):
                copy.wait()


def project_all(ints, dx, x, wq, wkv, n, first, size):
    rows, depth = x.shape
    cq, ckv = wq.shape[1], wkv.shape[1]
    lq = cq // HD
    count = (rows - first) // size
    smem, vmem = pl.BlockSpec(memory_space=SMEM), pl.BlockSpec(memory_space=VMEM)
    hbm = pl.BlockSpec(memory_space=pl.ANY)
    return pl.pallas_call(
        functools.partial(project, n, lq, first, size),
        grid=(1 + count,),
        in_specs=[smem] * 5 + [hbm] * 4,
        out_specs=[hbm, hbm, vmem, vmem],
        out_shape=[
            jax.ShapeDtypeStruct((rows, cq), jnp.bfloat16),
            jax.ShapeDtypeStruct((rows, ckv), jnp.bfloat16),
            jax.ShapeDtypeStruct((lq * n * GROUP_ROWS, HD), jnp.bfloat16),
            jax.ShapeDtypeStruct((n * GROUP_ROWS, cq + ckv), jnp.bfloat16),
        ],
        scratch_shapes=[
            VMEM((first + dx.shape[0], depth), jnp.bfloat16),
            VMEM((count, size, depth), jnp.bfloat16),
            VMEM((depth, cq + ckv), jnp.bfloat16),
            VMEM((rows, cq), jnp.bfloat16),
            VMEM((rows, ckv), jnp.bfloat16),
            pltpu.SemaphoreType.DMA((count, STRIPS)),
            pltpu.SemaphoreType.DMA((4, PIECES)),
            pltpu.SemaphoreType.DMA((2, count + 1)),
        ],
        compiler_params=pltpu.CompilerParams(vmem_limit_bytes=62 * MIB),
        cost_estimate=pl.CostEstimate(
            flops=2 * rows * depth * (cq + ckv),
            bytes_accessed=2 * (rows + cq + ckv) * depth + 2 * rows * (cq + ckv),
            transcendentals=0,
        ),
        name="project",
    )(*ints, dx, x, wq, wkv)


def attend_prompt(lq, half, counts, q_hbm, kv_hbm, *refs):
    o_hbm, qs, kvs, outs, sems = refs[-5:]
    group = lax.axis_index("pool")
    c0, c1 = counts[group, 0], counts[group, 1]
    big = jnp.where(c0 == MOST_BLOCKS, 0, jnp.where(c1 == MOST_BLOCKS, c0, c0 + c1))
    cut = jnp.where(c0 == MOST_BLOCKS, c1, c0)
    loads, stores = [], []
    strip, early = (4, 3) if half == 0 else (1, 5)
    for j in range(0, MOST_BLOCKS, strip):
        block = big + j if half == 0 else j + jnp.where(j >= big, MOST_BLOCKS, 0)
        rows = pl.ds(pl.multiple_of(block * BLOCK_TOKENS, BLOCK_TOKENS), strip * BLOCK_TOKENS)
        here = pl.ds(j * BLOCK_TOKENS, strip * BLOCK_TOKENS)
        loads.append(pltpu.make_async_copy(kv_hbm.at[rows], kvs.at[here], sems.at[0, j]))
        loads.append(pltpu.make_async_copy(q_hbm.at[rows], qs.at[here], sems.at[1, j]))
        stores.append(pltpu.make_async_copy(outs.at[here], o_hbm.at[rows], sems.at[2, j]))
    for copy in loads:
        copy.start()
    near = len(loads) // 2
    for copy in loads[:near]:
        copy.wait()
    shape = (BLOCK_TOKENS, lq * BLOCK_TOKENS)
    causal = iota(shape, 0) <= iota(shape, 1) % BLOCK_TOKENS
    tokens = MOST_BLOCKS * BLOCK_TOKENS
    flipped = kvs[: tokens // 2, HD:].T

    def scores_of(j):
        q = qs[j * BLOCK_TOKENS : (j + 1) * BLOCK_TOKENS, :]
        q = jnp.concatenate([q[:, h * HD : (h + 1) * HD] for h in range(lq)], axis=0)
        return dot_t(kvs[: (j + 1) * BLOCK_TOKENS, :HD], q)

    scores = scores_of(0)
    for j in range(MOST_BLOCKS):
        if j + 1 == MOST_BLOCKS // 2:
            for copy in loads[near:]:
                copy.wait()
            flipped = jnp.concatenate([flipped, kvs[tokens // 2 :, HD:].T], axis=1)
        later = scores_of(j + 1) if j + 1 < MOST_BLOCKS else None
        weights = []
        for h in range(lq):
            cols = slice(h * BLOCK_TOKENS, (h + 1) * BLOCK_TOKENS)
            tiles = []
            for i in range(j + 1):
                tile = scores[i * BLOCK_TOKENS : (i + 1) * BLOCK_TOKENS, cols]
                if i == j:
                    tile = jnp.where(causal[:, cols], tile, MASKED)
                elif half == 1:
                    tile = tile + jnp.where((i < cut) & (cut <= j), MASKED, 0.0)
                tiles.append(tile)
            peak = jnp.max(functools.reduce(jnp.maximum, tiles), axis=0, keepdims=True)
            raised = [jnp.exp2((tile - peak) * (SCALE * LOG2E)) for tile in tiles]
            inverse = 1.0 / jnp.sum(functools.reduce(jnp.add, raised), axis=0, keepdims=True)
            weights.append(jnp.concatenate([(t * inverse).astype(jnp.bfloat16) for t in raised], axis=0))
        mixed = dot(flipped[:, : (j + 1) * BLOCK_TOKENS], jnp.concatenate(weights, axis=1))
        mixed = mixed.astype(jnp.bfloat16)
        for h in range(lq):
            part = mixed[:, h * BLOCK_TOKENS : (h + 1) * BLOCK_TOKENS].T
            outs[j * BLOCK_TOKENS : (j + 1) * BLOCK_TOKENS, h * HD : (h + 1) * HD] = part
        scores = later
        if j == early:
            for copy in stores[: (j + 1) // strip]:
                copy.start()
    for copy in stores[(early + 1) // strip :]:
        copy.start()
    for copy in stores:
        copy.wait()


def prompt_attention(counts, q, kv, half, so_far=None):
    rows, cq = q.shape
    hbm = pl.BlockSpec(memory_space=pl.ANY)
    more = () if so_far is None else (so_far,)
    tokens = MOST_BLOCKS * BLOCK_TOKENS
    return pl.pallas_call(
        functools.partial(attend_prompt, cq // HD, half),
        in_specs=[pl.BlockSpec(memory_space=SMEM), hbm, hbm] + [hbm] * len(more),
        out_specs=hbm,
        out_shape=jax.ShapeDtypeStruct((rows, cq), jnp.bfloat16),
        scratch_shapes=[
            VMEM((tokens, cq), jnp.bfloat16),
            VMEM((tokens, 2 * HD), jnp.bfloat16),
            VMEM((tokens, cq), jnp.bfloat16),
            pltpu.SemaphoreType.DMA((3, MOST_BLOCKS)),
        ],
        input_output_aliases={3: 0} if more else {},
        compiler_params=pltpu.CompilerParams(vmem_limit_bytes=62 * MIB),
        cost_estimate=pl.CostEstimate(flops=2 * rows * rows * cq, bytes_accessed=4 * rows * cq, transcendentals=rows * rows // 2),
        name="long_prompt" if half == 0 else "short_prompts",
    )(counts, q, kv, *more)


def row_head(n, lq, h, hh):
    at = h * GQ + hh
    return at // lq, at % lq


def handed_part(n, lq, kv_ref, q_ref, msg_ref, o_ref):
    rows = lq * n * GROUP_ROWS
    shape = (rows, HD)
    at_row, lane = iota(shape, 0), iota(shape, 1)
    rs = at_row % GROUP_ROWS
    facts = msg_ref[:, :HD].astype(jnp.float32).reshape(n, GROUP_ROWS, HD)[:, 6:7, :]
    facts = jnp.broadcast_to(facts, (n, GROUP_ROWS, HD)).reshape(n * GROUP_ROWS, HD)
    facts = jnp.concatenate([facts] * lq, axis=0)

    def column(kind):
        return jnp.sum(jnp.where(lane == kind * GROUP_ROWS + rs, facts, 0.0), axis=1, keepdims=True)

    first_block, second_block, length = [column(kind) for kind in range(3)]
    scores = dot_t(q_ref[...], kv_ref[:, :HD]) * SCALE
    lane_f = lane.astype(jnp.float32)
    parts = []
    for b in range(NBLK):
        limit = jnp.where(
            first_block == b, length, jnp.where(second_block == b, length - BLOCK_TOKENS, 0.0)
        )
        part = scores[:, b * BLOCK_TOKENS : (b + 1) * BLOCK_TOKENS]
        parts.append(jnp.where(lane_f < limit, part, MASKED))
    scores = jnp.concatenate(parts, axis=1)
    top = jnp.max(scores, axis=1, keepdims=True)
    raised = jnp.exp(scores - top)
    total = jnp.sum(raised, axis=1, keepdims=True)
    near = raised.astype(jnp.bfloat16)
    rest = (raised - near.astype(jnp.float32)).astype(jnp.bfloat16)
    values = kv_ref[:, HD:]
    mixed = (dot(near, values) + dot(rest, values)).reshape(lq * n, GROUP_ROWS, HD)

    def line(col):
        spread = jnp.where(lane == rs, col, 0.0).reshape(lq * n, GROUP_ROWS, HD)
        return jnp.sum(spread, axis=1, keepdims=True)

    rs3 = rs.reshape(lq * n, GROUP_ROWS, HD)
    mixed = jnp.where(rs3 == 6, line(top), jnp.where(rs3 == 7, line(total), mixed))
    for h in range(lq):
        o_ref[:, h * GROUP_ROWS : (h + 1) * GROUP_ROWS, :] = mixed[h * n : (h + 1) * n]


def exchange_part(n, lq, *refs):
    counts, done, placed, table, lens, cache_hbm, msgs, kv_ref, q_ref, _ = refs[:10]
    handed_ref, s_hbm, v_ref, new_ref, _, s_ref, cache, sems, slot_row, slot_limit = refs[10:]
    loads = []
    for slot in range(DEVICE_SLOTS):
        part = pl.ds(slot * BLOCK_TOKENS, BLOCK_TOKENS)
        loads.append(pltpu.make_async_copy(cache_hbm.at[part], cache.at[part], sems.at[slot]))
    for load in loads:
        load.start()
    handed_part(n, lq, kv_ref, q_ref, msgs, handed_ref)
    held = msgs[...].astype(jnp.float32)
    found = block_of_pages(counts, done, placed, table)
    for r in range(ROWS_DEV):
        for p in range(PAGES):
            slot_row[table[p, r]] = jnp.int32(r)
            slot_limit[table[p, r]] = jnp.where(found[r][p] < 0, lens[r] - p * BLOCK_TOKENS, 0)
    cq = lq * HD
    rows = QH * GROUP_ROWS
    span = GQ * GROUP_ROWS
    queries, keys = [], []
    for h in range(KVH):
        for hh in range(GQ):
            t, at = row_head(n, lq, h, hh)
            queries.append(held[t * GROUP_ROWS : (t + 1) * GROUP_ROWS, at * HD : (at + 1) * HD])
        t, _ = row_head(n, lq, h, 0)
        keys += [held[t * GROUP_ROWS : (t + 1) * GROUP_ROWS, cq : cq + HD]] * GQ
        new_ref[h * GROUP_ROWS : (h + 1) * GROUP_ROWS, :] = held[
            t * GROUP_ROWS : (t + 1) * GROUP_ROWS, cq + HD : cq + 2 * HD
        ]
    queries = jnp.concatenate(queries, axis=0)
    earlier = jnp.concatenate([pltpu.roll(key, ROWS_DEV, 0) for key in keys], axis=0)
    keys = jnp.concatenate(keys, axis=0)
    at_row, lane = iota((rows, HD), 0), iota((rows, HD), 1)
    rs = at_row % GROUP_ROWS
    r = row_of(rs)
    rounded = queries.astype(jnp.bfloat16)
    now = jnp.sum(queries * keys, axis=1, keepdims=True) * SCALE
    before = jnp.sum(queries * earlier, axis=1, keepdims=True) * SCALE
    second = (rs >= ROWS_DEV) & (rs < STEPS * ROWS_DEV)
    before = jnp.where(second, before, MASKED)
    for load in loads:
        load.wait()
    scores = jnp.concatenate(
        [dot_t(rounded[h * span : (h + 1) * span], cache[:, 2 * h * HD : (2 * h + 1) * HD]) for h in range(KVH)],
        axis=0,
    )
    for slot in range(DEVICE_SLOTS):
        part = slice(slot * BLOCK_TOKENS, (slot + 1) * BLOCK_TOKENS)
        usable = (r == slot_row[slot]) & (lane < slot_limit[slot])
        s_ref[:, part] = jnp.where(usable, scores[:, part] * SCALE, MASKED)
    last = jnp.where(lane == 0, now, jnp.where(lane == 1, before, MASKED))
    s_ref[:, DEVICE_SLOTS * BLOCK_TOKENS :] = last
    save = pltpu.make_async_copy(s_ref, s_hbm.at[:, pl.ds(0, s_ref.shape[1])], sems.at[DEVICE_SLOTS])
    save.start()
    for h in range(KVH):
        v_ref[:, h * HD : (h + 1) * HD] = cache[:, (2 * h + 1) * HD : (2 * h + 2) * HD]
    save.wait()


def decode_scores(ints, cache, msgs, kv, q_own, prompt_attn, n, lq):
    smem, vmem, hbm = [pl.BlockSpec(memory_space=space) for space in (SMEM, VMEM, pl.ANY)]
    rows = QH * GROUP_ROWS
    return pl.pallas_call(
        functools.partial(exchange_part, n, lq),
        in_specs=[smem] * 5 + [hbm, vmem, vmem, vmem, hbm],
        out_specs=[vmem, hbm, vmem, vmem, hbm],
        out_shape=[
            jax.ShapeDtypeStruct((n, lq * GROUP_ROWS, HD), jnp.float32),
            jax.ShapeDtypeStruct((rows, WIDE), jnp.float32),
            jax.ShapeDtypeStruct((cache.shape[0], KVH * HD), jnp.bfloat16),
            jax.ShapeDtypeStruct((KVH * GROUP_ROWS, HD), jnp.float32),
            jax.ShapeDtypeStruct(prompt_attn.shape, prompt_attn.dtype),
        ],
        input_output_aliases={9: 4},
        scratch_shapes=[
            VMEM((rows, (DEVICE_SLOTS + 1) * BLOCK_TOKENS), jnp.float32),
            VMEM(cache.shape, jnp.bfloat16),
            pltpu.SemaphoreType.DMA((DEVICE_SLOTS + 1,)),
            SMEM((DEVICE_SLOTS,), jnp.int32),
            SMEM((DEVICE_SLOTS,), jnp.int32),
        ],
        compiler_params=pltpu.CompilerParams(vmem_limit_bytes=103 * MIB // 2),
        cost_estimate=pl.CostEstimate(flops=2 * rows * HD * 768, bytes_accessed=4 * MIB, transcendentals=0),
        name="decode_scores",
    )(*ints, cache, msgs, kv, q_own, prompt_attn)


def owner_mix(s_hbm, v_hbm, new_ref, handed, o_ref, s_ref, v_ref, sems):
    loads = []
    for k, (source, to) in enumerate(((s_hbm, s_ref), (v_hbm, v_ref))):
        strip = to.shape[0] // MIX_STRIPS
        for i in range(MIX_STRIPS):
            part, cols = pl.ds(i * strip, strip), pl.ds(0, to.shape[1])
            loads.append(pltpu.make_async_copy(source.at[part, cols], to.at[part], sems.at[k, i]))
    for load in loads:
        load.start()
    groups = QH
    rows = groups * GROUP_ROWS
    span = GQ * GROUP_ROWS
    mixed = handed[...].reshape(groups, GROUP_ROWS, HD)
    shape = (groups, GROUP_ROWS, HD)
    mine = iota(shape, 1) == iota(shape, 2)

    def column(at):
        line = jnp.broadcast_to(mixed[:, at : at + 1, :], shape)
        return jnp.sum(jnp.where(mine, line, 0.0), axis=2, keepdims=True).reshape(rows, 1)

    other_peak, other_total = column(6), column(7)
    for load in loads[:MIX_STRIPS]:
        load.wait()
    scores = s_ref[...]
    peak = jnp.maximum(jnp.max(scores, axis=1, keepdims=True), other_peak)
    raised = jnp.exp(scores - peak)
    other = jnp.exp(other_peak - peak)
    inverse = 1.0 / (jnp.sum(raised, axis=1, keepdims=True) + other * other_total)
    weights = (raised * inverse).astype(jnp.bfloat16)
    old = DEVICE_SLOTS * BLOCK_TOKENS
    fresh = weights[:, old:].astype(jnp.float32)
    now, before = fresh[:, 0:1], fresh[:, 1:2]
    mixed = mixed.reshape(rows, HD) * (other * inverse)
    for load in loads[MIX_STRIPS:]:
        load.wait()
    out = []
    for h in range(KVH):
        part = slice(h * span, (h + 1) * span)
        own = mixed[part] + dot(weights[part, :old], v_ref[:, h * HD : (h + 1) * HD])
        value = new_ref[h * GROUP_ROWS : (h + 1) * GROUP_ROWS, :]
        last = pltpu.roll(value, ROWS_DEV, 0)
        for hh in range(GQ):
            some = slice(h * span + hh * GROUP_ROWS, h * span + (hh + 1) * GROUP_ROWS)
            line = own[hh * GROUP_ROWS : (hh + 1) * GROUP_ROWS]
            out.append(line + now[some] * value + before[some] * last)
    out = jnp.concatenate(out, axis=1)
    for k in range(ROWS_DEV):
        steps = [out[s * ROWS_DEV + k : s * ROWS_DEV + k + 1] for s in range(STEPS)]
        o_ref[k] = jnp.concatenate(steps, axis=0).astype(jnp.bfloat16)


def decode_mix(scores, values, new, parts):
    vmem, hbm = pl.BlockSpec(memory_space=VMEM), pl.BlockSpec(memory_space=pl.ANY)
    rows = QH * GROUP_ROWS
    return pl.pallas_call(
        owner_mix,
        in_specs=[hbm, hbm, vmem, vmem],
        out_specs=vmem,
        out_shape=jax.ShapeDtypeStruct((ROWS_DEV, STEPS, QH * HD), jnp.bfloat16),
        scratch_shapes=[
            VMEM((rows, (DEVICE_SLOTS + 1) * BLOCK_TOKENS), jnp.float32),
            VMEM(values.shape, values.dtype),
            pltpu.SemaphoreType.DMA((2, MIX_STRIPS)),
        ],
        compiler_params=pltpu.CompilerParams(vmem_limit_bytes=533 * MIB // 10),
        cost_estimate=pl.CostEstimate(flops=2 * rows * HD * 768, bytes_accessed=4 * MIB, transcendentals=rows * 768),
        name="decode_mix",
    )(scores, values, new, parts)


def local(
    prompt_x,
    q_weight,
    kv_weight,
    prompt_blocks,
    finished,
    placement,
    page_table,
    row_lens,
    kv_cache,
    decode_x,
):
    n = lax.axis_size("tp")
    lq = q_weight.shape[1] // HD
    share = GQ // lq
    if share > 1:
        sets = [[k * share + i for i in range(share)] for k in range(n // share)]
        kv_weight = lax.all_gather(kv_weight, "tp", axis=1, tiled=True, axis_index_groups=sets)
    cache = kv_cache.reshape(-1, kv_cache.shape[2])
    dx = decode_x.reshape(-1, decode_x.shape[2])
    placement = placement.transpose(0, 2, 1)
    page_table = page_table.transpose(1, 0)
    ints = (prompt_blocks, finished, placement, page_table, row_lens)
    first, size = 512, 512
    q, kv, q_own, msgs = project_all(ints, dx, prompt_x, q_weight, kv_weight, n, first, size)
    msgs = lax.all_to_all(msgs, "tp", split_axis=0, concat_axis=0, tiled=True)
    kv_other = lax.ppermute(kv, "pool", [(0, 1), (1, 0)])
    prompt_attn = prompt_attention(prompt_blocks, q, kv, 0)
    handed, scores, values, new, prompt_attn = decode_scores(
        ints, cache, msgs, kv_other, q_own, prompt_attn, n, lq
    )
    parts = lax.all_to_all(handed, "tp", split_axis=0, concat_axis=0, tiled=True)
    prompt_attn = prompt_attention(prompt_blocks, q, kv, 1, prompt_attn)
    decode_attn = decode_mix(scores, values, new, parts)
    return prompt_attn, decode_attn.transpose(1, 0, 2)


def solution(mesh):
    return jax.shard_map(
        local,
        mesh=mesh,
        in_specs=(
            P(("rep", "pool"), None),
            P(None, "tp"),
            P(None, "tp"),
            P("rep", None),
            P("rep", None),
            P("rep", None, None),
            P(("rep", "pool", "tp"), None),
            P(("rep", "pool", "tp")),
            P(("rep", "pool", "tp"), None, None),
            P(None, ("rep", "pool"), None),
        ),
        out_specs=(P(("rep", "pool"), "tp"), P(None, ("rep", "pool", "tp"), None)),
        check_vma=False,
    )
```

```python
import functools

import jax
import jax.numpy as jnp
from jax import lax
from jax.experimental import pallas as pl
from jax.experimental.pallas import tpu as pltpu
from jax.sharding import PartitionSpec as P

QH = 32
KVH = 8
GQ = QH // KVH
HD = 128
BLOCK_TOKENS = 128
PTOK = 2048
NPROMPT = 3
MOST_BLOCKS = 8
PAGES = 2
STEPS = 2
NBLK = 16
DEVICE_SLOTS = 6
ROWS_DEV = 3
GROUP_ROWS = 8
KEY_VALUE_COLUMNS = 2048
SCALE = HD ** (-0.5)
MASKED = -1e30
PIECES = 5
STRIPS = 4
LOG2E = 1.4426950408889634
AHEAD = 2
MIB = 1 << 20
VMEM = pltpu.VMEM
SMEM = pltpu.SMEM


def dot(a, b):
    return jnp.dot(a, b, preferred_element_type=jnp.float32)


def dot_t(a, b):
    return lax.dot_general(a, b, (((1,), (1,)), ((), ())), preferred_element_type=jnp.float32)


def iota(shape, axis):
    return lax.broadcasted_iota(jnp.int32, shape, axis)


def row_of(rs):
    return jnp.where(rs >= 2 * ROWS_DEV, ROWS_DEV, jnp.where(rs >= ROWS_DEV, rs - ROWS_DEV, rs))


def block_of_pages(counts, done, placed, table):
    me = lax.axis_index("tp")
    other = 1 - lax.axis_index("pool")
    first_end = counts[other, 0]
    second_end = first_end + counts[other, 1]
    found = [[jnp.int32(-1)] * PAGES for _ in range(ROWS_DEV)]
    for b in range(NBLK):
        live = jnp.where(
            b < first_end, done[other, 0], jnp.where(b < second_end, done[other, 1], done[other, 2])
        )
        slot = jnp.where((live > 0) & (placed[other, 0, b] == me), placed[other, 1, b], -1)
        for r in range(ROWS_DEV):
            for p in range(PAGES):
                found[r][p] = jnp.where(slot == table[p, r], b, found[r][p])
    return found


def by_row(r, values, rest):
    out = jnp.full(r.shape, rest, jnp.int32)
    for k in range(ROWS_DEV):
        out = jnp.where(r == k, values[k], out)
    return out


def int_scratch(ints):
    return [SMEM(x.shape, jnp.int32) for x in ints] + [pltpu.SemaphoreType.DMA((len(ints),))]


def int_copies(sources, targets, sems):
    return [pltpu.make_async_copy(a, b, sems.at[i]) for i, (a, b) in enumerate(zip(sources, targets))]


def project(n, lq, first, size, *refs):
    dx_hbm, x_hbm, wq_hbm, wkv_hbm = refs[5:9]
    q_hbm, kv_hbm, own_ref, msg_ref = refs[9:13]
    x0, xs, w, q_out, kv_out, x_sems, w_sems, out_sems = refs[13:21]
    counts, done, placed, table, lens, int_sems = refs[21:]
    ints = int_copies(refs[:5], refs[21:26], int_sems)
    depth = w.shape[0]
    count = xs.shape[0]
    cq = lq * HD
    piece = depth // PIECES
    own_rows = dx_hbm.shape[0]
    step = pl.program_id(0)

    def piece_copies(c):
        part = pl.ds(c * piece, piece)
        return [
            pltpu.make_async_copy(x_hbm.at[pl.ds(0, first), part], x0.at[pl.ds(0, first), part], w_sems.at[0, c]),
            pltpu.make_async_copy(dx_hbm.at[:, part], x0.at[pl.ds(first, own_rows), part], w_sems.at[1, c]),
            pltpu.make_async_copy(wq_hbm.at[part], w.at[part, pl.ds(0, cq)], w_sems.at[2, c]),
            pltpu.make_async_copy(wkv_hbm.at[part], w.at[part, pl.ds(cq, 2 * HD)], w_sems.at[3, c]),
        ]

    def x_copies(k):
        strip = size // STRIPS
        copies = []
        for i in range(STRIPS):
            rows = pl.ds(pl.multiple_of(first + k * size + i * strip, 16), strip)
            copies.append(
                pltpu.make_async_copy(x_hbm.at[rows], xs.at[k, pl.ds(i * strip, strip)], x_sems.at[k, i])
            )
        return copies

    def out_copies(k):
        if isinstance(k, int):
            rows = pl.ds(0, first)
        else:
            rows = pl.ds(pl.multiple_of(first + (k - 1) * size, 64), size)
        return [
            pltpu.make_async_copy(q_out.at[rows], q_hbm.at[rows], out_sems.at[0, k]),
            pltpu.make_async_copy(kv_out.at[rows], kv_hbm.at[rows], out_sems.at[1, k]),
        ]

    def keep(total, rows):
        q_out[rows, :] = total[:, :cq].astype(jnp.bfloat16)
        kv_out[rows, :] = total[:, cq:].astype(jnp.bfloat16)

    @pl.when(step == 0)
    def _():
        for c in range(AHEAD):
            for copy in piece_copies(c):
                copy.start()
        for copy in ints:
            copy.start()
        total = 0.0
        for c in range(PIECES):
            for copy in piece_copies(c):
                copy.wait()
            if c + AHEAD < PIECES:
                for copy in piece_copies(c + AHEAD):
                    copy.start()
            if c + AHEAD >= PIECES:
                for copy in x_copies(c + AHEAD - PIECES):
                    copy.start()
            part = slice(c * piece, (c + 1) * piece)
            total += dot(x0[:, part], w[part, :])
        keep(total[:first], pl.ds(0, first))
        for copy in out_copies(0):
            copy.start()
        shape = (n * GROUP_ROWS, own_rows)
        to, fro = iota(shape, 0), iota(shape, 1)
        owner, rs = to // GROUP_ROWS, to % GROUP_ROWS
        wanted = owner * ROWS_DEV + row_of(rs) + jnp.where(rs >= ROWS_DEV, ROWS_DEV * n, 0)
        pick = ((fro == wanted) & (rs < STEPS * ROWS_DEV)).astype(jnp.float32).astype(jnp.bfloat16)
        own = dot(pick, total[first:].astype(jnp.bfloat16))
        own_ref[...] = own.astype(jnp.bfloat16)
        for copy in ints:
            copy.wait()
        found = block_of_pages(counts, done, placed, table)
        lane = iota((n * GROUP_ROWS, HD), 1)
        r = row_of(lane % GROUP_ROWS)
        kind = lane // GROUP_ROWS
        facts = jnp.where(
            kind == 0,
            by_row(r, [found[i][0] for i in range(ROWS_DEV)], -1),
            jnp.where(
                kind == 1,
                by_row(r, [found[i][1] for i in range(ROWS_DEV)], -1),
                by_row(r, [lens[i] for i in range(ROWS_DEV)], 0),
            ),
        ).astype(jnp.float32)
        sixth = iota((n * GROUP_ROWS, HD), 0) % GROUP_ROWS == 6
        msg_ref[:, :HD] = jnp.where(sixth, facts, own[:, :HD]).astype(jnp.bfloat16)
        msg_ref[:, HD:] = own[:, HD:].astype(jnp.bfloat16)

    @pl.when((step > 0) & (step + AHEAD <= count))
    def _():
        for copy in x_copies(step + AHEAD - 1):
            copy.start()

    @pl.when(step > 0)
    def _():
        for copy in x_copies(step - 1):
            copy.wait()
        keep(dot(xs[step - 1], w[...]), pl.ds(pl.multiple_of(first + (step - 1) * size, 64), size))
        for copy in out_copies(step):
            copy.start()

    @pl.when(step == count)
    def _():
        for copy in out_copies(0):
            copy.wait()
        for k in range(1, count + 1):
            for copy in out_copies(jnp.int32(k)):
                copy.wait()


def project_all(ints, dx, x, wq, wkv, n, first, size):
    rows, depth = x.shape
    cq, ckv = wq.shape[1], wkv.shape[1]
    lq = cq // HD
    count = (rows - first) // size
    vmem, hbm = pl.BlockSpec(memory_space=VMEM), pl.BlockSpec(memory_space=pl.ANY)
    return pl.pallas_call(
        functools.partial(project, n, lq, first, size),
        grid=(1 + count,),
        in_specs=[hbm] * 9,
        out_specs=[hbm, hbm, vmem, vmem],
        out_shape=[
            jax.ShapeDtypeStruct((rows, cq), jnp.bfloat16),
            jax.ShapeDtypeStruct((rows, ckv), jnp.bfloat16),
            jax.ShapeDtypeStruct((n * GROUP_ROWS, cq + ckv), jnp.bfloat16),
            jax.ShapeDtypeStruct((n * GROUP_ROWS, cq + ckv), jnp.bfloat16),
        ],
        scratch_shapes=[
            VMEM((first + dx.shape[0], depth), jnp.bfloat16),
            VMEM((count, size, depth), jnp.bfloat16),
            VMEM((depth, cq + ckv), jnp.bfloat16),
            VMEM((rows, cq), jnp.bfloat16),
            VMEM((rows, ckv), jnp.bfloat16),
            pltpu.SemaphoreType.DMA((count, STRIPS)),
            pltpu.SemaphoreType.DMA((4, PIECES)),
            pltpu.SemaphoreType.DMA((2, count + 1)),
        ]
        + int_scratch(ints),
        compiler_params=pltpu.CompilerParams(vmem_limit_bytes=62 * MIB),
        cost_estimate=pl.CostEstimate(
            flops=2 * rows * depth * (cq + ckv),
            bytes_accessed=2 * (rows + cq + ckv) * depth + 2 * rows * (cq + ckv),
            transcendentals=0,
        ),
        name="project",
    )(*ints, dx, x, wq, wkv)


def attend_prompt(lq, half, counts, q_hbm, kv_hbm, *refs):
    o_hbm, qs, kvs, outs, sems = refs[-5:]
    group = lax.axis_index("pool")
    c0, c1 = counts[group, 0], counts[group, 1]
    big = jnp.where(c0 == MOST_BLOCKS, 0, jnp.where(c1 == MOST_BLOCKS, c0, c0 + c1))
    cut = jnp.where(c0 == MOST_BLOCKS, c1, c0)
    loads, stores = [], []
    strip, early = (4, 3) if half == 0 else (1, 5)
    for j in range(0, MOST_BLOCKS, strip):
        block = big + j if half == 0 else j + jnp.where(j >= big, MOST_BLOCKS, 0)
        rows = pl.ds(pl.multiple_of(block * BLOCK_TOKENS, BLOCK_TOKENS), strip * BLOCK_TOKENS)
        here = pl.ds(j * BLOCK_TOKENS, strip * BLOCK_TOKENS)
        loads.append(pltpu.make_async_copy(kv_hbm.at[rows], kvs.at[here], sems.at[0, j]))
        loads.append(pltpu.make_async_copy(q_hbm.at[rows], qs.at[here], sems.at[1, j]))
        stores.append(pltpu.make_async_copy(outs.at[here], o_hbm.at[rows], sems.at[2, j]))
    for copy in loads:
        copy.start()
    near = len(loads) // 2
    for copy in loads[:near]:
        copy.wait()
    shape = (BLOCK_TOKENS, lq * BLOCK_TOKENS)
    causal = iota(shape, 0) <= iota(shape, 1) % BLOCK_TOKENS
    tokens = MOST_BLOCKS * BLOCK_TOKENS
    flipped = kvs[: tokens // 2, HD:].T

    def scores_of(j):
        q = qs[j * BLOCK_TOKENS : (j + 1) * BLOCK_TOKENS, :]
        q = jnp.concatenate([q[:, h * HD : (h + 1) * HD] for h in range(lq)], axis=0)
        return dot_t(kvs[: (j + 1) * BLOCK_TOKENS, :HD], q)

    scores = scores_of(0)
    for j in range(MOST_BLOCKS):
        if j + 1 == MOST_BLOCKS // 2:
            for copy in loads[near:]:
                copy.wait()
            flipped = jnp.concatenate([flipped, kvs[tokens // 2 :, HD:].T], axis=1)
        later = scores_of(j + 1) if j + 1 < MOST_BLOCKS else None
        weights = []
        for h in range(lq):
            cols = slice(h * BLOCK_TOKENS, (h + 1) * BLOCK_TOKENS)
            tiles = []
            for i in range(j + 1):
                tile = scores[i * BLOCK_TOKENS : (i + 1) * BLOCK_TOKENS, cols]
                if i == j:
                    tile = jnp.where(causal[:, cols], tile, MASKED)
                elif half == 1:
                    tile = tile + jnp.where((i < cut) & (cut <= j), MASKED, 0.0)
                tiles.append(tile)
            peak = jnp.max(functools.reduce(jnp.maximum, tiles), axis=0, keepdims=True)
            raised = [jnp.exp2((tile - peak) * (SCALE * LOG2E)) for tile in tiles]
            inverse = 1.0 / jnp.sum(functools.reduce(jnp.add, raised), axis=0, keepdims=True)
            weights.append(jnp.concatenate([(t * inverse).astype(jnp.bfloat16) for t in raised], axis=0))
        mixed = dot(flipped[:, : (j + 1) * BLOCK_TOKENS], jnp.concatenate(weights, axis=1))
        mixed = mixed.astype(jnp.bfloat16)
        for h in range(lq):
            part = mixed[:, h * BLOCK_TOKENS : (h + 1) * BLOCK_TOKENS].T
            outs[j * BLOCK_TOKENS : (j + 1) * BLOCK_TOKENS, h * HD : (h + 1) * HD] = part
        scores = later
        if j == early:
            for copy in stores[: (j + 1) // strip]:
                copy.start()
    for copy in stores[(early + 1) // strip :]:
        copy.start()
    for copy in stores:
        copy.wait()


def prompt_attention(counts, q, kv, half, so_far=None):
    rows, cq = q.shape
    hbm = pl.BlockSpec(memory_space=pl.ANY)
    more = () if so_far is None else (so_far,)
    tokens = MOST_BLOCKS * BLOCK_TOKENS
    return pl.pallas_call(
        functools.partial(attend_prompt, cq // HD, half),
        in_specs=[pl.BlockSpec(memory_space=SMEM), hbm, hbm] + [hbm] * len(more),
        out_specs=hbm,
        out_shape=jax.ShapeDtypeStruct((rows, cq), jnp.bfloat16),
        scratch_shapes=[
            VMEM((tokens, cq), jnp.bfloat16),
            VMEM((tokens, 2 * HD), jnp.bfloat16),
            VMEM((tokens, cq), jnp.bfloat16),
            pltpu.SemaphoreType.DMA((3, MOST_BLOCKS)),
        ],
        input_output_aliases={3: 0} if more else {},
        compiler_params=pltpu.CompilerParams(vmem_limit_bytes=62 * MIB),
        cost_estimate=pl.CostEstimate(flops=2 * rows * rows * cq, bytes_accessed=4 * rows * cq, transcendentals=rows * rows // 2),
        name="long_prompt" if half == 0 else "short_prompts",
    )(counts, q, kv, *more)


def row_head(n, lq, h, hh):
    at = h * GQ + hh
    return at // lq, at % lq


def handed_part(n, lq, kv_ref, own_ref, msg_ref, _, o_ref, __):
    rows = lq * n * GROUP_ROWS
    shape = (rows, HD)
    at_row, lane = iota(shape, 0), iota(shape, 1)
    rs = at_row % GROUP_ROWS
    facts = msg_ref[:, :HD].astype(jnp.float32).reshape(n, GROUP_ROWS, HD)[:, 6:7, :]
    facts = jnp.broadcast_to(facts, (n, GROUP_ROWS, HD)).reshape(n * GROUP_ROWS, HD)
    facts = jnp.concatenate([facts] * lq, axis=0)

    def column(kind):
        return jnp.sum(jnp.where(lane == kind * GROUP_ROWS + rs, facts, 0.0), axis=1, keepdims=True)

    first_block, second_block, length = [column(kind) for kind in range(3)]
    own = own_ref[...]
    queries = jnp.concatenate([own[:, h * HD : (h + 1) * HD] for h in range(lq)], axis=0)
    scores = dot_t(queries, kv_ref[:, :HD]) * SCALE
    lane_f = lane.astype(jnp.float32)
    parts = []
    for b in range(NBLK):
        limit = jnp.where(
            first_block == b, length, jnp.where(second_block == b, length - BLOCK_TOKENS, 0.0)
        )
        part = scores[:, b * BLOCK_TOKENS : (b + 1) * BLOCK_TOKENS]
        parts.append(jnp.where(lane_f < limit, part, MASKED))
    scores = jnp.concatenate(parts, axis=1)
    top = jnp.max(scores, axis=1, keepdims=True)
    raised = jnp.exp(scores - top)
    total = jnp.sum(raised, axis=1, keepdims=True)
    near = raised.astype(jnp.bfloat16)
    rest = (raised - near.astype(jnp.float32)).astype(jnp.bfloat16)
    values = kv_ref[:, HD:]
    mixed = (dot(near, values) + dot(rest, values)).reshape(lq * n, GROUP_ROWS, HD)

    def line(col):
        spread = jnp.where(lane == rs, col, 0.0).reshape(lq * n, GROUP_ROWS, HD)
        return jnp.sum(spread, axis=1, keepdims=True)

    rs3 = rs.reshape(lq * n, GROUP_ROWS, HD)
    mixed = jnp.where(rs3 == 6, line(top), jnp.where(rs3 == 7, line(total), mixed))
    for h in range(lq):
        o_ref[:, h * GROUP_ROWS : (h + 1) * GROUP_ROWS, :] = mixed[h * n : (h + 1) * n]


def handed_attention(kv, own, msgs, prompt_attn, n, lq):
    rows = lq * n * GROUP_ROWS
    vmem, hbm = pl.BlockSpec(memory_space=VMEM), pl.BlockSpec(memory_space=pl.ANY)
    return pl.pallas_call(
        functools.partial(handed_part, n, lq),
        in_specs=[vmem] * 3 + [hbm],
        out_specs=[vmem, hbm],
        out_shape=[
            jax.ShapeDtypeStruct((n, lq * GROUP_ROWS, HD), jnp.float32),
            jax.ShapeDtypeStruct(prompt_attn.shape, prompt_attn.dtype),
        ],
        input_output_aliases={3: 1},
        compiler_params=pltpu.CompilerParams(vmem_limit_bytes=24 * MIB),
        cost_estimate=pl.CostEstimate(flops=6 * rows * HD * PTOK, bytes_accessed=2 * MIB, transcendentals=rows * PTOK),
        name="handed_attention",
    )(kv, own, msgs, prompt_attn)


def owner_part(n, lq, *refs):
    cache_hbm, msgs, handed, o_ref, cache, sems, slot_row, slot_limit = refs[5:13]
    counts, done, placed, table, lens, int_sems = refs[13:]
    ints = int_copies(refs[:5], refs[13:18], int_sems)
    for copy in ints:
        copy.start()
    loads = []
    for slot in range(DEVICE_SLOTS):
        part = pl.ds(slot * BLOCK_TOKENS, BLOCK_TOKENS)
        loads.append(pltpu.make_async_copy(cache_hbm.at[part], cache.at[part], sems.at[slot]))
    for load in loads:
        load.start()
    held = msgs[...].astype(jnp.float32)

    def tile(t, k):
        return held[t * GROUP_ROWS : (t + 1) * GROUP_ROWS, k * HD : (k + 1) * HD]

    groups = QH
    rows = groups * GROUP_ROWS
    span = GQ * GROUP_ROWS
    queries, keys, values = [], [], []
    for h in range(KVH):
        for hh in range(GQ):
            t, at = row_head(n, lq, h, hh)
            queries.append(tile(t, at))
        t, _ = row_head(n, lq, h, 0)
        keys += [tile(t, lq)] * GQ
        values.append(tile(t, lq + 1))
    queries = jnp.concatenate(queries, axis=0)
    earlier = jnp.concatenate([pltpu.roll(key, ROWS_DEV, 0) for key in keys], axis=0)
    keys = jnp.concatenate(keys, axis=0)
    at_row, lane = iota((rows, HD), 0), iota((rows, HD), 1)
    r = row_of(at_row % GROUP_ROWS)
    rounded = queries.astype(jnp.bfloat16)
    now = jnp.sum(queries * keys, axis=1, keepdims=True) * SCALE
    before = jnp.sum(queries * earlier, axis=1, keepdims=True) * SCALE
    rs1 = iota((rows, 1), 0) % GROUP_ROWS
    before = jnp.where((rs1 >= ROWS_DEV) & (rs1 < STEPS * ROWS_DEV), before, MASKED)
    mixed = handed[...].reshape(groups, GROUP_ROWS, HD)
    shape = (groups, GROUP_ROWS, HD)
    mine = iota(shape, 1) == iota(shape, 2)

    def column(at):
        line = jnp.broadcast_to(mixed[:, at : at + 1, :], shape)
        return jnp.sum(jnp.where(mine, line, 0.0), axis=2, keepdims=True).reshape(rows, 1)

    other_peak, other_total = column(6), column(7)
    for copy in ints:
        copy.wait()
    found = block_of_pages(counts, done, placed, table)
    for k in range(ROWS_DEV):
        for p in range(PAGES):
            slot_row[table[p, k]] = jnp.int32(k)
            slot_limit[table[p, k]] = jnp.where(found[k][p] < 0, lens[k] - p * BLOCK_TOKENS, 0)
    for load in loads:
        load.wait()
    scores = jnp.concatenate(
        [dot_t(rounded[h * span : (h + 1) * span], cache[:, 2 * h * HD : (2 * h + 1) * HD]) for h in range(KVH)],
        axis=0,
    )
    parts = []
    for slot in range(DEVICE_SLOTS):
        part = scores[:, slot * BLOCK_TOKENS : (slot + 1) * BLOCK_TOKENS]
        usable = (r == slot_row[slot]) & (lane < slot_limit[slot])
        parts.append(jnp.where(usable, part * SCALE, MASKED))
    scores = jnp.concatenate(parts, axis=1)
    peak = jnp.maximum(jnp.max(scores, axis=1, keepdims=True), jnp.maximum(now, before))
    peak = jnp.maximum(peak, other_peak)
    raised, now, before = jnp.exp(scores - peak), jnp.exp(now - peak), jnp.exp(before - peak)
    other = jnp.exp(other_peak - peak)
    inverse = 1.0 / (jnp.sum(raised, axis=1, keepdims=True) + now + before + other * other_total)
    weights = (raised * inverse).astype(jnp.bfloat16)
    now = (now * inverse).astype(jnp.bfloat16).astype(jnp.float32)
    before = (before * inverse).astype(jnp.bfloat16).astype(jnp.float32)
    mixed = mixed.reshape(rows, HD) * (other * inverse)
    out = []
    for h in range(KVH):
        part = slice(h * span, (h + 1) * span)
        own = mixed[part] + dot(weights[part], cache[:, (2 * h + 1) * HD : (2 * h + 2) * HD])
        last = pltpu.roll(values[h], ROWS_DEV, 0)
        for hh in range(GQ):
            some = slice(h * span + hh * GROUP_ROWS, h * span + (hh + 1) * GROUP_ROWS)
            line = own[hh * GROUP_ROWS : (hh + 1) * GROUP_ROWS]
            out.append(line + now[some] * values[h] + before[some] * last)
    out = jnp.concatenate(out, axis=1)
    for k in range(ROWS_DEV):
        steps = [out[s * ROWS_DEV + k : s * ROWS_DEV + k + 1] for s in range(STEPS)]
        o_ref[k] = jnp.concatenate(steps, axis=0).astype(jnp.bfloat16)


def decode_attention(ints, cache, msgs, parts, n, lq):
    vmem, hbm = pl.BlockSpec(memory_space=VMEM), pl.BlockSpec(memory_space=pl.ANY)
    rows = QH * GROUP_ROWS
    return pl.pallas_call(
        functools.partial(owner_part, n, lq),
        in_specs=[hbm] * 6 + [vmem, vmem],
        out_specs=vmem,
        out_shape=jax.ShapeDtypeStruct((ROWS_DEV, STEPS, QH * HD), jnp.bfloat16),
        scratch_shapes=[
            VMEM(cache.shape, jnp.bfloat16),
            pltpu.SemaphoreType.DMA((DEVICE_SLOTS,)),
            SMEM((DEVICE_SLOTS,), jnp.int32),
            SMEM((DEVICE_SLOTS,), jnp.int32),
        ]
        + int_scratch(ints),
        compiler_params=pltpu.CompilerParams(vmem_limit_bytes=54 * MIB),
        cost_estimate=pl.CostEstimate(flops=4 * rows * HD * 768, bytes_accessed=4 * MIB, transcendentals=rows * 768),
        name="decode_attention",
    )(*ints, cache, msgs, parts)


def local(
    prompt_x,
    q_weight,
    kv_weight,
    prompt_blocks,
    finished,
    placement,
    page_table,
    row_lens,
    kv_cache,
    decode_x,
):
    n = lax.axis_size("tp")
    lq = q_weight.shape[1] // HD
    share = GQ // lq
    if share > 1:
        sets = [[k * share + i for i in range(share)] for k in range(n // share)]
        kv_weight = lax.all_gather(kv_weight, "tp", axis=1, tiled=True, axis_index_groups=sets)
    cache = kv_cache.reshape(-1, kv_cache.shape[2])
    dx = decode_x.reshape(-1, decode_x.shape[2])
    placement = placement.transpose(0, 2, 1)
    page_table = page_table.transpose(1, 0)
    ints = (prompt_blocks, finished, placement, page_table, row_lens)
    first, size = 512, 512
    q, kv, own, msgs = project_all(ints, dx, prompt_x, q_weight, kv_weight, n, first, size)
    kv_other = lax.ppermute(kv, "pool", [(0, 1), (1, 0)])
    msgs = lax.all_to_all(msgs, "tp", split_axis=0, concat_axis=0, tiled=True)
    prompt_attn = prompt_attention(prompt_blocks, q, kv, 0)
    handed, prompt_attn = handed_attention(kv_other, own, msgs, prompt_attn, n, lq)
    parts = lax.all_to_all(handed, "tp", split_axis=0, concat_axis=0, tiled=True)
    prompt_attn = prompt_attention(prompt_blocks, q, kv, 1, prompt_attn)
    decode_attn = decode_attention(ints, cache, msgs, parts, n, lq)
    return prompt_attn, decode_attn.transpose(1, 0, 2)


def solution(mesh):
    return jax.shard_map(
        local,
        mesh=mesh,
        in_specs=(
            P(("rep", "pool"), None),
            P(None, "tp"),
            P(None, "tp"),
            P("rep", None),
            P("rep", None),
            P("rep", None, None),
            P(("rep", "pool", "tp"), None),
            P(("rep", "pool", "tp")),
            P(("rep", "pool", "tp"), None, None),
            P(None, ("rep", "pool"), None),
        ),
        out_specs=(P(("rep", "pool"), "tp"), P(None, ("rep", "pool", "tp"), None)),
        check_vma=False,
    )
```

```python
import functools

import jax
import jax.numpy as jnp
from jax import lax
from jax.experimental import pallas as pl
from jax.experimental.pallas import tpu as pltpu
from jax.sharding import PartitionSpec as P

QH = 32
KVH = 8
GQ = QH // KVH
HD = 128
BLOCK_TOKENS = 128
PTOK = 2048
NPROMPT = 3
MOST_BLOCKS = 8
PAGES = 2
STEPS = 2
NBLK = 16
DEVICE_SLOTS = 6
ROWS_DEV = 3
GROUP_ROWS = 8
KEY_VALUE_COLUMNS = 2048
SCALE = HD ** (-0.5)
MASKED = -1e30
PIECES = 5
STRIPS = 4
LOG2E = 1.4426950408889634
AHEAD = 2
MIB = 1 << 20
VMEM = pltpu.VMEM
SMEM = pltpu.SMEM


def dot(a, b):
    return jnp.dot(a, b, preferred_element_type=jnp.float32)


def dot_t(a, b):
    return lax.dot_general(a, b, (((1,), (1,)), ((), ())), preferred_element_type=jnp.float32)


def iota(shape, axis):
    return lax.broadcasted_iota(jnp.int32, shape, axis)


def row_of(rs):
    return jnp.where(rs >= 2 * ROWS_DEV, ROWS_DEV, jnp.where(rs >= ROWS_DEV, rs - ROWS_DEV, rs))


def block_of_pages(counts, done, placed, table):
    me = lax.axis_index("tp")
    other = 1 - lax.axis_index("pool")
    first_end = counts[other, 0]
    second_end = first_end + counts[other, 1]
    found = [[jnp.int32(-1)] * PAGES for _ in range(ROWS_DEV)]
    for b in range(NBLK):
        live = jnp.where(
            b < first_end, done[other, 0], jnp.where(b < second_end, done[other, 1], done[other, 2])
        )
        slot = jnp.where((live > 0) & (placed[other, 0, b] == me), placed[other, 1, b], -1)
        for r in range(ROWS_DEV):
            for p in range(PAGES):
                found[r][p] = jnp.where(slot == table[p, r], b, found[r][p])
    return found


def by_row(r, values, rest):
    out = jnp.full(r.shape, rest, jnp.int32)
    for k in range(ROWS_DEV):
        out = jnp.where(r == k, values[k], out)
    return out


def int_scratch(ints):
    return [SMEM(x.shape, jnp.int32) for x in ints] + [pltpu.SemaphoreType.DMA((len(ints),))]


def int_copies(sources, targets, sems):
    return [pltpu.make_async_copy(a, b, sems.at[i]) for i, (a, b) in enumerate(zip(sources, targets))]


def project(n, lq, first, size, *refs):
    dx_hbm, x_hbm, wq_hbm, wkv_hbm = refs[5:9]
    q_hbm, kv_hbm, own_ref, msg_ref = refs[9:13]
    x0, xs, w, q_out, kv_out, x_sems, w_sems, out_sems = refs[13:21]
    counts, done, placed, table, lens, int_sems = refs[21:]
    ints = int_copies(refs[:5], refs[21:26], int_sems)
    depth = w.shape[0]
    count = xs.shape[0]
    cq = lq * HD
    piece = depth // PIECES
    own_rows = dx_hbm.shape[0]
    step = pl.program_id(0)

    def piece_copies(c):
        part = pl.ds(c * piece, piece)
        return [
            pltpu.make_async_copy(x_hbm.at[pl.ds(0, first), part], x0.at[pl.ds(0, first), part], w_sems.at[0, c]),
            pltpu.make_async_copy(dx_hbm.at[:, part], x0.at[pl.ds(first, own_rows), part], w_sems.at[1, c]),
            pltpu.make_async_copy(wq_hbm.at[part], w.at[part, pl.ds(0, cq)], w_sems.at[2, c]),
            pltpu.make_async_copy(wkv_hbm.at[part], w.at[part, pl.ds(cq, 2 * HD)], w_sems.at[3, c]),
        ]

    def x_copies(k):
        strip = size // STRIPS
        copies = []
        for i in range(STRIPS):
            rows = pl.ds(pl.multiple_of(first + k * size + i * strip, 16), strip)
            copies.append(
                pltpu.make_async_copy(x_hbm.at[rows], xs.at[k, pl.ds(i * strip, strip)], x_sems.at[k, i])
            )
        return copies

    def out_copies(k):
        if isinstance(k, int):
            rows = pl.ds(0, first)
        else:
            rows = pl.ds(pl.multiple_of(first + (k - 1) * size, 64), size)
        return [
            pltpu.make_async_copy(q_out.at[rows], q_hbm.at[rows], out_sems.at[0, k]),
            pltpu.make_async_copy(kv_out.at[rows], kv_hbm.at[rows], out_sems.at[1, k]),
        ]

    def keep(total, rows):
        q_out[rows, :] = total[:, :cq].astype(jnp.bfloat16)
        kv_out[rows, :] = total[:, cq:].astype(jnp.bfloat16)

    @pl.when(step == 0)
    def _():
        for c in range(AHEAD):
            for copy in piece_copies(c):
                copy.start()
        for copy in ints:
            copy.start()
        total = 0.0
        for c in range(PIECES):
            for copy in piece_copies(c):
                copy.wait()
            if c + AHEAD < PIECES:
                for copy in piece_copies(c + AHEAD):
                    copy.start()
            if c + AHEAD >= PIECES:
                for copy in x_copies(c + AHEAD - PIECES):
                    copy.start()
            part = slice(c * piece, (c + 1) * piece)
            total += dot(x0[:, part], w[part, :])
        keep(total[:first], pl.ds(0, first))
        for copy in out_copies(0):
            copy.start()
        shape = (n * GROUP_ROWS, own_rows)
        to, fro = iota(shape, 0), iota(shape, 1)
        owner, rs = to // GROUP_ROWS, to % GROUP_ROWS
        wanted = owner * ROWS_DEV + row_of(rs) + jnp.where(rs >= ROWS_DEV, ROWS_DEV * n, 0)
        pick = ((fro == wanted) & (rs < STEPS * ROWS_DEV)).astype(jnp.float32).astype(jnp.bfloat16)
        own = dot(pick, total[first:].astype(jnp.bfloat16))
        own_ref[...] = own.astype(jnp.bfloat16)
        for copy in ints:
            copy.wait()
        found = block_of_pages(counts, done, placed, table)
        lane = iota((n * GROUP_ROWS, HD), 1)
        r = row_of(lane % GROUP_ROWS)
        kind = lane // GROUP_ROWS
        facts = jnp.where(
            kind == 0,
            by_row(r, [found[i][0] for i in range(ROWS_DEV)], -1),
            jnp.where(
                kind == 1,
                by_row(r, [found[i][1] for i in range(ROWS_DEV)], -1),
                by_row(r, [lens[i] for i in range(ROWS_DEV)], 0),
            ),
        ).astype(jnp.float32)
        sixth = iota((n * GROUP_ROWS, HD), 0) % GROUP_ROWS == 6
        msg_ref[:, :HD] = jnp.where(sixth, facts, own[:, :HD]).astype(jnp.bfloat16)
        msg_ref[:, HD:] = own[:, HD:].astype(jnp.bfloat16)

    @pl.when((step > 0) & (step + AHEAD <= count))
    def _():
        for copy in x_copies(step + AHEAD - 1):
            copy.start()

    @pl.when(step > 0)
    def _():
        for copy in x_copies(step - 1):
            copy.wait()
        keep(dot(xs[step - 1], w[...]), pl.ds(pl.multiple_of(first + (step - 1) * size, 64), size))
        for copy in out_copies(step):
            copy.start()

    @pl.when(step == count)
    def _():
        for copy in out_copies(0):
            copy.wait()
        for k in range(1, count + 1):
            for copy in out_copies(jnp.int32(k)):
                copy.wait()


def project_all(ints, dx, x, wq, wkv, n, first, size):
    rows, depth = x.shape
    cq, ckv = wq.shape[1], wkv.shape[1]
    lq = cq // HD
    count = (rows - first) // size
    vmem, hbm = pl.BlockSpec(memory_space=VMEM), pl.BlockSpec(memory_space=pl.ANY)
    return pl.pallas_call(
        functools.partial(project, n, lq, first, size),
        grid=(1 + count,),
        in_specs=[hbm] * 9,
        out_specs=[hbm, hbm, vmem, vmem],
        out_shape=[
            jax.ShapeDtypeStruct((rows, cq), jnp.bfloat16),
            jax.ShapeDtypeStruct((rows, ckv), jnp.bfloat16),
            jax.ShapeDtypeStruct((n * GROUP_ROWS, cq + ckv), jnp.bfloat16),
            jax.ShapeDtypeStruct((n * GROUP_ROWS, cq + ckv), jnp.bfloat16),
        ],
        scratch_shapes=[
            VMEM((first + dx.shape[0], depth), jnp.bfloat16),
            VMEM((count, size, depth), jnp.bfloat16),
            VMEM((depth, cq + ckv), jnp.bfloat16),
            VMEM((rows, cq), jnp.bfloat16),
            VMEM((rows, ckv), jnp.bfloat16),
            pltpu.SemaphoreType.DMA((count, STRIPS)),
            pltpu.SemaphoreType.DMA((4, PIECES)),
            pltpu.SemaphoreType.DMA((2, count + 1)),
        ]
        + int_scratch(ints),
        compiler_params=pltpu.CompilerParams(vmem_limit_bytes=62 * MIB),
        cost_estimate=pl.CostEstimate(
            flops=2 * rows * depth * (cq + ckv),
            bytes_accessed=2 * (rows + cq + ckv) * depth + 2 * rows * (cq + ckv),
            transcendentals=0,
        ),
        name="project",
    )(*ints, dx, x, wq, wkv)


def attend_prompt(lq, half, counts, q_hbm, kv_hbm, *refs):
    o_hbm, qs, kvs, outs, sems = refs[-5:]
    group = lax.axis_index("pool")
    c0, c1 = counts[group, 0], counts[group, 1]
    big = jnp.where(c0 == MOST_BLOCKS, 0, jnp.where(c1 == MOST_BLOCKS, c0, c0 + c1))
    cut = jnp.where(c0 == MOST_BLOCKS, c1, c0)
    loads, stores = [], []
    strip, early = (4, 3) if half == 0 else (1, 5)
    for j in range(0, MOST_BLOCKS, strip):
        block = big + j if half == 0 else j + jnp.where(j >= big, MOST_BLOCKS, 0)
        rows = pl.ds(pl.multiple_of(block * BLOCK_TOKENS, BLOCK_TOKENS), strip * BLOCK_TOKENS)
        here = pl.ds(j * BLOCK_TOKENS, strip * BLOCK_TOKENS)
        loads.append(pltpu.make_async_copy(kv_hbm.at[rows], kvs.at[here], sems.at[0, j]))
        loads.append(pltpu.make_async_copy(q_hbm.at[rows], qs.at[here], sems.at[1, j]))
        stores.append(pltpu.make_async_copy(outs.at[here], o_hbm.at[rows], sems.at[2, j]))
    for copy in loads:
        copy.start()
    near = len(loads) // 2
    for copy in loads[:near]:
        copy.wait()
    shape = (BLOCK_TOKENS, lq * BLOCK_TOKENS)
    causal = iota(shape, 0) <= iota(shape, 1) % BLOCK_TOKENS
    tokens = MOST_BLOCKS * BLOCK_TOKENS
    flipped = kvs[: tokens // 2, HD:].T

    def scores_of(j):
        q = qs[j * BLOCK_TOKENS : (j + 1) * BLOCK_TOKENS, :]
        q = jnp.concatenate([q[:, h * HD : (h + 1) * HD] for h in range(lq)], axis=0)
        return dot_t(kvs[: (j + 1) * BLOCK_TOKENS, :HD], q)

    scores = scores_of(0)
    for j in range(MOST_BLOCKS):
        if j + 1 == MOST_BLOCKS // 2:
            for copy in loads[near:]:
                copy.wait()
            flipped = jnp.concatenate([flipped, kvs[tokens // 2 :, HD:].T], axis=1)
        later = scores_of(j + 1) if j + 1 < MOST_BLOCKS else None
        weights = []
        for h in range(lq):
            cols = slice(h * BLOCK_TOKENS, (h + 1) * BLOCK_TOKENS)
            tiles = []
            for i in range(j + 1):
                tile = scores[i * BLOCK_TOKENS : (i + 1) * BLOCK_TOKENS, cols]
                if i == j:
                    tile = jnp.where(causal[:, cols], tile, MASKED)
                elif half == 1:
                    tile = tile + jnp.where((i < cut) & (cut <= j), MASKED, 0.0)
                tiles.append(tile)
            peak = jnp.max(functools.reduce(jnp.maximum, tiles), axis=0, keepdims=True)
            raised = [jnp.exp2((tile - peak) * (SCALE * LOG2E)) for tile in tiles]
            inverse = 1.0 / jnp.sum(functools.reduce(jnp.add, raised), axis=0, keepdims=True)
            weights.append(jnp.concatenate([(t * inverse).astype(jnp.bfloat16) for t in raised], axis=0))
        mixed = dot(flipped[:, : (j + 1) * BLOCK_TOKENS], jnp.concatenate(weights, axis=1))
        mixed = mixed.astype(jnp.bfloat16)
        for h in range(lq):
            part = mixed[:, h * BLOCK_TOKENS : (h + 1) * BLOCK_TOKENS].T
            outs[j * BLOCK_TOKENS : (j + 1) * BLOCK_TOKENS, h * HD : (h + 1) * HD] = part
        scores = later
        if j == early:
            for copy in stores[: (j + 1) // strip]:
                copy.start()
    for copy in stores[(early + 1) // strip :]:
        copy.start()
    for copy in stores:
        copy.wait()


def prompt_attention(counts, q, kv, half, so_far=None):
    rows, cq = q.shape
    hbm = pl.BlockSpec(memory_space=pl.ANY)
    more = () if so_far is None else (so_far,)
    tokens = MOST_BLOCKS * BLOCK_TOKENS
    return pl.pallas_call(
        functools.partial(attend_prompt, cq // HD, half),
        in_specs=[pl.BlockSpec(memory_space=SMEM), hbm, hbm] + [hbm] * len(more),
        out_specs=hbm,
        out_shape=jax.ShapeDtypeStruct((rows, cq), jnp.bfloat16),
        scratch_shapes=[
            VMEM((tokens, cq), jnp.bfloat16),
            VMEM((tokens, 2 * HD), jnp.bfloat16),
            VMEM((tokens, cq), jnp.bfloat16),
            pltpu.SemaphoreType.DMA((3, MOST_BLOCKS)),
        ],
        input_output_aliases={3: 0} if more else {},
        compiler_params=pltpu.CompilerParams(vmem_limit_bytes=62 * MIB),
        cost_estimate=pl.CostEstimate(flops=2 * rows * rows * cq, bytes_accessed=4 * rows * cq, transcendentals=rows * rows // 2),
        name="long_prompt" if half == 0 else "short_prompts",
    )(counts, q, kv, *more)


def row_head(n, lq, h, hh):
    at = h * GQ + hh
    return at // lq, at % lq


def handed_part(n, lq, kv_ref, own_ref, msg_ref, _, o_ref, __):
    rows = lq * n * GROUP_ROWS
    shape = (rows, HD)
    at_row, lane = iota(shape, 0), iota(shape, 1)
    rs = at_row % GROUP_ROWS
    facts = msg_ref[:, :HD].astype(jnp.float32).reshape(n, GROUP_ROWS, HD)[:, 6:7, :]
    facts = jnp.broadcast_to(facts, (n, GROUP_ROWS, HD)).reshape(n * GROUP_ROWS, HD)
    facts = jnp.concatenate([facts] * lq, axis=0)

    def column(kind):
        return jnp.sum(jnp.where(lane == kind * GROUP_ROWS + rs, facts, 0.0), axis=1, keepdims=True)

    first_block, second_block, length = [column(kind) for kind in range(3)]
    own = own_ref[...]
    queries = jnp.concatenate([own[:, h * HD : (h + 1) * HD] for h in range(lq)], axis=0)
    scores = dot_t(queries, kv_ref[:, :HD]) * SCALE
    lane_f = lane.astype(jnp.float32)
    parts = []
    for b in range(NBLK):
        limit = jnp.where(
            first_block == b, length, jnp.where(second_block == b, length - BLOCK_TOKENS, 0.0)
        )
        part = scores[:, b * BLOCK_TOKENS : (b + 1) * BLOCK_TOKENS]
        parts.append(jnp.where(lane_f < limit, part, MASKED))
    scores = jnp.concatenate(parts, axis=1)
    top = jnp.max(scores, axis=1, keepdims=True)
    raised = jnp.exp(scores - top)
    total = jnp.sum(raised, axis=1, keepdims=True)
    near = raised.astype(jnp.bfloat16)
    rest = (raised - near.astype(jnp.float32)).astype(jnp.bfloat16)
    values = kv_ref[:, HD:]
    mixed = (dot(near, values) + dot(rest, values)).reshape(lq * n, GROUP_ROWS, HD)

    def line(col):
        spread = jnp.where(lane == rs, col, 0.0).reshape(lq * n, GROUP_ROWS, HD)
        return jnp.sum(spread, axis=1, keepdims=True)

    rs3 = rs.reshape(lq * n, GROUP_ROWS, HD)
    mixed = jnp.where(rs3 == 6, line(top), jnp.where(rs3 == 7, line(total), mixed))
    for h in range(lq):
        o_ref[:, h * GROUP_ROWS : (h + 1) * GROUP_ROWS, :] = mixed[h * n : (h + 1) * n]


def handed_attention(kv, own, msgs, prompt_attn, n, lq):
    rows = lq * n * GROUP_ROWS
    vmem, hbm = pl.BlockSpec(memory_space=VMEM), pl.BlockSpec(memory_space=pl.ANY)
    return pl.pallas_call(
        functools.partial(handed_part, n, lq),
        in_specs=[vmem] * 3 + [hbm],
        out_specs=[vmem, hbm],
        out_shape=[
            jax.ShapeDtypeStruct((n, lq * GROUP_ROWS, HD), jnp.float32),
            jax.ShapeDtypeStruct(prompt_attn.shape, prompt_attn.dtype),
        ],
        input_output_aliases={3: 1},
        compiler_params=pltpu.CompilerParams(vmem_limit_bytes=24 * MIB),
        cost_estimate=pl.CostEstimate(flops=6 * rows * HD * PTOK, bytes_accessed=2 * MIB, transcendentals=rows * PTOK),
        name="handed_attention",
    )(kv, own, msgs, prompt_attn)


def owner_part(n, lq, *refs):
    cache_hbm, msgs_hbm, handed_hbm, o_ref, cache, msgs, handed, sems, slot_row, slot_limit = refs[5:15]
    counts, done, placed, table, lens, int_sems = refs[15:]
    ints = int_copies(refs[:5], refs[15:20], int_sems)
    first = [
        pltpu.make_async_copy(msgs_hbm, msgs, sems.at[DEVICE_SLOTS]),
        pltpu.make_async_copy(handed_hbm, handed, sems.at[DEVICE_SLOTS + 1]),
    ]
    for copy in first:
        copy.start()
    loads = []
    for slot in range(DEVICE_SLOTS):
        part = pl.ds(slot * BLOCK_TOKENS, BLOCK_TOKENS)
        loads.append(pltpu.make_async_copy(cache_hbm.at[part], cache.at[part], sems.at[slot]))
    for load in loads:
        load.start()
    for copy in ints:
        copy.start()
    for copy in first:
        copy.wait()
    held = msgs[...].astype(jnp.float32)

    def tile(t, k):
        return held[t * GROUP_ROWS : (t + 1) * GROUP_ROWS, k * HD : (k + 1) * HD]

    groups = QH
    rows = groups * GROUP_ROWS
    span = GQ * GROUP_ROWS
    queries, keys, values = [], [], []
    for h in range(KVH):
        for hh in range(GQ):
            t, at = row_head(n, lq, h, hh)
            queries.append(tile(t, at))
        t, _ = row_head(n, lq, h, 0)
        keys += [tile(t, lq)] * GQ
        values.append(tile(t, lq + 1))
    queries = jnp.concatenate(queries, axis=0)
    earlier = jnp.concatenate([pltpu.roll(key, ROWS_DEV, 0) for key in keys], axis=0)
    keys = jnp.concatenate(keys, axis=0)
    at_row, lane = iota((rows, HD), 0), iota((rows, HD), 1)
    r = row_of(at_row % GROUP_ROWS)
    rounded = queries.astype(jnp.bfloat16)
    now = jnp.sum(queries * keys, axis=1, keepdims=True) * SCALE
    before = jnp.sum(queries * earlier, axis=1, keepdims=True) * SCALE
    rs1 = iota((rows, 1), 0) % GROUP_ROWS
    before = jnp.where((rs1 >= ROWS_DEV) & (rs1 < STEPS * ROWS_DEV), before, MASKED)
    mixed = handed[...].reshape(groups, GROUP_ROWS, HD)
    shape = (groups, GROUP_ROWS, HD)
    mine = iota(shape, 1) == iota(shape, 2)

    def column(at):
        line = jnp.broadcast_to(mixed[:, at : at + 1, :], shape)
        return jnp.sum(jnp.where(mine, line, 0.0), axis=2, keepdims=True).reshape(rows, 1)

    other_peak, other_total = column(6), column(7)
    for copy in ints:
        copy.wait()
    found = block_of_pages(counts, done, placed, table)
    for k in range(ROWS_DEV):
        for p in range(PAGES):
            slot_row[table[p, k]] = jnp.int32(k)
            slot_limit[table[p, k]] = jnp.where(found[k][p] < 0, lens[k] - p * BLOCK_TOKENS, 0)
    for load in loads:
        load.wait()
    scores = jnp.concatenate(
        [dot_t(rounded[h * span : (h + 1) * span], cache[:, 2 * h * HD : (2 * h + 1) * HD]) for h in range(KVH)],
        axis=0,
    )
    parts = []
    for slot in range(DEVICE_SLOTS):
        part = scores[:, slot * BLOCK_TOKENS : (slot + 1) * BLOCK_TOKENS]
        usable = (r == slot_row[slot]) & (lane < slot_limit[slot])
        parts.append(jnp.where(usable, part * SCALE, MASKED))
    scores = jnp.concatenate(parts, axis=1)
    peak = jnp.maximum(jnp.max(scores, axis=1, keepdims=True), jnp.maximum(now, before))
    peak = jnp.maximum(peak, other_peak)
    raised, now, before = jnp.exp(scores - peak), jnp.exp(now - peak), jnp.exp(before - peak)
    other = jnp.exp(other_peak - peak)
    inverse = 1.0 / (jnp.sum(raised, axis=1, keepdims=True) + now + before + other * other_total)
    weights = (raised * inverse).astype(jnp.bfloat16)
    now = (now * inverse).astype(jnp.bfloat16).astype(jnp.float32)
    before = (before * inverse).astype(jnp.bfloat16).astype(jnp.float32)
    mixed = mixed.reshape(rows, HD) * (other * inverse)
    out = []
    for h in range(KVH):
        part = slice(h * span, (h + 1) * span)
        own = mixed[part] + dot(weights[part], cache[:, (2 * h + 1) * HD : (2 * h + 2) * HD])
        last = pltpu.roll(values[h], ROWS_DEV, 0)
        for hh in range(GQ):
            some = slice(h * span + hh * GROUP_ROWS, h * span + (hh + 1) * GROUP_ROWS)
            line = own[hh * GROUP_ROWS : (hh + 1) * GROUP_ROWS]
            out.append(line + now[some] * values[h] + before[some] * last)
    out = jnp.concatenate(out, axis=1)
    for k in range(ROWS_DEV):
        steps = [out[s * ROWS_DEV + k : s * ROWS_DEV + k + 1] for s in range(STEPS)]
        o_ref[k] = jnp.concatenate(steps, axis=0).astype(jnp.bfloat16)


def decode_attention(ints, cache, msgs, parts, n, lq):
    vmem, hbm = pl.BlockSpec(memory_space=VMEM), pl.BlockSpec(memory_space=pl.ANY)
    rows = QH * GROUP_ROWS
    return pl.pallas_call(
        functools.partial(owner_part, n, lq),
        in_specs=[hbm] * 8,
        out_specs=vmem,
        out_shape=jax.ShapeDtypeStruct((ROWS_DEV, STEPS, QH * HD), jnp.bfloat16),
        scratch_shapes=[
            VMEM(cache.shape, jnp.bfloat16),
            VMEM(msgs.shape, msgs.dtype),
            VMEM(parts.shape, parts.dtype),
            pltpu.SemaphoreType.DMA((DEVICE_SLOTS + 2,)),
            SMEM((DEVICE_SLOTS,), jnp.int32),
            SMEM((DEVICE_SLOTS,), jnp.int32),
        ]
        + int_scratch(ints),
        compiler_params=pltpu.CompilerParams(vmem_limit_bytes=52 * MIB),
        cost_estimate=pl.CostEstimate(flops=4 * rows * HD * 768, bytes_accessed=4 * MIB, transcendentals=rows * 768),
        name="decode_attention",
    )(*ints, cache, msgs, parts)


def local(
    prompt_x,
    q_weight,
    kv_weight,
    prompt_blocks,
    finished,
    placement,
    page_table,
    row_lens,
    kv_cache,
    decode_x,
):
    n = lax.axis_size("tp")
    lq = q_weight.shape[1] // HD
    share = GQ // lq
    if share > 1:
        sets = [[k * share + i for i in range(share)] for k in range(n // share)]
        kv_weight = lax.all_gather(kv_weight, "tp", axis=1, tiled=True, axis_index_groups=sets)
    cache = kv_cache.reshape(-1, kv_cache.shape[2])
    dx = decode_x.reshape(-1, decode_x.shape[2])
    placement = placement.transpose(0, 2, 1)
    page_table = page_table.transpose(1, 0)
    ints = (prompt_blocks, finished, placement, page_table, row_lens)
    first, size = 256, 448
    q, kv, own, msgs = project_all(ints, dx, prompt_x, q_weight, kv_weight, n, first, size)
    kv_other = lax.ppermute(kv, "pool", [(0, 1), (1, 0)])
    msgs = lax.all_to_all(msgs, "tp", split_axis=0, concat_axis=0, tiled=True)
    prompt_attn = prompt_attention(prompt_blocks, q, kv, 0)
    handed, prompt_attn = handed_attention(kv_other, own, msgs, prompt_attn, n, lq)
    parts = lax.all_to_all(handed, "tp", split_axis=0, concat_axis=0, tiled=True)
    prompt_attn = prompt_attention(prompt_blocks, q, kv, 1, prompt_attn)
    decode_attn = decode_attention(ints, cache, msgs, parts, n, lq)
    return prompt_attn, decode_attn.transpose(1, 0, 2)


def solution(mesh):
    return jax.shard_map(
        local,
        mesh=mesh,
        in_specs=(
            P(("rep", "pool"), None),
            P(None, "tp"),
            P(None, "tp"),
            P("rep", None),
            P("rep", None),
            P("rep", None, None),
            P(("rep", "pool", "tp"), None),
            P(("rep", "pool", "tp")),
            P(("rep", "pool", "tp"), None, None),
            P(None, ("rep", "pool"), None),
        ),
        out_specs=(P(("rep", "pool"), "tp"), P(None, ("rep", "pool", "tp"), None)),
        check_vma=False,
    )
```

```python
import functools

import jax
import jax.numpy as jnp
from jax import lax
from jax.experimental import pallas as pl
from jax.experimental.pallas import tpu as pltpu
from jax.sharding import PartitionSpec as P

QH = 32
KVH = 8
GQ = QH // KVH
HD = 128
BLOCK_TOKENS = 128
PTOK = 2048
NPROMPT = 3
MOST_BLOCKS = 8
PAGES = 2
STEPS = 2
NBLK = 16
DEVICE_SLOTS = 6
ROWS_DEV = 3
GROUP_ROWS = 8
KEY_VALUE_COLUMNS = 2048
SCALE = HD ** (-0.5)
MASKED = -1e30
PIECES = 5
STRIPS = 4
LOG2E = 1.4426950408889634
AHEAD = 2
MIB = 1 << 20
VMEM = pltpu.VMEM
SMEM = pltpu.SMEM


def dot(a, b):
    return jnp.dot(a, b, preferred_element_type=jnp.float32)


def dot_t(a, b):
    return lax.dot_general(a, b, (((1,), (1,)), ((), ())), preferred_element_type=jnp.float32)


def iota(shape, axis):
    return lax.broadcasted_iota(jnp.int32, shape, axis)


def row_of(rs):
    return jnp.where(rs >= 2 * ROWS_DEV, ROWS_DEV, jnp.where(rs >= ROWS_DEV, rs - ROWS_DEV, rs))


def block_of_pages(counts, done, placed, table):
    me = lax.axis_index("tp")
    other = 1 - lax.axis_index("pool")
    first_end = counts[other, 0]
    second_end = first_end + counts[other, 1]
    found = [[jnp.int32(-1)] * PAGES for _ in range(ROWS_DEV)]
    for b in range(NBLK):
        live = jnp.where(
            b < first_end, done[other, 0], jnp.where(b < second_end, done[other, 1], done[other, 2])
        )
        slot = jnp.where((live > 0) & (placed[other, 0, b] == me), placed[other, 1, b], -1)
        for r in range(ROWS_DEV):
            for p in range(PAGES):
                found[r][p] = jnp.where(slot == table[p, r], b, found[r][p])
    return found


def by_row(r, values, rest):
    out = jnp.full(r.shape, rest, jnp.int32)
    for k in range(ROWS_DEV):
        out = jnp.where(r == k, values[k], out)
    return out


def int_scratch(ints):
    return [SMEM(x.shape, jnp.int32) for x in ints] + [pltpu.SemaphoreType.DMA((len(ints),))]


def int_copies(sources, targets, sems):
    return [pltpu.make_async_copy(a, b, sems.at[i]) for i, (a, b) in enumerate(zip(sources, targets))]


def project(n, lq, first, size, *refs):
    dx_hbm, x_hbm, wq_hbm, wkv_hbm = refs[5:9]
    q_hbm, kv_hbm, own_ref, msg_ref = refs[9:13]
    x0, xs, w, flipped, q_out, kv_out, x_sems, w_sems, out_sems = refs[13:22]
    counts, done, placed, table, lens, int_sems = refs[22:]
    ints = int_copies(refs[:5], refs[22:27], int_sems)
    depth = w.shape[0]
    count = xs.shape[0]
    cq = lq * HD
    piece = depth // PIECES
    own_rows = dx_hbm.shape[0]
    step = pl.program_id(0)

    def piece_copies(c):
        part = pl.ds(c * piece, piece)
        return [
            pltpu.make_async_copy(x_hbm.at[pl.ds(0, first), part], x0.at[pl.ds(0, first), part], w_sems.at[0, c]),
            pltpu.make_async_copy(dx_hbm.at[:, part], x0.at[pl.ds(first, own_rows), part], w_sems.at[1, c]),
            pltpu.make_async_copy(wq_hbm.at[part], w.at[part, pl.ds(0, cq)], w_sems.at[2, c]),
            pltpu.make_async_copy(wkv_hbm.at[part], w.at[part, pl.ds(cq, 2 * HD)], w_sems.at[3, c]),
        ]

    def x_copies(k):
        strip = size // STRIPS
        copies = []
        for i in range(STRIPS):
            rows = pl.ds(pl.multiple_of(first + k * size + i * strip, 16), strip)
            copies.append(
                pltpu.make_async_copy(x_hbm.at[rows], xs.at[k, pl.ds(i * strip, strip)], x_sems.at[k, i])
            )
        return copies

    def out_copies(k):
        if isinstance(k, int):
            rows = pl.ds(0, first)
        else:
            rows = pl.ds(pl.multiple_of(first + (k - 1) * size, 64), size)
        return [
            pltpu.make_async_copy(q_out.at[rows], q_hbm.at[rows], out_sems.at[0, k]),
            pltpu.make_async_copy(kv_out.at[rows], kv_hbm.at[rows], out_sems.at[1, k]),
        ]

    def keep(total, rows):
        q_out[rows, :] = total[:, :cq].astype(jnp.bfloat16)
        kv_out[rows, :] = total[:, cq:].astype(jnp.bfloat16)

    @pl.when(step == 0)
    def _():
        for c in range(AHEAD):
            for copy in piece_copies(c):
                copy.start()
        for copy in ints:
            copy.start()
        total = 0.0
        for c in range(PIECES):
            for copy in piece_copies(c):
                copy.wait()
            if c + AHEAD < PIECES:
                for copy in piece_copies(c + AHEAD):
                    copy.start()
            if c + AHEAD >= PIECES:
                for copy in x_copies(c + AHEAD - PIECES):
                    copy.start()
            part = slice(c * piece, (c + 1) * piece)
            total += dot(x0[:, part], w[part, :])
            flipped[:, part] = w[part, cq:].T
        keep(total[:first], pl.ds(0, first))
        for copy in out_copies(0):
            copy.start()
        shape = (n * GROUP_ROWS, own_rows)
        to, fro = iota(shape, 0), iota(shape, 1)
        owner, rs = to // GROUP_ROWS, to % GROUP_ROWS
        wanted = owner * ROWS_DEV + row_of(rs) + jnp.where(rs >= ROWS_DEV, ROWS_DEV * n, 0)
        pick = ((fro == wanted) & (rs < STEPS * ROWS_DEV)).astype(jnp.float32).astype(jnp.bfloat16)
        own = dot(pick, total[first:].astype(jnp.bfloat16))
        own_ref[...] = own.astype(jnp.bfloat16)
        for copy in ints:
            copy.wait()
        found = block_of_pages(counts, done, placed, table)
        lane = iota((n * GROUP_ROWS, HD), 1)
        r = row_of(lane % GROUP_ROWS)
        kind = lane // GROUP_ROWS
        facts = jnp.where(
            kind == 0,
            by_row(r, [found[i][0] for i in range(ROWS_DEV)], -1),
            jnp.where(
                kind == 1,
                by_row(r, [found[i][1] for i in range(ROWS_DEV)], -1),
                by_row(r, [lens[i] for i in range(ROWS_DEV)], 0),
            ),
        ).astype(jnp.float32)
        sixth = iota((n * GROUP_ROWS, HD), 0) % GROUP_ROWS == 6
        msg_ref[:, :HD] = jnp.where(sixth, facts, own[:, :HD]).astype(jnp.bfloat16)
        msg_ref[:, HD:] = own[:, HD:].astype(jnp.bfloat16)

    @pl.when((step > 0) & (step + AHEAD <= count))
    def _():
        for copy in x_copies(step + AHEAD - 1):
            copy.start()

    @pl.when(step > 0)
    def _():
        for copy in x_copies(step - 1):
            copy.wait()
        rows = pl.ds(pl.multiple_of(first + (step - 1) * size, 64), size)
        q_out[rows, :] = dot(xs[step - 1], w[:, :cq]).astype(jnp.bfloat16)
        kv_out[rows, :] = dot_t(flipped[...], xs[step - 1]).astype(jnp.bfloat16).T
        for copy in out_copies(step):
            copy.start()

    @pl.when(step == count)
    def _():
        for copy in out_copies(0):
            copy.wait()
        for k in range(1, count + 1):
            for copy in out_copies(jnp.int32(k)):
                copy.wait()


def project_all(ints, dx, x, wq, wkv, n, first, size):
    rows, depth = x.shape
    cq, ckv = wq.shape[1], wkv.shape[1]
    lq = cq // HD
    count = (rows - first) // size
    vmem, hbm = pl.BlockSpec(memory_space=VMEM), pl.BlockSpec(memory_space=pl.ANY)
    return pl.pallas_call(
        functools.partial(project, n, lq, first, size),
        grid=(1 + count,),
        in_specs=[hbm] * 9,
        out_specs=[hbm, hbm, vmem, vmem],
        out_shape=[
            jax.ShapeDtypeStruct((rows, cq), jnp.bfloat16),
            jax.ShapeDtypeStruct((rows, ckv), jnp.bfloat16),
            jax.ShapeDtypeStruct((n * GROUP_ROWS, cq + ckv), jnp.bfloat16),
            jax.ShapeDtypeStruct((n * GROUP_ROWS, cq + ckv), jnp.bfloat16),
        ],
        scratch_shapes=[
            VMEM((first + dx.shape[0], depth), jnp.bfloat16),
            VMEM((count, size, depth), jnp.bfloat16),
            VMEM((depth, cq + ckv), jnp.bfloat16),
            VMEM((ckv, depth), jnp.bfloat16),
            VMEM((rows, cq), jnp.bfloat16),
            VMEM((rows, ckv), jnp.bfloat16),
            pltpu.SemaphoreType.DMA((count, STRIPS)),
            pltpu.SemaphoreType.DMA((4, PIECES)),
            pltpu.SemaphoreType.DMA((2, count + 1)),
        ]
        + int_scratch(ints),
        compiler_params=pltpu.CompilerParams(vmem_limit_bytes=62 * MIB),
        cost_estimate=pl.CostEstimate(
            flops=2 * rows * depth * (cq + ckv),
            bytes_accessed=2 * (rows + cq + ckv) * depth + 2 * rows * (cq + ckv),
            transcendentals=0,
        ),
        name="project",
    )(*ints, dx, x, wq, wkv)


def attend_prompt(lq, half, counts, q_hbm, kv_hbm, *refs):
    o_hbm, qs, kvs, outs, sems = refs[-5:]
    group = lax.axis_index("pool")
    c0, c1 = counts[group, 0], counts[group, 1]
    big = jnp.where(c0 == MOST_BLOCKS, 0, jnp.where(c1 == MOST_BLOCKS, c0, c0 + c1))
    cut = jnp.where(c0 == MOST_BLOCKS, c1, c0)
    loads, stores = [], []
    strip, early = (4, 3) if half == 0 else (1, 5)
    for j in range(0, MOST_BLOCKS, strip):
        block = big + j if half == 0 else j + jnp.where(j >= big, MOST_BLOCKS, 0)
        rows = pl.ds(pl.multiple_of(block * BLOCK_TOKENS, BLOCK_TOKENS), strip * BLOCK_TOKENS)
        here = pl.ds(j * BLOCK_TOKENS, strip * BLOCK_TOKENS)
        loads.append(pltpu.make_async_copy(kv_hbm.at[rows], kvs.at[here], sems.at[0, j]))
        loads.append(pltpu.make_async_copy(q_hbm.at[rows], qs.at[here], sems.at[1, j]))
        stores.append(pltpu.make_async_copy(outs.at[here], o_hbm.at[rows], sems.at[2, j]))
    for copy in loads:
        copy.start()
    near = len(loads) // 2
    for copy in loads[:near]:
        copy.wait()
    shape = (BLOCK_TOKENS, lq * BLOCK_TOKENS)
    causal = iota(shape, 0) <= iota(shape, 1) % BLOCK_TOKENS
    tokens = MOST_BLOCKS * BLOCK_TOKENS
    flipped = kvs[: tokens // 2, HD:].T

    def scores_of(j):
        q = qs[j * BLOCK_TOKENS : (j + 1) * BLOCK_TOKENS, :]
        q = jnp.concatenate([q[:, h * HD : (h + 1) * HD] for h in range(lq)], axis=0)
        return dot_t(kvs[: (j + 1) * BLOCK_TOKENS, :HD], q)

    scores = scores_of(0)
    for j in range(MOST_BLOCKS):
        if j + 1 == MOST_BLOCKS // 2:
            for copy in loads[near:]:
                copy.wait()
            flipped = jnp.concatenate([flipped, kvs[tokens // 2 :, HD:].T], axis=1)
        later = scores_of(j + 1) if j + 1 < MOST_BLOCKS else None
        weights = []
        for h in range(lq):
            cols = slice(h * BLOCK_TOKENS, (h + 1) * BLOCK_TOKENS)
            tiles = []
            for i in range(j + 1):
                tile = scores[i * BLOCK_TOKENS : (i + 1) * BLOCK_TOKENS, cols]
                if i == j:
                    tile = jnp.where(causal[:, cols], tile, MASKED)
                elif half == 1:
                    tile = tile + jnp.where((i < cut) & (cut <= j), MASKED, 0.0)
                tiles.append(tile)
            peak = jnp.max(functools.reduce(jnp.maximum, tiles), axis=0, keepdims=True)
            raised = [jnp.exp2((tile - peak) * (SCALE * LOG2E)) for tile in tiles]
            inverse = 1.0 / jnp.sum(functools.reduce(jnp.add, raised), axis=0, keepdims=True)
            weights.append(jnp.concatenate([(t * inverse).astype(jnp.bfloat16) for t in raised], axis=0))
        mixed = dot(flipped[:, : (j + 1) * BLOCK_TOKENS], jnp.concatenate(weights, axis=1))
        mixed = mixed.astype(jnp.bfloat16)
        for h in range(lq):
            part = mixed[:, h * BLOCK_TOKENS : (h + 1) * BLOCK_TOKENS].T
            outs[j * BLOCK_TOKENS : (j + 1) * BLOCK_TOKENS, h * HD : (h + 1) * HD] = part
        scores = later
        if j == early:
            for copy in stores[: (j + 1) // strip]:
                copy.start()
    for copy in stores[(early + 1) // strip :]:
        copy.start()
    for copy in stores:
        copy.wait()


def prompt_attention(counts, q, kv, half, so_far=None):
    rows, cq = q.shape
    hbm = pl.BlockSpec(memory_space=pl.ANY)
    more = () if so_far is None else (so_far,)
    tokens = MOST_BLOCKS * BLOCK_TOKENS
    return pl.pallas_call(
        functools.partial(attend_prompt, cq // HD, half),
        in_specs=[pl.BlockSpec(memory_space=SMEM), hbm, hbm] + [hbm] * len(more),
        out_specs=hbm,
        out_shape=jax.ShapeDtypeStruct((rows, cq), jnp.bfloat16),
        scratch_shapes=[
            VMEM((tokens, cq), jnp.bfloat16),
            VMEM((tokens, 2 * HD), jnp.bfloat16),
            VMEM((tokens, cq), jnp.bfloat16),
            pltpu.SemaphoreType.DMA((3, MOST_BLOCKS)),
        ],
        input_output_aliases={3: 0} if more else {},
        compiler_params=pltpu.CompilerParams(vmem_limit_bytes=62 * MIB),
        cost_estimate=pl.CostEstimate(flops=2 * rows * rows * cq, bytes_accessed=4 * rows * cq, transcendentals=rows * rows // 2),
        name="long_prompt" if half == 0 else "short_prompts",
    )(counts, q, kv, *more)


def row_head(n, lq, h, hh):
    at = h * GQ + hh
    return at // lq, at % lq


def handed_part(n, lq, kv_ref, own_ref, msg_ref, _, o_ref, __):
    rows = lq * n * GROUP_ROWS
    shape = (rows, HD)
    at_row, lane = iota(shape, 0), iota(shape, 1)
    rs = at_row % GROUP_ROWS
    facts = msg_ref[:, :HD].astype(jnp.float32).reshape(n, GROUP_ROWS, HD)[:, 6:7, :]
    facts = jnp.broadcast_to(facts, (n, GROUP_ROWS, HD)).reshape(n * GROUP_ROWS, HD)
    facts = jnp.concatenate([facts] * lq, axis=0)

    def column(kind):
        return jnp.sum(jnp.where(lane == kind * GROUP_ROWS + rs, facts, 0.0), axis=1, keepdims=True)

    first_block, second_block, length = [column(kind) for kind in range(3)]
    own = own_ref[...]
    queries = jnp.concatenate([own[:, h * HD : (h + 1) * HD] for h in range(lq)], axis=0)
    scores = dot_t(queries, kv_ref[:, :HD]) * SCALE
    lane_f = lane.astype(jnp.float32)
    parts = []
    for b in range(NBLK):
        limit = jnp.where(
            first_block == b, length, jnp.where(second_block == b, length - BLOCK_TOKENS, 0.0)
        )
        part = scores[:, b * BLOCK_TOKENS : (b + 1) * BLOCK_TOKENS]
        parts.append(jnp.where(lane_f < limit, part, MASKED))
    scores = jnp.concatenate(parts, axis=1)
    top = jnp.max(scores, axis=1, keepdims=True)
    raised = jnp.exp(scores - top)
    total = jnp.sum(raised, axis=1, keepdims=True)
    near = raised.astype(jnp.bfloat16)
    rest = (raised - near.astype(jnp.float32)).astype(jnp.bfloat16)
    values = kv_ref[:, HD:]
    mixed = (dot(near, values) + dot(rest, values)).reshape(lq * n, GROUP_ROWS, HD)

    def line(col):
        spread = jnp.where(lane == rs, col, 0.0).reshape(lq * n, GROUP_ROWS, HD)
        return jnp.sum(spread, axis=1, keepdims=True)

    rs3 = rs.reshape(lq * n, GROUP_ROWS, HD)
    mixed = jnp.where(rs3 == 6, line(top), jnp.where(rs3 == 7, line(total), mixed))
    for h in range(lq):
        o_ref[:, h * GROUP_ROWS : (h + 1) * GROUP_ROWS, :] = mixed[h * n : (h + 1) * n]


def handed_attention(kv, own, msgs, prompt_attn, n, lq):
    rows = lq * n * GROUP_ROWS
    vmem, hbm = pl.BlockSpec(memory_space=VMEM), pl.BlockSpec(memory_space=pl.ANY)
    return pl.pallas_call(
        functools.partial(handed_part, n, lq),
        in_specs=[vmem] * 3 + [hbm],
        out_specs=[vmem, hbm],
        out_shape=[
            jax.ShapeDtypeStruct((n, lq * GROUP_ROWS, HD), jnp.float32),
            jax.ShapeDtypeStruct(prompt_attn.shape, prompt_attn.dtype),
        ],
        input_output_aliases={3: 1},
        compiler_params=pltpu.CompilerParams(vmem_limit_bytes=24 * MIB),
        cost_estimate=pl.CostEstimate(flops=6 * rows * HD * PTOK, bytes_accessed=2 * MIB, transcendentals=rows * PTOK),
        name="handed_attention",
    )(kv, own, msgs, prompt_attn)


def owner_part(n, lq, *refs):
    cache_hbm, msgs_hbm, handed_hbm, o_ref, cache, msgs, handed, sems, slot_row, slot_limit = refs[5:15]
    counts, done, placed, table, lens, int_sems = refs[15:]
    ints = int_copies(refs[:5], refs[15:20], int_sems)
    first = [
        pltpu.make_async_copy(msgs_hbm, msgs, sems.at[DEVICE_SLOTS]),
        pltpu.make_async_copy(handed_hbm, handed, sems.at[DEVICE_SLOTS + 1]),
    ]
    for copy in first:
        copy.start()
    loads = []
    for slot in range(DEVICE_SLOTS):
        part = pl.ds(slot * BLOCK_TOKENS, BLOCK_TOKENS)
        loads.append(pltpu.make_async_copy(cache_hbm.at[part], cache.at[part], sems.at[slot]))
    for load in loads:
        load.start()
    for copy in ints:
        copy.start()
    for copy in first:
        copy.wait()
    held = msgs[...].astype(jnp.float32)

    def tile(t, k):
        return held[t * GROUP_ROWS : (t + 1) * GROUP_ROWS, k * HD : (k + 1) * HD]

    groups = QH
    rows = groups * GROUP_ROWS
    span = GQ * GROUP_ROWS
    queries, keys, values = [], [], []
    for h in range(KVH):
        for hh in range(GQ):
            t, at = row_head(n, lq, h, hh)
            queries.append(tile(t, at))
        t, _ = row_head(n, lq, h, 0)
        keys += [tile(t, lq)] * GQ
        values.append(tile(t, lq + 1))
    queries = jnp.concatenate(queries, axis=0)
    earlier = jnp.concatenate([pltpu.roll(key, ROWS_DEV, 0) for key in keys], axis=0)
    keys = jnp.concatenate(keys, axis=0)
    at_row, lane = iota((rows, HD), 0), iota((rows, HD), 1)
    r = row_of(at_row % GROUP_ROWS)
    rounded = queries.astype(jnp.bfloat16)
    now = jnp.sum(queries * keys, axis=1, keepdims=True) * SCALE
    before = jnp.sum(queries * earlier, axis=1, keepdims=True) * SCALE
    rs1 = iota((rows, 1), 0) % GROUP_ROWS
    before = jnp.where((rs1 >= ROWS_DEV) & (rs1 < STEPS * ROWS_DEV), before, MASKED)
    mixed = handed[...].reshape(groups, GROUP_ROWS, HD)
    shape = (groups, GROUP_ROWS, HD)
    mine = iota(shape, 1) == iota(shape, 2)

    def column(at):
        line = jnp.broadcast_to(mixed[:, at : at + 1, :], shape)
        return jnp.sum(jnp.where(mine, line, 0.0), axis=2, keepdims=True).reshape(rows, 1)

    other_peak, other_total = column(6), column(7)
    for copy in ints:
        copy.wait()
    found = block_of_pages(counts, done, placed, table)
    for k in range(ROWS_DEV):
        for p in range(PAGES):
            slot_row[table[p, k]] = jnp.int32(k)
            slot_limit[table[p, k]] = jnp.where(found[k][p] < 0, lens[k] - p * BLOCK_TOKENS, 0)
    for load in loads:
        load.wait()
    scores = jnp.concatenate(
        [dot_t(rounded[h * span : (h + 1) * span], cache[:, 2 * h * HD : (2 * h + 1) * HD]) for h in range(KVH)],
        axis=0,
    )
    parts = []
    for slot in range(DEVICE_SLOTS):
        part = scores[:, slot * BLOCK_TOKENS : (slot + 1) * BLOCK_TOKENS]
        usable = (r == slot_row[slot]) & (lane < slot_limit[slot])
        parts.append(jnp.where(usable, part * SCALE, MASKED))
    scores = jnp.concatenate(parts, axis=1)
    peak = jnp.maximum(jnp.max(scores, axis=1, keepdims=True), jnp.maximum(now, before))
    peak = jnp.maximum(peak, other_peak)
    raised, now, before = jnp.exp(scores - peak), jnp.exp(now - peak), jnp.exp(before - peak)
    other = jnp.exp(other_peak - peak)
    inverse = 1.0 / (jnp.sum(raised, axis=1, keepdims=True) + now + before + other * other_total)
    weights = (raised * inverse).astype(jnp.bfloat16)
    now = (now * inverse).astype(jnp.bfloat16).astype(jnp.float32)
    before = (before * inverse).astype(jnp.bfloat16).astype(jnp.float32)
    mixed = mixed.reshape(rows, HD) * (other * inverse)
    out = []
    for h in range(KVH):
        part = slice(h * span, (h + 1) * span)
        own = mixed[part] + dot(weights[part], cache[:, (2 * h + 1) * HD : (2 * h + 2) * HD])
        last = pltpu.roll(values[h], ROWS_DEV, 0)
        for hh in range(GQ):
            some = slice(h * span + hh * GROUP_ROWS, h * span + (hh + 1) * GROUP_ROWS)
            line = own[hh * GROUP_ROWS : (hh + 1) * GROUP_ROWS]
            out.append(line + now[some] * values[h] + before[some] * last)
    out = jnp.concatenate(out, axis=1)
    for k in range(ROWS_DEV):
        steps = [out[s * ROWS_DEV + k : s * ROWS_DEV + k + 1] for s in range(STEPS)]
        o_ref[k] = jnp.concatenate(steps, axis=0).astype(jnp.bfloat16)


def decode_attention(ints, cache, msgs, parts, n, lq):
    vmem, hbm = pl.BlockSpec(memory_space=VMEM), pl.BlockSpec(memory_space=pl.ANY)
    rows = QH * GROUP_ROWS
    return pl.pallas_call(
        functools.partial(owner_part, n, lq),
        in_specs=[hbm] * 8,
        out_specs=vmem,
        out_shape=jax.ShapeDtypeStruct((ROWS_DEV, STEPS, QH * HD), jnp.bfloat16),
        scratch_shapes=[
            VMEM(cache.shape, jnp.bfloat16),
            VMEM(msgs.shape, msgs.dtype),
            VMEM(parts.shape, parts.dtype),
            pltpu.SemaphoreType.DMA((DEVICE_SLOTS + 2,)),
            SMEM((DEVICE_SLOTS,), jnp.int32),
            SMEM((DEVICE_SLOTS,), jnp.int32),
        ]
        + int_scratch(ints),
        compiler_params=pltpu.CompilerParams(vmem_limit_bytes=52 * MIB),
        cost_estimate=pl.CostEstimate(flops=4 * rows * HD * 768, bytes_accessed=4 * MIB, transcendentals=rows * 768),
        name="decode_attention",
    )(*ints, cache, msgs, parts)


def local(
    prompt_x,
    q_weight,
    kv_weight,
    prompt_blocks,
    finished,
    placement,
    page_table,
    row_lens,
    kv_cache,
    decode_x,
):
    n = lax.axis_size("tp")
    lq = q_weight.shape[1] // HD
    share = GQ // lq
    if share > 1:
        sets = [[k * share + i for i in range(share)] for k in range(n // share)]
        kv_weight = lax.all_gather(kv_weight, "tp", axis=1, tiled=True, axis_index_groups=sets)
    cache = kv_cache.reshape(-1, kv_cache.shape[2])
    dx = decode_x.reshape(-1, decode_x.shape[2])
    placement = placement.transpose(0, 2, 1)
    page_table = page_table.transpose(1, 0)
    ints = (prompt_blocks, finished, placement, page_table, row_lens)
    first, size = 512, 512
    q, kv, own, msgs = project_all(ints, dx, prompt_x, q_weight, kv_weight, n, first, size)
    kv_other = lax.ppermute(kv, "pool", [(0, 1), (1, 0)])
    msgs = lax.all_to_all(msgs, "tp", split_axis=0, concat_axis=0, tiled=True)
    prompt_attn = prompt_attention(prompt_blocks, q, kv, 0)
    handed, prompt_attn = handed_attention(kv_other, own, msgs, prompt_attn, n, lq)
    parts = lax.all_to_all(handed, "tp", split_axis=0, concat_axis=0, tiled=True)
    prompt_attn = prompt_attention(prompt_blocks, q, kv, 1, prompt_attn)
    decode_attn = decode_attention(ints, cache, msgs, parts, n, lq)
    return prompt_attn, decode_attn.transpose(1, 0, 2)


def solution(mesh):
    return jax.shard_map(
        local,
        mesh=mesh,
        in_specs=(
            P(("rep", "pool"), None),
            P(None, "tp"),
            P(None, "tp"),
            P("rep", None),
            P("rep", None),
            P("rep", None, None),
            P(("rep", "pool", "tp"), None),
            P(("rep", "pool", "tp")),
            P(("rep", "pool", "tp"), None, None),
            P(None, ("rep", "pool"), None),
        ),
        out_specs=(P(("rep", "pool"), "tp"), P(None, ("rep", "pool", "tp"), None)),
        check_vma=False,
    )
```

```python
import functools

import jax
import jax.numpy as jnp
from jax import lax
from jax.experimental import pallas as pl
from jax.experimental.pallas import tpu as pltpu
from jax.sharding import PartitionSpec as P

QH = 32
KVH = 8
GQ = QH // KVH
HD = 128
BLOCK_TOKENS = 128
PTOK = 2048
NPROMPT = 3
MOST_BLOCKS = 8
PAGES = 2
STEPS = 2
NBLK = 16
DEVICE_SLOTS = 6
ROWS_DEV = 3
GROUP_ROWS = 8
KEY_VALUE_COLUMNS = 2048
SCALE = HD ** (-0.5)
MASKED = -1e30
PIECES = 5
STRIPS = 4
LOG2E = 1.4426950408889634
AHEAD = 2
MIB = 1 << 20
VMEM = pltpu.VMEM
SMEM = pltpu.SMEM


def dot(a, b):
    return jnp.dot(a, b, preferred_element_type=jnp.float32)


def dot_t(a, b):
    return lax.dot_general(a, b, (((1,), (1,)), ((), ())), preferred_element_type=jnp.float32)


def iota(shape, axis):
    return lax.broadcasted_iota(jnp.int32, shape, axis)


def row_of(rs):
    return jnp.where(rs >= 2 * ROWS_DEV, ROWS_DEV, jnp.where(rs >= ROWS_DEV, rs - ROWS_DEV, rs))


def block_of_pages(counts, done, placed, table):
    me = lax.axis_index("tp")
    other = 1 - lax.axis_index("pool")
    first_end = counts[other, 0]
    second_end = first_end + counts[other, 1]
    found = [[jnp.int32(-1)] * PAGES for _ in range(ROWS_DEV)]
    for b in range(NBLK):
        live = jnp.where(
            b < first_end, done[other, 0], jnp.where(b < second_end, done[other, 1], done[other, 2])
        )
        slot = jnp.where((live > 0) & (placed[other, 0, b] == me), placed[other, 1, b], -1)
        for r in range(ROWS_DEV):
            for p in range(PAGES):
                found[r][p] = jnp.where(slot == table[p, r], b, found[r][p])
    return found


def by_row(r, values, rest):
    out = jnp.full(r.shape, rest, jnp.int32)
    for k in range(ROWS_DEV):
        out = jnp.where(r == k, values[k], out)
    return out


def int_scratch(ints):
    return [SMEM(x.shape, jnp.int32) for x in ints] + [pltpu.SemaphoreType.DMA((len(ints),))]


def int_copies(sources, targets, sems):
    return [pltpu.make_async_copy(a, b, sems.at[i]) for i, (a, b) in enumerate(zip(sources, targets))]


def start_all(copies):
    for i, copy in enumerate(copies):
        copy.start(priority=i % 2)


def project(n, lq, first, size, *refs):
    dx_hbm, x_hbm, wq_hbm, wkv_hbm = refs[5:9]
    q_hbm, kv_hbm, own_ref, msg_ref = refs[9:13]
    x0, xs, w, q_out, kv_out, x_sems, w_sems, out_sems = refs[13:21]
    counts, done, placed, table, lens, int_sems = refs[21:]
    ints = int_copies(refs[:5], refs[21:26], int_sems)
    depth = w.shape[0]
    count = xs.shape[0]
    cq = lq * HD
    piece = depth // PIECES
    own_rows = dx_hbm.shape[0]
    step = pl.program_id(0)

    def piece_copies(c):
        part = pl.ds(c * piece, piece)
        return [
            pltpu.make_async_copy(x_hbm.at[pl.ds(0, first), part], x0.at[pl.ds(0, first), part], w_sems.at[0, c]),
            pltpu.make_async_copy(wq_hbm.at[part], w.at[part, pl.ds(0, cq)], w_sems.at[2, c]),
            pltpu.make_async_copy(wkv_hbm.at[part], w.at[part, pl.ds(cq, 2 * HD)], w_sems.at[3, c]),
            pltpu.make_async_copy(dx_hbm.at[:, part], x0.at[pl.ds(first, own_rows), part], w_sems.at[1, c]),
        ]

    def x_copies(k):
        strip = size // STRIPS
        copies = []
        for i in range(STRIPS):
            rows = pl.ds(pl.multiple_of(first + k * size + i * strip, 16), strip)
            copies.append(
                pltpu.make_async_copy(x_hbm.at[rows], xs.at[k, pl.ds(i * strip, strip)], x_sems.at[k, i])
            )
        return copies

    def out_copies(k):
        if isinstance(k, int):
            rows = pl.ds(0, first)
        else:
            rows = pl.ds(pl.multiple_of(first + (k - 1) * size, 64), size)
        return [
            pltpu.make_async_copy(q_out.at[rows], q_hbm.at[rows], out_sems.at[0, k]),
            pltpu.make_async_copy(kv_out.at[rows], kv_hbm.at[rows], out_sems.at[1, k]),
        ]

    def keep(total, rows):
        q_out[rows, :] = total[:, :cq].astype(jnp.bfloat16)
        kv_out[rows, :] = total[:, cq:].astype(jnp.bfloat16)

    @pl.when(step == 0)
    def _():
        for c in range(AHEAD):
            start_all(piece_copies(c))
        for copy in ints:
            copy.start()
        total = 0.0
        for c in range(PIECES):
            for copy in piece_copies(c):
                copy.wait()
            if c + AHEAD < PIECES:
                start_all(piece_copies(c + AHEAD))
            if c + AHEAD >= PIECES:
                start_all(x_copies(c + AHEAD - PIECES))
            part = slice(c * piece, (c + 1) * piece)
            total += dot(x0[:, part], w[part, :])
        keep(total[:first], pl.ds(0, first))
        for copy in out_copies(0):
            copy.start()
        shape = (n * GROUP_ROWS, own_rows)
        to, fro = iota(shape, 0), iota(shape, 1)
        owner, rs = to // GROUP_ROWS, to % GROUP_ROWS
        wanted = owner * ROWS_DEV + row_of(rs) + jnp.where(rs >= ROWS_DEV, ROWS_DEV * n, 0)
        pick = ((fro == wanted) & (rs < STEPS * ROWS_DEV)).astype(jnp.float32).astype(jnp.bfloat16)
        own = dot(pick, total[first:].astype(jnp.bfloat16))
        own_ref[...] = own.astype(jnp.bfloat16)
        for copy in ints:
            copy.wait()
        found = block_of_pages(counts, done, placed, table)
        lane = iota((n * GROUP_ROWS, HD), 1)
        r = row_of(lane % GROUP_ROWS)
        kind = lane // GROUP_ROWS
        facts = jnp.where(
            kind == 0,
            by_row(r, [found[i][0] for i in range(ROWS_DEV)], -1),
            jnp.where(
                kind == 1,
                by_row(r, [found[i][1] for i in range(ROWS_DEV)], -1),
                by_row(r, [lens[i] for i in range(ROWS_DEV)], 0),
            ),
        ).astype(jnp.float32)
        sixth = iota((n * GROUP_ROWS, HD), 0) % GROUP_ROWS == 6
        msg_ref[:, :HD] = jnp.where(sixth, facts, own[:, :HD]).astype(jnp.bfloat16)
        msg_ref[:, HD:] = own[:, HD:].astype(jnp.bfloat16)

    @pl.when((step > 0) & (step + AHEAD <= count))
    def _():
        start_all(x_copies(step + AHEAD - 1))

    @pl.when(step > 0)
    def _():
        for copy in x_copies(step - 1):
            copy.wait()
        keep(dot(xs[step - 1], w[...]), pl.ds(pl.multiple_of(first + (step - 1) * size, 64), size))
        for copy in out_copies(step):
            copy.start()

    @pl.when(step == count)
    def _():
        for copy in out_copies(0):
            copy.wait()
        for k in range(1, count + 1):
            for copy in out_copies(jnp.int32(k)):
                copy.wait()


def project_all(ints, dx, x, wq, wkv, n, first, size):
    rows, depth = x.shape
    cq, ckv = wq.shape[1], wkv.shape[1]
    lq = cq // HD
    count = (rows - first) // size
    vmem, hbm = pl.BlockSpec(memory_space=VMEM), pl.BlockSpec(memory_space=pl.ANY)
    return pl.pallas_call(
        functools.partial(project, n, lq, first, size),
        grid=(1 + count,),
        in_specs=[hbm] * 9,
        out_specs=[hbm, hbm, vmem, vmem],
        out_shape=[
            jax.ShapeDtypeStruct((rows, cq), jnp.bfloat16),
            jax.ShapeDtypeStruct((rows, ckv), jnp.bfloat16),
            jax.ShapeDtypeStruct((n * GROUP_ROWS, cq + ckv), jnp.bfloat16),
            jax.ShapeDtypeStruct((n * GROUP_ROWS, cq + ckv), jnp.bfloat16),
        ],
        scratch_shapes=[
            VMEM((first + dx.shape[0], depth), jnp.bfloat16),
            VMEM((count, size, depth), jnp.bfloat16),
            VMEM((depth, cq + ckv), jnp.bfloat16),
            VMEM((rows, cq), jnp.bfloat16),
            VMEM((rows, ckv), jnp.bfloat16),
            pltpu.SemaphoreType.DMA((count, STRIPS)),
            pltpu.SemaphoreType.DMA((4, PIECES)),
            pltpu.SemaphoreType.DMA((2, count + 1)),
        ]
        + int_scratch(ints),
        compiler_params=pltpu.CompilerParams(vmem_limit_bytes=62 * MIB),
        cost_estimate=pl.CostEstimate(
            flops=2 * rows * depth * (cq + ckv),
            bytes_accessed=2 * (rows + cq + ckv) * depth + 2 * rows * (cq + ckv),
            transcendentals=0,
        ),
        name="project",
    )(*ints, dx, x, wq, wkv)


def attend_prompt(lq, half, counts, q_hbm, kv_hbm, *refs):
    o_hbm, qs, kvs, outs, sems = refs[-5:]
    group = lax.axis_index("pool")
    c0, c1 = counts[group, 0], counts[group, 1]
    big = jnp.where(c0 == MOST_BLOCKS, 0, jnp.where(c1 == MOST_BLOCKS, c0, c0 + c1))
    cut = jnp.where(c0 == MOST_BLOCKS, c1, c0)
    loads, stores = [], []
    strip, early = (4, 3) if half == 0 else (1, 5)
    for j in range(0, MOST_BLOCKS, strip):
        block = big + j if half == 0 else j + jnp.where(j >= big, MOST_BLOCKS, 0)
        rows = pl.ds(pl.multiple_of(block * BLOCK_TOKENS, BLOCK_TOKENS), strip * BLOCK_TOKENS)
        here = pl.ds(j * BLOCK_TOKENS, strip * BLOCK_TOKENS)
        loads.append(pltpu.make_async_copy(kv_hbm.at[rows], kvs.at[here], sems.at[0, j]))
        loads.append(pltpu.make_async_copy(q_hbm.at[rows], qs.at[here], sems.at[1, j]))
        stores.append(pltpu.make_async_copy(outs.at[here], o_hbm.at[rows], sems.at[2, j]))
    start_all(loads)
    near = len(loads) // 2
    for copy in loads[:near]:
        copy.wait()
    shape = (BLOCK_TOKENS, lq * BLOCK_TOKENS)
    causal = iota(shape, 0) <= iota(shape, 1) % BLOCK_TOKENS
    tokens = MOST_BLOCKS * BLOCK_TOKENS
    flipped = kvs[: tokens // 2, HD:].T

    def scores_of(j):
        q = qs[j * BLOCK_TOKENS : (j + 1) * BLOCK_TOKENS, :]
        q = jnp.concatenate([q[:, h * HD : (h + 1) * HD] for h in range(lq)], axis=0)
        return dot_t(kvs[: (j + 1) * BLOCK_TOKENS, :HD], q)

    scores = scores_of(0)
    for j in range(MOST_BLOCKS):
        if j + 1 == MOST_BLOCKS // 2:
            for copy in loads[near:]:
                copy.wait()
            flipped = jnp.concatenate([flipped, kvs[tokens // 2 :, HD:].T], axis=1)
        later = scores_of(j + 1) if j + 1 < MOST_BLOCKS else None
        weights = []
        for h in range(lq):
            cols = slice(h * BLOCK_TOKENS, (h + 1) * BLOCK_TOKENS)
            tiles = []
            for i in range(j + 1):
                tile = scores[i * BLOCK_TOKENS : (i + 1) * BLOCK_TOKENS, cols]
                if i == j:
                    tile = jnp.where(causal[:, cols], tile, MASKED)
                elif half == 1:
                    tile = tile + jnp.where((i < cut) & (cut <= j), MASKED, 0.0)
                tiles.append(tile)
            peak = jnp.max(functools.reduce(jnp.maximum, tiles), axis=0, keepdims=True)
            raised = [jnp.exp2((tile - peak) * (SCALE * LOG2E)) for tile in tiles]
            inverse = 1.0 / jnp.sum(functools.reduce(jnp.add, raised), axis=0, keepdims=True)
            weights.append(jnp.concatenate([(t * inverse).astype(jnp.bfloat16) for t in raised], axis=0))
        mixed = dot(flipped[:, : (j + 1) * BLOCK_TOKENS], jnp.concatenate(weights, axis=1))
        mixed = mixed.astype(jnp.bfloat16)
        for h in range(lq):
            part = mixed[:, h * BLOCK_TOKENS : (h + 1) * BLOCK_TOKENS].T
            outs[j * BLOCK_TOKENS : (j + 1) * BLOCK_TOKENS, h * HD : (h + 1) * HD] = part
        scores = later
        if j == early:
            for copy in stores[: (j + 1) // strip]:
                copy.start()
    for copy in stores[(early + 1) // strip :]:
        copy.start()
    for copy in stores:
        copy.wait()


def prompt_attention(counts, q, kv, half, so_far=None):
    rows, cq = q.shape
    hbm = pl.BlockSpec(memory_space=pl.ANY)
    more = () if so_far is None else (so_far,)
    tokens = MOST_BLOCKS * BLOCK_TOKENS
    return pl.pallas_call(
        functools.partial(attend_prompt, cq // HD, half),
        in_specs=[pl.BlockSpec(memory_space=SMEM), hbm, hbm] + [hbm] * len(more),
        out_specs=hbm,
        out_shape=jax.ShapeDtypeStruct((rows, cq), jnp.bfloat16),
        scratch_shapes=[
            VMEM((tokens, cq), jnp.bfloat16),
            VMEM((tokens, 2 * HD), jnp.bfloat16),
            VMEM((tokens, cq), jnp.bfloat16),
            pltpu.SemaphoreType.DMA((3, MOST_BLOCKS)),
        ],
        input_output_aliases={3: 0} if more else {},
        compiler_params=pltpu.CompilerParams(vmem_limit_bytes=62 * MIB),
        cost_estimate=pl.CostEstimate(flops=2 * rows * rows * cq, bytes_accessed=4 * rows * cq, transcendentals=rows * rows // 2),
        name="long_prompt" if half == 0 else "short_prompts",
    )(counts, q, kv, *more)


def row_head(n, lq, h, hh):
    at = h * GQ + hh
    return at // lq, at % lq


def handed_part(n, lq, kv_ref, own_ref, msg_ref, _, o_ref, __):
    rows = lq * n * GROUP_ROWS
    shape = (rows, HD)
    at_row, lane = iota(shape, 0), iota(shape, 1)
    rs = at_row % GROUP_ROWS
    facts = msg_ref[:, :HD].astype(jnp.float32).reshape(n, GROUP_ROWS, HD)[:, 6:7, :]
    facts = jnp.broadcast_to(facts, (n, GROUP_ROWS, HD)).reshape(n * GROUP_ROWS, HD)
    facts = jnp.concatenate([facts] * lq, axis=0)

    def column(kind):
        return jnp.sum(jnp.where(lane == kind * GROUP_ROWS + rs, facts, 0.0), axis=1, keepdims=True)

    first_block, second_block, length = [column(kind) for kind in range(3)]
    own = own_ref[...]
    queries = jnp.concatenate([own[:, h * HD : (h + 1) * HD] for h in range(lq)], axis=0)
    scores = dot_t(queries, kv_ref[:, :HD]) * SCALE
    lane_f = lane.astype(jnp.float32)
    parts = []
    for b in range(NBLK):
        limit = jnp.where(
            first_block == b, length, jnp.where(second_block == b, length - BLOCK_TOKENS, 0.0)
        )
        part = scores[:, b * BLOCK_TOKENS : (b + 1) * BLOCK_TOKENS]
        parts.append(jnp.where(lane_f < limit, part, MASKED))
    scores = jnp.concatenate(parts, axis=1)
    top = jnp.max(scores, axis=1, keepdims=True)
    raised = jnp.exp(scores - top)
    total = jnp.sum(raised, axis=1, keepdims=True)
    near = raised.astype(jnp.bfloat16)
    rest = (raised - near.astype(jnp.float32)).astype(jnp.bfloat16)
    values = kv_ref[:, HD:]
    mixed = (dot(near, values) + dot(rest, values)).reshape(lq * n, GROUP_ROWS, HD)

    def line(col):
        spread = jnp.where(lane == rs, col, 0.0).reshape(lq * n, GROUP_ROWS, HD)
        return jnp.sum(spread, axis=1, keepdims=True)

    rs3 = rs.reshape(lq * n, GROUP_ROWS, HD)
    mixed = jnp.where(rs3 == 6, line(top), jnp.where(rs3 == 7, line(total), mixed))
    for h in range(lq):
        o_ref[:, h * GROUP_ROWS : (h + 1) * GROUP_ROWS, :] = mixed[h * n : (h + 1) * n]


def handed_attention(kv, own, msgs, prompt_attn, n, lq):
    rows = lq * n * GROUP_ROWS
    vmem, hbm = pl.BlockSpec(memory_space=VMEM), pl.BlockSpec(memory_space=pl.ANY)
    return pl.pallas_call(
        functools.partial(handed_part, n, lq),
        in_specs=[vmem] * 3 + [hbm],
        out_specs=[vmem, hbm],
        out_shape=[
            jax.ShapeDtypeStruct((n, lq * GROUP_ROWS, HD), jnp.float32),
            jax.ShapeDtypeStruct(prompt_attn.shape, prompt_attn.dtype),
        ],
        input_output_aliases={3: 1},
        compiler_params=pltpu.CompilerParams(vmem_limit_bytes=24 * MIB),
        cost_estimate=pl.CostEstimate(flops=6 * rows * HD * PTOK, bytes_accessed=2 * MIB, transcendentals=rows * PTOK),
        name="handed_attention",
    )(kv, own, msgs, prompt_attn)


def owner_part(n, lq, *refs):
    cache_hbm, msgs_hbm, handed_hbm, o_ref, cache, msgs, handed, sems, slot_row, slot_limit = refs[5:15]
    counts, done, placed, table, lens, int_sems = refs[15:]
    ints = int_copies(refs[:5], refs[15:20], int_sems)
    first = [
        pltpu.make_async_copy(msgs_hbm, msgs, sems.at[DEVICE_SLOTS]),
        pltpu.make_async_copy(handed_hbm, handed, sems.at[DEVICE_SLOTS + 1]),
    ]
    for copy in first:
        copy.start()
    loads = []
    for slot in range(DEVICE_SLOTS):
        part = pl.ds(slot * BLOCK_TOKENS, BLOCK_TOKENS)
        loads.append(pltpu.make_async_copy(cache_hbm.at[part], cache.at[part], sems.at[slot]))
    start_all(loads)
    for copy in ints:
        copy.start()
    for copy in first:
        copy.wait()
    held = msgs[...].astype(jnp.float32)

    def tile(t, k):
        return held[t * GROUP_ROWS : (t + 1) * GROUP_ROWS, k * HD : (k + 1) * HD]

    groups = QH
    rows = groups * GROUP_ROWS
    span = GQ * GROUP_ROWS
    queries, keys, values = [], [], []
    for h in range(KVH):
        for hh in range(GQ):
            t, at = row_head(n, lq, h, hh)
            queries.append(tile(t, at))
        t, _ = row_head(n, lq, h, 0)
        keys += [tile(t, lq)] * GQ
        values.append(tile(t, lq + 1))
    queries = jnp.concatenate(queries, axis=0)
    earlier = jnp.concatenate([pltpu.roll(key, ROWS_DEV, 0) for key in keys], axis=0)
    keys = jnp.concatenate(keys, axis=0)
    at_row, lane = iota((rows, HD), 0), iota((rows, HD), 1)
    r = row_of(at_row % GROUP_ROWS)
    rounded = queries.astype(jnp.bfloat16)
    now = jnp.sum(queries * keys, axis=1, keepdims=True) * SCALE
    before = jnp.sum(queries * earlier, axis=1, keepdims=True) * SCALE
    rs1 = iota((rows, 1), 0) % GROUP_ROWS
    before = jnp.where((rs1 >= ROWS_DEV) & (rs1 < STEPS * ROWS_DEV), before, MASKED)
    mixed = handed[...].reshape(groups, GROUP_ROWS, HD)
    shape = (groups, GROUP_ROWS, HD)
    mine = iota(shape, 1) == iota(shape, 2)

    def column(at):
        line = jnp.broadcast_to(mixed[:, at : at + 1, :], shape)
        return jnp.sum(jnp.where(mine, line, 0.0), axis=2, keepdims=True).reshape(rows, 1)

    other_peak, other_total = column(6), column(7)
    for copy in ints:
        copy.wait()
    found = block_of_pages(counts, done, placed, table)
    for k in range(ROWS_DEV):
        for p in range(PAGES):
            slot_row[table[p, k]] = jnp.int32(k)
            slot_limit[table[p, k]] = jnp.where(found[k][p] < 0, lens[k] - p * BLOCK_TOKENS, 0)
    for load in loads:
        load.wait()
    scores = jnp.concatenate(
        [dot_t(rounded[h * span : (h + 1) * span], cache[:, 2 * h * HD : (2 * h + 1) * HD]) for h in range(KVH)],
        axis=0,
    )
    parts = []
    for slot in range(DEVICE_SLOTS):
        part = scores[:, slot * BLOCK_TOKENS : (slot + 1) * BLOCK_TOKENS]
        usable = (r == slot_row[slot]) & (lane < slot_limit[slot])
        parts.append(jnp.where(usable, part * SCALE, MASKED))
    scores = jnp.concatenate(parts, axis=1)
    peak = jnp.maximum(jnp.max(scores, axis=1, keepdims=True), jnp.maximum(now, before))
    peak = jnp.maximum(peak, other_peak)
    raised, now, before = jnp.exp(scores - peak), jnp.exp(now - peak), jnp.exp(before - peak)
    other = jnp.exp(other_peak - peak)
    inverse = 1.0 / (jnp.sum(raised, axis=1, keepdims=True) + now + before + other * other_total)
    weights = (raised * inverse).astype(jnp.bfloat16)
    now = (now * inverse).astype(jnp.bfloat16).astype(jnp.float32)
    before = (before * inverse).astype(jnp.bfloat16).astype(jnp.float32)
    mixed = mixed.reshape(rows, HD) * (other * inverse)
    out = []
    for h in range(KVH):
        part = slice(h * span, (h + 1) * span)
        own = mixed[part] + dot(weights[part], cache[:, (2 * h + 1) * HD : (2 * h + 2) * HD])
        last = pltpu.roll(values[h], ROWS_DEV, 0)
        for hh in range(GQ):
            some = slice(h * span + hh * GROUP_ROWS, h * span + (hh + 1) * GROUP_ROWS)
            line = own[hh * GROUP_ROWS : (hh + 1) * GROUP_ROWS]
            out.append(line + now[some] * values[h] + before[some] * last)
    out = jnp.concatenate(out, axis=1)
    for k in range(ROWS_DEV):
        steps = [out[s * ROWS_DEV + k : s * ROWS_DEV + k + 1] for s in range(STEPS)]
        o_ref[k] = jnp.concatenate(steps, axis=0).astype(jnp.bfloat16)


def decode_attention(ints, cache, msgs, parts, n, lq):
    vmem, hbm = pl.BlockSpec(memory_space=VMEM), pl.BlockSpec(memory_space=pl.ANY)
    rows = QH * GROUP_ROWS
    return pl.pallas_call(
        functools.partial(owner_part, n, lq),
        in_specs=[hbm] * 8,
        out_specs=vmem,
        out_shape=jax.ShapeDtypeStruct((ROWS_DEV, STEPS, QH * HD), jnp.bfloat16),
        scratch_shapes=[
            VMEM(cache.shape, jnp.bfloat16),
            VMEM(msgs.shape, msgs.dtype),
            VMEM(parts.shape, parts.dtype),
            pltpu.SemaphoreType.DMA((DEVICE_SLOTS + 2,)),
            SMEM((DEVICE_SLOTS,), jnp.int32),
            SMEM((DEVICE_SLOTS,), jnp.int32),
        ]
        + int_scratch(ints),
        compiler_params=pltpu.CompilerParams(vmem_limit_bytes=52 * MIB),
        cost_estimate=pl.CostEstimate(flops=4 * rows * HD * 768, bytes_accessed=4 * MIB, transcendentals=rows * 768),
        name="decode_attention",
    )(*ints, cache, msgs, parts)


def local(
    prompt_x,
    q_weight,
    kv_weight,
    prompt_blocks,
    finished,
    placement,
    page_table,
    row_lens,
    kv_cache,
    decode_x,
):
    n = lax.axis_size("tp")
    lq = q_weight.shape[1] // HD
    share = GQ // lq
    if share > 1:
        sets = [[k * share + i for i in range(share)] for k in range(n // share)]
        kv_weight = lax.all_gather(kv_weight, "tp", axis=1, tiled=True, axis_index_groups=sets)
    cache = kv_cache.reshape(-1, kv_cache.shape[2])
    dx = decode_x.reshape(-1, decode_x.shape[2])
    placement = placement.transpose(0, 2, 1)
    page_table = page_table.transpose(1, 0)
    ints = (prompt_blocks, finished, placement, page_table, row_lens)
    first, size = 256, 448
    q, kv, own, msgs = project_all(ints, dx, prompt_x, q_weight, kv_weight, n, first, size)
    kv_other = lax.ppermute(kv, "pool", [(0, 1), (1, 0)])
    msgs = lax.all_to_all(msgs, "tp", split_axis=0, concat_axis=0, tiled=True)
    prompt_attn = prompt_attention(prompt_blocks, q, kv, 0)
    handed, prompt_attn = handed_attention(kv_other, own, msgs, prompt_attn, n, lq)
    parts = lax.all_to_all(handed, "tp", split_axis=0, concat_axis=0, tiled=True)
    prompt_attn = prompt_attention(prompt_blocks, q, kv, 1, prompt_attn)
    decode_attn = decode_attention(ints, cache, msgs, parts, n, lq)
    return prompt_attn, decode_attn.transpose(1, 0, 2)


def solution(mesh):
    return jax.shard_map(
        local,
        mesh=mesh,
        in_specs=(
            P(("rep", "pool"), None),
            P(None, "tp"),
            P(None, "tp"),
            P("rep", None),
            P("rep", None),
            P("rep", None, None),
            P(("rep", "pool", "tp"), None),
            P(("rep", "pool", "tp")),
            P(("rep", "pool", "tp"), None, None),
            P(None, ("rep", "pool"), None),
        ),
        out_specs=(P(("rep", "pool"), "tp"), P(None, ("rep", "pool", "tp"), None)),
        check_vma=False,
    )
```

```python
import functools

import jax
import jax.numpy as jnp
from jax import lax
from jax.experimental import pallas as pl
from jax.experimental.pallas import tpu as pltpu
from jax.sharding import PartitionSpec as P

QH = 32
KVH = 8
GQ = QH // KVH
HD = 128
BLOCK_TOKENS = 128
PTOK = 2048
NPROMPT = 3
MOST_BLOCKS = 8
PAGES = 2
STEPS = 2
NBLK = 16
DEVICE_SLOTS = 6
ROWS_DEV = 3
GROUP_ROWS = 8
KEY_VALUE_COLUMNS = 2048
SCALE = HD ** (-0.5)
MASKED = -1e30
PIECES = 5
STRIPS = 4
WIDE = 2048
LOG2E = 1.4426950408889634
AHEAD = 2
MIB = 1 << 20
VMEM = pltpu.VMEM
SMEM = pltpu.SMEM


def dot(a, b):
    return jnp.dot(a, b, preferred_element_type=jnp.float32)


def dot_t(a, b):
    return lax.dot_general(a, b, (((1,), (1,)), ((), ())), preferred_element_type=jnp.float32)


def iota(shape, axis):
    return lax.broadcasted_iota(jnp.int32, shape, axis)


def row_of(rs):
    return jnp.where(rs >= 2 * ROWS_DEV, ROWS_DEV, jnp.where(rs >= ROWS_DEV, rs - ROWS_DEV, rs))


def block_of_pages(counts, done, placed, table):
    me = lax.axis_index("tp")
    other = 1 - lax.axis_index("pool")
    first_end = counts[other, 0]
    second_end = first_end + counts[other, 1]
    found = [[jnp.int32(-1)] * PAGES for _ in range(ROWS_DEV)]
    for b in range(NBLK):
        live = jnp.where(
            b < first_end, done[other, 0], jnp.where(b < second_end, done[other, 1], done[other, 2])
        )
        slot = jnp.where((live > 0) & (placed[other, 0, b] == me), placed[other, 1, b], -1)
        for r in range(ROWS_DEV):
            for p in range(PAGES):
                found[r][p] = jnp.where(slot == table[p, r], b, found[r][p])
    return found


def by_row(r, values, rest):
    out = jnp.full(r.shape, rest, jnp.int32)
    for k in range(ROWS_DEV):
        out = jnp.where(r == k, values[k], out)
    return out


def int_scratch(ints):
    return [SMEM(x.shape, jnp.int32) for x in ints] + [pltpu.SemaphoreType.DMA((len(ints),))]


def int_copies(sources, targets, sems):
    return [pltpu.make_async_copy(a, b, sems.at[i]) for i, (a, b) in enumerate(zip(sources, targets))]


def project(n, lq, first, size, *refs):
    dx_hbm, x_hbm, wq_hbm, wkv_hbm = refs[5:9]
    q_hbm, kv_hbm, own_ref, msg_ref = refs[9:13]
    x0, xs, w, q_out, kv_out, x_sems, w_sems, out_sems = refs[13:21]
    counts, done, placed, table, lens, int_sems = refs[21:]
    ints = int_copies(refs[:5], refs[21:26], int_sems)
    depth = w.shape[0]
    count = xs.shape[0]
    cq = lq * HD
    piece = depth // PIECES
    own_rows = dx_hbm.shape[0]
    step = pl.program_id(0)

    def piece_copies(c):
        part = pl.ds(c * piece, piece)
        return [
            pltpu.make_async_copy(x_hbm.at[pl.ds(0, first), part], x0.at[pl.ds(0, first), part], w_sems.at[0, c]),
            pltpu.make_async_copy(dx_hbm.at[:, part], x0.at[pl.ds(first, own_rows), part], w_sems.at[1, c]),
            pltpu.make_async_copy(wq_hbm.at[part], w.at[part, pl.ds(0, cq)], w_sems.at[2, c]),
            pltpu.make_async_copy(wkv_hbm.at[part], w.at[part, pl.ds(cq, 2 * HD)], w_sems.at[3, c]),
        ]

    def x_copies(k):
        strip = size // STRIPS
        copies = []
        for i in range(STRIPS):
            rows = pl.ds(pl.multiple_of(first + k * size + i * strip, 16), strip)
            copies.append(
                pltpu.make_async_copy(x_hbm.at[rows], xs.at[k, pl.ds(i * strip, strip)], x_sems.at[k, i])
            )
        return copies

    def out_copies(k):
        if isinstance(k, int):
            rows = pl.ds(0, first)
        else:
            rows = pl.ds(pl.multiple_of(first + (k - 1) * size, 64), size)
        return [
            pltpu.make_async_copy(q_out.at[rows], q_hbm.at[rows, pl.ds(0, cq)], out_sems.at[0, k]),
            pltpu.make_async_copy(kv_out.at[rows], q_hbm.at[rows, pl.ds(cq, 2 * HD)], out_sems.at[1, k]),
            pltpu.make_async_copy(kv_out.at[rows], kv_hbm.at[rows], out_sems.at[2, k]),
        ]

    def keep(total, rows):
        q_out[rows, :] = total[:, :cq].astype(jnp.bfloat16)
        kv_out[rows, :] = total[:, cq:].astype(jnp.bfloat16)

    @pl.when(step == 0)
    def _():
        for c in range(AHEAD):
            for copy in piece_copies(c):
                copy.start()
        for copy in ints:
            copy.start()
        total = 0.0
        for c in range(PIECES):
            for copy in piece_copies(c):
                copy.wait()
            if c + AHEAD < PIECES:
                for copy in piece_copies(c + AHEAD):
                    copy.start()
            if c + AHEAD >= PIECES:
                for copy in x_copies(c + AHEAD - PIECES):
                    copy.start()
            part = slice(c * piece, (c + 1) * piece)
            total += dot(x0[:, part], w[part, :])
        keep(total[:first], pl.ds(0, first))
        for copy in out_copies(0):
            copy.start()
        shape = (n * GROUP_ROWS, own_rows)
        to, fro = iota(shape, 0), iota(shape, 1)
        owner, rs = to // GROUP_ROWS, to % GROUP_ROWS
        wanted = owner * ROWS_DEV + row_of(rs) + jnp.where(rs >= ROWS_DEV, ROWS_DEV * n, 0)
        pick = ((fro == wanted) & (rs < STEPS * ROWS_DEV)).astype(jnp.float32).astype(jnp.bfloat16)
        own = dot(pick, total[first:].astype(jnp.bfloat16))
        own_ref[...] = own.astype(jnp.bfloat16)
        for copy in ints:
            copy.wait()
        found = block_of_pages(counts, done, placed, table)
        lane = iota((n * GROUP_ROWS, HD), 1)
        r = row_of(lane % GROUP_ROWS)
        kind = lane // GROUP_ROWS
        facts = jnp.where(
            kind == 0,
            by_row(r, [found[i][0] for i in range(ROWS_DEV)], -1),
            jnp.where(
                kind == 1,
                by_row(r, [found[i][1] for i in range(ROWS_DEV)], -1),
                by_row(r, [lens[i] for i in range(ROWS_DEV)], 0),
            ),
        ).astype(jnp.float32)
        sixth = iota((n * GROUP_ROWS, HD), 0) % GROUP_ROWS == 6
        msg_ref[:, :HD] = jnp.where(sixth, facts, own[:, :HD]).astype(jnp.bfloat16)
        msg_ref[:, HD:] = own[:, HD:].astype(jnp.bfloat16)

    @pl.when((step > 0) & (step + AHEAD <= count))
    def _():
        for copy in x_copies(step + AHEAD - 1):
            copy.start()

    @pl.when(step > 0)
    def _():
        for copy in x_copies(step - 1):
            copy.wait()
        keep(dot(xs[step - 1], w[...]), pl.ds(pl.multiple_of(first + (step - 1) * size, 64), size))
        for copy in out_copies(step):
            copy.start()

    @pl.when(step == count)
    def _():
        for copy in out_copies(0):
            copy.wait()
        for k in range(1, count + 1):
            for copy in out_copies(jnp.int32(k)):
                copy.wait()


def project_all(ints, dx, x, wq, wkv, n, first, size):
    rows, depth = x.shape
    cq, ckv = wq.shape[1], wkv.shape[1]
    lq = cq // HD
    count = (rows - first) // size
    vmem, hbm = pl.BlockSpec(memory_space=VMEM), pl.BlockSpec(memory_space=pl.ANY)
    return pl.pallas_call(
        functools.partial(project, n, lq, first, size),
        grid=(1 + count,),
        in_specs=[hbm] * 9,
        out_specs=[hbm, hbm, vmem, vmem],
        out_shape=[
            jax.ShapeDtypeStruct((rows, WIDE), jnp.bfloat16),
            jax.ShapeDtypeStruct((rows, ckv), jnp.bfloat16),
            jax.ShapeDtypeStruct((n * GROUP_ROWS, cq + ckv), jnp.bfloat16),
            jax.ShapeDtypeStruct((n * GROUP_ROWS, cq + ckv), jnp.bfloat16),
        ],
        scratch_shapes=[
            VMEM((first + dx.shape[0], depth), jnp.bfloat16),
            VMEM((count, size, depth), jnp.bfloat16),
            VMEM((depth, cq + ckv), jnp.bfloat16),
            VMEM((rows, cq), jnp.bfloat16),
            VMEM((rows, ckv), jnp.bfloat16),
            pltpu.SemaphoreType.DMA((count, STRIPS)),
            pltpu.SemaphoreType.DMA((4, PIECES)),
            pltpu.SemaphoreType.DMA((3, count + 1)),
        ]
        + int_scratch(ints),
        compiler_params=pltpu.CompilerParams(vmem_limit_bytes=62 * MIB),
        cost_estimate=pl.CostEstimate(
            flops=2 * rows * depth * (cq + ckv),
            bytes_accessed=2 * (rows + cq + ckv) * depth + 2 * rows * (cq + ckv),
            transcendentals=0,
        ),
        name="project",
    )(*ints, dx, x, wq, wkv)


def attend_prompt(lq, half, counts, q_hbm, *refs):
    o_hbm, qs, kvs, outs, sems = refs[-5:]
    group = lax.axis_index("pool")
    c0, c1 = counts[group, 0], counts[group, 1]
    big = jnp.where(c0 == MOST_BLOCKS, 0, jnp.where(c1 == MOST_BLOCKS, c0, c0 + c1))
    cut = jnp.where(c0 == MOST_BLOCKS, c1, c0)
    loads, stores = [], []
    strip, early = (4, 3) if half == 0 else (1, 5)
    for j in range(0, MOST_BLOCKS, strip):
        block = big + j if half == 0 else j + jnp.where(j >= big, MOST_BLOCKS, 0)
        rows = pl.ds(pl.multiple_of(block * BLOCK_TOKENS, BLOCK_TOKENS), strip * BLOCK_TOKENS)
        here = pl.ds(j * BLOCK_TOKENS, strip * BLOCK_TOKENS)
        cq = lq * HD
        keys_values, queries = q_hbm.at[rows, pl.ds(cq, 2 * HD)], q_hbm.at[rows, pl.ds(0, cq)]
        loads.append(pltpu.make_async_copy(keys_values, kvs.at[here], sems.at[0, j]))
        loads.append(pltpu.make_async_copy(queries, qs.at[here], sems.at[1, j]))
        stores.append(pltpu.make_async_copy(outs.at[here], o_hbm.at[rows], sems.at[2, j]))
    for copy in loads:
        copy.start()
    near = len(loads) // 2
    for copy in loads[:near]:
        copy.wait()
    shape = (BLOCK_TOKENS, lq * BLOCK_TOKENS)
    causal = iota(shape, 0) <= iota(shape, 1) % BLOCK_TOKENS
    tokens = MOST_BLOCKS * BLOCK_TOKENS
    flipped = kvs[: tokens // 2, HD:].T

    def scores_of(j):
        q = qs[j * BLOCK_TOKENS : (j + 1) * BLOCK_TOKENS, :]
        q = jnp.concatenate([q[:, h * HD : (h + 1) * HD] for h in range(lq)], axis=0)
        return dot_t(kvs[: (j + 1) * BLOCK_TOKENS, :HD], q)

    scores = scores_of(0)
    for j in range(MOST_BLOCKS):
        if j + 1 == MOST_BLOCKS // 2:
            for copy in loads[near:]:
                copy.wait()
            flipped = jnp.concatenate([flipped, kvs[tokens // 2 :, HD:].T], axis=1)
        later = scores_of(j + 1) if j + 1 < MOST_BLOCKS else None
        weights = []
        for h in range(lq):
            cols = slice(h * BLOCK_TOKENS, (h + 1) * BLOCK_TOKENS)
            tiles = []
            for i in range(j + 1):
                tile = scores[i * BLOCK_TOKENS : (i + 1) * BLOCK_TOKENS, cols]
                if i == j:
                    tile = jnp.where(causal[:, cols], tile, MASKED)
                elif half == 1:
                    tile = tile + jnp.where((i < cut) & (cut <= j), MASKED, 0.0)
                tiles.append(tile)
            peak = jnp.max(functools.reduce(jnp.maximum, tiles), axis=0, keepdims=True)
            raised = [jnp.exp2((tile - peak) * (SCALE * LOG2E)) for tile in tiles]
            inverse = 1.0 / jnp.sum(functools.reduce(jnp.add, raised), axis=0, keepdims=True)
            weights.append(jnp.concatenate([(t * inverse).astype(jnp.bfloat16) for t in raised], axis=0))
        mixed = dot(flipped[:, : (j + 1) * BLOCK_TOKENS], jnp.concatenate(weights, axis=1))
        mixed = mixed.astype(jnp.bfloat16)
        for h in range(lq):
            part = mixed[:, h * BLOCK_TOKENS : (h + 1) * BLOCK_TOKENS].T
            outs[j * BLOCK_TOKENS : (j + 1) * BLOCK_TOKENS, h * HD : (h + 1) * HD] = part
        scores = later
        if j == early:
            for copy in stores[: (j + 1) // strip]:
                copy.start()
    for copy in stores[(early + 1) // strip :]:
        copy.start()
    for copy in stores:
        copy.wait()


def prompt_attention(counts, q, cq, half, so_far=None):
    rows = q.shape[0]
    hbm = pl.BlockSpec(memory_space=pl.ANY)
    more = () if so_far is None else (so_far,)
    tokens = MOST_BLOCKS * BLOCK_TOKENS
    return pl.pallas_call(
        functools.partial(attend_prompt, cq // HD, half),
        in_specs=[pl.BlockSpec(memory_space=SMEM), hbm] + [hbm] * len(more),
        out_specs=hbm,
        out_shape=jax.ShapeDtypeStruct((rows, cq), jnp.bfloat16),
        scratch_shapes=[
            VMEM((tokens, cq), jnp.bfloat16),
            VMEM((tokens, 2 * HD), jnp.bfloat16),
            VMEM((tokens, cq), jnp.bfloat16),
            pltpu.SemaphoreType.DMA((3, MOST_BLOCKS)),
        ],
        input_output_aliases={2: 0} if more else {},
        compiler_params=pltpu.CompilerParams(vmem_limit_bytes=(62 if half == 0 else 48) * MIB),
        cost_estimate=pl.CostEstimate(flops=2 * rows * rows * cq, bytes_accessed=4 * rows * cq, transcendentals=rows * rows // 2),
        name="long_prompt" if half == 0 else "short_prompts",
    )(counts, q, *more)


def row_head(n, lq, h, hh):
    at = h * GQ + hh
    return at // lq, at % lq


def handed_part(n, lq, kv_ref, own_ref, msg_ref, _, o_ref, __):
    rows = lq * n * GROUP_ROWS
    shape = (rows, HD)
    at_row, lane = iota(shape, 0), iota(shape, 1)
    rs = at_row % GROUP_ROWS
    facts = msg_ref[:, :HD].astype(jnp.float32).reshape(n, GROUP_ROWS, HD)[:, 6:7, :]
    facts = jnp.broadcast_to(facts, (n, GROUP_ROWS, HD)).reshape(n * GROUP_ROWS, HD)
    facts = jnp.concatenate([facts] * lq, axis=0)

    def column(kind):
        return jnp.sum(jnp.where(lane == kind * GROUP_ROWS + rs, facts, 0.0), axis=1, keepdims=True)

    first_block, second_block, length = [column(kind) for kind in range(3)]
    own = own_ref[...]
    queries = jnp.concatenate([own[:, h * HD : (h + 1) * HD] for h in range(lq)], axis=0)
    scores = dot_t(queries, kv_ref[:, :HD]) * SCALE
    lane_f = lane.astype(jnp.float32)
    parts = []
    for b in range(NBLK):
        limit = jnp.where(
            first_block == b, length, jnp.where(second_block == b, length - BLOCK_TOKENS, 0.0)
        )
        part = scores[:, b * BLOCK_TOKENS : (b + 1) * BLOCK_TOKENS]
        parts.append(jnp.where(lane_f < limit, part, MASKED))
    scores = jnp.concatenate(parts, axis=1)
    top = jnp.max(scores, axis=1, keepdims=True)
    raised = jnp.exp(scores - top)
    total = jnp.sum(raised, axis=1, keepdims=True)
    near = raised.astype(jnp.bfloat16)
    rest = (raised - near.astype(jnp.float32)).astype(jnp.bfloat16)
    values = kv_ref[:, HD:]
    mixed = (dot(near, values) + dot(rest, values)).reshape(lq * n, GROUP_ROWS, HD)

    def line(col):
        spread = jnp.where(lane == rs, col, 0.0).reshape(lq * n, GROUP_ROWS, HD)
        return jnp.sum(spread, axis=1, keepdims=True)

    rs3 = rs.reshape(lq * n, GROUP_ROWS, HD)
    mixed = jnp.where(rs3 == 6, line(top), jnp.where(rs3 == 7, line(total), mixed))
    for h in range(lq):
        o_ref[:, h * GROUP_ROWS : (h + 1) * GROUP_ROWS, :] = mixed[h * n : (h + 1) * n]


def handed_attention(kv, own, msgs, prompt_attn, n, lq):
    rows = lq * n * GROUP_ROWS
    vmem, hbm = pl.BlockSpec(memory_space=VMEM), pl.BlockSpec(memory_space=pl.ANY)
    return pl.pallas_call(
        functools.partial(handed_part, n, lq),
        in_specs=[vmem] * 3 + [hbm],
        out_specs=[vmem, hbm],
        out_shape=[
            jax.ShapeDtypeStruct((n, lq * GROUP_ROWS, HD), jnp.float32),
            jax.ShapeDtypeStruct(prompt_attn.shape, prompt_attn.dtype),
        ],
        input_output_aliases={3: 1},
        compiler_params=pltpu.CompilerParams(vmem_limit_bytes=24 * MIB),
        cost_estimate=pl.CostEstimate(flops=6 * rows * HD * PTOK, bytes_accessed=2 * MIB, transcendentals=rows * PTOK),
        name="handed_attention",
    )(kv, own, msgs, prompt_attn)


def owner_part(n, lq, *refs):
    cache, msgs, handed, o_ref, slot_row, slot_limit = refs[5:11]
    counts, done, placed, table, lens, int_sems = refs[11:]
    ints = int_copies(refs[:5], refs[11:16], int_sems)
    for copy in ints:
        copy.start()
    held = msgs[...].astype(jnp.float32)

    def tile(t, k):
        return held[t * GROUP_ROWS : (t + 1) * GROUP_ROWS, k * HD : (k + 1) * HD]

    groups = QH
    rows = groups * GROUP_ROWS
    span = GQ * GROUP_ROWS
    queries, keys, values = [], [], []
    for h in range(KVH):
        for hh in range(GQ):
            t, at = row_head(n, lq, h, hh)
            queries.append(tile(t, at))
        t, _ = row_head(n, lq, h, 0)
        keys += [tile(t, lq)] * GQ
        values.append(tile(t, lq + 1))
    queries = jnp.concatenate(queries, axis=0)
    earlier = jnp.concatenate([pltpu.roll(key, ROWS_DEV, 0) for key in keys], axis=0)
    keys = jnp.concatenate(keys, axis=0)
    at_row, lane = iota((rows, HD), 0), iota((rows, HD), 1)
    r = row_of(at_row % GROUP_ROWS)
    rounded = queries.astype(jnp.bfloat16)
    now = jnp.sum(queries * keys, axis=1, keepdims=True) * SCALE
    before = jnp.sum(queries * earlier, axis=1, keepdims=True) * SCALE
    rs1 = iota((rows, 1), 0) % GROUP_ROWS
    before = jnp.where((rs1 >= ROWS_DEV) & (rs1 < STEPS * ROWS_DEV), before, MASKED)
    mixed = handed[...].reshape(groups, GROUP_ROWS, HD)
    shape = (groups, GROUP_ROWS, HD)
    mine = iota(shape, 1) == iota(shape, 2)

    def column(at):
        line = jnp.broadcast_to(mixed[:, at : at + 1, :], shape)
        return jnp.sum(jnp.where(mine, line, 0.0), axis=2, keepdims=True).reshape(rows, 1)

    other_peak, other_total = column(6), column(7)
    for copy in ints:
        copy.wait()
    found = block_of_pages(counts, done, placed, table)
    for k in range(ROWS_DEV):
        for p in range(PAGES):
            slot_row[table[p, k]] = jnp.int32(k)
            slot_limit[table[p, k]] = jnp.where(found[k][p] < 0, lens[k] - p * BLOCK_TOKENS, 0)
    scores = jnp.concatenate(
        [dot_t(rounded[h * span : (h + 1) * span], cache[:, 2 * h * HD : (2 * h + 1) * HD]) for h in range(KVH)],
        axis=0,
    )
    parts = []
    for slot in range(DEVICE_SLOTS):
        part = scores[:, slot * BLOCK_TOKENS : (slot + 1) * BLOCK_TOKENS]
        usable = (r == slot_row[slot]) & (lane < slot_limit[slot])
        parts.append(jnp.where(usable, part * SCALE, MASKED))
    scores = jnp.concatenate(parts, axis=1)
    peak = jnp.maximum(jnp.max(scores, axis=1, keepdims=True), jnp.maximum(now, before))
    peak = jnp.maximum(peak, other_peak)
    raised, now, before = jnp.exp(scores - peak), jnp.exp(now - peak), jnp.exp(before - peak)
    other = jnp.exp(other_peak - peak)
    inverse = 1.0 / (jnp.sum(raised, axis=1, keepdims=True) + now + before + other * other_total)
    weights = (raised * inverse).astype(jnp.bfloat16)
    now = (now * inverse).astype(jnp.bfloat16).astype(jnp.float32)
    before = (before * inverse).astype(jnp.bfloat16).astype(jnp.float32)
    mixed = mixed.reshape(rows, HD) * (other * inverse)
    out = []
    for h in range(KVH):
        part = slice(h * span, (h + 1) * span)
        own = mixed[part] + dot(weights[part], cache[:, (2 * h + 1) * HD : (2 * h + 2) * HD])
        last = pltpu.roll(values[h], ROWS_DEV, 0)
        for hh in range(GQ):
            some = slice(h * span + hh * GROUP_ROWS, h * span + (hh + 1) * GROUP_ROWS)
            line = own[hh * GROUP_ROWS : (hh + 1) * GROUP_ROWS]
            out.append(line + now[some] * values[h] + before[some] * last)
    out = jnp.concatenate(out, axis=1)
    for k in range(ROWS_DEV):
        steps = [out[s * ROWS_DEV + k : s * ROWS_DEV + k + 1] for s in range(STEPS)]
        o_ref[k] = jnp.concatenate(steps, axis=0).astype(jnp.bfloat16)


def decode_attention(ints, cache, msgs, parts, n, lq):
    vmem, hbm = pl.BlockSpec(memory_space=VMEM), pl.BlockSpec(memory_space=pl.ANY)
    rows = QH * GROUP_ROWS
    return pl.pallas_call(
        functools.partial(owner_part, n, lq),
        in_specs=[hbm] * 5 + [vmem] * 3,
        out_specs=vmem,
        out_shape=jax.ShapeDtypeStruct((ROWS_DEV, STEPS, QH * HD), jnp.bfloat16),
        scratch_shapes=[
            SMEM((DEVICE_SLOTS,), jnp.int32),
            SMEM((DEVICE_SLOTS,), jnp.int32),
        ]
        + int_scratch(ints),
        compiler_params=pltpu.CompilerParams(vmem_limit_bytes=40 * MIB),
        cost_estimate=pl.CostEstimate(flops=4 * rows * HD * 768, bytes_accessed=4 * MIB, transcendentals=rows * 768),
        name="decode_attention",
    )(*ints, cache, msgs, parts)


def local(
    prompt_x,
    q_weight,
    kv_weight,
    prompt_blocks,
    finished,
    placement,
    page_table,
    row_lens,
    kv_cache,
    decode_x,
):
    n = lax.axis_size("tp")
    lq = q_weight.shape[1] // HD
    share = GQ // lq
    if share > 1:
        sets = [[k * share + i for i in range(share)] for k in range(n // share)]
        kv_weight = lax.all_gather(kv_weight, "tp", axis=1, tiled=True, axis_index_groups=sets)
    cache = kv_cache.reshape(-1, kv_cache.shape[2])
    dx = decode_x.reshape(-1, decode_x.shape[2])
    placement = placement.transpose(0, 2, 1)
    page_table = page_table.transpose(1, 0)
    ints = (prompt_blocks, finished, placement, page_table, row_lens)
    first, size = 256, 448
    q, kv, own, msgs = project_all(ints, dx, prompt_x, q_weight, kv_weight, n, first, size)
    kv_other = lax.ppermute(kv, "pool", [(0, 1), (1, 0)])
    msgs = lax.all_to_all(msgs, "tp", split_axis=0, concat_axis=0, tiled=True)
    prompt_attn = prompt_attention(prompt_blocks, q, q_weight.shape[1], 0)
    handed, prompt_attn = handed_attention(kv_other, own, msgs, prompt_attn, n, lq)
    parts = lax.all_to_all(handed, "tp", split_axis=0, concat_axis=0, tiled=True)
    prompt_attn = prompt_attention(prompt_blocks, q, q_weight.shape[1], 1, prompt_attn)
    decode_attn = decode_attention(ints, cache, msgs, parts, n, lq)
    return prompt_attn, decode_attn.transpose(1, 0, 2)


def solution(mesh):
    return jax.shard_map(
        local,
        mesh=mesh,
        in_specs=(
            P(("rep", "pool"), None),
            P(None, "tp"),
            P(None, "tp"),
            P("rep", None),
            P("rep", None),
            P("rep", None, None),
            P(("rep", "pool", "tp"), None),
            P(("rep", "pool", "tp")),
            P(("rep", "pool", "tp"), None, None),
            P(None, ("rep", "pool"), None),
        ),
        out_specs=(P(("rep", "pool"), "tp"), P(None, ("rep", "pool", "tp"), None)),
        check_vma=False,
    )
```

```python
import functools

import jax
import jax.numpy as jnp
from jax import lax
from jax.experimental import pallas as pl
from jax.experimental.pallas import tpu as pltpu
from jax.sharding import PartitionSpec as P

QH = 32
KVH = 8
GQ = QH // KVH
HD = 128
BLOCK_TOKENS = 128
PTOK = 2048
NPROMPT = 3
MOST_BLOCKS = 8
PAGES = 2
STEPS = 2
NBLK = 16
DEVICE_SLOTS = 6
ROWS_DEV = 3
GROUP_ROWS = 8
KEY_VALUE_COLUMNS = 2048
SCALE = HD ** (-0.5)
MASKED = -1e30
PIECES = 5
STRIPS = 4
WIDE = 2048
LOG2E = 1.4426950408889634
AHEAD = 2
MIB = 1 << 20
VMEM = pltpu.VMEM
SMEM = pltpu.SMEM


def dot(a, b):
    return jnp.dot(a, b, preferred_element_type=jnp.float32)


def dot_t(a, b):
    return lax.dot_general(a, b, (((1,), (1,)), ((), ())), preferred_element_type=jnp.float32)


def iota(shape, axis):
    return lax.broadcasted_iota(jnp.int32, shape, axis)


def row_of(rs):
    return jnp.where(rs >= 2 * ROWS_DEV, ROWS_DEV, jnp.where(rs >= ROWS_DEV, rs - ROWS_DEV, rs))


def block_of_pages(counts, done, placed, table):
    me = lax.axis_index("tp")
    other = 1 - lax.axis_index("pool")
    first_end = counts[other, 0]
    second_end = first_end + counts[other, 1]
    found = [[jnp.int32(-1)] * PAGES for _ in range(ROWS_DEV)]
    for b in range(NBLK):
        live = jnp.where(
            b < first_end, done[other, 0], jnp.where(b < second_end, done[other, 1], done[other, 2])
        )
        slot = jnp.where((live > 0) & (placed[other, 0, b] == me), placed[other, 1, b], -1)
        for r in range(ROWS_DEV):
            for p in range(PAGES):
                found[r][p] = jnp.where(slot == table[p, r], b, found[r][p])
    return found


def by_row(r, values, rest):
    out = jnp.full(r.shape, rest, jnp.int32)
    for k in range(ROWS_DEV):
        out = jnp.where(r == k, values[k], out)
    return out


def int_scratch(ints):
    return [SMEM(x.shape, jnp.int32) for x in ints] + [pltpu.SemaphoreType.DMA((len(ints),))]


def int_copies(sources, targets, sems):
    return [pltpu.make_async_copy(a, b, sems.at[i]) for i, (a, b) in enumerate(zip(sources, targets))]


def project(n, lq, first, size, *refs):
    dx_hbm, x_hbm, wq_hbm, wkv_hbm = refs[5:9]
    q_hbm, kv_hbm, own_ref, msg_ref = refs[9:13]
    x0, xs, w, q_out, kv_out, x_sems, w_sems, out_sems = refs[13:21]
    counts, done, placed, table, lens, int_sems = refs[21:]
    ints = int_copies(refs[:5], refs[21:26], int_sems)
    depth = w.shape[0]
    count = xs.shape[0]
    cq = lq * HD
    piece = depth // PIECES
    own_rows = dx_hbm.shape[0]
    step = pl.program_id(0)

    def piece_copies(c):
        part = pl.ds(c * piece, piece)
        return [
            pltpu.make_async_copy(x_hbm.at[pl.ds(0, first), part], x0.at[pl.ds(0, first), part], w_sems.at[0, c]),
            pltpu.make_async_copy(dx_hbm.at[:, part], x0.at[pl.ds(first, own_rows), part], w_sems.at[1, c]),
            pltpu.make_async_copy(wq_hbm.at[part], w.at[part, pl.ds(0, cq)], w_sems.at[2, c]),
            pltpu.make_async_copy(wkv_hbm.at[part], w.at[part, pl.ds(cq, 2 * HD)], w_sems.at[3, c]),
        ]

    def x_copies(k):
        strip = size // STRIPS
        copies = []
        for i in range(STRIPS):
            rows = pl.ds(pl.multiple_of(first + k * size + i * strip, 16), strip)
            copies.append(
                pltpu.make_async_copy(x_hbm.at[rows], xs.at[k, pl.ds(i * strip, strip)], x_sems.at[k, i])
            )
        return copies

    def out_copies(k):
        if isinstance(k, int):
            rows = pl.ds(0, first)
        else:
            rows = pl.ds(pl.multiple_of(first + (k - 1) * size, 64), size)
        return [
            pltpu.make_async_copy(q_out.at[rows], q_hbm.at[rows, pl.ds(0, cq)], out_sems.at[0, k]),
            pltpu.make_async_copy(kv_out.at[rows], q_hbm.at[rows, pl.ds(cq, 2 * HD)], out_sems.at[1, k]),
            pltpu.make_async_copy(kv_out.at[rows], kv_hbm.at[rows], out_sems.at[2, k]),
        ]

    def keep(total, rows):
        q_out[rows, :] = total[:, :cq].astype(jnp.bfloat16)
        kv_out[rows, :] = total[:, cq:].astype(jnp.bfloat16)

    @pl.when(step == 0)
    def _():
        for c in range(AHEAD):
            for copy in piece_copies(c):
                copy.start()
        for copy in ints:
            copy.start()
        total = 0.0
        for c in range(PIECES):
            for copy in piece_copies(c):
                copy.wait()
            if c + AHEAD < PIECES:
                for copy in piece_copies(c + AHEAD):
                    copy.start()
            if c + AHEAD >= PIECES:
                for copy in x_copies(c + AHEAD - PIECES):
                    copy.start()
            part = slice(c * piece, (c + 1) * piece)
            total += dot(x0[:, part], w[part, :])
        keep(total[:first], pl.ds(0, first))
        for copy in out_copies(0):
            copy.start()
        shape = (n * GROUP_ROWS, own_rows)
        to, fro = iota(shape, 0), iota(shape, 1)
        owner, rs = to // GROUP_ROWS, to % GROUP_ROWS
        wanted = owner * ROWS_DEV + row_of(rs) + jnp.where(rs >= ROWS_DEV, ROWS_DEV * n, 0)
        pick = ((fro == wanted) & (rs < STEPS * ROWS_DEV)).astype(jnp.float32).astype(jnp.bfloat16)
        own = dot(pick, total[first:].astype(jnp.bfloat16))
        own_ref[...] = own.astype(jnp.bfloat16)
        for copy in ints:
            copy.wait()
        found = block_of_pages(counts, done, placed, table)
        lane = iota((n * GROUP_ROWS, HD), 1)
        r = row_of(lane % GROUP_ROWS)
        kind = lane // GROUP_ROWS
        facts = jnp.where(
            kind == 0,
            by_row(r, [found[i][0] for i in range(ROWS_DEV)], -1),
            jnp.where(
                kind == 1,
                by_row(r, [found[i][1] for i in range(ROWS_DEV)], -1),
                by_row(r, [lens[i] for i in range(ROWS_DEV)], 0),
            ),
        ).astype(jnp.float32)
        sixth = iota((n * GROUP_ROWS, HD), 0) % GROUP_ROWS == 6
        msg_ref[:, :HD] = jnp.where(sixth, facts, own[:, :HD]).astype(jnp.bfloat16)
        msg_ref[:, HD:] = own[:, HD:].astype(jnp.bfloat16)

    @pl.when((step > 0) & (step + AHEAD <= count))
    def _():
        for copy in x_copies(step + AHEAD - 1):
            copy.start()

    @pl.when(step > 0)
    def _():
        for copy in x_copies(step - 1):
            copy.wait()
        keep(dot(xs[step - 1], w[...]), pl.ds(pl.multiple_of(first + (step - 1) * size, 64), size))
        for copy in out_copies(step):
            copy.start()

    @pl.when(step == count)
    def _():
        for copy in out_copies(0):
            copy.wait()
        for k in range(1, count + 1):
            for copy in out_copies(jnp.int32(k)):
                copy.wait()


def project_all(ints, dx, x, wq, wkv, n, first, size):
    rows, depth = x.shape
    cq, ckv = wq.shape[1], wkv.shape[1]
    lq = cq // HD
    count = (rows - first) // size
    vmem, hbm = pl.BlockSpec(memory_space=VMEM), pl.BlockSpec(memory_space=pl.ANY)
    return pl.pallas_call(
        functools.partial(project, n, lq, first, size),
        grid=(1 + count,),
        in_specs=[hbm] * 9,
        out_specs=[hbm, hbm, vmem, vmem],
        out_shape=[
            jax.ShapeDtypeStruct((rows, WIDE), jnp.bfloat16),
            jax.ShapeDtypeStruct((rows, ckv), jnp.bfloat16),
            jax.ShapeDtypeStruct((n * GROUP_ROWS, cq + ckv), jnp.bfloat16),
            jax.ShapeDtypeStruct((n * GROUP_ROWS, cq + ckv), jnp.bfloat16),
        ],
        scratch_shapes=[
            VMEM((first + dx.shape[0], depth), jnp.bfloat16),
            VMEM((count, size, depth), jnp.bfloat16),
            VMEM((depth, cq + ckv), jnp.bfloat16),
            VMEM((rows, cq), jnp.bfloat16),
            VMEM((rows, ckv), jnp.bfloat16),
            pltpu.SemaphoreType.DMA((count, STRIPS)),
            pltpu.SemaphoreType.DMA((4, PIECES)),
            pltpu.SemaphoreType.DMA((3, count + 1)),
        ]
        + int_scratch(ints),
        compiler_params=pltpu.CompilerParams(vmem_limit_bytes=62 * MIB),
        cost_estimate=pl.CostEstimate(
            flops=2 * rows * depth * (cq + ckv),
            bytes_accessed=2 * (rows + cq + ckv) * depth + 2 * rows * (cq + ckv),
            transcendentals=0,
        ),
        name="project",
    )(*ints, dx, x, wq, wkv)


def attend_prompt(lq, half, counts, q_hbm, *refs):
    o_hbm, qs, kvs, outs, sems = refs[-5:]
    group = lax.axis_index("pool")
    c0, c1 = counts[group, 0], counts[group, 1]
    big = jnp.where(c0 == MOST_BLOCKS, 0, jnp.where(c1 == MOST_BLOCKS, c0, c0 + c1))
    cut = jnp.where(c0 == MOST_BLOCKS, c1, c0)
    loads, stores = [], []
    strip, early = (4, 3) if half == 0 else (1, 5)
    for j in range(0, MOST_BLOCKS, strip):
        block = big + j if half == 0 else j + jnp.where(j >= big, MOST_BLOCKS, 0)
        rows = pl.ds(pl.multiple_of(block * BLOCK_TOKENS, BLOCK_TOKENS), strip * BLOCK_TOKENS)
        here = pl.ds(j * BLOCK_TOKENS, strip * BLOCK_TOKENS)
        cq = lq * HD
        keys_values, queries = q_hbm.at[rows, pl.ds(cq, 2 * HD)], q_hbm.at[rows, pl.ds(0, cq)]
        loads.append(pltpu.make_async_copy(keys_values, kvs.at[here], sems.at[0, j]))
        loads.append(pltpu.make_async_copy(queries, qs.at[here], sems.at[1, j]))
        stores.append(pltpu.make_async_copy(outs.at[here], o_hbm.at[rows], sems.at[2, j]))
    for copy in loads:
        copy.start()
    near = len(loads) // 2
    for copy in loads[:near]:
        copy.wait()
    shape = (BLOCK_TOKENS, lq * BLOCK_TOKENS)
    causal = iota(shape, 0) <= iota(shape, 1) % BLOCK_TOKENS
    tokens = MOST_BLOCKS * BLOCK_TOKENS
    flipped = kvs[: tokens // 2, HD:].T

    def scores_of(j):
        q = qs[j * BLOCK_TOKENS : (j + 1) * BLOCK_TOKENS, :]
        q = jnp.concatenate([q[:, h * HD : (h + 1) * HD] for h in range(lq)], axis=0)
        return dot_t(kvs[: (j + 1) * BLOCK_TOKENS, :HD], q)

    scores = scores_of(0)
    for j in range(MOST_BLOCKS):
        if j + 1 == MOST_BLOCKS // 2:
            for copy in loads[near:]:
                copy.wait()
            flipped = jnp.concatenate([flipped, kvs[tokens // 2 :, HD:].T], axis=1)
        later = scores_of(j + 1) if j + 1 < MOST_BLOCKS else None
        weights = []
        for h in range(lq):
            cols = slice(h * BLOCK_TOKENS, (h + 1) * BLOCK_TOKENS)
            tiles = []
            for i in range(j + 1):
                tile = scores[i * BLOCK_TOKENS : (i + 1) * BLOCK_TOKENS, cols]
                if i == j:
                    tile = jnp.where(causal[:, cols], tile, MASKED)
                elif half == 1:
                    tile = tile + jnp.where((i < cut) & (cut <= j), MASKED, 0.0)
                tiles.append(tile)
            peak = jnp.max(functools.reduce(jnp.maximum, tiles), axis=0, keepdims=True)
            raised = [jnp.exp2((tile - peak) * (SCALE * LOG2E)) for tile in tiles]
            inverse = 1.0 / jnp.sum(functools.reduce(jnp.add, raised), axis=0, keepdims=True)
            weights.append(jnp.concatenate([(t * inverse).astype(jnp.bfloat16) for t in raised], axis=0))
        mixed = dot(flipped[:, : (j + 1) * BLOCK_TOKENS], jnp.concatenate(weights, axis=1))
        mixed = mixed.astype(jnp.bfloat16)
        for h in range(lq):
            part = mixed[:, h * BLOCK_TOKENS : (h + 1) * BLOCK_TOKENS].T
            outs[j * BLOCK_TOKENS : (j + 1) * BLOCK_TOKENS, h * HD : (h + 1) * HD] = part
        scores = later
        if j == early:
            for copy in stores[: (j + 1) // strip]:
                copy.start()
    for copy in stores[(early + 1) // strip :]:
        copy.start()
    for copy in stores:
        copy.wait()


def prompt_attention(counts, q, cq, half, so_far=None):
    rows = q.shape[0]
    hbm = pl.BlockSpec(memory_space=pl.ANY)
    more = () if so_far is None else (so_far,)
    tokens = MOST_BLOCKS * BLOCK_TOKENS
    return pl.pallas_call(
        functools.partial(attend_prompt, cq // HD, half),
        in_specs=[pl.BlockSpec(memory_space=SMEM), hbm] + [hbm] * len(more),
        out_specs=hbm,
        out_shape=jax.ShapeDtypeStruct((rows, cq), jnp.bfloat16),
        scratch_shapes=[
            VMEM((tokens, cq), jnp.bfloat16),
            VMEM((tokens, 2 * HD), jnp.bfloat16),
            VMEM((tokens, cq), jnp.bfloat16),
            pltpu.SemaphoreType.DMA((3, MOST_BLOCKS)),
        ],
        input_output_aliases={2: 0} if more else {},
        compiler_params=pltpu.CompilerParams(vmem_limit_bytes=(62 if half == 0 else 48) * MIB),
        cost_estimate=pl.CostEstimate(flops=2 * rows * rows * cq, bytes_accessed=4 * rows * cq, transcendentals=rows * rows // 2),
        name="long_prompt" if half == 0 else "short_prompts",
    )(counts, q, *more)


def row_head(n, lq, h, hh):
    at = h * GQ + hh
    return at // lq, at % lq


def handed_part(n, lq, kv_ref, own_ref, msg_ref, _, o_ref, __):
    rows = lq * n * GROUP_ROWS
    shape = (rows, HD)
    at_row, lane = iota(shape, 0), iota(shape, 1)
    rs = at_row % GROUP_ROWS
    facts = msg_ref[:, :HD].astype(jnp.float32).reshape(n, GROUP_ROWS, HD)[:, 6:7, :]
    facts = jnp.broadcast_to(facts, (n, GROUP_ROWS, HD)).reshape(n * GROUP_ROWS, HD)
    facts = jnp.concatenate([facts] * lq, axis=0)

    def column(kind):
        return jnp.sum(jnp.where(lane == kind * GROUP_ROWS + rs, facts, 0.0), axis=1, keepdims=True)

    first_block, second_block, length = [column(kind) for kind in range(3)]
    own = own_ref[...]
    queries = jnp.concatenate([own[:, h * HD : (h + 1) * HD] for h in range(lq)], axis=0)
    scores = dot_t(queries, kv_ref[:, :HD]) * SCALE
    lane_f = lane.astype(jnp.float32)
    parts = []
    for b in range(NBLK):
        limit = jnp.where(
            first_block == b, length, jnp.where(second_block == b, length - BLOCK_TOKENS, 0.0)
        )
        part = scores[:, b * BLOCK_TOKENS : (b + 1) * BLOCK_TOKENS]
        parts.append(jnp.where(lane_f < limit, part, MASKED))
    scores = jnp.concatenate(parts, axis=1)
    top = jnp.max(scores, axis=1, keepdims=True)
    raised = jnp.exp(scores - top)
    total = jnp.sum(raised, axis=1, keepdims=True)
    near = raised.astype(jnp.bfloat16)
    rest = (raised - near.astype(jnp.float32)).astype(jnp.bfloat16)
    values = kv_ref[:, HD:]
    mixed = dot(jnp.concatenate([near, rest], axis=0), values)
    mixed = (mixed[:rows] + mixed[rows:]).reshape(lq * n, GROUP_ROWS, HD)

    def line(col):
        spread = jnp.where(lane == rs, col, 0.0).reshape(lq * n, GROUP_ROWS, HD)
        return jnp.sum(spread, axis=1, keepdims=True)

    rs3 = rs.reshape(lq * n, GROUP_ROWS, HD)
    mixed = jnp.where(rs3 == 6, line(top), jnp.where(rs3 == 7, line(total), mixed))
    for h in range(lq):
        o_ref[:, h * GROUP_ROWS : (h + 1) * GROUP_ROWS, :] = mixed[h * n : (h + 1) * n]


def handed_attention(kv, own, msgs, prompt_attn, n, lq):
    rows = lq * n * GROUP_ROWS
    vmem, hbm = pl.BlockSpec(memory_space=VMEM), pl.BlockSpec(memory_space=pl.ANY)
    return pl.pallas_call(
        functools.partial(handed_part, n, lq),
        in_specs=[vmem] * 3 + [hbm],
        out_specs=[vmem, hbm],
        out_shape=[
            jax.ShapeDtypeStruct((n, lq * GROUP_ROWS, HD), jnp.float32),
            jax.ShapeDtypeStruct(prompt_attn.shape, prompt_attn.dtype),
        ],
        input_output_aliases={3: 1},
        compiler_params=pltpu.CompilerParams(vmem_limit_bytes=24 * MIB),
        cost_estimate=pl.CostEstimate(flops=6 * rows * HD * PTOK, bytes_accessed=2 * MIB, transcendentals=rows * PTOK),
        name="handed_attention",
    )(kv, own, msgs, prompt_attn)


def owner_part(n, lq, *refs):
    cache, msgs, handed, o_ref, slot_row, slot_limit = refs[5:11]
    counts, done, placed, table, lens, int_sems = refs[11:]
    ints = int_copies(refs[:5], refs[11:16], int_sems)
    for copy in ints:
        copy.start()
    held = msgs[...].astype(jnp.float32)

    def tile(t, k):
        return held[t * GROUP_ROWS : (t + 1) * GROUP_ROWS, k * HD : (k + 1) * HD]

    groups = QH
    rows = groups * GROUP_ROWS
    span = GQ * GROUP_ROWS
    queries, keys, values = [], [], []
    for h in range(KVH):
        for hh in range(GQ):
            t, at = row_head(n, lq, h, hh)
            queries.append(tile(t, at))
        t, _ = row_head(n, lq, h, 0)
        keys += [tile(t, lq)] * GQ
        values.append(tile(t, lq + 1))
    queries = jnp.concatenate(queries, axis=0)
    earlier = jnp.concatenate([pltpu.roll(key, ROWS_DEV, 0) for key in keys], axis=0)
    keys = jnp.concatenate(keys, axis=0)
    at_row, lane = iota((rows, HD), 0), iota((rows, HD), 1)
    r = row_of(at_row % GROUP_ROWS)
    rounded = queries.astype(jnp.bfloat16)
    now = jnp.sum(queries * keys, axis=1, keepdims=True) * SCALE
    before = jnp.sum(queries * earlier, axis=1, keepdims=True) * SCALE
    rs1 = iota((rows, 1), 0) % GROUP_ROWS
    before = jnp.where((rs1 >= ROWS_DEV) & (rs1 < STEPS * ROWS_DEV), before, MASKED)
    mixed = handed[...].reshape(groups, GROUP_ROWS, HD)
    shape = (groups, GROUP_ROWS, HD)
    mine = iota(shape, 1) == iota(shape, 2)

    def column(at):
        line = jnp.broadcast_to(mixed[:, at : at + 1, :], shape)
        return jnp.sum(jnp.where(mine, line, 0.0), axis=2, keepdims=True).reshape(rows, 1)

    other_peak, other_total = column(6), column(7)
    for copy in ints:
        copy.wait()
    found = block_of_pages(counts, done, placed, table)
    for k in range(ROWS_DEV):
        for p in range(PAGES):
            slot_row[table[p, k]] = jnp.int32(k)
            slot_limit[table[p, k]] = jnp.where(found[k][p] < 0, lens[k] - p * BLOCK_TOKENS, 0)
    scores = jnp.concatenate(
        [dot_t(rounded[h * span : (h + 1) * span], cache[:, 2 * h * HD : (2 * h + 1) * HD]) for h in range(KVH)],
        axis=0,
    )
    parts = []
    for slot in range(DEVICE_SLOTS):
        part = scores[:, slot * BLOCK_TOKENS : (slot + 1) * BLOCK_TOKENS]
        usable = (r == slot_row[slot]) & (lane < slot_limit[slot])
        parts.append(jnp.where(usable, part * SCALE, MASKED))
    scores = jnp.concatenate(parts, axis=1)
    peak = jnp.maximum(jnp.max(scores, axis=1, keepdims=True), jnp.maximum(now, before))
    peak = jnp.maximum(peak, other_peak)
    raised, now, before = jnp.exp(scores - peak), jnp.exp(now - peak), jnp.exp(before - peak)
    other = jnp.exp(other_peak - peak)
    inverse = 1.0 / (jnp.sum(raised, axis=1, keepdims=True) + now + before + other * other_total)
    weights = (raised * inverse).astype(jnp.bfloat16)
    now = (now * inverse).astype(jnp.bfloat16).astype(jnp.float32)
    before = (before * inverse).astype(jnp.bfloat16).astype(jnp.float32)
    mixed = mixed.reshape(rows, HD) * (other * inverse)
    out = []
    for h in range(KVH):
        part = slice(h * span, (h + 1) * span)
        own = mixed[part] + dot(weights[part], cache[:, (2 * h + 1) * HD : (2 * h + 2) * HD])
        last = pltpu.roll(values[h], ROWS_DEV, 0)
        for hh in range(GQ):
            some = slice(h * span + hh * GROUP_ROWS, h * span + (hh + 1) * GROUP_ROWS)
            line = own[hh * GROUP_ROWS : (hh + 1) * GROUP_ROWS]
            out.append(line + now[some] * values[h] + before[some] * last)
    out = jnp.concatenate(out, axis=1)
    for k in range(ROWS_DEV):
        steps = [out[s * ROWS_DEV + k : s * ROWS_DEV + k + 1] for s in range(STEPS)]
        o_ref[k] = jnp.concatenate(steps, axis=0).astype(jnp.bfloat16)


def decode_attention(ints, cache, msgs, parts, n, lq):
    vmem, hbm = pl.BlockSpec(memory_space=VMEM), pl.BlockSpec(memory_space=pl.ANY)
    rows = QH * GROUP_ROWS
    return pl.pallas_call(
        functools.partial(owner_part, n, lq),
        in_specs=[hbm] * 5 + [vmem] * 3,
        out_specs=vmem,
        out_shape=jax.ShapeDtypeStruct((ROWS_DEV, STEPS, QH * HD), jnp.bfloat16),
        scratch_shapes=[
            SMEM((DEVICE_SLOTS,), jnp.int32),
            SMEM((DEVICE_SLOTS,), jnp.int32),
        ]
        + int_scratch(ints),
        compiler_params=pltpu.CompilerParams(vmem_limit_bytes=40 * MIB),
        cost_estimate=pl.CostEstimate(flops=4 * rows * HD * 768, bytes_accessed=4 * MIB, transcendentals=rows * 768),
        name="decode_attention",
    )(*ints, cache, msgs, parts)


def pass_on(*refs):
    pass


def hand_on(kv):
    hbm = pl.BlockSpec(memory_space=pl.ANY)
    return pl.pallas_call(
        pass_on,
        in_specs=[hbm],
        out_specs=hbm,
        out_shape=jax.ShapeDtypeStruct(kv.shape, kv.dtype),
        input_output_aliases={0: 0},
        compiler_params=pltpu.CompilerParams(vmem_limit_bytes=62 * MIB),
        name="hand_on",
    )(kv)


def local(
    prompt_x,
    q_weight,
    kv_weight,
    prompt_blocks,
    finished,
    placement,
    page_table,
    row_lens,
    kv_cache,
    decode_x,
):
    n = lax.axis_size("tp")
    lq = q_weight.shape[1] // HD
    share = GQ // lq
    if share > 1:
        sets = [[k * share + i for i in range(share)] for k in range(n // share)]
        kv_weight = lax.all_gather(kv_weight, "tp", axis=1, tiled=True, axis_index_groups=sets)
    cache = kv_cache.reshape(-1, kv_cache.shape[2])
    dx = decode_x.reshape(-1, decode_x.shape[2])
    placement = placement.transpose(0, 2, 1)
    page_table = page_table.transpose(1, 0)
    ints = (prompt_blocks, finished, placement, page_table, row_lens)
    first, size = 256, 448
    q, kv, own, msgs = project_all(ints, dx, prompt_x, q_weight, kv_weight, n, first, size)
    msgs = lax.all_to_all(msgs, "tp", split_axis=0, concat_axis=0, tiled=True)
    kv_other = lax.ppermute(hand_on(kv), "pool", [(0, 1), (1, 0)])
    prompt_attn = prompt_attention(prompt_blocks, q, q_weight.shape[1], 0)
    handed, prompt_attn = handed_attention(kv_other, own, msgs, prompt_attn, n, lq)
    parts = lax.all_to_all(handed, "tp", split_axis=0, concat_axis=0, tiled=True)
    prompt_attn = prompt_attention(prompt_blocks, q, q_weight.shape[1], 1, prompt_attn)
    decode_attn = decode_attention(ints, cache, msgs, parts, n, lq)
    return prompt_attn, decode_attn.transpose(1, 0, 2)


def solution(mesh):
    return jax.shard_map(
        local,
        mesh=mesh,
        in_specs=(
            P(("rep", "pool"), None),
            P(None, "tp"),
            P(None, "tp"),
            P("rep", None),
            P("rep", None),
            P("rep", None, None),
            P(("rep", "pool", "tp"), None),
            P(("rep", "pool", "tp")),
            P(("rep", "pool", "tp"), None, None),
            P(None, ("rep", "pool"), None),
        ),
        out_specs=(P(("rep", "pool"), "tp"), P(None, ("rep", "pool", "tp"), None)),
        check_vma=False,
    )
```

```python
import functools

import jax
import jax.numpy as jnp
from jax import lax
from jax.experimental import pallas as pl
from jax.experimental.pallas import tpu as pltpu
from jax.sharding import PartitionSpec as P

QH = 32
KVH = 8
GQ = QH // KVH
HD = 128
BLOCK_TOKENS = 128
PTOK = 2048
NPROMPT = 3
MOST_BLOCKS = 8
PAGES = 2
STEPS = 2
NBLK = 16
DEVICE_SLOTS = 6
ROWS_DEV = 3
GROUP_ROWS = 8
KEY_VALUE_COLUMNS = 2048
SCALE = HD ** (-0.5)
MASKED = -1e30
CUTS = (0, 1, 4, 8, 12, 16, 20)
PIECES = len(CUTS) - 1
STRIPS = 4
WIDE = 2048
LOG2E = 1.4426950408889634
AHEAD = 2
MIB = 1 << 20
VMEM = pltpu.VMEM
SMEM = pltpu.SMEM


def dot(a, b):
    return jnp.dot(a, b, preferred_element_type=jnp.float32)


def dot_t(a, b):
    return lax.dot_general(a, b, (((1,), (1,)), ((), ())), preferred_element_type=jnp.float32)


def iota(shape, axis):
    return lax.broadcasted_iota(jnp.int32, shape, axis)


def row_of(rs):
    return jnp.where(rs >= 2 * ROWS_DEV, ROWS_DEV, jnp.where(rs >= ROWS_DEV, rs - ROWS_DEV, rs))


def block_of_pages(counts, done, placed, table):
    me = lax.axis_index("tp")
    other = 1 - lax.axis_index("pool")
    first_end = counts[other, 0]
    second_end = first_end + counts[other, 1]
    found = [[jnp.int32(-1)] * PAGES for _ in range(ROWS_DEV)]
    for b in range(NBLK):
        live = jnp.where(
            b < first_end, done[other, 0], jnp.where(b < second_end, done[other, 1], done[other, 2])
        )
        slot = jnp.where((live > 0) & (placed[other, 0, b] == me), placed[other, 1, b], -1)
        for r in range(ROWS_DEV):
            for p in range(PAGES):
                found[r][p] = jnp.where(slot == table[p, r], b, found[r][p])
    return found


def by_row(r, values, rest):
    out = jnp.full(r.shape, rest, jnp.int32)
    for k in range(ROWS_DEV):
        out = jnp.where(r == k, values[k], out)
    return out


def int_scratch(ints):
    return [SMEM(x.shape, jnp.int32) for x in ints] + [pltpu.SemaphoreType.DMA((len(ints),))]


def int_copies(sources, targets, sems):
    return [pltpu.make_async_copy(a, b, sems.at[i]) for i, (a, b) in enumerate(zip(sources, targets))]


def project(n, lq, first, size, *refs):
    dx_hbm, x_hbm, wq_hbm, wkv_hbm = refs[5:9]
    q_hbm, kv_hbm, own_ref, msg_ref = refs[9:13]
    x0, xs, w, q_out, kv_out, x_sems, w_sems, out_sems = refs[13:21]
    counts, done, placed, table, lens, int_sems = refs[21:]
    ints = int_copies(refs[:5], refs[21:26], int_sems)
    depth = w.shape[0]
    count = xs.shape[0]
    cq = lq * HD
    cuts = [cut * depth // CUTS[-1] for cut in CUTS]
    own_rows = dx_hbm.shape[0]
    step = pl.program_id(0)

    def piece_copies(c):
        part = pl.ds(cuts[c], cuts[c + 1] - cuts[c])
        return [
            pltpu.make_async_copy(x_hbm.at[pl.ds(0, first), part], x0.at[pl.ds(0, first), part], w_sems.at[0, c]),
            pltpu.make_async_copy(dx_hbm.at[:, part], x0.at[pl.ds(first, own_rows), part], w_sems.at[1, c]),
            pltpu.make_async_copy(wq_hbm.at[part], w.at[part, pl.ds(0, cq)], w_sems.at[2, c]),
            pltpu.make_async_copy(wkv_hbm.at[part], w.at[part, pl.ds(cq, 2 * HD)], w_sems.at[3, c]),
        ]

    def x_copies(k):
        strip = size // STRIPS
        copies = []
        for i in range(STRIPS):
            rows = pl.ds(pl.multiple_of(first + k * size + i * strip, 16), strip)
            copies.append(
                pltpu.make_async_copy(x_hbm.at[rows], xs.at[k, pl.ds(i * strip, strip)], x_sems.at[k, i])
            )
        return copies

    def out_copies(k):
        if isinstance(k, int):
            rows = pl.ds(0, first)
        else:
            rows = pl.ds(pl.multiple_of(first + (k - 1) * size, 64), size)
        return [
            pltpu.make_async_copy(q_out.at[rows], q_hbm.at[rows, pl.ds(0, cq)], out_sems.at[0, k]),
            pltpu.make_async_copy(kv_out.at[rows], q_hbm.at[rows, pl.ds(cq, 2 * HD)], out_sems.at[1, k]),
            pltpu.make_async_copy(kv_out.at[rows], kv_hbm.at[rows], out_sems.at[2, k]),
        ]

    def keep(total, rows):
        q_out[rows, :] = total[:, :cq].astype(jnp.bfloat16)
        kv_out[rows, :] = total[:, cq:].astype(jnp.bfloat16)

    @pl.when(step == 0)
    def _():
        for c in range(AHEAD):
            for copy in piece_copies(c):
                copy.start()
        for copy in ints:
            copy.start()
        total = 0.0
        for c in range(PIECES):
            for copy in piece_copies(c):
                copy.wait()
            if c + AHEAD < PIECES:
                for copy in piece_copies(c + AHEAD):
                    copy.start()
            if c + AHEAD >= PIECES:
                for copy in x_copies(c + AHEAD - PIECES):
                    copy.start()
            part = slice(cuts[c], cuts[c + 1])
            total += dot(x0[:, part], w[part, :])
        keep(total[:first], pl.ds(0, first))
        for copy in out_copies(0):
            copy.start()
        shape = (n * GROUP_ROWS, own_rows)
        to, fro = iota(shape, 0), iota(shape, 1)
        owner, rs = to // GROUP_ROWS, to % GROUP_ROWS
        wanted = owner * ROWS_DEV + row_of(rs) + jnp.where(rs >= ROWS_DEV, ROWS_DEV * n, 0)
        pick = ((fro == wanted) & (rs < STEPS * ROWS_DEV)).astype(jnp.float32).astype(jnp.bfloat16)
        own = dot(pick, total[first:].astype(jnp.bfloat16))
        own_ref[...] = own.astype(jnp.bfloat16)
        for copy in ints:
            copy.wait()
        found = block_of_pages(counts, done, placed, table)
        lane = iota((n * GROUP_ROWS, HD), 1)
        r = row_of(lane % GROUP_ROWS)
        kind = lane // GROUP_ROWS
        facts = jnp.where(
            kind == 0,
            by_row(r, [found[i][0] for i in range(ROWS_DEV)], -1),
            jnp.where(
                kind == 1,
                by_row(r, [found[i][1] for i in range(ROWS_DEV)], -1),
                by_row(r, [lens[i] for i in range(ROWS_DEV)], 0),
            ),
        ).astype(jnp.float32)
        sixth = iota((n * GROUP_ROWS, HD), 0) % GROUP_ROWS == 6
        msg_ref[:, :HD] = jnp.where(sixth, facts, own[:, :HD]).astype(jnp.bfloat16)
        msg_ref[:, HD:] = own[:, HD:].astype(jnp.bfloat16)

    @pl.when((step > 0) & (step + AHEAD <= count))
    def _():
        for copy in x_copies(step + AHEAD - 1):
            copy.start()

    @pl.when(step > 0)
    def _():
        for copy in x_copies(step - 1):
            copy.wait()
        keep(dot(xs[step - 1], w[...]), pl.ds(pl.multiple_of(first + (step - 1) * size, 64), size))
        for copy in out_copies(step):
            copy.start()

    @pl.when(step == count)
    def _():
        for copy in out_copies(0):
            copy.wait()
        for k in range(1, count + 1):
            for copy in out_copies(jnp.int32(k)):
                copy.wait()


def project_all(ints, dx, x, wq, wkv, n, first, size):
    rows, depth = x.shape
    cq, ckv = wq.shape[1], wkv.shape[1]
    lq = cq // HD
    count = (rows - first) // size
    vmem, hbm = pl.BlockSpec(memory_space=VMEM), pl.BlockSpec(memory_space=pl.ANY)
    return pl.pallas_call(
        functools.partial(project, n, lq, first, size),
        grid=(1 + count,),
        in_specs=[hbm] * 9,
        out_specs=[hbm, hbm, vmem, vmem],
        out_shape=[
            jax.ShapeDtypeStruct((rows, WIDE), jnp.bfloat16),
            jax.ShapeDtypeStruct((rows, ckv), jnp.bfloat16),
            jax.ShapeDtypeStruct((n * GROUP_ROWS, cq + ckv), jnp.bfloat16),
            jax.ShapeDtypeStruct((n * GROUP_ROWS, cq + ckv), jnp.bfloat16),
        ],
        scratch_shapes=[
            VMEM((first + dx.shape[0], depth), jnp.bfloat16),
            VMEM((count, size, depth), jnp.bfloat16),
            VMEM((depth, cq + ckv), jnp.bfloat16),
            VMEM((rows, cq), jnp.bfloat16),
            VMEM((rows, ckv), jnp.bfloat16),
            pltpu.SemaphoreType.DMA((count, STRIPS)),
            pltpu.SemaphoreType.DMA((4, PIECES)),
            pltpu.SemaphoreType.DMA((3, count + 1)),
        ]
        + int_scratch(ints),
        compiler_params=pltpu.CompilerParams(vmem_limit_bytes=62 * MIB),
        cost_estimate=pl.CostEstimate(
            flops=2 * rows * depth * (cq + ckv),
            bytes_accessed=2 * (rows + cq + ckv) * depth + 2 * rows * (cq + ckv),
            transcendentals=0,
        ),
        name="project",
    )(*ints, dx, x, wq, wkv)


def attend_prompt(lq, half, counts, q_hbm, *refs):
    o_hbm, qs, kvs, outs, sems = refs[-5:]
    group = lax.axis_index("pool")
    c0, c1 = counts[group, 0], counts[group, 1]
    big = jnp.where(c0 == MOST_BLOCKS, 0, jnp.where(c1 == MOST_BLOCKS, c0, c0 + c1))
    cut = jnp.where(c0 == MOST_BLOCKS, c1, c0)
    loads, stores = [], []
    strip, early = (4, 3) if half == 0 else (1, 5)
    for j in range(0, MOST_BLOCKS, strip):
        block = big + j if half == 0 else j + jnp.where(j >= big, MOST_BLOCKS, 0)
        rows = pl.ds(pl.multiple_of(block * BLOCK_TOKENS, BLOCK_TOKENS), strip * BLOCK_TOKENS)
        here = pl.ds(j * BLOCK_TOKENS, strip * BLOCK_TOKENS)
        cq = lq * HD
        keys_values, queries = q_hbm.at[rows, pl.ds(cq, 2 * HD)], q_hbm.at[rows, pl.ds(0, cq)]
        loads.append(pltpu.make_async_copy(keys_values, kvs.at[here], sems.at[0, j]))
        loads.append(pltpu.make_async_copy(queries, qs.at[here], sems.at[1, j]))
        stores.append(pltpu.make_async_copy(outs.at[here], o_hbm.at[rows], sems.at[2, j]))
    for copy in loads:
        copy.start()
    near = len(loads) // 2
    for copy in loads[:near]:
        copy.wait()
    shape = (BLOCK_TOKENS, lq * BLOCK_TOKENS)
    causal = iota(shape, 0) <= iota(shape, 1) % BLOCK_TOKENS
    tokens = MOST_BLOCKS * BLOCK_TOKENS
    flipped = kvs[: tokens // 2, HD:].T

    def scores_of(j):
        q = qs[j * BLOCK_TOKENS : (j + 1) * BLOCK_TOKENS, :]
        q = jnp.concatenate([q[:, h * HD : (h + 1) * HD] for h in range(lq)], axis=0)
        return dot_t(kvs[: (j + 1) * BLOCK_TOKENS, :HD], q)

    scores = scores_of(0)
    for j in range(MOST_BLOCKS):
        if j + 1 == MOST_BLOCKS // 2:
            for copy in loads[near:]:
                copy.wait()
            flipped = jnp.concatenate([flipped, kvs[tokens // 2 :, HD:].T], axis=1)
        later = scores_of(j + 1) if j + 1 < MOST_BLOCKS else None
        weights = []
        for h in range(lq):
            cols = slice(h * BLOCK_TOKENS, (h + 1) * BLOCK_TOKENS)
            tiles = []
            for i in range(j + 1):
                tile = scores[i * BLOCK_TOKENS : (i + 1) * BLOCK_TOKENS, cols]
                if i == j:
                    tile = jnp.where(causal[:, cols], tile, MASKED)
                elif half == 1:
                    tile = tile + jnp.where((i < cut) & (cut <= j), MASKED, 0.0)
                tiles.append(tile)
            peak = jnp.max(functools.reduce(jnp.maximum, tiles), axis=0, keepdims=True)
            raised = [jnp.exp2((tile - peak) * (SCALE * LOG2E)) for tile in tiles]
            inverse = 1.0 / jnp.sum(functools.reduce(jnp.add, raised), axis=0, keepdims=True)
            weights.append(jnp.concatenate([(t * inverse).astype(jnp.bfloat16) for t in raised], axis=0))
        mixed = dot(flipped[:, : (j + 1) * BLOCK_TOKENS], jnp.concatenate(weights, axis=1))
        mixed = mixed.astype(jnp.bfloat16)
        for h in range(lq):
            part = mixed[:, h * BLOCK_TOKENS : (h + 1) * BLOCK_TOKENS].T
            outs[j * BLOCK_TOKENS : (j + 1) * BLOCK_TOKENS, h * HD : (h + 1) * HD] = part
        scores = later
        if j == early:
            for copy in stores[: (j + 1) // strip]:
                copy.start()
    for copy in stores[(early + 1) // strip :]:
        copy.start()
    for copy in stores:
        copy.wait()


def prompt_attention(counts, q, cq, half, so_far=None):
    rows = q.shape[0]
    hbm = pl.BlockSpec(memory_space=pl.ANY)
    more = () if so_far is None else (so_far,)
    tokens = MOST_BLOCKS * BLOCK_TOKENS
    return pl.pallas_call(
        functools.partial(attend_prompt, cq // HD, half),
        in_specs=[pl.BlockSpec(memory_space=SMEM), hbm] + [hbm] * len(more),
        out_specs=hbm,
        out_shape=jax.ShapeDtypeStruct((rows, cq), jnp.bfloat16),
        scratch_shapes=[
            VMEM((tokens, cq), jnp.bfloat16),
            VMEM((tokens, 2 * HD), jnp.bfloat16),
            VMEM((tokens, cq), jnp.bfloat16),
            pltpu.SemaphoreType.DMA((3, MOST_BLOCKS)),
        ],
        input_output_aliases={2: 0} if more else {},
        compiler_params=pltpu.CompilerParams(vmem_limit_bytes=(62 if half == 0 else 48) * MIB),
        cost_estimate=pl.CostEstimate(flops=2 * rows * rows * cq, bytes_accessed=4 * rows * cq, transcendentals=rows * rows // 2),
        name="long_prompt" if half == 0 else "short_prompts",
    )(counts, q, *more)


def row_head(n, lq, h, hh):
    at = h * GQ + hh
    return at // lq, at % lq


def handed_part(n, lq, kv_ref, own_ref, msg_ref, _, o_ref, __):
    rows = lq * n * GROUP_ROWS
    shape = (rows, HD)
    at_row, lane = iota(shape, 0), iota(shape, 1)
    rs = at_row % GROUP_ROWS
    facts = msg_ref[:, :HD].astype(jnp.float32).reshape(n, GROUP_ROWS, HD)[:, 6:7, :]
    facts = jnp.broadcast_to(facts, (n, GROUP_ROWS, HD)).reshape(n * GROUP_ROWS, HD)
    facts = jnp.concatenate([facts] * lq, axis=0)

    def column(kind):
        return jnp.sum(jnp.where(lane == kind * GROUP_ROWS + rs, facts, 0.0), axis=1, keepdims=True)

    first_block, second_block, length = [column(kind) for kind in range(3)]
    own = own_ref[...]
    queries = jnp.concatenate([own[:, h * HD : (h + 1) * HD] for h in range(lq)], axis=0)
    scores = dot_t(queries, kv_ref[:, :HD]) * SCALE
    lane_f = lane.astype(jnp.float32)
    parts = []
    for b in range(NBLK):
        limit = jnp.where(
            first_block == b, length, jnp.where(second_block == b, length - BLOCK_TOKENS, 0.0)
        )
        part = scores[:, b * BLOCK_TOKENS : (b + 1) * BLOCK_TOKENS]
        parts.append(jnp.where(lane_f < limit, part, MASKED))
    scores = jnp.concatenate(parts, axis=1)
    top = jnp.max(scores, axis=1, keepdims=True)
    raised = jnp.exp(scores - top)
    total = jnp.sum(raised, axis=1, keepdims=True)
    near = raised.astype(jnp.bfloat16)
    rest = (raised - near.astype(jnp.float32)).astype(jnp.bfloat16)
    values = kv_ref[:, HD:]
    mixed = (dot(near, values) + dot(rest, values)).reshape(lq * n, GROUP_ROWS, HD)

    def line(col):
        spread = jnp.where(lane == rs, col, 0.0).reshape(lq * n, GROUP_ROWS, HD)
        return jnp.sum(spread, axis=1, keepdims=True)

    rs3 = rs.reshape(lq * n, GROUP_ROWS, HD)
    mixed = jnp.where(rs3 == 6, line(top), jnp.where(rs3 == 7, line(total), mixed))
    for h in range(lq):
        o_ref[:, h * GROUP_ROWS : (h + 1) * GROUP_ROWS, :] = mixed[h * n : (h + 1) * n]


def handed_attention(kv, own, msgs, prompt_attn, n, lq):
    rows = lq * n * GROUP_ROWS
    vmem, hbm = pl.BlockSpec(memory_space=VMEM), pl.BlockSpec(memory_space=pl.ANY)
    return pl.pallas_call(
        functools.partial(handed_part, n, lq),
        in_specs=[vmem] * 3 + [hbm],
        out_specs=[vmem, hbm],
        out_shape=[
            jax.ShapeDtypeStruct((n, lq * GROUP_ROWS, HD), jnp.float32),
            jax.ShapeDtypeStruct(prompt_attn.shape, prompt_attn.dtype),
        ],
        input_output_aliases={3: 1},
        compiler_params=pltpu.CompilerParams(vmem_limit_bytes=24 * MIB),
        cost_estimate=pl.CostEstimate(flops=6 * rows * HD * PTOK, bytes_accessed=2 * MIB, transcendentals=rows * PTOK),
        name="handed_attention",
    )(kv, own, msgs, prompt_attn)


def owner_part(n, lq, *refs):
    cache, msgs, handed, o_ref, slot_row, slot_limit = refs[5:11]
    counts, done, placed, table, lens, int_sems = refs[11:]
    ints = int_copies(refs[:5], refs[11:16], int_sems)
    for copy in ints:
        copy.start()
    held = msgs[...].astype(jnp.float32)

    def tile(t, k):
        return held[t * GROUP_ROWS : (t + 1) * GROUP_ROWS, k * HD : (k + 1) * HD]

    groups = QH
    rows = groups * GROUP_ROWS
    span = GQ * GROUP_ROWS
    queries, keys, values = [], [], []
    for h in range(KVH):
        for hh in range(GQ):
            t, at = row_head(n, lq, h, hh)
            queries.append(tile(t, at))
        t, _ = row_head(n, lq, h, 0)
        keys += [tile(t, lq)] * GQ
        values.append(tile(t, lq + 1))
    queries = jnp.concatenate(queries, axis=0)
    earlier = jnp.concatenate([pltpu.roll(key, ROWS_DEV, 0) for key in keys], axis=0)
    keys = jnp.concatenate(keys, axis=0)
    at_row, lane = iota((rows, HD), 0), iota((rows, HD), 1)
    r = row_of(at_row % GROUP_ROWS)
    rounded = queries.astype(jnp.bfloat16)
    now = jnp.sum(queries * keys, axis=1, keepdims=True) * SCALE
    before = jnp.sum(queries * earlier, axis=1, keepdims=True) * SCALE
    rs1 = iota((rows, 1), 0) % GROUP_ROWS
    before = jnp.where((rs1 >= ROWS_DEV) & (rs1 < STEPS * ROWS_DEV), before, MASKED)
    mixed = handed[...].reshape(groups, GROUP_ROWS, HD)
    shape = (groups, GROUP_ROWS, HD)
    mine = iota(shape, 1) == iota(shape, 2)

    def column(at):
        line = jnp.broadcast_to(mixed[:, at : at + 1, :], shape)
        return jnp.sum(jnp.where(mine, line, 0.0), axis=2, keepdims=True).reshape(rows, 1)

    other_peak, other_total = column(6), column(7)
    for copy in ints:
        copy.wait()
    found = block_of_pages(counts, done, placed, table)
    for k in range(ROWS_DEV):
        for p in range(PAGES):
            slot_row[table[p, k]] = jnp.int32(k)
            slot_limit[table[p, k]] = jnp.where(found[k][p] < 0, lens[k] - p * BLOCK_TOKENS, 0)
    scores = jnp.concatenate(
        [dot_t(rounded[h * span : (h + 1) * span], cache[:, 2 * h * HD : (2 * h + 1) * HD]) for h in range(KVH)],
        axis=0,
    )
    parts = []
    for slot in range(DEVICE_SLOTS):
        part = scores[:, slot * BLOCK_TOKENS : (slot + 1) * BLOCK_TOKENS]
        usable = (r == slot_row[slot]) & (lane < slot_limit[slot])
        parts.append(jnp.where(usable, part * SCALE, MASKED))
    scores = jnp.concatenate(parts, axis=1)
    peak = jnp.maximum(jnp.max(scores, axis=1, keepdims=True), jnp.maximum(now, before))
    peak = jnp.maximum(peak, other_peak)
    raised, now, before = jnp.exp(scores - peak), jnp.exp(now - peak), jnp.exp(before - peak)
    other = jnp.exp(other_peak - peak)
    inverse = 1.0 / (jnp.sum(raised, axis=1, keepdims=True) + now + before + other * other_total)
    weights = (raised * inverse).astype(jnp.bfloat16)
    now = (now * inverse).astype(jnp.bfloat16).astype(jnp.float32)
    before = (before * inverse).astype(jnp.bfloat16).astype(jnp.float32)
    mixed = mixed.reshape(rows, HD) * (other * inverse)
    out = []
    for h in range(KVH):
        part = slice(h * span, (h + 1) * span)
        own = mixed[part] + dot(weights[part], cache[:, (2 * h + 1) * HD : (2 * h + 2) * HD])
        last = pltpu.roll(values[h], ROWS_DEV, 0)
        for hh in range(GQ):
            some = slice(h * span + hh * GROUP_ROWS, h * span + (hh + 1) * GROUP_ROWS)
            line = own[hh * GROUP_ROWS : (hh + 1) * GROUP_ROWS]
            out.append(line + now[some] * values[h] + before[some] * last)
    out = jnp.concatenate(out, axis=1)
    for k in range(ROWS_DEV):
        steps = [out[s * ROWS_DEV + k : s * ROWS_DEV + k + 1] for s in range(STEPS)]
        o_ref[k] = jnp.concatenate(steps, axis=0).astype(jnp.bfloat16)


def decode_attention(ints, cache, msgs, parts, n, lq):
    vmem, hbm = pl.BlockSpec(memory_space=VMEM), pl.BlockSpec(memory_space=pl.ANY)
    rows = QH * GROUP_ROWS
    return pl.pallas_call(
        functools.partial(owner_part, n, lq),
        in_specs=[hbm] * 5 + [vmem] * 3,
        out_specs=vmem,
        out_shape=jax.ShapeDtypeStruct((ROWS_DEV, STEPS, QH * HD), jnp.bfloat16),
        scratch_shapes=[
            SMEM((DEVICE_SLOTS,), jnp.int32),
            SMEM((DEVICE_SLOTS,), jnp.int32),
        ]
        + int_scratch(ints),
        compiler_params=pltpu.CompilerParams(vmem_limit_bytes=40 * MIB),
        cost_estimate=pl.CostEstimate(flops=4 * rows * HD * 768, bytes_accessed=4 * MIB, transcendentals=rows * 768),
        name="decode_attention",
    )(*ints, cache, msgs, parts)


def local(
    prompt_x,
    q_weight,
    kv_weight,
    prompt_blocks,
    finished,
    placement,
    page_table,
    row_lens,
    kv_cache,
    decode_x,
):
    n = lax.axis_size("tp")
    lq = q_weight.shape[1] // HD
    share = GQ // lq
    if share > 1:
        sets = [[k * share + i for i in range(share)] for k in range(n // share)]
        kv_weight = lax.all_gather(kv_weight, "tp", axis=1, tiled=True, axis_index_groups=sets)
    cache = kv_cache.reshape(-1, kv_cache.shape[2])
    dx = decode_x.reshape(-1, decode_x.shape[2])
    placement = placement.transpose(0, 2, 1)
    page_table = page_table.transpose(1, 0)
    ints = (prompt_blocks, finished, placement, page_table, row_lens)
    first, size = 256, 448
    q, kv, own, msgs = project_all(ints, dx, prompt_x, q_weight, kv_weight, n, first, size)
    kv_other = lax.ppermute(kv, "pool", [(0, 1), (1, 0)])
    msgs = lax.all_to_all(msgs, "tp", split_axis=0, concat_axis=0, tiled=True)
    prompt_attn = prompt_attention(prompt_blocks, q, q_weight.shape[1], 0)
    handed, prompt_attn = handed_attention(kv_other, own, msgs, prompt_attn, n, lq)
    parts = lax.all_to_all(handed, "tp", split_axis=0, concat_axis=0, tiled=True)
    prompt_attn = prompt_attention(prompt_blocks, q, q_weight.shape[1], 1, prompt_attn)
    decode_attn = decode_attention(ints, cache, msgs, parts, n, lq)
    return prompt_attn, decode_attn.transpose(1, 0, 2)


def solution(mesh):
    return jax.shard_map(
        local,
        mesh=mesh,
        in_specs=(
            P(("rep", "pool"), None),
            P(None, "tp"),
            P(None, "tp"),
            P("rep", None),
            P("rep", None),
            P("rep", None, None),
            P(("rep", "pool", "tp"), None),
            P(("rep", "pool", "tp")),
            P(("rep", "pool", "tp"), None, None),
            P(None, ("rep", "pool"), None),
        ),
        out_specs=(P(("rep", "pool"), "tp"), P(None, ("rep", "pool", "tp"), None)),
        check_vma=False,
    )
```

```python
import functools

import jax
import jax.numpy as jnp
from jax import lax
from jax.experimental import pallas as pl
from jax.experimental.pallas import tpu as pltpu
from jax.sharding import PartitionSpec as P

QH = 32
KVH = 8
GQ = QH // KVH
HD = 128
BLOCK_TOKENS = 128
PTOK = 2048
NPROMPT = 3
MOST_BLOCKS = 8
PAGES = 2
STEPS = 2
NBLK = 16
DEVICE_SLOTS = 6
ROWS_DEV = 3
GROUP_ROWS = 8
KEY_VALUE_COLUMNS = 2048
SCALE = HD ** (-0.5)
MASKED = -1e30
PIECES = 5
STRIPS = 4
WIDE = 2048
LOG2E = 1.4426950408889634
AHEAD = 3
MIB = 1 << 20
VMEM = pltpu.VMEM
SMEM = pltpu.SMEM


def dot(a, b):
    return jnp.dot(a, b, preferred_element_type=jnp.float32)


def dot_t(a, b):
    return lax.dot_general(a, b, (((1,), (1,)), ((), ())), preferred_element_type=jnp.float32)


def iota(shape, axis):
    return lax.broadcasted_iota(jnp.int32, shape, axis)


def row_of(rs):
    return jnp.where(rs >= 2 * ROWS_DEV, ROWS_DEV, jnp.where(rs >= ROWS_DEV, rs - ROWS_DEV, rs))


def block_of_pages(counts, done, placed, table):
    me = lax.axis_index("tp")
    other = 1 - lax.axis_index("pool")
    first_end = counts[other, 0]
    second_end = first_end + counts[other, 1]
    found = [[jnp.int32(-1)] * PAGES for _ in range(ROWS_DEV)]
    for b in range(NBLK):
        live = jnp.where(
            b < first_end, done[other, 0], jnp.where(b < second_end, done[other, 1], done[other, 2])
        )
        slot = jnp.where((live > 0) & (placed[other, 0, b] == me), placed[other, 1, b], -1)
        for r in range(ROWS_DEV):
            for p in range(PAGES):
                found[r][p] = jnp.where(slot == table[p, r], b, found[r][p])
    return found


def by_row(r, values, rest):
    out = jnp.full(r.shape, rest, jnp.int32)
    for k in range(ROWS_DEV):
        out = jnp.where(r == k, values[k], out)
    return out


def int_scratch(ints):
    return [SMEM(x.shape, jnp.int32) for x in ints] + [pltpu.SemaphoreType.DMA((len(ints),))]


def int_copies(sources, targets, sems):
    return [pltpu.make_async_copy(a, b, sems.at[i]) for i, (a, b) in enumerate(zip(sources, targets))]


def project(n, lq, first, size, *refs):
    dx_hbm, x_hbm, wq_hbm, wkv_hbm = refs[5:9]
    q_hbm, kv_hbm, own_ref, msg_ref = refs[9:13]
    x0, xs, w, q_out, kv_out, x_sems, w_sems, out_sems = refs[13:21]
    counts, done, placed, table, lens, int_sems = refs[21:]
    ints = int_copies(refs[:5], refs[21:26], int_sems)
    depth = w.shape[0]
    count = xs.shape[0]
    cq = lq * HD
    piece = depth // PIECES
    own_rows = dx_hbm.shape[0]
    step = pl.program_id(0)

    def piece_copies(c):
        part = pl.ds(c * piece, piece)
        return [
            pltpu.make_async_copy(x_hbm.at[pl.ds(0, first), part], x0.at[pl.ds(0, first), part], w_sems.at[0, c]),
            pltpu.make_async_copy(dx_hbm.at[:, part], x0.at[pl.ds(first, own_rows), part], w_sems.at[1, c]),
            pltpu.make_async_copy(wq_hbm.at[part], w.at[part, pl.ds(0, cq)], w_sems.at[2, c]),
            pltpu.make_async_copy(wkv_hbm.at[part], w.at[part, pl.ds(cq, 2 * HD)], w_sems.at[3, c]),
        ]

    def x_copies(k):
        strip = size // STRIPS
        copies = []
        for i in range(STRIPS):
            rows = pl.ds(pl.multiple_of(first + k * size + i * strip, 16), strip)
            copies.append(
                pltpu.make_async_copy(x_hbm.at[rows], xs.at[k, pl.ds(i * strip, strip)], x_sems.at[k, i])
            )
        return copies

    def out_copies(k):
        if isinstance(k, int):
            rows = pl.ds(0, first)
        else:
            rows = pl.ds(pl.multiple_of(first + (k - 1) * size, 64), size)
        return [
            pltpu.make_async_copy(q_out.at[rows], q_hbm.at[rows, pl.ds(0, cq)], out_sems.at[0, k]),
            pltpu.make_async_copy(kv_out.at[rows], q_hbm.at[rows, pl.ds(cq, 2 * HD)], out_sems.at[1, k]),
            pltpu.make_async_copy(kv_out.at[rows], kv_hbm.at[rows], out_sems.at[2, k]),
        ]

    def keep(total, rows):
        q_out[rows, :] = total[:, :cq].astype(jnp.bfloat16)
        kv_out[rows, :] = total[:, cq:].astype(jnp.bfloat16)

    @pl.when(step == 0)
    def _():
        for c in range(AHEAD):
            for copy in piece_copies(c):
                copy.start()
        for copy in ints:
            copy.start()
        total = 0.0
        for c in range(PIECES):
            for copy in piece_copies(c):
                copy.wait()
            if c + AHEAD < PIECES:
                for copy in piece_copies(c + AHEAD):
                    copy.start()
            if c + AHEAD >= PIECES:
                for copy in x_copies(c + AHEAD - PIECES):
                    copy.start()
            part = slice(c * piece, (c + 1) * piece)
            total += dot(x0[:, part], w[part, :])
        keep(total[:first], pl.ds(0, first))
        for copy in out_copies(0):
            copy.start()
        shape = (n * GROUP_ROWS, own_rows)
        to, fro = iota(shape, 0), iota(shape, 1)
        owner, rs = to // GROUP_ROWS, to % GROUP_ROWS
        wanted = owner * ROWS_DEV + row_of(rs) + jnp.where(rs >= ROWS_DEV, ROWS_DEV * n, 0)
        pick = ((fro == wanted) & (rs < STEPS * ROWS_DEV)).astype(jnp.float32).astype(jnp.bfloat16)
        own = dot(pick, total[first:].astype(jnp.bfloat16))
        own_ref[...] = own.astype(jnp.bfloat16)
        for copy in ints:
            copy.wait()
        found = block_of_pages(counts, done, placed, table)
        lane = iota((n * GROUP_ROWS, HD), 1)
        r = row_of(lane % GROUP_ROWS)
        kind = lane // GROUP_ROWS
        facts = jnp.where(
            kind == 0,
            by_row(r, [found[i][0] for i in range(ROWS_DEV)], -1),
            jnp.where(
                kind == 1,
                by_row(r, [found[i][1] for i in range(ROWS_DEV)], -1),
                by_row(r, [lens[i] for i in range(ROWS_DEV)], 0),
            ),
        ).astype(jnp.float32)
        sixth = iota((n * GROUP_ROWS, HD), 0) % GROUP_ROWS == 6
        msg_ref[:, :HD] = jnp.where(sixth, facts, own[:, :HD]).astype(jnp.bfloat16)
        msg_ref[:, HD:] = own[:, HD:].astype(jnp.bfloat16)

    @pl.when((step > 0) & (step + AHEAD <= count))
    def _():
        for copy in x_copies(step + AHEAD - 1):
            copy.start()

    @pl.when(step > 0)
    def _():
        for copy in x_copies(step - 1):
            copy.wait()
        keep(dot(xs[step - 1], w[...]), pl.ds(pl.multiple_of(first + (step - 1) * size, 64), size))
        for copy in out_copies(step):
            copy.start()

    @pl.when(step == count)
    def _():
        for copy in out_copies(0):
            copy.wait()
        for k in range(1, count + 1):
            for copy in out_copies(jnp.int32(k)):
                copy.wait()


def project_all(ints, dx, x, wq, wkv, n, first, size):
    rows, depth = x.shape
    cq, ckv = wq.shape[1], wkv.shape[1]
    lq = cq // HD
    count = (rows - first) // size
    vmem, hbm = pl.BlockSpec(memory_space=VMEM), pl.BlockSpec(memory_space=pl.ANY)
    return pl.pallas_call(
        functools.partial(project, n, lq, first, size),
        grid=(1 + count,),
        in_specs=[hbm] * 9,
        out_specs=[hbm, hbm, vmem, vmem],
        out_shape=[
            jax.ShapeDtypeStruct((rows, WIDE), jnp.bfloat16),
            jax.ShapeDtypeStruct((rows, ckv), jnp.bfloat16),
            jax.ShapeDtypeStruct((n * GROUP_ROWS, cq + ckv), jnp.bfloat16),
            jax.ShapeDtypeStruct((n * GROUP_ROWS, cq + ckv), jnp.bfloat16),
        ],
        scratch_shapes=[
            VMEM((first + dx.shape[0], depth), jnp.bfloat16),
            VMEM((count, size, depth), jnp.bfloat16),
            VMEM((depth, cq + ckv), jnp.bfloat16),
            VMEM((rows, cq), jnp.bfloat16),
            VMEM((rows, ckv), jnp.bfloat16),
            pltpu.SemaphoreType.DMA((count, STRIPS)),
            pltpu.SemaphoreType.DMA((4, PIECES)),
            pltpu.SemaphoreType.DMA((3, count + 1)),
        ]
        + int_scratch(ints),
        compiler_params=pltpu.CompilerParams(vmem_limit_bytes=62 * MIB),
        cost_estimate=pl.CostEstimate(
            flops=2 * rows * depth * (cq + ckv),
            bytes_accessed=2 * (rows + cq + ckv) * depth + 2 * rows * (cq + ckv),
            transcendentals=0,
        ),
        name="project",
    )(*ints, dx, x, wq, wkv)


def attend_prompt(lq, half, counts, q_hbm, *refs):
    o_hbm, qs, kvs, outs, sems = refs[-5:]
    group = lax.axis_index("pool")
    c0, c1 = counts[group, 0], counts[group, 1]
    big = jnp.where(c0 == MOST_BLOCKS, 0, jnp.where(c1 == MOST_BLOCKS, c0, c0 + c1))
    cut = jnp.where(c0 == MOST_BLOCKS, c1, c0)
    loads, stores = [], []
    strip, early = (4, 3) if half == 0 else (1, 5)
    for j in range(0, MOST_BLOCKS, strip):
        block = big + j if half == 0 else j + jnp.where(j >= big, MOST_BLOCKS, 0)
        rows = pl.ds(pl.multiple_of(block * BLOCK_TOKENS, BLOCK_TOKENS), strip * BLOCK_TOKENS)
        here = pl.ds(j * BLOCK_TOKENS, strip * BLOCK_TOKENS)
        cq = lq * HD
        keys_values, queries = q_hbm.at[rows, pl.ds(cq, 2 * HD)], q_hbm.at[rows, pl.ds(0, cq)]
        loads.append(pltpu.make_async_copy(keys_values, kvs.at[here], sems.at[0, j]))
        loads.append(pltpu.make_async_copy(queries, qs.at[here], sems.at[1, j]))
        stores.append(pltpu.make_async_copy(outs.at[here], o_hbm.at[rows], sems.at[2, j]))
    for copy in loads:
        copy.start()
    near = len(loads) // 2
    for copy in loads[:near]:
        copy.wait()
    shape = (BLOCK_TOKENS, lq * BLOCK_TOKENS)
    causal = iota(shape, 0) <= iota(shape, 1) % BLOCK_TOKENS
    tokens = MOST_BLOCKS * BLOCK_TOKENS
    flipped = kvs[: tokens // 2, HD:].T

    def scores_of(j):
        q = qs[j * BLOCK_TOKENS : (j + 1) * BLOCK_TOKENS, :]
        q = jnp.concatenate([q[:, h * HD : (h + 1) * HD] for h in range(lq)], axis=0)
        return dot_t(kvs[: (j + 1) * BLOCK_TOKENS, :HD], q)

    scores = scores_of(0)
    for j in range(MOST_BLOCKS):
        if j + 1 == MOST_BLOCKS // 2:
            for copy in loads[near:]:
                copy.wait()
            flipped = jnp.concatenate([flipped, kvs[tokens // 2 :, HD:].T], axis=1)
        later = scores_of(j + 1) if j + 1 < MOST_BLOCKS else None
        weights = []
        for h in range(lq):
            cols = slice(h * BLOCK_TOKENS, (h + 1) * BLOCK_TOKENS)
            tiles = []
            for i in range(j + 1):
                tile = scores[i * BLOCK_TOKENS : (i + 1) * BLOCK_TOKENS, cols]
                if i == j:
                    tile = jnp.where(causal[:, cols], tile, MASKED)
                elif half == 1:
                    tile = tile + jnp.where((i < cut) & (cut <= j), MASKED, 0.0)
                tiles.append(tile)
            peak = jnp.max(functools.reduce(jnp.maximum, tiles), axis=0, keepdims=True)
            raised = [jnp.exp2((tile - peak) * (SCALE * LOG2E)) for tile in tiles]
            inverse = 1.0 / jnp.sum(functools.reduce(jnp.add, raised), axis=0, keepdims=True)
            weights.append(jnp.concatenate([(t * inverse).astype(jnp.bfloat16) for t in raised], axis=0))
        mixed = dot(flipped[:, : (j + 1) * BLOCK_TOKENS], jnp.concatenate(weights, axis=1))
        mixed = mixed.astype(jnp.bfloat16)
        for h in range(lq):
            part = mixed[:, h * BLOCK_TOKENS : (h + 1) * BLOCK_TOKENS].T
            outs[j * BLOCK_TOKENS : (j + 1) * BLOCK_TOKENS, h * HD : (h + 1) * HD] = part
        scores = later
        if j == early:
            for copy in stores[: (j + 1) // strip]:
                copy.start()
    for copy in stores[(early + 1) // strip :]:
        copy.start()
    for copy in stores:
        copy.wait()


def prompt_attention(counts, q, cq, half, so_far=None):
    rows = q.shape[0]
    hbm = pl.BlockSpec(memory_space=pl.ANY)
    more = () if so_far is None else (so_far,)
    tokens = MOST_BLOCKS * BLOCK_TOKENS
    return pl.pallas_call(
        functools.partial(attend_prompt, cq // HD, half),
        in_specs=[pl.BlockSpec(memory_space=SMEM), hbm] + [hbm] * len(more),
        out_specs=hbm,
        out_shape=jax.ShapeDtypeStruct((rows, cq), jnp.bfloat16),
        scratch_shapes=[
            VMEM((tokens, cq), jnp.bfloat16),
            VMEM((tokens, 2 * HD), jnp.bfloat16),
            VMEM((tokens, cq), jnp.bfloat16),
            pltpu.SemaphoreType.DMA((3, MOST_BLOCKS)),
        ],
        input_output_aliases={2: 0} if more else {},
        compiler_params=pltpu.CompilerParams(vmem_limit_bytes=(62 if half == 0 else 48) * MIB),
        cost_estimate=pl.CostEstimate(flops=2 * rows * rows * cq, bytes_accessed=4 * rows * cq, transcendentals=rows * rows // 2),
        name="long_prompt" if half == 0 else "short_prompts",
    )(counts, q, *more)


def row_head(n, lq, h, hh):
    at = h * GQ + hh
    return at // lq, at % lq


def handed_part(n, lq, kv_ref, own_ref, msg_ref, _, o_ref, __):
    rows = lq * n * GROUP_ROWS
    shape = (rows, HD)
    at_row, lane = iota(shape, 0), iota(shape, 1)
    rs = at_row % GROUP_ROWS
    facts = msg_ref[:, :HD].astype(jnp.float32).reshape(n, GROUP_ROWS, HD)[:, 6:7, :]
    facts = jnp.broadcast_to(facts, (n, GROUP_ROWS, HD)).reshape(n * GROUP_ROWS, HD)
    facts = jnp.concatenate([facts] * lq, axis=0)

    def column(kind):
        return jnp.sum(jnp.where(lane == kind * GROUP_ROWS + rs, facts, 0.0), axis=1, keepdims=True)

    first_block, second_block, length = [column(kind) for kind in range(3)]
    own = own_ref[...]
    queries = jnp.concatenate([own[:, h * HD : (h + 1) * HD] for h in range(lq)], axis=0)
    scores = dot_t(queries, kv_ref[:, :HD]) * SCALE
    lane_f = lane.astype(jnp.float32)
    parts = []
    for b in range(NBLK):
        limit = jnp.where(
            first_block == b, length, jnp.where(second_block == b, length - BLOCK_TOKENS, 0.0)
        )
        part = scores[:, b * BLOCK_TOKENS : (b + 1) * BLOCK_TOKENS]
        parts.append(jnp.where(lane_f < limit, part, MASKED))
    scores = jnp.concatenate(parts, axis=1)
    top = jnp.max(scores, axis=1, keepdims=True)
    raised = jnp.exp(scores - top)
    total = jnp.sum(raised, axis=1, keepdims=True)
    near = raised.astype(jnp.bfloat16)
    rest = (raised - near.astype(jnp.float32)).astype(jnp.bfloat16)
    values = kv_ref[:, HD:]
    mixed = (dot(near, values) + dot(rest, values)).reshape(lq * n, GROUP_ROWS, HD)

    def line(col):
        spread = jnp.where(lane == rs, col, 0.0).reshape(lq * n, GROUP_ROWS, HD)
        return jnp.sum(spread, axis=1, keepdims=True)

    rs3 = rs.reshape(lq * n, GROUP_ROWS, HD)
    mixed = jnp.where(rs3 == 6, line(top), jnp.where(rs3 == 7, line(total), mixed))
    for h in range(lq):
        o_ref[:, h * GROUP_ROWS : (h + 1) * GROUP_ROWS, :] = mixed[h * n : (h + 1) * n]


def handed_attention(kv, own, msgs, prompt_attn, n, lq):
    rows = lq * n * GROUP_ROWS
    vmem, hbm = pl.BlockSpec(memory_space=VMEM), pl.BlockSpec(memory_space=pl.ANY)
    return pl.pallas_call(
        functools.partial(handed_part, n, lq),
        in_specs=[vmem] * 3 + [hbm],
        out_specs=[vmem, hbm],
        out_shape=[
            jax.ShapeDtypeStruct((n, lq * GROUP_ROWS, HD), jnp.float32),
            jax.ShapeDtypeStruct(prompt_attn.shape, prompt_attn.dtype),
        ],
        input_output_aliases={3: 1},
        compiler_params=pltpu.CompilerParams(vmem_limit_bytes=24 * MIB),
        cost_estimate=pl.CostEstimate(flops=6 * rows * HD * PTOK, bytes_accessed=2 * MIB, transcendentals=rows * PTOK),
        name="handed_attention",
    )(kv, own, msgs, prompt_attn)


def owner_part(n, lq, *refs):
    cache, msgs, handed, o_ref, slot_row, slot_limit = refs[5:11]
    counts, done, placed, table, lens, int_sems = refs[11:]
    ints = int_copies(refs[:5], refs[11:16], int_sems)
    for copy in ints:
        copy.start()
    held = msgs[...].astype(jnp.float32)

    def tile(t, k):
        return held[t * GROUP_ROWS : (t + 1) * GROUP_ROWS, k * HD : (k + 1) * HD]

    groups = QH
    rows = groups * GROUP_ROWS
    span = GQ * GROUP_ROWS
    queries, keys, values = [], [], []
    for h in range(KVH):
        for hh in range(GQ):
            t, at = row_head(n, lq, h, hh)
            queries.append(tile(t, at))
        t, _ = row_head(n, lq, h, 0)
        keys += [tile(t, lq)] * GQ
        values.append(tile(t, lq + 1))
    queries = jnp.concatenate(queries, axis=0)
    earlier = jnp.concatenate([pltpu.roll(key, ROWS_DEV, 0) for key in keys], axis=0)
    keys = jnp.concatenate(keys, axis=0)
    at_row, lane = iota((rows, HD), 0), iota((rows, HD), 1)
    r = row_of(at_row % GROUP_ROWS)
    rounded = queries.astype(jnp.bfloat16)
    now = jnp.sum(queries * keys, axis=1, keepdims=True) * SCALE
    before = jnp.sum(queries * earlier, axis=1, keepdims=True) * SCALE
    rs1 = iota((rows, 1), 0) % GROUP_ROWS
    before = jnp.where((rs1 >= ROWS_DEV) & (rs1 < STEPS * ROWS_DEV), before, MASKED)
    mixed = handed[...].reshape(groups, GROUP_ROWS, HD)
    shape = (groups, GROUP_ROWS, HD)
    mine = iota(shape, 1) == iota(shape, 2)

    def column(at):
        line = jnp.broadcast_to(mixed[:, at : at + 1, :], shape)
        return jnp.sum(jnp.where(mine, line, 0.0), axis=2, keepdims=True).reshape(rows, 1)

    other_peak, other_total = column(6), column(7)
    for copy in ints:
        copy.wait()
    found = block_of_pages(counts, done, placed, table)
    for k in range(ROWS_DEV):
        for p in range(PAGES):
            slot_row[table[p, k]] = jnp.int32(k)
            slot_limit[table[p, k]] = jnp.where(found[k][p] < 0, lens[k] - p * BLOCK_TOKENS, 0)
    scores = jnp.concatenate(
        [dot_t(rounded[h * span : (h + 1) * span], cache[:, 2 * h * HD : (2 * h + 1) * HD]) for h in range(KVH)],
        axis=0,
    )
    parts = []
    for slot in range(DEVICE_SLOTS):
        part = scores[:, slot * BLOCK_TOKENS : (slot + 1) * BLOCK_TOKENS]
        usable = (r == slot_row[slot]) & (lane < slot_limit[slot])
        parts.append(jnp.where(usable, part * SCALE, MASKED))
    scores = jnp.concatenate(parts, axis=1)
    peak = jnp.maximum(jnp.max(scores, axis=1, keepdims=True), jnp.maximum(now, before))
    peak = jnp.maximum(peak, other_peak)
    raised, now, before = jnp.exp(scores - peak), jnp.exp(now - peak), jnp.exp(before - peak)
    other = jnp.exp(other_peak - peak)
    inverse = 1.0 / (jnp.sum(raised, axis=1, keepdims=True) + now + before + other * other_total)
    weights = (raised * inverse).astype(jnp.bfloat16)
    now = (now * inverse).astype(jnp.bfloat16).astype(jnp.float32)
    before = (before * inverse).astype(jnp.bfloat16).astype(jnp.float32)
    mixed = mixed.reshape(rows, HD) * (other * inverse)
    out = []
    for h in range(KVH):
        part = slice(h * span, (h + 1) * span)
        own = mixed[part] + dot(weights[part], cache[:, (2 * h + 1) * HD : (2 * h + 2) * HD])
        last = pltpu.roll(values[h], ROWS_DEV, 0)
        for hh in range(GQ):
            some = slice(h * span + hh * GROUP_ROWS, h * span + (hh + 1) * GROUP_ROWS)
            line = own[hh * GROUP_ROWS : (hh + 1) * GROUP_ROWS]
            out.append(line + now[some] * values[h] + before[some] * last)
    out = jnp.concatenate(out, axis=1)
    for k in range(ROWS_DEV):
        steps = [out[s * ROWS_DEV + k : s * ROWS_DEV + k + 1] for s in range(STEPS)]
        o_ref[k] = jnp.concatenate(steps, axis=0).astype(jnp.bfloat16)


def decode_attention(ints, cache, msgs, parts, n, lq):
    vmem, hbm = pl.BlockSpec(memory_space=VMEM), pl.BlockSpec(memory_space=pl.ANY)
    rows = QH * GROUP_ROWS
    return pl.pallas_call(
        functools.partial(owner_part, n, lq),
        in_specs=[hbm] * 5 + [vmem] * 3,
        out_specs=vmem,
        out_shape=jax.ShapeDtypeStruct((ROWS_DEV, STEPS, QH * HD), jnp.bfloat16),
        scratch_shapes=[
            SMEM((DEVICE_SLOTS,), jnp.int32),
            SMEM((DEVICE_SLOTS,), jnp.int32),
        ]
        + int_scratch(ints),
        compiler_params=pltpu.CompilerParams(vmem_limit_bytes=40 * MIB),
        cost_estimate=pl.CostEstimate(flops=4 * rows * HD * 768, bytes_accessed=4 * MIB, transcendentals=rows * 768),
        name="decode_attention",
    )(*ints, cache, msgs, parts)


def local(
    prompt_x,
    q_weight,
    kv_weight,
    prompt_blocks,
    finished,
    placement,
    page_table,
    row_lens,
    kv_cache,
    decode_x,
):
    n = lax.axis_size("tp")
    lq = q_weight.shape[1] // HD
    share = GQ // lq
    if share > 1:
        sets = [[k * share + i for i in range(share)] for k in range(n // share)]
        kv_weight = lax.all_gather(kv_weight, "tp", axis=1, tiled=True, axis_index_groups=sets)
    cache = kv_cache.reshape(-1, kv_cache.shape[2])
    dx = decode_x.reshape(-1, decode_x.shape[2])
    placement = placement.transpose(0, 2, 1)
    page_table = page_table.transpose(1, 0)
    ints = (prompt_blocks, finished, placement, page_table, row_lens)
    first, size = 256, 448
    q, kv, own, msgs = project_all(ints, dx, prompt_x, q_weight, kv_weight, n, first, size)
    kv_other = lax.ppermute(kv, "pool", [(0, 1), (1, 0)])
    msgs = lax.all_to_all(msgs, "tp", split_axis=0, concat_axis=0, tiled=True)
    prompt_attn = prompt_attention(prompt_blocks, q, q_weight.shape[1], 0)
    handed, prompt_attn = handed_attention(kv_other, own, msgs, prompt_attn, n, lq)
    parts = lax.all_to_all(handed, "tp", split_axis=0, concat_axis=0, tiled=True)
    prompt_attn = prompt_attention(prompt_blocks, q, q_weight.shape[1], 1, prompt_attn)
    decode_attn = decode_attention(ints, cache, msgs, parts, n, lq)
    return prompt_attn, decode_attn.transpose(1, 0, 2)


def solution(mesh):
    return jax.shard_map(
        local,
        mesh=mesh,
        in_specs=(
            P(("rep", "pool"), None),
            P(None, "tp"),
            P(None, "tp"),
            P("rep", None),
            P("rep", None),
            P("rep", None, None),
            P(("rep", "pool", "tp"), None),
            P(("rep", "pool", "tp")),
            P(("rep", "pool", "tp"), None, None),
            P(None, ("rep", "pool"), None),
        ),
        out_specs=(P(("rep", "pool"), "tp"), P(None, ("rep", "pool", "tp"), None)),
        check_vma=False,
    )
```

```python
import functools

import jax
import jax.numpy as jnp
from jax import lax
from jax.experimental import pallas as pl
from jax.experimental.pallas import tpu as pltpu
from jax.sharding import PartitionSpec as P

QH = 32
KVH = 8
GQ = QH // KVH
HD = 128
BLOCK_TOKENS = 128
PTOK = 2048
NPROMPT = 3
MOST_BLOCKS = 8
PAGES = 2
STEPS = 2
NBLK = 16
DEVICE_SLOTS = 6
ROWS_DEV = 3
GROUP_ROWS = 8
KEY_VALUE_COLUMNS = 2048
SCALE = HD ** (-0.5)
MASKED = -1e30
PIECES = 5
STRIPS = 4
WIDE = 2048
LOG2E = 1.4426950408889634
AHEAD = 4
MIB = 1 << 20
VMEM = pltpu.VMEM
SMEM = pltpu.SMEM


def dot(a, b):
    return jnp.dot(a, b, preferred_element_type=jnp.float32)


def dot_t(a, b):
    return lax.dot_general(a, b, (((1,), (1,)), ((), ())), preferred_element_type=jnp.float32)


def iota(shape, axis):
    return lax.broadcasted_iota(jnp.int32, shape, axis)


def row_of(rs):
    return jnp.where(rs >= 2 * ROWS_DEV, ROWS_DEV, jnp.where(rs >= ROWS_DEV, rs - ROWS_DEV, rs))


def block_of_pages(counts, done, placed, table):
    me = lax.axis_index("tp")
    other = 1 - lax.axis_index("pool")
    first_end = counts[other, 0]
    second_end = first_end + counts[other, 1]
    found = [[jnp.int32(-1)] * PAGES for _ in range(ROWS_DEV)]
    for b in range(NBLK):
        live = jnp.where(
            b < first_end, done[other, 0], jnp.where(b < second_end, done[other, 1], done[other, 2])
        )
        slot = jnp.where((live > 0) & (placed[other, 0, b] == me), placed[other, 1, b], -1)
        for r in range(ROWS_DEV):
            for p in range(PAGES):
                found[r][p] = jnp.where(slot == table[p, r], b, found[r][p])
    return found


def by_row(r, values, rest):
    out = jnp.full(r.shape, rest, jnp.int32)
    for k in range(ROWS_DEV):
        out = jnp.where(r == k, values[k], out)
    return out


def int_scratch(ints):
    return [SMEM(x.shape, jnp.int32) for x in ints] + [pltpu.SemaphoreType.DMA((len(ints),))]


def int_copies(sources, targets, sems):
    return [pltpu.make_async_copy(a, b, sems.at[i]) for i, (a, b) in enumerate(zip(sources, targets))]


def project(n, lq, first, size, *refs):
    dx_hbm, x_hbm, wq_hbm, wkv_hbm = refs[5:9]
    q_hbm, kv_hbm, own_ref, msg_ref = refs[9:13]
    x0, xs, w, q_out, kv_out, x_sems, w_sems, out_sems = refs[13:21]
    counts, done, placed, table, lens, int_sems = refs[21:]
    ints = int_copies(refs[:5], refs[21:26], int_sems)
    depth = w.shape[0]
    count = xs.shape[0]
    cq = lq * HD
    piece = depth // PIECES
    own_rows = dx_hbm.shape[0]
    step = pl.program_id(0)

    def piece_copies(c):
        part = pl.ds(c * piece, piece)
        return [
            pltpu.make_async_copy(x_hbm.at[pl.ds(0, first), part], x0.at[pl.ds(0, first), part], w_sems.at[0, c]),
            pltpu.make_async_copy(dx_hbm.at[:, part], x0.at[pl.ds(first, own_rows), part], w_sems.at[1, c]),
            pltpu.make_async_copy(wq_hbm.at[part], w.at[part, pl.ds(0, cq)], w_sems.at[2, c]),
            pltpu.make_async_copy(wkv_hbm.at[part], w.at[part, pl.ds(cq, 2 * HD)], w_sems.at[3, c]),
        ]

    def x_copies(k):
        strip = size // STRIPS
        copies = []
        for i in range(STRIPS):
            rows = pl.ds(pl.multiple_of(first + k * size + i * strip, 16), strip)
            copies.append(
                pltpu.make_async_copy(x_hbm.at[rows], xs.at[k, pl.ds(i * strip, strip)], x_sems.at[k, i])
            )
        return copies

    def out_copies(k):
        if isinstance(k, int):
            rows = pl.ds(0, first)
        else:
            rows = pl.ds(pl.multiple_of(first + (k - 1) * size, 64), size)
        return [
            pltpu.make_async_copy(q_out.at[rows], q_hbm.at[rows, pl.ds(0, cq)], out_sems.at[0, k]),
            pltpu.make_async_copy(kv_out.at[rows], q_hbm.at[rows, pl.ds(cq, 2 * HD)], out_sems.at[1, k]),
            pltpu.make_async_copy(kv_out.at[rows], kv_hbm.at[rows], out_sems.at[2, k]),
        ]

    def keep(total, rows):
        q_out[rows, :] = total[:, :cq].astype(jnp.bfloat16)
        kv_out[rows, :] = total[:, cq:].astype(jnp.bfloat16)

    @pl.when(step == 0)
    def _():
        for c in range(AHEAD):
            for copy in piece_copies(c):
                copy.start()
        for copy in ints:
            copy.start()
        total = 0.0
        for c in range(PIECES):
            for copy in piece_copies(c):
                copy.wait()
            if c + AHEAD < PIECES:
                for copy in piece_copies(c + AHEAD):
                    copy.start()
            if c + AHEAD >= PIECES:
                for copy in x_copies(c + AHEAD - PIECES):
                    copy.start()
            part = slice(c * piece, (c + 1) * piece)
            total += dot(x0[:, part], w[part, :])
        keep(total[:first], pl.ds(0, first))
        for copy in out_copies(0):
            copy.start()
        shape = (n * GROUP_ROWS, own_rows)
        to, fro = iota(shape, 0), iota(shape, 1)
        owner, rs = to // GROUP_ROWS, to % GROUP_ROWS
        wanted = owner * ROWS_DEV + row_of(rs) + jnp.where(rs >= ROWS_DEV, ROWS_DEV * n, 0)
        pick = ((fro == wanted) & (rs < STEPS * ROWS_DEV)).astype(jnp.float32).astype(jnp.bfloat16)
        own = dot(pick, total[first:].astype(jnp.bfloat16))
        own_ref[...] = own.astype(jnp.bfloat16)
        for copy in ints:
            copy.wait()
        found = block_of_pages(counts, done, placed, table)
        lane = iota((n * GROUP_ROWS, HD), 1)
        r = row_of(lane % GROUP_ROWS)
        kind = lane // GROUP_ROWS
        facts = jnp.where(
            kind == 0,
            by_row(r, [found[i][0] for i in range(ROWS_DEV)], -1),
            jnp.where(
                kind == 1,
                by_row(r, [found[i][1] for i in range(ROWS_DEV)], -1),
                by_row(r, [lens[i] for i in range(ROWS_DEV)], 0),
            ),
        ).astype(jnp.float32)
        sixth = iota((n * GROUP_ROWS, HD), 0) % GROUP_ROWS == 6
        msg_ref[:, :HD] = jnp.where(sixth, facts, own[:, :HD]).astype(jnp.bfloat16)
        msg_ref[:, HD:] = own[:, HD:].astype(jnp.bfloat16)

    @pl.when((step > 0) & (step + AHEAD <= count))
    def _():
        for copy in x_copies(step + AHEAD - 1):
            copy.start()

    @pl.when(step > 0)
    def _():
        for copy in x_copies(step - 1):
            copy.wait()
        keep(dot(xs[step - 1], w[...]), pl.ds(pl.multiple_of(first + (step - 1) * size, 64), size))
        for copy in out_copies(step):
            copy.start()

    @pl.when(step == count)
    def _():
        for copy in out_copies(0):
            copy.wait()
        for k in range(1, count + 1):
            for copy in out_copies(jnp.int32(k)):
                copy.wait()


def project_all(ints, dx, x, wq, wkv, n, first, size):
    rows, depth = x.shape
    cq, ckv = wq.shape[1], wkv.shape[1]
    lq = cq // HD
    count = (rows - first) // size
    vmem, hbm = pl.BlockSpec(memory_space=VMEM), pl.BlockSpec(memory_space=pl.ANY)
    return pl.pallas_call(
        functools.partial(project, n, lq, first, size),
        grid=(1 + count,),
        in_specs=[hbm] * 9,
        out_specs=[hbm, hbm, vmem, vmem],
        out_shape=[
            jax.ShapeDtypeStruct((rows, WIDE), jnp.bfloat16),
            jax.ShapeDtypeStruct((rows, ckv), jnp.bfloat16),
            jax.ShapeDtypeStruct((n * GROUP_ROWS, cq + ckv), jnp.bfloat16),
            jax.ShapeDtypeStruct((n * GROUP_ROWS, cq + ckv), jnp.bfloat16),
        ],
        scratch_shapes=[
            VMEM((first + dx.shape[0], depth), jnp.bfloat16),
            VMEM((count, size, depth), jnp.bfloat16),
            VMEM((depth, cq + ckv), jnp.bfloat16),
            VMEM((rows, cq), jnp.bfloat16),
            VMEM((rows, ckv), jnp.bfloat16),
            pltpu.SemaphoreType.DMA((count, STRIPS)),
            pltpu.SemaphoreType.DMA((4, PIECES)),
            pltpu.SemaphoreType.DMA((3, count + 1)),
        ]
        + int_scratch(ints),
        compiler_params=pltpu.CompilerParams(vmem_limit_bytes=62 * MIB),
        cost_estimate=pl.CostEstimate(
            flops=2 * rows * depth * (cq + ckv),
            bytes_accessed=2 * (rows + cq + ckv) * depth + 2 * rows * (cq + ckv),
            transcendentals=0,
        ),
        name="project",
    )(*ints, dx, x, wq, wkv)


def attend_prompt(lq, half, counts, q_hbm, *refs):
    o_hbm, qs, kvs, outs, sems = refs[-5:]
    group = lax.axis_index("pool")
    c0, c1 = counts[group, 0], counts[group, 1]
    big = jnp.where(c0 == MOST_BLOCKS, 0, jnp.where(c1 == MOST_BLOCKS, c0, c0 + c1))
    cut = jnp.where(c0 == MOST_BLOCKS, c1, c0)
    loads, stores = [], []
    strip, early = (4, 3) if half == 0 else (1, 5)
    for j in range(0, MOST_BLOCKS, strip):
        block = big + j if half == 0 else j + jnp.where(j >= big, MOST_BLOCKS, 0)
        rows = pl.ds(pl.multiple_of(block * BLOCK_TOKENS, BLOCK_TOKENS), strip * BLOCK_TOKENS)
        here = pl.ds(j * BLOCK_TOKENS, strip * BLOCK_TOKENS)
        cq = lq * HD
        keys_values, queries = q_hbm.at[rows, pl.ds(cq, 2 * HD)], q_hbm.at[rows, pl.ds(0, cq)]
        loads.append(pltpu.make_async_copy(keys_values, kvs.at[here], sems.at[0, j]))
        loads.append(pltpu.make_async_copy(queries, qs.at[here], sems.at[1, j]))
        stores.append(pltpu.make_async_copy(outs.at[here], o_hbm.at[rows], sems.at[2, j]))
    for copy in loads:
        copy.start()
    near = len(loads) // 2
    for copy in loads[:near]:
        copy.wait()
    shape = (BLOCK_TOKENS, lq * BLOCK_TOKENS)
    causal = iota(shape, 0) <= iota(shape, 1) % BLOCK_TOKENS
    tokens = MOST_BLOCKS * BLOCK_TOKENS
    flipped = kvs[: tokens // 2, HD:].T

    def scores_of(j):
        q = qs[j * BLOCK_TOKENS : (j + 1) * BLOCK_TOKENS, :]
        q = jnp.concatenate([q[:, h * HD : (h + 1) * HD] for h in range(lq)], axis=0)
        return dot_t(kvs[: (j + 1) * BLOCK_TOKENS, :HD], q)

    scores = scores_of(0)
    for j in range(MOST_BLOCKS):
        if j + 1 == MOST_BLOCKS // 2:
            for copy in loads[near:]:
                copy.wait()
            flipped = jnp.concatenate([flipped, kvs[tokens // 2 :, HD:].T], axis=1)
        later = scores_of(j + 1) if j + 1 < MOST_BLOCKS else None
        weights = []
        for h in range(lq):
            cols = slice(h * BLOCK_TOKENS, (h + 1) * BLOCK_TOKENS)
            tiles = []
            for i in range(j + 1):
                tile = scores[i * BLOCK_TOKENS : (i + 1) * BLOCK_TOKENS, cols]
                if i == j:
                    tile = jnp.where(causal[:, cols], tile, MASKED)
                elif half == 1:
                    tile = tile + jnp.where((i < cut) & (cut <= j), MASKED, 0.0)
                tiles.append(tile)
            peak = jnp.max(functools.reduce(jnp.maximum, tiles), axis=0, keepdims=True)
            raised = [jnp.exp2((tile - peak) * (SCALE * LOG2E)) for tile in tiles]
            inverse = 1.0 / jnp.sum(functools.reduce(jnp.add, raised), axis=0, keepdims=True)
            weights.append(jnp.concatenate([(t * inverse).astype(jnp.bfloat16) for t in raised], axis=0))
        mixed = dot(flipped[:, : (j + 1) * BLOCK_TOKENS], jnp.concatenate(weights, axis=1))
        mixed = mixed.astype(jnp.bfloat16)
        for h in range(lq):
            part = mixed[:, h * BLOCK_TOKENS : (h + 1) * BLOCK_TOKENS].T
            outs[j * BLOCK_TOKENS : (j + 1) * BLOCK_TOKENS, h * HD : (h + 1) * HD] = part
        scores = later
        if j == early:
            for copy in stores[: (j + 1) // strip]:
                copy.start()
    for copy in stores[(early + 1) // strip :]:
        copy.start()
    for copy in stores:
        copy.wait()


def prompt_attention(counts, q, cq, half, so_far=None):
    rows = q.shape[0]
    hbm = pl.BlockSpec(memory_space=pl.ANY)
    more = () if so_far is None else (so_far,)
    tokens = MOST_BLOCKS * BLOCK_TOKENS
    return pl.pallas_call(
        functools.partial(attend_prompt, cq // HD, half),
        in_specs=[pl.BlockSpec(memory_space=SMEM), hbm] + [hbm] * len(more),
        out_specs=hbm,
        out_shape=jax.ShapeDtypeStruct((rows, cq), jnp.bfloat16),
        scratch_shapes=[
            VMEM((tokens, cq), jnp.bfloat16),
            VMEM((tokens, 2 * HD), jnp.bfloat16),
            VMEM((tokens, cq), jnp.bfloat16),
            pltpu.SemaphoreType.DMA((3, MOST_BLOCKS)),
        ],
        input_output_aliases={2: 0} if more else {},
        compiler_params=pltpu.CompilerParams(vmem_limit_bytes=(62 if half == 0 else 48) * MIB),
        cost_estimate=pl.CostEstimate(flops=2 * rows * rows * cq, bytes_accessed=4 * rows * cq, transcendentals=rows * rows // 2),
        name="long_prompt" if half == 0 else "short_prompts",
    )(counts, q, *more)


def row_head(n, lq, h, hh):
    at = h * GQ + hh
    return at // lq, at % lq


def handed_part(n, lq, kv_ref, own_ref, msg_ref, _, o_ref, __):
    rows = lq * n * GROUP_ROWS
    shape = (rows, HD)
    at_row, lane = iota(shape, 0), iota(shape, 1)
    rs = at_row % GROUP_ROWS
    facts = msg_ref[:, :HD].astype(jnp.float32).reshape(n, GROUP_ROWS, HD)[:, 6:7, :]
    facts = jnp.broadcast_to(facts, (n, GROUP_ROWS, HD)).reshape(n * GROUP_ROWS, HD)
    facts = jnp.concatenate([facts] * lq, axis=0)

    def column(kind):
        return jnp.sum(jnp.where(lane == kind * GROUP_ROWS + rs, facts, 0.0), axis=1, keepdims=True)

    first_block, second_block, length = [column(kind) for kind in range(3)]
    own = own_ref[...]
    queries = jnp.concatenate([own[:, h * HD : (h + 1) * HD] for h in range(lq)], axis=0)
    scores = dot_t(queries, kv_ref[:, :HD]) * SCALE
    lane_f = lane.astype(jnp.float32)
    parts = []
    for b in range(NBLK):
        limit = jnp.where(
            first_block == b, length, jnp.where(second_block == b, length - BLOCK_TOKENS, 0.0)
        )
        part = scores[:, b * BLOCK_TOKENS : (b + 1) * BLOCK_TOKENS]
        parts.append(jnp.where(lane_f < limit, part, MASKED))
    scores = jnp.concatenate(parts, axis=1)
    top = jnp.max(scores, axis=1, keepdims=True)
    raised = jnp.exp(scores - top)
    total = jnp.sum(raised, axis=1, keepdims=True)
    near = raised.astype(jnp.bfloat16)
    rest = (raised - near.astype(jnp.float32)).astype(jnp.bfloat16)
    values = kv_ref[:, HD:]
    mixed = dot(jnp.concatenate([near, rest], axis=0), values)
    mixed = (mixed[:rows] + mixed[rows:]).reshape(lq * n, GROUP_ROWS, HD)

    def line(col):
        spread = jnp.where(lane == rs, col, 0.0).reshape(lq * n, GROUP_ROWS, HD)
        return jnp.sum(spread, axis=1, keepdims=True)

    rs3 = rs.reshape(lq * n, GROUP_ROWS, HD)
    mixed = jnp.where(rs3 == 6, line(top), jnp.where(rs3 == 7, line(total), mixed))
    for h in range(lq):
        o_ref[:, h * GROUP_ROWS : (h + 1) * GROUP_ROWS, :] = mixed[h * n : (h + 1) * n]


def handed_attention(kv, own, msgs, prompt_attn, n, lq):
    rows = lq * n * GROUP_ROWS
    vmem, hbm = pl.BlockSpec(memory_space=VMEM), pl.BlockSpec(memory_space=pl.ANY)
    return pl.pallas_call(
        functools.partial(handed_part, n, lq),
        in_specs=[vmem] * 3 + [hbm],
        out_specs=[vmem, hbm],
        out_shape=[
            jax.ShapeDtypeStruct((n, lq * GROUP_ROWS, HD), jnp.float32),
            jax.ShapeDtypeStruct(prompt_attn.shape, prompt_attn.dtype),
        ],
        input_output_aliases={3: 1},
        compiler_params=pltpu.CompilerParams(vmem_limit_bytes=24 * MIB),
        cost_estimate=pl.CostEstimate(flops=6 * rows * HD * PTOK, bytes_accessed=2 * MIB, transcendentals=rows * PTOK),
        name="handed_attention",
    )(kv, own, msgs, prompt_attn)


def owner_part(n, lq, *refs):
    cache, msgs, handed, o_ref, slot_row, slot_limit = refs[5:11]
    counts, done, placed, table, lens, int_sems = refs[11:]
    ints = int_copies(refs[:5], refs[11:16], int_sems)
    for copy in ints:
        copy.start()
    held = msgs[...].astype(jnp.float32)

    def tile(t, k):
        return held[t * GROUP_ROWS : (t + 1) * GROUP_ROWS, k * HD : (k + 1) * HD]

    groups = QH
    rows = groups * GROUP_ROWS
    span = GQ * GROUP_ROWS
    queries, keys, values = [], [], []
    for h in range(KVH):
        for hh in range(GQ):
            t, at = row_head(n, lq, h, hh)
            queries.append(tile(t, at))
        t, _ = row_head(n, lq, h, 0)
        keys += [tile(t, lq)] * GQ
        values.append(tile(t, lq + 1))
    queries = jnp.concatenate(queries, axis=0)
    earlier = jnp.concatenate([pltpu.roll(key, ROWS_DEV, 0) for key in keys], axis=0)
    keys = jnp.concatenate(keys, axis=0)
    at_row, lane = iota((rows, HD), 0), iota((rows, HD), 1)
    r = row_of(at_row % GROUP_ROWS)
    rounded = queries.astype(jnp.bfloat16)
    now = jnp.sum(queries * keys, axis=1, keepdims=True) * SCALE
    before = jnp.sum(queries * earlier, axis=1, keepdims=True) * SCALE
    rs1 = iota((rows, 1), 0) % GROUP_ROWS
    before = jnp.where((rs1 >= ROWS_DEV) & (rs1 < STEPS * ROWS_DEV), before, MASKED)
    mixed = handed[...].reshape(groups, GROUP_ROWS, HD)
    shape = (groups, GROUP_ROWS, HD)
    mine = iota(shape, 1) == iota(shape, 2)

    def column(at):
        line = jnp.broadcast_to(mixed[:, at : at + 1, :], shape)
        return jnp.sum(jnp.where(mine, line, 0.0), axis=2, keepdims=True).reshape(rows, 1)

    other_peak, other_total = column(6), column(7)
    for copy in ints:
        copy.wait()
    found = block_of_pages(counts, done, placed, table)
    for k in range(ROWS_DEV):
        for p in range(PAGES):
            slot_row[table[p, k]] = jnp.int32(k)
            slot_limit[table[p, k]] = jnp.where(found[k][p] < 0, lens[k] - p * BLOCK_TOKENS, 0)
    scores = jnp.concatenate(
        [dot_t(rounded[h * span : (h + 1) * span], cache[:, 2 * h * HD : (2 * h + 1) * HD]) for h in range(KVH)],
        axis=0,
    )
    parts = []
    for slot in range(DEVICE_SLOTS):
        part = scores[:, slot * BLOCK_TOKENS : (slot + 1) * BLOCK_TOKENS]
        usable = (r == slot_row[slot]) & (lane < slot_limit[slot])
        parts.append(jnp.where(usable, part * SCALE, MASKED))
    scores = jnp.concatenate(parts, axis=1)
    peak = jnp.maximum(jnp.max(scores, axis=1, keepdims=True), jnp.maximum(now, before))
    peak = jnp.maximum(peak, other_peak)
    raised, now, before = jnp.exp(scores - peak), jnp.exp(now - peak), jnp.exp(before - peak)
    other = jnp.exp(other_peak - peak)
    inverse = 1.0 / (jnp.sum(raised, axis=1, keepdims=True) + now + before + other * other_total)
    weights = (raised * inverse).astype(jnp.bfloat16)
    now = (now * inverse).astype(jnp.bfloat16).astype(jnp.float32)
    before = (before * inverse).astype(jnp.bfloat16).astype(jnp.float32)
    mixed = mixed.reshape(rows, HD) * (other * inverse)
    out = []
    for h in range(KVH):
        part = slice(h * span, (h + 1) * span)
        own = mixed[part] + dot(weights[part], cache[:, (2 * h + 1) * HD : (2 * h + 2) * HD])
        last = pltpu.roll(values[h], ROWS_DEV, 0)
        for hh in range(GQ):
            some = slice(h * span + hh * GROUP_ROWS, h * span + (hh + 1) * GROUP_ROWS)
            line = own[hh * GROUP_ROWS : (hh + 1) * GROUP_ROWS]
            out.append(line + now[some] * values[h] + before[some] * last)
    out = jnp.concatenate(out, axis=1)
    for k in range(ROWS_DEV):
        steps = [out[s * ROWS_DEV + k : s * ROWS_DEV + k + 1] for s in range(STEPS)]
        o_ref[k] = jnp.concatenate(steps, axis=0).astype(jnp.bfloat16)


def decode_attention(ints, cache, msgs, parts, n, lq):
    vmem, hbm = pl.BlockSpec(memory_space=VMEM), pl.BlockSpec(memory_space=pl.ANY)
    rows = QH * GROUP_ROWS
    return pl.pallas_call(
        functools.partial(owner_part, n, lq),
        in_specs=[hbm] * 5 + [vmem] * 3,
        out_specs=vmem,
        out_shape=jax.ShapeDtypeStruct((ROWS_DEV, STEPS, QH * HD), jnp.bfloat16),
        scratch_shapes=[
            SMEM((DEVICE_SLOTS,), jnp.int32),
            SMEM((DEVICE_SLOTS,), jnp.int32),
        ]
        + int_scratch(ints),
        compiler_params=pltpu.CompilerParams(vmem_limit_bytes=40 * MIB),
        cost_estimate=pl.CostEstimate(flops=4 * rows * HD * 768, bytes_accessed=4 * MIB, transcendentals=rows * 768),
        name="decode_attention",
    )(*ints, cache, msgs, parts)


def local(
    prompt_x,
    q_weight,
    kv_weight,
    prompt_blocks,
    finished,
    placement,
    page_table,
    row_lens,
    kv_cache,
    decode_x,
):
    n = lax.axis_size("tp")
    lq = q_weight.shape[1] // HD
    share = GQ // lq
    if share > 1:
        sets = [[k * share + i for i in range(share)] for k in range(n // share)]
        kv_weight = lax.all_gather(kv_weight, "tp", axis=1, tiled=True, axis_index_groups=sets)
    cache = kv_cache.reshape(-1, kv_cache.shape[2])
    dx = decode_x.reshape(-1, decode_x.shape[2])
    placement = placement.transpose(0, 2, 1)
    page_table = page_table.transpose(1, 0)
    ints = (prompt_blocks, finished, placement, page_table, row_lens)
    first, size = 256, 448
    q, kv, own, msgs = project_all(ints, dx, prompt_x, q_weight, kv_weight, n, first, size)
    kv_other = lax.ppermute(kv, "pool", [(0, 1), (1, 0)])
    msgs = lax.all_to_all(msgs, "tp", split_axis=0, concat_axis=0, tiled=True)
    prompt_attn = prompt_attention(prompt_blocks, q, q_weight.shape[1], 0)
    handed, prompt_attn = handed_attention(kv_other, own, msgs, prompt_attn, n, lq)
    parts = lax.all_to_all(handed, "tp", split_axis=0, concat_axis=0, tiled=True)
    prompt_attn = prompt_attention(prompt_blocks, q, q_weight.shape[1], 1, prompt_attn)
    decode_attn = decode_attention(ints, cache, msgs, parts, n, lq)
    return prompt_attn, decode_attn.transpose(1, 0, 2)


def solution(mesh):
    return jax.shard_map(
        local,
        mesh=mesh,
        in_specs=(
            P(("rep", "pool"), None),
            P(None, "tp"),
            P(None, "tp"),
            P("rep", None),
            P("rep", None),
            P("rep", None, None),
            P(("rep", "pool", "tp"), None),
            P(("rep", "pool", "tp")),
            P(("rep", "pool", "tp"), None, None),
            P(None, ("rep", "pool"), None),
        ),
        out_specs=(P(("rep", "pool"), "tp"), P(None, ("rep", "pool", "tp"), None)),
        check_vma=False,
    )
```
